32 devices in a mesh: seq: 8 (over z, x), tp: 4 (over y, core).
Axes of the slice: x: 2, y: 2, z: 4, core: 2. Of those that a mesh axis runs over, the one named last changes fastest.
Arguments:
- tokens: bfloat16 [4, 4096, 768], P(None, 'seq'), may hold values from -6 to 6
- query_weight: bfloat16 [768, 768], P(None, 'tp'), may hold values from -0.21875 to 0.21875
- query_bias: bfloat16 [12, 64], P('tp'), may hold values from -4 to 4
- key_weight: bfloat16 [768, 768], P(None, 'tp'), may hold values from -0.21875 to 0.21875
- value_weight: bfloat16 [768, 768], P(None, 'tp'), may hold values from -0.21875 to 0.21875
- value_bias: bfloat16 [12, 64], P('tp'), may hold values from -4 to 4
- conv_weight: bfloat16 [12, 33], P('tp'), may hold values from -1 to 1
- output_weight: bfloat16 [768, 768], P('tp'), may hold values from -0.21875 to 0.21875
- output_bias: bfloat16 [768], replicated, may hold values from -3 to 3
- first_gain: bfloat16 [768], replicated, may hold values from 0.5 to 1.5
- first_shift: bfloat16 [768], replicated, may hold values from -3 to 3
- up_weight: bfloat16 [768, 3072], P(None, 'tp'), may hold values from -0.21875 to 0.21875
- up_bias: bfloat16 [3072], P('tp'), may hold values from -6 to 6
- down_weight: bfloat16 [3072, 768], P('tp'), may hold values from -0.109375 to 0.109375
- down_bias: bfloat16 [768], replicated, may hold values from -3 to 3
- second_gain: bfloat16 [768], replicated, may hold values from 0.5 to 1.5
- second_shift: bfloat16 [768], replicated, may hold values from -3 to 3
- segment_sizes: int32 [4, 8, 64], replicated, may hold values from 0 to 96, as said below
- cotangent: bfloat16 [4, 4096, 768], P(None, 'seq'), may hold values from -6 to 6
Outputs:
- layer_out: bfloat16 [4, 4096, 768], P(None, 'seq')
- grad_tokens: float32 [4, 4096, 768], P(None, 'seq')
- grad_query_weight: float32 [768, 768], P('seq', 'tp')
- grad_query_bias: float32 [12, 64], P('tp', 'seq')
- grad_key_weight: float32 [768, 768], P('seq', 'tp')
- grad_value_weight: float32 [768, 768], P('seq', 'tp')
- grad_value_bias: float32 [12, 64], P('tp')
- grad_conv_weight: float32 [12, 33], P('tp')
- grad_output_weight: float32 [768, 768], P('tp', 'seq')
- grad_output_bias: float32 [768], replicated
- grad_first_gain: float32 [768], replicated
- grad_first_shift: float32 [768], replicated
- grad_up_weight: float32 [768, 3072], P('seq', 'tp')
- grad_up_bias: float32 [3072], P('tp')
- grad_down_weight: float32 [3072, 768], P('tp', 'seq')
- grad_down_bias: float32 [768], replicated
- grad_second_gain: float32 [768], replicated
- grad_second_shift: float32 [768], replicated
The draws below stay inside these ranges and needn't reach their ends.
Inputs may be any that keep to these rules, and one draw needn't show every extreme that they name: `segment_sizes`: row by row, the sizes of the 64 consecutive landmark segments of each of up to 8 items packed in order; a row's sizes add up to 4096; each item holds a multiple of 512 tokens and each of its segments at least one; unused item places come last and hold zeros; for every g below 1, some row r + g is one single item.
All inputs are finite; a program needn't handle non-finite values.
Results may differ from the reference program's by a relative error of at most 0.023.
Values may be sent and summed in bfloat16 or wider, within the bound.
No kernel may reach another device: no remote copies, remote signals or barrier semaphores. Data moves between devices by JAX's collectives and lax.ppermute only.
A program may use at most 192 MiB of HBM per device.

```python
import math
import jax
import jax.numpy as jnp
from jax import lax

D = 768
HEADS = 12
FF = 3072
LANDMARKS = 64
HEAD_DIM = 64
TAPS = 33
SWEEPS = 6
SPAN = 4096
BASE_LEN = 512
STACK = 4
GROUPS = 1
ROWS = 4
ITEM_CAP = 8


def draw_tokens(key, part):
    key = jax.random.fold_in(key, 11)
    keys = jax.random.split(key, 12)
    position = jnp.arange(SPAN, dtype=jnp.float32)[None, None, :, None]
    smooth = jnp.zeros((STACK, GROUPS, SPAN, D), jnp.float32)
    for wave in range(3):
        rates = jnp.exp(jax.random.uniform(keys[3 * wave], (1, 1, 1, D), minval=math.log(1.0 / 1024.0), maxval=math.log(1.0 / 64.0)))
        phases = jax.random.uniform(keys[3 * wave + 1], (STACK, GROUPS, 1, D), minval=-math.pi, maxval=math.pi)
        heights = 0.5 * jax.random.normal(keys[3 * wave + 2], (1, 1, 1, D))
        smooth = smooth + heights * jnp.sin(2.0 * math.pi * rates * position + phases)
    smooth = smooth.reshape(STACK, GROUPS * SPAN, D)
    rough = 0.8 * jax.random.normal(keys[9], (STACK, GROUPS * SPAN, D))
    return jnp.clip(smooth + rough, -6.0, 6.0).astype(jnp.bfloat16)


def draw_segment_sizes(key, part):
    key = jax.random.fold_in(key, 23)
    keys = jax.random.split(key, 4)
    whole_stack = jax.random.randint(keys[0], (GROUPS,), 0, STACK)
    cut_stack = (whole_stack + 1 + jax.random.randint(keys[1], (GROUPS,), 0, max(STACK - 1, 1))) % STACK
    row_number = jnp.arange(ROWS, dtype=jnp.int32)
    row_stack = row_number // GROUPS
    row_group = row_number % GROUPS
    group_hot = row_group[:, None] == jnp.arange(GROUPS, dtype=jnp.int32)[None, :]
    whole_here = jnp.sum(jnp.where(group_hot, whole_stack[None, :], 0), axis=1)
    cut_here = jnp.sum(jnp.where(group_hot, cut_stack[None, :], 0), axis=1)
    is_whole = (row_stack == whole_here)[:, None]
    is_cut = (row_stack == cut_here)[:, None]
    cuts = jax.random.randint(keys[2], (ROWS, ITEM_CAP - 1), 0, 4) > 0
    cuts = jnp.where(is_cut, True, cuts)
    cuts = jnp.where(is_whole, False, cuts)
    starts = jnp.concatenate([jnp.ones((ROWS, 1), jnp.int32), cuts.astype(jnp.int32)], axis=1)
    owner = jnp.cumsum(starts, axis=1) - 1
    blocks = jnp.sum((owner[:, :, None] == jnp.arange(ITEM_CAP, dtype=jnp.int32)[None, None, :]).astype(jnp.int32), axis=1)
    quota = (blocks * (BASE_LEN // LANDMARKS))[:, :, None]
    halves = quota // 2
    raw = jax.random.randint(keys[3], (ROWS, ITEM_CAP, LANDMARKS), 0, 1 << 20)
    lift = raw % (halves + 1)
    row_full = is_whole[:, :, None]
    mark_number = jnp.arange(LANDMARKS, dtype=jnp.int32)[None, None, :]
    lift = jnp.where(row_full & (mark_number == 0), halves, lift)
    lift = jnp.where(row_full & (mark_number == LANDMARKS - 1), 0, lift)
    return quota + lift - jnp.roll(lift, 1, axis=2)


def steps_of(key, dims, pieces, smallest, high):
    level, own = 1.0, jax.random.fold_in(key, 6)
    for dim, parts in pieces:
        draws = jnp.exp(jax.random.uniform(jax.random.fold_in(own, dim), (parts,), jnp.float32, smallest / len(pieces), high / len(pieces)))
        level = level * jnp.repeat(draws, dims[dim] // parts).reshape([-1 if axis == dim else 1 for axis in range(len(dims))])
    return level


def bell_draw(rng, dims, scale, limit, cuts=(), kind=jnp.bfloat16):
    values = jax.random.normal(rng, dims, jnp.float32) * scale
    if len(cuts) > 0:
        values = steps_of(rng, dims, cuts, -0.22, 0.18) * values
    return jnp.clip(values, min=-limit, max=limit).astype(kind)


def setup_inputs(seed: int = 0) -> dict:
    splits = jax.random.split(jax.random.key(seed), 20)
    return {
        "tokens": draw_tokens(jax.random.fold_in(splits[19], 71), 0),
        "query_weight": bell_draw(splits[1], (D, D), D ** -0.5, 0.21875, ((1, 4),)),
        "query_bias": bell_draw(splits[2], (HEADS, HEAD_DIM), 0.3, 4.0, ((0, 4),)),
        "key_weight": bell_draw(splits[3], (D, D), D ** -0.5, 0.21875, ((1, 4),)),
        "value_weight": bell_draw(splits[4], (D, D), D ** -0.5, 0.21875, ((1, 4),)),
        "value_bias": bell_draw(splits[5], (HEADS, HEAD_DIM), 0.3, 4.0, ((0, 4),)),
        "conv_weight": bell_draw(splits[6], (HEADS, TAPS), TAPS ** -0.5, 1.0, ((0, 4),)),
        "output_weight": bell_draw(splits[7], (D, D), D ** -0.5, 0.21875, ((0, 4),)),
        "output_bias": bell_draw(splits[8], (D,), 0.2, 3.0),
        "first_gain": jnp.clip(1.0 + 0.1 * jax.random.normal(splits[9], (D,), jnp.float32), 0.5, 1.5).astype(jnp.bfloat16),
        "first_shift": bell_draw(splits[10], (D,), 0.2, 3.0),
        "up_weight": bell_draw(splits[11], (D, FF), D ** -0.5, 0.21875, ((1, 4),)),
        "up_bias": bell_draw(splits[12], (FF,), 0.5, 6.0, ((0, 4),)),
        "down_weight": bell_draw(splits[13], (FF, D), FF ** -0.5, 0.109375, ((0, 4),)),
        "down_bias": bell_draw(splits[14], (D,), 0.2, 3.0),
        "second_gain": jnp.clip(1.0 + 0.1 * jax.random.normal(splits[15], (D,), jnp.float32), 0.5, 1.5).astype(jnp.bfloat16),
        "second_shift": bell_draw(splits[16], (D,), 0.2, 3.0),
        "segment_sizes": draw_segment_sizes(jax.random.fold_in(splits[19], 71), 0),
        "cotangent": bell_draw(splits[18], (STACK, GROUPS * SPAN, D), 1.0, 6.0, ((1, 8),)),
    }


highest = lax.Precision.HIGHEST
epsilon = 1e-05
very_negative = -1e+30

@jax.custom_vjp
def low(v):
    return lax.optimization_barrier(v.astype(jnp.bfloat16)).astype(jnp.float32)

@jax.custom_vjp
def low_back(v):
    return v

def low_keep(v):
    return (low(v), None)

def low_pass(kept, grad):
    return (grad,)

def back_keep(v):
    return (v, None)

def back_low(kept, grad):
    return (low(grad),)
low.defvjp(low_keep, low_pass)
low_back.defvjp(back_keep, back_low)

def segment_index(sizes_row, positions):
    ends = jnp.cumsum(sizes_row.reshape(-1))
    return lax.optimization_barrier(jnp.sum((ends[None, :] <= positions[:, None]).astype(jnp.int32), axis=1))

def softmax_last(scores):
    powers = jnp.exp(scores - lax.optimization_barrier(jnp.max(scores, axis=-1, keepdims=True)))
    return powers / lax.optimization_barrier(jnp.sum(powers, axis=-1, keepdims=True))

def masked_softmax(scores, allowed):
    top = lax.optimization_barrier(jnp.max(jnp.where(allowed, scores, very_negative), axis=-1, keepdims=True))
    powers = jnp.exp(jnp.where(allowed, scores - top, very_negative))
    return powers / lax.optimization_barrier(jnp.sum(powers, axis=-1, keepdims=True))

def floored_softmax(scores, allowed):
    top = lax.optimization_barrier(jnp.max(jnp.where(allowed, scores, very_negative), axis=-1, keepdims=True))
    powers = jnp.exp(jnp.where(allowed, scores - top, very_negative))
    return powers / jnp.maximum(lax.optimization_barrier(jnp.sum(powers, axis=-1, keepdims=True)), 1.0)

def newton_inverse(kernel):
    size = kernel.shape[-1]
    column_sums = lax.optimization_barrier(jnp.sum(kernel, axis=-2))
    bound = jnp.sqrt(lax.optimization_barrier(jnp.sum(column_sums * column_sums, axis=-1)))[..., None, None]
    identity = jnp.eye(size, dtype=kernel.dtype)
    inverse = jnp.swapaxes(kernel, -1, -2) / bound
    for sweep in range(SWEEPS):
        product = jnp.matmul(kernel, inverse, precision=highest)
        inner = 7.0 * identity - product
        inner = 15.0 * identity - jnp.matmul(product, inner, precision=highest)
        inner = 13.0 * identity - jnp.matmul(product, inner, precision=highest)
        inverse = 0.25 * jnp.matmul(inverse, inner, precision=highest)
    return inverse

def layer_norm(values, gain, shift):
    centred = values - lax.optimization_barrier(jnp.mean(values, axis=-1, keepdims=True))
    spread = lax.optimization_barrier(jnp.mean(centred * centred, axis=-1, keepdims=True))
    return centred * lax.rsqrt(spread + epsilon) * gain + shift

def gelu(values):
    return 0.5 * values * (1.0 + lax.erf(values * 0.7071067811865476))

def split_heads(array):
    return array.reshape(array.shape[0], HEADS, HEAD_DIM)

def row_forward(tokens, sizes_row, params):
    query_weight, query_bias, key_weight, value_weight, value_bias, conv_weight, output_weight, output_bias, first_gain, first_shift, up_weight, up_bias, down_weight, down_bias, second_gain, second_shift = params
    slots = ITEM_CAP * LANDMARKS
    reach = TAPS // 2
    scale = HEAD_DIM ** (-0.25)
    positions = jnp.arange(SPAN, dtype=jnp.int32)
    token_slot = segment_index(sizes_row, positions)
    token_item = token_slot // LANDMARKS
    slot_item = jnp.arange(slots, dtype=jnp.int32) // LANDMARKS
    counts = jnp.maximum(sizes_row.reshape(-1), 1).astype(jnp.float32)[:, None]
    query = low(low_back(scale * (jnp.dot(tokens, query_weight, precision=highest) + query_bias.reshape(-1))))
    keys = low(low_back(scale * jnp.dot(tokens, key_weight, precision=highest)))
    values = low(low_back(jnp.dot(tokens, value_weight, precision=highest) + value_bias.reshape(-1)))
    query_land = low(jax.ops.segment_sum(query, token_slot, num_segments=slots) / counts)
    key_land = low(jax.ops.segment_sum(keys, token_slot, num_segments=slots) / counts)
    query_heads = split_heads(query)
    key_heads = split_heads(keys)
    value_heads = split_heads(values)
    land_query = split_heads(query_land)
    land_key = split_heads(key_land)
    same = token_item[:, None] == slot_item[None, :]
    token_scores = low_back(jnp.einsum('thd,lhd->htl', query_heads, land_key, precision=highest))
    token_weights = masked_softmax(token_scores, same[None])
    key_scores = low_back(jnp.einsum('lhd,thd->hlt', land_query, key_heads, precision=highest))
    key_weights = floored_softmax(key_scores, same.T[None])
    mixed_values = low_back(jnp.einsum('hlt,thd->hld', low(key_weights), value_heads, precision=highest))
    block_query = land_query.reshape(ITEM_CAP, LANDMARKS, HEADS, HEAD_DIM)
    block_key = land_key.reshape(ITEM_CAP, LANDMARKS, HEADS, HEAD_DIM)
    kernel = softmax_last(jnp.einsum('ilhd,imhd->hilm', block_query, block_key, precision=highest))
    inverse = newton_inverse(kernel)
    block_mixed = mixed_values.reshape(HEADS, ITEM_CAP, LANDMARKS, HEAD_DIM)
    mixed_land = low(jnp.einsum('hilm,himd->hild', inverse, block_mixed, precision=highest))
    mixed_land = mixed_land.reshape(HEADS, slots, HEAD_DIM)
    nystrom = jnp.einsum('htl,hld->thd', low(token_weights), mixed_land, precision=highest)
    padded_values = jnp.pad(value_heads, ((reach, reach), (0, 0), (0, 0)))
    padded_pos = jnp.arange(SPAN + 2 * reach, dtype=jnp.int32) - reach
    inside = (padded_pos >= 0) & (padded_pos < SPAN)
    padded_item = segment_index(sizes_row, jnp.clip(padded_pos, 0, SPAN - 1)) // LANDMARKS
    convolved = jnp.zeros_like(nystrom)
    for offset in range(TAPS):
        nearby = padded_values[offset:offset + SPAN]
        keep = inside[offset:offset + SPAN] & (padded_item[offset:offset + SPAN] == token_item)
        convolved = convolved + jnp.where(keep[:, None, None], nearby, 0.0) * conv_weight[None, :, offset, None]
    context = low(low_back((nystrom + convolved).reshape(SPAN, D)))
    attention = low_back(jnp.dot(context, output_weight, precision=highest) + output_bias)
    first_out = layer_norm(tokens + attention, first_gain, first_shift)
    hidden = low_back(jnp.dot(low(first_out), up_weight, precision=highest) + up_bias)
    active = low(gelu(hidden))
    feed = low_back(jnp.dot(active, down_weight, precision=highest) + down_bias)
    return layer_norm(first_out + feed, second_gain, second_shift)

def forward(tokens, segment_sizes, params):
    row_tokens = tokens.reshape(ROWS, SPAN, D)

    def one_row(pair):
        return row_forward(pair[0], pair[1], params)
    result = lax.map(jax.checkpoint(one_row), (row_tokens, segment_sizes))
    return result.reshape(STACK, GROUPS * SPAN, D)

def reference(tokens, query_weight, query_bias, key_weight, value_weight, value_bias, conv_weight, output_weight, output_bias, first_gain, first_shift, up_weight, up_bias, down_weight, down_bias, second_gain, second_shift, segment_sizes, cotangent):
    weights = (query_weight, query_bias, key_weight, value_weight, value_bias, conv_weight, output_weight, output_bias, first_gain, first_shift, up_weight, up_bias, down_weight, down_bias, second_gain, second_shift)
    weights = tuple((array.astype(jnp.float32) for array in weights))

    def whole(inputs, *params):
        return forward(inputs, segment_sizes, params)
    layer_out, pullback = jax.vjp(whole, tokens.astype(jnp.float32), *weights)
    grads = pullback(cotangent.astype(jnp.float32))
    return (layer_out.astype(jnp.bfloat16), grads[0], grads[1], grads[2], grads[3], grads[4], grads[5], grads[6], grads[7], grads[8], grads[9], grads[10], grads[11], grads[12], grads[13], grads[14], grads[15], grads[16])
```

```python
import jax
import jax.numpy as jnp
from jax import lax
from jax.sharding import PartitionSpec as P

HEAD_DIM = 64
TAPS = 33
SWEEPS = 6
SPAN = 4096
LANES = 128


highest = lax.Precision.HIGHEST
epsilon = 1e-05
very_negative = -1e30
f32 = jnp.float32
bf16 = jnp.bfloat16


def swap(value, axis, step):
    return lax.ppermute(value, axis, [(i, i ^ step) for i in range(lax.axis_size(axis))])


def dot(a, b):
    return jnp.dot(a, b, preferred_element_type=f32)


def outer(a, b):
    return lax.dot_general(a, b, (((0,), (0,)), ((), ())), preferred_element_type=f32)


def dot_t(a, b):
    return lax.dot_general(a, b, (((1,), (1,)), ((), ())), preferred_element_type=f32)


def rounded(value):
    return lax.reduce_precision(value, 8, 7)


def count_below(ends, positions):
    return jnp.sum((ends[None, :] <= positions[:, None]).astype(jnp.int32), axis=1)


def spread_shards(shard):
    core = swap(shard, "tp", 1)
    far = swap(shard, "tp", 2)
    return (shard, core, far, swap(far, "tp", 1))


def segment_exchange(state, index, item_of, levels, pack, unpack, merge):
    own_item = item_of[index]
    own = left_edge = right_edge = state
    for level in range(levels):
        size = 1 << level
        start = (index >> level) << level
        other = start ^ size
        is_left = (index & size) == 0

        def choose(a, b):
            return jax.tree.map(lambda x, y: jnp.where(is_left, x, y), a, b)

        far_edge_item = jnp.where(is_left, item_of[other], item_of[other + size - 1])
        far_outer_item = jnp.where(is_left, item_of[other + size - 1], item_of[other])
        facing_item = jnp.where(is_left, item_of[start + size - 1], item_of[start])
        outer_item = jnp.where(is_left, item_of[start], item_of[start + size - 1])
        last = level == levels - 1
        if level == 0:
            facing = outer_edge = state
            got = unpack(swap(pack(state), "seq", size))
            far_facing = far_outer = got
        else:
            facing = choose(right_edge, left_edge)
            outer_edge = choose(left_edge, right_edge)
            if last:
                far_facing = far_outer = unpack(swap(pack(facing), "seq", size))
            else:
                got = swap((pack(facing), pack(outer_edge)), "seq", size)
                far_facing, far_outer = unpack(got[0]), unpack(got[1])
        own = merge(own, far_facing, own_item == far_edge_item)
        if not last:
            near = merge(outer_edge, far_facing, outer_item == far_edge_item)
            away = merge(far_outer, facing, far_outer_item == facing_item)
            left_edge = choose(near, away)
            right_edge = choose(away, near)
    return own


def add_where(a, b, use):
    return a + jnp.where(use, b, 0.0)


def segment_sum(value, index, item_of, levels):
    return segment_exchange(
        value,
        index,
        item_of,
        levels,
        lambda v: v.astype(bf16),
        lambda v: v.astype(f32),
        add_where,
    )


def soft_pack(state):
    mixed, top, total = state
    high = rounded(total)
    low = total - high
    heads = top.shape[1]
    pad = jnp.zeros((top.shape[0], LANES - 3 * heads), f32)
    return jnp.concatenate((mixed, top, high, low, pad), axis=1).astype(bf16)


def soft_unpack(heads, width):
    def unpack(message):
        message = message.astype(f32)
        return (
            message[:, :width],
            message[:, width : width + heads],
            message[:, width + heads : width + 2 * heads]
            + message[:, width + 2 * heads : width + 3 * heads],
        )

    return unpack


def soft_merge(a, b, use):
    mixed_a, top_a, total_a = a
    mixed_b, top_b, total_b = b
    top = jnp.where(use, jnp.maximum(top_a, top_b), top_a)
    scale_a = jnp.exp(top_a - top)
    scale_b = jnp.where(use, jnp.exp(jnp.where(use, top_b - top, 0.0)), 0.0)
    wide_a = jnp.repeat(scale_a, HEAD_DIM, axis=1)
    wide_b = jnp.repeat(scale_b, HEAD_DIM, axis=1)
    return (mixed_a * wide_a + mixed_b * wide_b, top, total_a * scale_a + total_b * scale_b)


def scatter_weight(blocks, seq_index):
    blocks = [b.astype(bf16) for b in blocks]
    got = swap((blocks[1], blocks[3]), "tp", 1)
    mine = blocks[0].astype(f32) + got[0].astype(f32)
    away = (blocks[2].astype(f32) + got[1].astype(f32)).astype(bf16)
    total = mine + swap(away, "tp", 2).astype(f32)
    count = lax.axis_size("seq")
    rows, columns = total.shape
    size = 1
    total = total.reshape(count, rows // count, columns)
    while size < count:
        bit = (seq_index // size) % 2
        view = total.reshape(total.shape[0] // 2, 2, rows // count, columns)
        keep = lax.dynamic_index_in_dim(view, bit, axis=1, keepdims=False)
        send = lax.dynamic_index_in_dim(view, 1 - bit, axis=1, keepdims=False).astype(bf16)
        total = keep + swap(send, "seq", size).astype(f32)
        size *= 2
    return total[0]


def sum_everywhere(value):
    for axis in ("tp", "seq"):
        size = 1
        while size < lax.axis_size(axis):
            value = value + swap(value, axis, size)
            size *= 2
    return value


def newton_inverse(kernel):
    size = kernel.shape[-1]
    column_sums = jnp.sum(kernel, axis=-2)
    bound = jnp.sqrt(jnp.sum(column_sums * column_sums, axis=-1))[..., None, None]
    identity = jnp.eye(size, dtype=kernel.dtype)
    inverse = jnp.swapaxes(kernel, -1, -2) / bound
    for sweep in range(SWEEPS):
        product = jnp.matmul(kernel, inverse, precision=highest)
        inner = 7.0 * identity - product
        inner = 15.0 * identity - jnp.matmul(product, inner, precision=highest)
        inner = 13.0 * identity - jnp.matmul(product, inner, precision=highest)
        inverse = 0.25 * jnp.matmul(inverse, inner, precision=highest)
    return inverse


def landmark_core(land_query, land_key, mixed_values):
    scores = jnp.einsum("mhd,nhd->hmn", land_query, land_key, precision=highest)
    powers = jnp.exp(scores - jnp.max(scores, axis=-1, keepdims=True))
    kernel = powers / jnp.sum(powers, axis=-1, keepdims=True)
    return jnp.einsum("hmn,hnd->hmd", newton_inverse(kernel), mixed_values, precision=highest)


def layer_norm(values, gain, shift):
    centred = values - jnp.mean(values, axis=-1, keepdims=True)
    inverse = lax.rsqrt(jnp.mean(centred * centred, axis=-1, keepdims=True) + epsilon)
    normed = centred * inverse
    return (normed * gain + shift, normed, inverse)


def norm_back(upstream, gain, normed, inverse):
    scaled = upstream * gain
    centred = scaled - jnp.mean(scaled, axis=-1, keepdims=True)
    return (centred - normed * jnp.mean(scaled * normed, axis=-1, keepdims=True)) * inverse


def gelu(values):
    return 0.5 * values * (1.0 + lax.erf(values * 0.7071067811865476))


def per_device(
    tokens,
    query_weight,
    query_bias,
    key_weight,
    value_weight,
    value_bias,
    conv_weight,
    output_weight,
    output_bias,
    first_gain,
    first_shift,
    up_weight,
    up_bias,
    down_weight,
    down_bias,
    second_gain,
    second_shift,
    segment_sizes,
    cotangent,
):
    rows, width, model = tokens.shape
    channels = query_weight.shape[1]
    ranks = lax.axis_size("tp")
    own_heads = channels // HEAD_DIM
    heads = ranks * own_heads
    hidden_units = up_weight.shape[1]
    items = segment_sizes.shape[1]
    marks = segment_sizes.shape[2]
    reach = TAPS // 2
    scale = HEAD_DIM ** (-0.25)
    group = SPAN // width
    levels = group.bit_length() - 1
    device = lax.axis_index("seq")
    rank = lax.axis_index("tp")
    local_index = device % group
    group_number = device // group
    groups = segment_sizes.shape[0] // rows
    start = local_index * width

    row_sizes = lax.dynamic_index_in_dim(
        segment_sizes, rank * groups + group_number, axis=0, keepdims=False
    )
    item_ends = jnp.cumsum(jnp.sum(row_sizes, axis=1))
    item_of = count_below(item_ends, width * jnp.arange(group, dtype=jnp.int32))
    own_item = item_of[local_index]
    slot_ends = jnp.cumsum(row_sizes.reshape(-1))
    positions = start + jnp.arange(width, dtype=jnp.int32)
    token_mark = count_below(slot_ends, positions) - own_item * marks
    own_sizes = lax.dynamic_index_in_dim(row_sizes, own_item, axis=0, keepdims=False)
    own_count = jnp.maximum(own_sizes, 1).astype(f32)[:, None]
    member = token_mark[:, None] == jnp.arange(marks, dtype=jnp.int32)[None, :]
    member_low = member.astype(bf16)

    def by_rank(stacked):
        return jnp.take(stacked, jnp.arange(ranks) ^ rank, axis=0)

    small = jnp.concatenate(
        (
            query_bias.reshape(-1),
            value_bias.reshape(-1),
            conv_weight.reshape(-1),
            up_bias.reshape(-1),
        )
    )
    wide = 2 * channels
    small_rows = -(-small.shape[0] // wide)
    small_rows += -small_rows % 16
    small = jnp.pad(small, (0, small_rows * wide - small.shape[0])).reshape(small_rows, wide)
    query_key = jnp.concatenate(
        (jnp.concatenate((query_weight, key_weight), axis=1), small), axis=0
    )
    query_key = spread_shards(query_key)
    value_blocks = spread_shards(value_weight)
    output_blocks = spread_shards(output_weight)
    up_blocks = spread_shards(up_weight)
    down_blocks = spread_shards(down_weight)
    smalls = [block[model:].reshape(-1).astype(f32) for block in query_key]
    query_bias_all = jnp.concatenate([s[:channels] for s in smalls])
    value_bias_all = jnp.concatenate([s[channels : 2 * channels] for s in smalls])
    taps_all = jnp.concatenate(
        [s[2 * channels : 2 * channels + own_heads * TAPS].reshape(own_heads, TAPS) for s in smalls]
    )
    up_start = 2 * channels + own_heads * TAPS
    up_bias_all = [s[up_start : up_start + hidden_units] for s in smalls]

    flat = lax.dynamic_index_in_dim(tokens, rank, axis=0, keepdims=False)
    upstream = lax.dynamic_index_in_dim(cotangent, rank, axis=0, keepdims=False).astype(f32)
    products = [dot(flat, block[:model]) for block in query_key]
    query = (
        scale * (jnp.concatenate([p[:, :channels] for p in products], axis=1) + query_bias_all)
    ).astype(bf16)
    keys = (scale * jnp.concatenate([p[:, channels:] for p in products], axis=1)).astype(bf16)
    part = outer(member_low, jnp.concatenate((query, keys), axis=1))
    sums = segment_sum(part, local_index, item_of, levels)
    land = (sums / own_count).astype(bf16)
    land_query, land_key = land[:, :model], land[:, model:]
    values = (
        jnp.concatenate([dot(flat, block) for block in value_blocks], axis=1) + value_bias_all
    ).astype(bf16)

    def split_heads(array):
        return array.reshape(array.shape[0], heads, HEAD_DIM)

    def neighbours(cells):
        count = lax.axis_size("seq")
        before = lax.ppermute(cells[width - reach :], "seq", [(i, i + 1) for i in range(count - 1)])
        after = lax.ppermute(cells[:reach], "seq", [(i + 1, i) for i in range(count - 1)])
        return jnp.concatenate((before, cells, after), axis=0)

    value_rim = neighbours(values)
    query_heads = split_heads(query)
    key_heads = split_heads(keys)
    value_heads = split_heads(values)
    land_query_heads = split_heads(land_query)
    land_key_heads = split_heads(land_key)

    key_scores = jnp.einsum(
        "mhd,thd->hmt", land_query_heads, key_heads, preferred_element_type=f32
    )
    local_top = rounded(jnp.max(key_scores, axis=-1))
    powers = jnp.exp(key_scores - local_top[..., None])
    part_mixed = jnp.einsum(
        "hmt,thd->mhd", powers.astype(bf16), value_heads, preferred_element_type=f32
    ).reshape(marks, model)
    mixed, key_top, key_total = segment_exchange(
        (part_mixed, local_top.T, jnp.sum(powers, axis=-1).T),
        local_index,
        item_of,
        levels,
        soft_pack,
        soft_unpack(heads, model),
        soft_merge,
    )
    mixed_values = mixed.reshape(marks, heads, HEAD_DIM) / key_total[:, :, None]
    mixed_values = mixed_values.transpose(1, 0, 2)

    token_scores = jnp.einsum(
        "thd,mhd->htm", query_heads, land_key_heads, preferred_element_type=f32
    )
    token_powers = jnp.exp(token_scores - jnp.max(token_scores, axis=-1, keepdims=True))
    token_weights = token_powers / jnp.sum(token_powers, axis=-1, keepdims=True)
    token_low = token_weights.astype(bf16)

    mixed_land, core_back = jax.vjp(
        landmark_core, land_query_heads.astype(f32), land_key_heads.astype(f32), mixed_values
    )
    mixed_low = mixed_land.astype(bf16)
    nystrom = jnp.einsum("htm,hmd->thd", token_low, mixed_low, preferred_element_type=f32)

    rim_pos = start - reach + jnp.arange(width + 2 * reach, dtype=jnp.int32)
    rim_item = count_below(item_ends, jnp.clip(rim_pos, 0, SPAN - 1))
    rim_keep = ((rim_pos >= 0) & (rim_pos < SPAN) & (rim_item == own_item))[:, None]
    kept_values = jnp.where(rim_keep, value_rim, 0).astype(f32)
    taps_wide = jnp.repeat(taps_all, HEAD_DIM, axis=0).T
    convolved = jnp.zeros((width, model), f32)
    for offset in range(TAPS):
        convolved = convolved + kept_values[offset : offset + width] * taps_wide[offset][None, :]
    context = (nystrom.reshape(width, model) + convolved).astype(bf16)
    output_all = jnp.concatenate(output_blocks, axis=0)
    attention = dot(context, output_all) + output_bias.astype(f32)
    first_gain32 = first_gain.astype(f32)
    second_gain32 = second_gain.astype(f32)
    first_out, first_normed, first_inverse = layer_norm(
        flat.astype(f32) + attention, first_gain32, first_shift.astype(f32)
    )
    first_low = first_out.astype(bf16)
    hidden = [dot(first_low, w) + b for w, b in zip(up_blocks, up_bias_all)]
    active = [gelu(h).astype(bf16) for h in hidden]
    feed = down_bias.astype(f32)
    for a, w in zip(active, down_blocks):
        feed = feed + dot(a, w)
    layer_out, second_normed, second_inverse = layer_norm(
        first_out + feed, second_gain32, second_shift.astype(f32)
    )
    grad_second_gain = jnp.sum(upstream * second_normed, axis=0)
    grad_second_shift = jnp.sum(upstream, axis=0)
    back_second = norm_back(upstream, second_gain32, second_normed, second_inverse)
    back_feed = back_second.astype(bf16)
    grad_down_bias = jnp.sum(back_feed.astype(f32), axis=0)
    grad_down_weight = scatter_weight([outer(back_feed, a) for a in active], device)
    back_hidden = [
        jax.vjp(gelu, h)[1](dot_t(back_feed, w))[0].astype(bf16)
        for h, w in zip(hidden, down_blocks)
    ]
    grad_up_bias = [jnp.sum(b.astype(f32), axis=0) for b in back_hidden]
    grad_up_weight = scatter_weight([outer(first_low, b) for b in back_hidden], device)
    back_first = back_second
    for b, w in zip(back_hidden, up_blocks):
        back_first = back_first + dot_t(b, w)
    grad_first_gain = jnp.sum(back_first * first_normed, axis=0)
    grad_first_shift = jnp.sum(back_first, axis=0)
    back_input = norm_back(back_first, first_gain32, first_normed, first_inverse)
    back_attention = back_input.astype(bf16)
    grad_output_bias = jnp.sum(back_attention.astype(f32), axis=0)
    context_parts = [context[:, r * channels : (r + 1) * channels] for r in range(ranks)]
    grad_output_weight = scatter_weight([outer(back_attention, c) for c in context_parts], device)
    back_context = dot_t(back_attention, output_all).astype(bf16)

    context_rim = neighbours(back_context)
    kept_back = jnp.where(rim_keep, context_rim, 0).astype(f32)
    back_wide = back_context.astype(f32)
    conv_values = jnp.zeros((width, model), f32)
    tap_terms = []
    for offset in range(TAPS):
        lower = 2 * reach - offset
        conv_values = conv_values + kept_back[lower : lower + width] * taps_wide[offset][None, :]
        tap_terms.append(jnp.sum(back_wide * kept_values[offset : offset + width], axis=0))
    conv_part = jnp.sum(jnp.stack(tap_terms, axis=1).reshape(heads, HEAD_DIM, TAPS), axis=1)

    back_heads = split_heads(back_context)
    part_back = jnp.einsum(
        "htm,thd->mhd", token_low, back_heads, preferred_element_type=f32
    ).reshape(marks, model)
    back_token = jnp.einsum("thd,hmd->htm", back_heads, mixed_low, preferred_element_type=f32)
    back_token_scores = (
        token_weights * (back_token - jnp.sum(token_weights * back_token, axis=-1, keepdims=True))
    ).astype(bf16)
    back_query_token = jnp.einsum(
        "htm,mhd->thd", back_token_scores, land_key_heads, preferred_element_type=f32
    ).reshape(width, model)
    part_land_key = jnp.einsum(
        "htm,thd->mhd", back_token_scores, query_heads, preferred_element_type=f32
    ).reshape(marks, model)
    back_mixed_land = segment_sum(part_back, local_index, item_of, levels)
    sum_land_key = segment_sum(part_land_key, local_index, item_of, levels)
    back_land_query_a, back_land_key_a, back_mixed = core_back(
        back_mixed_land.reshape(marks, heads, HEAD_DIM).transpose(1, 0, 2)
    )
    back_mixed_low = back_mixed.astype(bf16)
    key_weights = jnp.exp(key_scores - key_top.T[..., None]) / key_total.T[..., None]
    back_key_weights = jnp.einsum(
        "hmd,thd->hmt", back_mixed_low, value_heads, preferred_element_type=f32
    )
    key_dots = jnp.sum(back_mixed_low.astype(f32) * mixed_values, axis=-1)
    back_key_scores = (key_weights * (back_key_weights - key_dots[..., None])).astype(bf16)
    part_land_query = jnp.einsum(
        "hmt,thd->mhd", back_key_scores, key_heads, preferred_element_type=f32
    ).reshape(marks, model)
    sum_land_query = segment_sum(part_land_query, local_index, item_of, levels)
    back_key_direct = jnp.einsum(
        "hmt,mhd->thd", back_key_scores, land_query_heads, preferred_element_type=f32
    ).reshape(width, model)
    back_value_direct = jnp.einsum(
        "hmt,hmd->thd", key_weights.astype(bf16), back_mixed_low, preferred_element_type=f32
    ).reshape(width, model)
    back_values = (back_value_direct + conv_values).astype(bf16)
    back_land_query = sum_land_query + back_land_query_a.reshape(marks, model)
    back_land_key = sum_land_key + back_land_key_a.reshape(marks, model)
    member_wide = member.astype(f32)
    back_query = (
        back_query_token + jnp.dot(member_wide, back_land_query / own_count, precision=highest)
    ).astype(bf16)
    back_keys = (
        back_key_direct + jnp.dot(member_wide, back_land_key / own_count, precision=highest)
    ).astype(bf16)

    def block(array, r):
        return array[:, r * channels : (r + 1) * channels]

    projection = [
        jnp.concatenate(
            (
                scale * outer(flat, block(back_query, r)),
                scale * outer(flat, block(back_keys, r)),
                outer(flat, block(back_values, r)),
            ),
            axis=1,
        )
        for r in range(ranks)
    ]
    grad_projection = scatter_weight(projection, device)
    projected = jnp.zeros((width, model), f32)
    for r in range(ranks):
        both = jnp.concatenate((block(back_query, r), block(back_keys, r)), axis=1)
        projected = projected + scale * dot_t(both, query_key[r][:model])
        projected = projected + dot_t(block(back_values, r), value_blocks[r])
    grad_rows = jnp.stack(spread_shards((back_input + projected).astype(bf16)))
    grad_tokens = by_rank(grad_rows).astype(f32)
    layer_rows = by_rank(jnp.stack(spread_shards(layer_out.astype(bf16))))

    ranked = jnp.stack(
        [
            jnp.concatenate(
                (
                    grad_up_bias[r],
                    jnp.sum(block(back_values, r).astype(f32), axis=0),
                    scale * jnp.sum(block(back_query, r).astype(f32), axis=0),
                    conv_part[r * own_heads : (r + 1) * own_heads].reshape(-1),
                )
            )
            for r in range(ranks)
        ]
    )
    ranked = by_rank(ranked)
    ranked_size = ranked.size
    shared = [
        grad_output_bias,
        grad_first_gain,
        grad_first_shift,
        grad_down_bias,
        grad_second_gain,
        grad_second_shift,
    ]
    bundle = jnp.concatenate([ranked.reshape(-1)] + shared)
    bundle = jnp.pad(bundle, (0, -bundle.shape[0] % (8 * LANES))).reshape(-1, LANES)
    bundle = sum_everywhere(bundle).reshape(-1)
    own_ranked = lax.dynamic_index_in_dim(
        bundle[:ranked_size].reshape(ranks, -1), rank, axis=0, keepdims=False
    )
    grad_up_bias = own_ranked[:hidden_units]
    at = hidden_units
    grad_value_bias = own_ranked[at : at + channels].reshape(own_heads, HEAD_DIM)
    at += channels
    share = HEAD_DIM // lax.axis_size("seq")
    grad_query_bias = lax.dynamic_slice_in_dim(
        own_ranked[at : at + channels].reshape(own_heads, HEAD_DIM), device * share, share, axis=1
    )
    at += channels
    grad_conv_weight = own_ranked[at : at + own_heads * TAPS].reshape(own_heads, TAPS)
    shared = [
        bundle[ranked_size + k * model : ranked_size + (k + 1) * model] for k in range(len(shared))
    ]
    return (
        layer_rows,
        grad_tokens,
        grad_projection[:, :channels],
        grad_query_bias,
        grad_projection[:, channels : 2 * channels],
        grad_projection[:, 2 * channels :],
        grad_value_bias,
        grad_conv_weight,
        grad_output_weight.T,
        shared[0],
        shared[1],
        shared[2],
        grad_up_weight,
        grad_up_bias,
        grad_down_weight.T,
        shared[3],
        shared[4],
        shared[5],
    )


def solution(mesh):
    placed = (
        P(None, "seq", None),
        P(None, "tp"),
        P("tp", None),
        P(None, "tp"),
        P(None, "tp"),
        P("tp", None),
        P("tp", None),
        P("tp", None),
        P(),
        P(),
        P(),
        P(None, "tp"),
        P("tp"),
        P("tp", None),
        P(),
        P(),
        P(),
        P(),
        P(None, "seq", None),
    )
    return jax.shard_map(
        per_device,
        mesh=mesh,
        in_specs=placed,
        out_specs=(
            P(None, "seq", None),
            P(None, "seq", None),
            P("seq", "tp"),
            P("tp", "seq"),
            P("seq", "tp"),
            P("seq", "tp"),
            P("tp", None),
            P("tp", None),
            P("tp", "seq"),
            P(),
            P(),
            P(),
            P("seq", "tp"),
            P("tp"),
            P("tp", "seq"),
            P(),
            P(),
            P(),
        ),
        check_vma=False,
    )
```

```python
import functools

import jax
import jax.numpy as jnp
from jax import lax
from jax.experimental import pallas as pl
from jax.experimental.pallas import tpu as pltpu
from jax.sharding import PartitionSpec as P

HEAD_DIM = 64
TAPS = 33
SWEEPS = 6
SPAN = 4096
LANES = 128
STRIPE = 128
TILE = 256
VMEM_LIMIT = 44 << 20


highest = lax.Precision.HIGHEST
epsilon = 1e-05
very_negative = -1e30
f32 = jnp.float32
bf16 = jnp.bfloat16


def swap(value, axis, step):
    return lax.ppermute(value, axis, [(i, i ^ step) for i in range(lax.axis_size(axis))])


def dot(a, b):
    return jnp.dot(a, b, preferred_element_type=f32)


def outer(a, b):
    return lax.dot_general(a, b, (((0,), (0,)), ((), ())), preferred_element_type=f32)


def dot_t(a, b):
    return lax.dot_general(a, b, (((1,), (1,)), ((), ())), preferred_element_type=f32)


def rounded(value):
    return lax.reduce_precision(value, 8, 7)


def count_below(ends, positions):
    return jnp.sum((ends[None, :] <= positions[:, None]).astype(jnp.int32), axis=1)


def spread_shards(shard):
    core = swap(shard, "tp", 1)
    far = swap(shard, "tp", 2)
    return (shard, core, far, swap(far, "tp", 1))


def level_flags(index, item_of, levels):
    own_item = item_of[index]
    flags = []
    for level in range(levels):
        size = 1 << level
        start = (index >> level) << level
        other = start ^ size
        is_left = (index & size) == 0
        far_facing = jnp.where(is_left, item_of[other], item_of[other + size - 1])
        far_outer = jnp.where(is_left, item_of[other + size - 1], item_of[other])
        facing = jnp.where(is_left, item_of[start + size - 1], item_of[start])
        outer_edge = jnp.where(is_left, item_of[start], item_of[start + size - 1])
        next_left = (index & (2 * size)) == 0
        flags.append(
            jnp.stack(
                (
                    own_item == far_facing,
                    outer_edge == far_facing,
                    far_outer == facing,
                    is_left != next_left,
                )
            ).astype(f32)
        )
    return flags


def segment_sum(value, flags):
    own = facing = outer_edge = value
    for level, flag in enumerate(flags):
        size = 1 << level
        last = level == len(flags) - 1
        got = swap(facing.astype(bf16), "seq", size).astype(f32)
        own = own + flag[0] * got
        if not last:
            got_outer = got
            if level > 0:
                got_outer = swap(outer_edge.astype(bf16), "seq", size).astype(f32)
            near = outer_edge + flag[1] * got
            away = got_outer + flag[2] * facing
            facing = jnp.where(flag[3] > 0.5, near, away)
            outer_edge = jnp.where(flag[3] > 0.5, away, near)
    return own


def soft_sum(state, flags, heads):
    marks, width = state.shape
    packed = ((marks, width), bf16)
    whole = ((marks, width), f32)
    specs = [pl.BlockSpec(memory_space=pltpu.SMEM)]

    def run(kernel, outs, name, *operands):
        return pl.pallas_call(
            functools.partial(kernel, heads),
            out_shape=tuple(jax.ShapeDtypeStruct(*out) for out in outs),
            in_specs=specs + [WHOLE] * (len(operands) - 1),
            out_specs=(WHOLE,) * len(outs),
            name=name,
        )(*operands)

    own = facing = outer_edge = state
    for level, flag in enumerate(flags):
        size = 1 << level
        last = level == len(flags) - 1
        message = call(functools.partial(pack_kernel, heads), (packed,), "pack_state")
        got = swap(message(facing)[0], "seq", size)
        if last:
            (own,) = run(soft_last_kernel, (whole,), "merge_last", flag, own, got)
        elif level == 0:
            own, facing, outer_edge = run(
                soft_first_kernel, (whole,) * 3, "merge_first", flag, own, got
            )
        else:
            got_outer = swap(message(outer_edge)[0], "seq", size)
            own, facing, outer_edge = run(
                soft_next_kernel, (whole,) * 3, "merge_next", flag, own, facing, outer_edge, got,
                got_outer,
            )
    return own


def scatter_weight(blocks, seq_index):
    blocks = [b.astype(bf16) for b in blocks]
    got = swap((blocks[1], blocks[3]), "tp", 1)
    mine = blocks[0].astype(f32) + got[0].astype(f32)
    away = (blocks[2].astype(f32) + got[1].astype(f32)).astype(bf16)
    total = mine + swap(away, "tp", 2).astype(f32)
    count = lax.axis_size("seq")
    rows, columns = total.shape
    size = 1
    total = total.reshape(count, rows // count, columns)
    while size < count:
        bit = (seq_index // size) % 2
        view = total.reshape(total.shape[0] // 2, 2, rows // count, columns)
        keep = lax.dynamic_index_in_dim(view, bit, axis=1, keepdims=False)
        send = lax.dynamic_index_in_dim(view, 1 - bit, axis=1, keepdims=False).astype(bf16)
        total = keep + swap(send, "seq", size).astype(f32)
        size *= 2
    return total[0]


def sum_everywhere(value):
    for axis in ("tp", "seq"):
        size = 1
        while size < lax.axis_size(axis):
            value = value + swap(value, axis, size)
            size *= 2
    return value


def newton_inverse(kernel):
    size = kernel.shape[-1]
    column_sums = jnp.sum(kernel, axis=-2)
    bound = jnp.sqrt(jnp.sum(column_sums * column_sums, axis=-1))[..., None, None]
    identity = jnp.eye(size, dtype=kernel.dtype)
    inverse = jnp.swapaxes(kernel, -1, -2) / bound
    for sweep in range(SWEEPS):
        product = jnp.matmul(kernel, inverse, precision=highest)
        inner = 7.0 * identity - product
        inner = 15.0 * identity - jnp.matmul(product, inner, precision=highest)
        inner = 13.0 * identity - jnp.matmul(product, inner, precision=highest)
        inverse = 0.25 * jnp.matmul(inverse, inner, precision=highest)
    return inverse


def landmark_inverse(land_query, land_key):
    scores = jnp.einsum("mhd,nhd->hmn", land_query, land_key, precision=highest)
    powers = jnp.exp(scores - jnp.max(scores, axis=-1, keepdims=True))
    return newton_inverse(powers / jnp.sum(powers, axis=-1, keepdims=True))


WHOLE = pl.BlockSpec(memory_space=pltpu.VMEM)


def call(kernel, outs, name, scratch=(), limit=24 << 20, flops=0, moved=0):
    outs = tuple(jax.ShapeDtypeStruct(shape, dtype) for shape, dtype in outs)

    def run(*operands):
        return pl.pallas_call(
            kernel,
            out_shape=outs,
            in_specs=[WHOLE] * len(operands),
            out_specs=(WHOLE,) * len(outs),
            scratch_shapes=list(scratch),
            compiler_params=pltpu.CompilerParams(vmem_limit_bytes=limit),
            cost_estimate=pl.CostEstimate(flops=flops, bytes_accessed=moved, transcendentals=0),
            name=name,
        )(*operands)

    return run


def lane_ids(shape):
    return lax.broadcasted_iota(jnp.int32, shape, len(shape) - 1)


def row_ids(shape):
    return lax.broadcasted_iota(jnp.int32, shape, len(shape) - 2)


def spread_heads(block):
    heads = block.shape[1] // HEAD_DIM
    tall = jnp.concatenate([block] * heads, axis=0)
    same = row_ids(tall.shape) // HEAD_DIM == lane_ids(tall.shape) // HEAD_DIM
    return jnp.where(same, tall, jnp.zeros_like(tall))


def gather_heads(square):
    heads = square.shape[1] // HEAD_DIM
    result = jnp.zeros((HEAD_DIM, square.shape[1]), square.dtype)
    lane = lane_ids(result.shape) // HEAD_DIM
    for j in range(heads):
        result = jnp.where(lane == j, square[j * HEAD_DIM : (j + 1) * HEAD_DIM], result)
    return result


def two_parts(value):
    high = value.astype(bf16)
    return high, (value - high.astype(f32)).astype(bf16)


def dot_fine(a, b):
    a_high, a_low = two_parts(a)
    b_high, b_low = two_parts(b)
    return dot(a_high, b_high) + (dot(a_high, b_low) + dot(a_low, b_high))


def group_of(array, r, channels):
    return array[:, r * channels : (r + 1) * channels]


def query_key_kernel(flat_ref, w0, w1, bias_ref, member_ref, query_ref, keys_ref, part_ref):
    model = flat_ref.shape[1]
    channels = query_ref.shape[2]
    scale = HEAD_DIM ** (-0.25)
    parts = []
    for r, w in enumerate((w0, w1)):
        product = dot(flat_ref[...], w[0:model, :])
        query = (scale * (product[:, :channels] + bias_ref[r : r + 1, :])).astype(bf16)
        keys = (scale * product[:, channels:]).astype(bf16)
        query_ref[r] = query
        keys_ref[r] = keys
        parts += [dot(member_ref[...], query), dot(member_ref[...], keys)]
    part_ref[...] = jnp.concatenate(parts, axis=1)


def value_kernel(flat_ref, w0, w1, w2, w3, bias_ref, values_ref, head_ref, tail_ref):
    reach = head_ref.shape[0]
    heads, tails = [], []
    for r, w in enumerate((w0, w1, w2, w3)):
        values = (dot(flat_ref[...], w[...]) + bias_ref[r : r + 1, :]).astype(bf16)
        values_ref[r] = values
        heads.append(values[:reach])
        tails.append(values[values.shape[0] - reach :])
    head_ref[...] = jnp.concatenate(heads, axis=1)
    tail_ref[...] = jnp.concatenate(tails, axis=1)


def key_kernel(k0, k1, values_ref, land_query_ref, state_ref):
    channels = values_ref.shape[2]
    heads = channels // HEAD_DIM
    mixed = []
    marks = land_query_ref.shape[0]
    stats = jnp.zeros((marks, LANES), f32)
    lane = lane_ids(stats.shape)
    groups = values_ref.shape[0]
    for r in range(groups):
        keys = (k0, k1)[r // 2][r % 2]
        scores = dot_t(spread_heads(group_of(land_query_ref[...], r, channels)), keys)
        top = jnp.max(scores, axis=1, keepdims=True).astype(bf16).astype(f32)
        powers = jnp.exp(scores - top)
        total = jnp.sum(powers, axis=1, keepdims=True)
        mixed.append(gather_heads(dot(powers.astype(bf16), values_ref[r])))
        for j in range(heads):
            h = r * heads + j
            at = slice(j * marks, (j + 1) * marks)
            stats = jnp.where(lane == h, top[at], stats)
            stats = jnp.where(lane == groups * heads + h, total[at], stats)
    state_ref[...] = jnp.concatenate(mixed + [stats], axis=1)


def state_message(state, heads):
    width = state.shape[1] - LANES
    stats = state[:, width:]
    lane = lane_ids(stats.shape)
    high = stats.astype(bf16).astype(f32)
    low = pltpu.roll(stats - high, heads, 1)
    last = jnp.where(lane < 2 * heads, high, jnp.where(lane < 3 * heads, low, 0.0))
    return jnp.concatenate((state[:, :width], last), axis=1).astype(bf16)


def message_state(message, heads):
    message = message.astype(f32)
    width = message.shape[1] - LANES
    stats = message[:, width:]
    lane = lane_ids(stats.shape)
    low = pltpu.roll(stats, LANES - heads, 1)
    stats = stats + jnp.where((lane >= heads) & (lane < 2 * heads), low, 0.0)
    stats = jnp.where(lane < 2 * heads, stats, 0.0)
    return jnp.concatenate((message[:, :width], stats), axis=1)


def widen(stats, first, width):
    pieces = []
    rows = stats.shape[0]
    for pair in range(width // LANES):
        lane = lane_ids((rows, LANES))
        at = first + 2 * pair
        pieces.append(
            jnp.where(lane < HEAD_DIM, stats[:, at : at + 1], stats[:, at + 1 : at + 2])
        )
    return jnp.concatenate(pieces, axis=1)


def merge_states(a, b, use, heads):
    width = a.shape[1] - LANES
    stats_a, stats_b = a[:, width:], b[:, width:]
    lane = lane_ids(stats_a.shape)
    use = use > 0.5
    top = jnp.where(use, jnp.maximum(stats_a, stats_b), stats_a)
    is_top = lane < heads
    scale_a = jnp.exp(jnp.where(is_top, stats_a - top, 0.0))
    scale_b = jnp.where(use, jnp.exp(jnp.where(is_top & use, stats_b - top, 0.0)), 0.0)
    values = a[:, :width] * widen(scale_a, 0, width) + b[:, :width] * widen(scale_b, 0, width)
    total = stats_a * pltpu.roll(scale_a, heads, 1) + stats_b * pltpu.roll(scale_b, heads, 1)
    stats = jnp.where(is_top, top, jnp.where(lane < 2 * heads, total, 0.0))
    return jnp.concatenate((values, stats), axis=1)


def pack_kernel(heads, state_ref, message_ref):
    message_ref[...] = state_message(state_ref[...], heads)


def soft_first_kernel(heads, flags_ref, own_ref, got_ref, new_ref, facing_ref, outer_ref):
    soft_level(heads, flags_ref, own_ref[...], own_ref[...], own_ref[...], got_ref[...],
               got_ref[...], new_ref, facing_ref, outer_ref)


def soft_level(heads, flags_ref, own, facing, outer_edge, got, got_outer, new_ref, facing_ref,
               outer_ref):
    got = message_state(got, heads)
    got_outer = message_state(got_outer, heads)
    new_ref[...] = merge_states(own, got, flags_ref[0], heads)
    near = merge_states(outer_edge, got, flags_ref[1], heads)
    away = merge_states(got_outer, facing, flags_ref[2], heads)
    swap_edges = flags_ref[3] > 0.5
    facing_ref[...] = jnp.where(swap_edges, near, away)
    outer_ref[...] = jnp.where(swap_edges, away, near)


def soft_next_kernel(heads, flags_ref, own_ref, facing_in, outer_in, got_ref, got_outer_ref,
                     new_ref, facing_ref, outer_ref):
    soft_level(heads, flags_ref, own_ref[...], facing_in[...], outer_in[...], got_ref[...],
               got_outer_ref[...], new_ref, facing_ref, outer_ref)


def soft_last_kernel(heads, flags_ref, own_ref, got_ref, new_ref):
    new_ref[...] = merge_states(own_ref[...], message_state(got_ref[...], heads), flags_ref[0], heads)


def token_kernel(q0, q1, land_key_ref, weights_ref):
    groups, rows, width = weights_ref.shape
    channels = q0.shape[2]
    heads = channels // HEAD_DIM
    for r in range(groups):
        query = (q0, q1)[r // 2][r % 2]
        scores = dot_t(spread_heads(group_of(land_key_ref[...], r, channels)), query)
        scores = scores.reshape(heads, rows // heads, width)
        powers = jnp.exp(scores - jnp.max(scores, axis=1, keepdims=True))
        weights = powers / jnp.sum(powers, axis=1, keepdims=True)
        weights_ref[r] = weights.reshape(rows, width)


def toeplitz(taps_row, rows, width):
    wide = jnp.broadcast_to(taps_row, (rows, taps_row.shape[1]))
    return pltpu.roll(wide, 0, 1, stride=1, stride_axis=0)[:, :width]


def with_rim(cells, before, after, keep_ref):
    keep = keep_ref[...]
    return jnp.concatenate(
        (
            jnp.where(keep[:, 0:1] > 0, before, jnp.zeros_like(before)),
            cells,
            jnp.where(keep[:, 1:2] > 0, after, jnp.zeros_like(after)),
        ),
        axis=0,
    )


def convolve(rim, filters):
    tall = jnp.concatenate(filters, axis=0)
    span = tall.shape[1]
    pieces = []
    for start in range(0, rim.shape[0] - (span - STRIPE), STRIPE):
        product = dot(tall, rim[start : start + span])
        lane = lane_ids((STRIPE, rim.shape[1])) // HEAD_DIM
        piece = product[:STRIPE]
        for j in range(1, len(filters)):
            piece = jnp.where(lane == j, product[j * STRIPE : (j + 1) * STRIPE], piece)
        pieces.append(piece)
    return jnp.concatenate(pieces, axis=0)


def context_kernel(state_ref, inverse_ref, weights_ref, values_ref, before_ref, after_ref, keep_ref,
                   taps_ref, context_ref, mixed_ref, low_ref):
    groups, width, channels = values_ref.shape
    heads = channels // HEAD_DIM
    reach = before_ref.shape[0]
    state = state_ref[...]
    model = groups * channels
    mixed = state[:, :model] / widen(state[:, model:], groups * heads, model)
    mixed_ref[...] = mixed
    lows = []
    for r in range(groups):
        land = dot_fine(inverse_ref[r], spread_heads(group_of(mixed, r, channels)))
        low = land.astype(bf16)
        lows.append(low)
        nystrom = outer(weights_ref[r].astype(bf16), spread_heads(low))
        rim = with_rim(
            values_ref[r],
            group_of(before_ref[...], r, channels),
            group_of(after_ref[...], r, channels),
            keep_ref,
        )
        filters = [
            toeplitz(taps_ref[r * heads + j : r * heads + j + 1, :], STRIPE, STRIPE + 2 * reach)
            .astype(bf16)
            for j in range(heads)
        ]
        context_ref[r] = (nystrom + convolve(rim, filters)).astype(bf16)
    low_ref[...] = jnp.concatenate(lows, axis=1)


def edges_kernel(cells_ref, head_ref, tail_ref):
    groups, width, _ = cells_ref.shape
    reach = head_ref.shape[0]
    head_ref[...] = jnp.concatenate([cells_ref[r, :reach] for r in range(groups)], axis=1)
    tail_ref[...] = jnp.concatenate([cells_ref[r, width - reach :] for r in range(groups)], axis=1)


def token_back_kernel(back_ref, weights_ref, low_ref, q0, q1, land_key_ref, part_ref, part_key_ref,
                      direct_ref, head_ref, tail_ref):
    groups, width, channels = back_ref.shape
    heads = channels // HEAD_DIM
    reach = head_ref.shape[0]
    parts, key_parts = [], []
    for r in range(groups):
        back = back_ref[r]
        query = (q0, q1)[r // 2][r % 2]
        weights = weights_ref[r]
        parts.append(gather_heads(dot(weights.astype(bf16), back)))
        slope = dot_t(spread_heads(group_of(low_ref[...], r, channels)), back)
        product = (weights * slope).reshape(heads, -1, width)
        rows = jnp.sum(product, axis=1, keepdims=True)
        rows = jnp.broadcast_to(rows, product.shape).reshape(weights.shape)
        scores = (weights * (slope - rows)).astype(bf16)
        key_parts.append(gather_heads(dot(scores, query)))
        direct_ref[r] = outer(scores, spread_heads(group_of(land_key_ref[...], r, channels)))
    part_ref[...] = jnp.concatenate(parts, axis=1)
    part_key_ref[...] = jnp.concatenate(key_parts, axis=1)
    head_ref[...] = jnp.concatenate([back_ref[r, :reach] for r in range(groups)], axis=1)
    tail_ref[...] = jnp.concatenate([back_ref[r, width - reach :] for r in range(groups)], axis=1)


def conv_back_kernel(back_ref, before_ref, after_ref, values_ref, vbefore_ref, vafter_ref, keep_ref,
                     flipped_ref, conv_ref, taps_ref):
    groups, width, channels = back_ref.shape
    heads = channels // HEAD_DIM
    reach = before_ref.shape[0]
    span = STRIPE + 2 * reach
    order = row_ids((STRIPE, STRIPE)) + lane_ids((STRIPE, STRIPE)) == STRIPE - 1
    order = jnp.where(order, 1.0, 0.0).astype(bf16)
    lane = lane_ids((STRIPE, channels)) // HEAD_DIM
    for r in range(groups):
        rim = with_rim(
            back_ref[r],
            group_of(before_ref[...], r, channels),
            group_of(after_ref[...], r, channels),
            keep_ref,
        )
        filters = [
            toeplitz(flipped_ref[r * heads + j : r * heads + j + 1, :], STRIPE, span).astype(bf16)
            for j in range(heads)
        ]
        conv_ref[r] = convolve(rim, filters)
        value_rim = with_rim(
            values_ref[r],
            group_of(vbefore_ref[...], r, channels),
            group_of(vafter_ref[...], r, channels),
            keep_ref,
        )
        total = jnp.zeros((heads * STRIPE, span), f32)
        for start in range(0, width, STRIPE):
            turned = dot(order, back_ref[r, start : start + STRIPE])
            tall = [jnp.where(lane == j, turned, 0.0).astype(bf16) for j in range(heads)]
            total = total + dot_t(jnp.concatenate(tall, axis=0), value_rim[start : start + span])
        total = jnp.concatenate(
            (total, jnp.zeros((heads * STRIPE, 2 * LANES - span), f32)), axis=1
        )
        for j in range(heads):
            skewed = pltpu.roll(
                total[j * STRIPE : (j + 1) * STRIPE], 0, 1, stride=1, stride_axis=0
            )
            h = r * heads + j
            taps_ref[h : h + 1, :] = jnp.sum(skewed, axis=0, keepdims=True)


def key_back_kernel(k0, k1, values_ref, land_query_ref, state_ref, mixed_ref, back_mixed_ref,
                    conv_ref, part_ref, direct_ref, back_values_ref, bias_ref):
    groups, width, channels = values_ref.shape
    heads = channels // HEAD_DIM
    model = groups * channels
    marks = land_query_ref.shape[0]
    stats = state_ref[:, model:]
    parts = []
    for r in range(groups):
        keys = (k0, k1)[r // 2][r % 2]
        land = spread_heads(group_of(land_query_ref[...], r, channels))
        scores = dot_t(land, keys)
        first = r * heads
        tops = jnp.concatenate([stats[:, first + j : first + j + 1] for j in range(heads)], axis=0)
        first += groups * heads
        totals = jnp.concatenate(
            [stats[:, first + j : first + j + 1] for j in range(heads)], axis=0
        )
        weights = jnp.exp(scores - tops) * (1.0 / totals)
        back_mixed = group_of(back_mixed_ref[...], r, channels).astype(bf16)
        spread = spread_heads(back_mixed)
        dots = jnp.sum(
            spread_heads(group_of(mixed_ref[...], r, channels)) * spread.astype(f32),
            axis=1,
            keepdims=True,
        )
        slope = dot_t(spread, values_ref[r])
        back_scores = (weights * (slope - dots)).astype(bf16)
        parts.append(gather_heads(dot(back_scores, keys)))
        direct_ref[r] = outer(back_scores, land)
        back_values = (outer(weights.astype(bf16), spread) + conv_ref[r]).astype(bf16)
        back_values_ref[r] = back_values
        bias_ref[r : r + 1, :] = jnp.sum(back_values.astype(f32), axis=0, keepdims=True)
    part_ref[...] = jnp.concatenate(parts, axis=1)


def input_back_kernel(flat_ref, query_direct_ref, key_direct_ref, back_values_ref, land_query_ref,
                      land_key_ref, member_ref, back_input_ref, w0, w1, w2, w3, v0, v1, v2, v3,
                      grad_ref, bias_ref, g0, g1, g2, g3, turned_ref):
    groups, width, channels = back_values_ref.shape
    model = flat_ref.shape[1]
    scale = HEAD_DIM ** (-0.25)
    member = member_ref[...]
    total = back_input_ref[...]
    turned_ref[...] = flat_ref[...].T
    for r in range(groups):
        w, v = (w0, w1, w2, w3)[r], (v0, v1, v2, v3)[r]
        sides = []
        for direct_ref, land_ref in ((query_direct_ref, land_query_ref), (key_direct_ref, land_key_ref)):
            high, low = two_parts(group_of(land_ref[...], r, channels))
            sides.append((direct_ref[r] + (dot(member, high) + dot(member, low))).astype(bf16))
        bias_ref[r : r + 1, :] = scale * jnp.sum(sides[0].astype(f32), axis=0, keepdims=True)
        both = jnp.concatenate(sides, axis=1)
        total = total + scale * dot_t(both, w[0:model, :])
        total = total + dot_t(back_values_ref[r], v[...])
        turned = turned_ref[...]
        gradient = (scale * dot(turned, both)).astype(bf16)
        (g0, g1, g2, g3)[r][...] = jnp.concatenate(
            (gradient, dot(turned, back_values_ref[r]).astype(bf16)), axis=1
        )
    grad_ref[...] = total.astype(bf16)


def feed_kernel(
    flat_ref, context_ref, out0, out1, out2, out3, up0, up1, up2, up3, down0, down1, down2, down3,
    up_bias_ref, params_ref, cotangent_ref,
    layer_ref, back_input_ref, back_attention_ref, back_context_ref, active_ref, back_hidden_ref,
    first_low_ref, back_feed_ref, sums_ref, up_sums_ref,
    slope_ref, first_ref, total_ref,
):
    outs, ups, downs = (out0, out1, out2, out3), (up0, up1, up2, up3), (down0, down1, down2, down3)
    units = up0.shape[1]
    tile = TILE
    steps = units // tile
    output_bias, first_gain, first_shift, down_bias, second_gain, second_shift = [
        params_ref[k : k + 1, :] for k in range(6)
    ]

    def mean(value):
        return jnp.mean(value, axis=1, keepdims=True)

    attention = dot(context_ref[0], out0[...])
    for r in range(1, len(outs)):
        attention = attention + dot(context_ref[r], outs[r][...])
    value = flat_ref[...].astype(f32) + attention + output_bias
    centred = value - mean(value)
    first_inverse = lax.rsqrt(mean(centred * centred) + epsilon)
    first_normed = centred * first_inverse
    first_ref[...] = first_normed
    first_out = first_normed * first_gain + first_shift
    first_low_ref[...] = first_out.astype(bf16)
    total_ref[...] = first_out + down_bias
    for r in range(len(ups)):

        def forward(step, carry):
            at = pl.multiple_of(step * tile, tile)
            whole = pl.multiple_of(r * units + at, tile)
            hidden = dot(first_low_ref[...], ups[r][:, pl.ds(at, tile)])
            hidden = hidden + up_bias_ref[:, pl.ds(whole, tile)]
            cdf = 0.5 * (1.0 + lax.erf(hidden * 0.7071067811865476))
            slope_ref[:, pl.ds(whole, tile)] = cdf + hidden * (
                0.3989422804014327 * jnp.exp(-0.5 * hidden * hidden)
            )
            active = (hidden * cdf).astype(bf16)
            active_ref[:, pl.ds(whole, tile)] = active
            total_ref[...] += dot(active, downs[r][pl.ds(at, tile), :])
            return carry

        lax.fori_loop(0, steps, forward, 0)

    value = total_ref[...]
    centred = value - mean(value)
    second_inverse = lax.rsqrt(mean(centred * centred) + epsilon)
    normed = centred * second_inverse
    layer_ref[...] = (normed * second_gain + second_shift).astype(bf16)
    upstream = cotangent_ref[...].astype(f32)
    sums_ref[4:5, :] = jnp.sum(upstream * normed, axis=0, keepdims=True)
    sums_ref[5:6, :] = jnp.sum(upstream, axis=0, keepdims=True)
    scaled = upstream * second_gain
    back_second = (scaled - mean(scaled) - normed * mean(scaled * normed)) * second_inverse
    back_feed = back_second.astype(bf16)
    back_feed_ref[...] = back_feed
    sums_ref[3:4, :] = jnp.sum(back_feed.astype(f32), axis=0, keepdims=True)
    total_ref[...] = back_second
    for r in range(len(ups)):

        def backward(step, carry):
            at = pl.multiple_of(step * tile, tile)
            whole = pl.multiple_of(r * units + at, tile)
            back_active = dot_t(back_feed_ref[...], downs[r][pl.ds(at, tile), :])
            back_hidden = (back_active * slope_ref[:, pl.ds(whole, tile)]).astype(bf16)
            back_hidden_ref[:, pl.ds(whole, tile)] = back_hidden
            up_sums_ref[:, pl.ds(whole, tile)] = jnp.sum(
                back_hidden.astype(f32), axis=0, keepdims=True
            )
            total_ref[...] += dot_t(back_hidden, ups[r][:, pl.ds(at, tile)])
            return carry

        lax.fori_loop(0, steps, backward, 0)

    back_first = total_ref[...]
    first_normed = first_ref[...]
    sums_ref[1:2, :] = jnp.sum(back_first * first_normed, axis=0, keepdims=True)
    sums_ref[2:3, :] = jnp.sum(back_first, axis=0, keepdims=True)
    scaled = back_first * first_gain
    back_input = (scaled - mean(scaled) - first_normed * mean(scaled * first_normed)) * first_inverse
    back_input_ref[...] = back_input
    back_attention = back_input.astype(bf16)
    back_attention_ref[...] = back_attention
    sums_ref[0:1, :] = jnp.sum(back_attention.astype(f32), axis=0, keepdims=True)
    for r in range(len(outs)):
        back_context_ref[r] = dot_t(back_attention, outs[r][...]).astype(bf16)


def feed_layer(flat, context, outputs, ups, downs, up_bias, params, cotangent):
    width, model = flat.shape
    ranks, units = len(ups), ups[0].shape[1]
    channels = outputs[0].shape[0]
    shape = jax.ShapeDtypeStruct
    whole = pl.BlockSpec(memory_space=pltpu.VMEM)
    return pl.pallas_call(
        feed_kernel,
        out_shape=(
            shape((width, model), bf16),
            shape((width, model), f32),
            shape((width, model), bf16),
            shape((ranks, width, channels), bf16),
            shape((width, ranks * units), bf16),
            shape((width, ranks * units), bf16),
            shape((width, model), bf16),
            shape((width, model), bf16),
            shape((6, model), f32),
            shape((1, ranks * units), f32),
        ),
        in_specs=[whole] * 17,
        out_specs=(whole,) * 10,
        scratch_shapes=[
            pltpu.VMEM((width, ranks * units), f32),
            pltpu.VMEM((width, model), f32),
            pltpu.VMEM((width, model), f32),
        ],
        compiler_params=pltpu.CompilerParams(vmem_limit_bytes=VMEM_LIMIT),
        cost_estimate=pl.CostEstimate(
            flops=2 * width * model * (4 * ranks * units + 2 * ranks * channels),
            bytes_accessed=30 << 20,
            transcendentals=2 * width * ranks * units,
        ),
        name="feed_layer",
    )(flat, context, *outputs, *ups, *downs, up_bias, params, cotangent)


def per_device(
    tokens,
    query_weight,
    query_bias,
    key_weight,
    value_weight,
    value_bias,
    conv_weight,
    output_weight,
    output_bias,
    first_gain,
    first_shift,
    up_weight,
    up_bias,
    down_weight,
    down_bias,
    second_gain,
    second_shift,
    segment_sizes,
    cotangent,
):
    rows, width, model = tokens.shape
    channels = query_weight.shape[1]
    ranks = lax.axis_size("tp")
    own_heads = channels // HEAD_DIM
    heads = ranks * own_heads
    hidden_units = up_weight.shape[1]
    items = segment_sizes.shape[1]
    marks = segment_sizes.shape[2]
    reach = TAPS // 2
    group = SPAN // width
    levels = group.bit_length() - 1
    device = lax.axis_index("seq")
    rank = lax.axis_index("tp")
    local_index = device % group
    group_number = device // group
    groups = segment_sizes.shape[0] // rows
    start = local_index * width

    row_sizes = lax.dynamic_index_in_dim(
        segment_sizes, rank * groups + group_number, axis=0, keepdims=False
    )
    item_ends = jnp.cumsum(jnp.sum(row_sizes, axis=1))
    item_of = count_below(item_ends, width * jnp.arange(group, dtype=jnp.int32))
    own_item = item_of[local_index]
    flags = level_flags(local_index, item_of, levels)
    slot_ends = jnp.cumsum(row_sizes.reshape(-1))
    positions = start + jnp.arange(width, dtype=jnp.int32)
    token_mark = count_below(slot_ends, positions) - own_item * marks
    own_sizes = lax.dynamic_index_in_dim(row_sizes, own_item, axis=0, keepdims=False)
    own_count = jnp.maximum(own_sizes, 1).astype(f32)[:, None]
    mark_ids = jnp.arange(marks, dtype=jnp.int32)
    member = (token_mark[:, None] == mark_ids[None, :]).astype(bf16)
    member_turned = (token_mark[None, :] == mark_ids[:, None]).astype(bf16)

    def by_rank(stacked):
        return jnp.take(stacked, jnp.arange(ranks) ^ rank, axis=0)

    small = jnp.concatenate(
        (
            query_bias.reshape(-1),
            value_bias.reshape(-1),
            conv_weight.reshape(-1),
            up_bias.reshape(-1),
        )
    )
    wide = 2 * channels
    small_rows = -(-small.shape[0] // wide)
    small_rows += -small_rows % 16
    small = jnp.pad(small, (0, small_rows * wide - small.shape[0])).reshape(small_rows, wide)
    query_key = jnp.concatenate(
        (jnp.concatenate((query_weight, key_weight), axis=1), small), axis=0
    )
    query_key = spread_shards(query_key)
    value_blocks = spread_shards(value_weight)
    output_blocks = spread_shards(output_weight)
    up_blocks = spread_shards(up_weight)
    down_blocks = spread_shards(down_weight)
    smalls = [block[model:].reshape(-1).astype(f32) for block in query_key]
    query_bias_all = jnp.stack([s[:channels] for s in smalls])
    value_bias_all = jnp.stack([s[channels : 2 * channels] for s in smalls])
    taps_all = jnp.concatenate(
        [s[2 * channels : 2 * channels + own_heads * TAPS].reshape(own_heads, TAPS) for s in smalls]
    )
    up_start = 2 * channels + own_heads * TAPS
    up_bias_all = jnp.concatenate([s[up_start : up_start + hidden_units] for s in smalls])
    taps_wide = jnp.pad(taps_all, ((0, 0), (0, 2 * LANES - TAPS)))
    taps_flipped = jnp.pad(taps_all[:, ::-1], ((0, 0), (0, 2 * LANES - TAPS)))

    flat = lax.dynamic_index_in_dim(tokens, rank, axis=0, keepdims=False)
    upstream = lax.dynamic_index_in_dim(cotangent, rank, axis=0, keepdims=False)
    half = ((2, width, channels), bf16)
    full = ((ranks, width, channels), bf16)
    full32 = ((ranks, width, channels), f32)
    edge = ((reach, model), bf16)
    marked = ((marks, model), f32)
    query, keys, lands = [], [], []
    for pair in range(2):
        project = call(
            query_key_kernel, (half, half, marked), "query_key", flops=2 * width * model * 768
        )
        q, k, part = project(
            flat,
            query_key[2 * pair],
            query_key[2 * pair + 1],
            query_bias_all[2 * pair : 2 * pair + 2],
            member_turned,
        )
        query.append(q)
        keys.append(k)
        lands.append((segment_sum(part, flags) / own_count).astype(bf16))
    land_query = jnp.concatenate(
        [group_of(lands[r // 2], 2 * (r % 2), channels) for r in range(ranks)], axis=1
    )
    land_key = jnp.concatenate(
        [group_of(lands[r // 2], 2 * (r % 2) + 1, channels) for r in range(ranks)], axis=1
    )
    values, value_head, value_tail = call(
        value_kernel, (full, edge, edge), "values", flops=2 * width * model * 768
    )(flat, *value_blocks, value_bias_all)

    def neighbours(head, tail):
        count = lax.axis_size("seq")
        before = lax.ppermute(tail, "seq", [(i, i + 1) for i in range(count - 1)])
        after = lax.ppermute(head, "seq", [(i + 1, i) for i in range(count - 1)])
        return before, after

    value_before, value_after = neighbours(value_head, value_tail)
    (state,) = call(
        key_kernel, (((marks, model + LANES), f32),), "key_softmax", flops=4 * width * 768 * 192
    )(*keys, values, land_query)
    state = soft_sum(state, flags, heads)
    (token_weights,) = call(
        token_kernel, (((ranks, own_heads * marks, width), f32),), "token_softmax",
        flops=2 * width * 768 * 192,
    )(*query, land_key)

    def split_heads(array):
        return array.reshape(array.shape[0], heads, HEAD_DIM)

    inverse, inverse_back = jax.vjp(
        landmark_inverse, split_heads(land_query).astype(f32), split_heads(land_key).astype(f32)
    )
    inverse_wide = (
        inverse.reshape(ranks, own_heads, marks, marks)
        .transpose(0, 2, 1, 3)
        .reshape(ranks, marks, channels)
    )
    edge_item = count_below(
        item_ends,
        jnp.clip(
            jnp.stack((start - 1, start + width)), 0, SPAN - 1
        ),
    )
    inside = jnp.stack((start > 0, start + width < SPAN))
    keep = (inside & (edge_item == own_item)).astype(f32)
    keep = jnp.broadcast_to(keep[None, :], (reach, 2))
    context, mixed, mixed_low = call(
        context_kernel, (full, marked, ((marks, model), bf16)), "context",
        flops=6 * width * 768 * 192,
    )(state, inverse_wide, token_weights, values, value_before, value_after, keep, taps_wide)

    params = jnp.stack(
        (output_bias, first_gain, first_shift, down_bias, second_gain, second_shift)
    ).astype(f32)
    (
        layer_out,
        back_input,
        back_attention,
        back_context,
        active,
        back_hidden,
        first_low,
        back_feed,
        norm_sums,
        up_sums,
    ) = feed_layer(
        flat, context, output_blocks, up_blocks, down_blocks, up_bias_all[None, :], params, upstream
    )

    part_back, part_land_key, query_direct, back_head, back_tail = call(
        token_back_kernel, (marked, marked, full32, edge, edge), "token_back",
        flops=8 * width * 768 * 192,
    )(back_context, token_weights, mixed_low, *query, land_key)
    back_mixed_land = segment_sum(part_back, flags)
    sum_land_key = segment_sum(part_land_key, flags)
    back_before, back_after = neighbours(back_head, back_tail)
    conv_back, tap_rows = call(
        conv_back_kernel, (full32, ((heads, 2 * LANES), f32)), "conv_back",
        flops=6 * width * 768 * 192,
    )(
        back_context, back_before, back_after, values, value_before, value_after, keep,
        taps_flipped,
    )
    conv_part = tap_rows[:, STRIPE - 1 : STRIPE - 1 + TAPS]
    units_of = functools.partial(group_of, channels=hidden_units)
    grad_down_weight = scatter_weight(
        [outer(back_feed, units_of(active, r)) for r in range(ranks)], device
    )
    grad_up_weight = scatter_weight(
        [outer(first_low, units_of(back_hidden, r)) for r in range(ranks)], device
    )
    grad_up_bias = [units_of(up_sums, r)[0] for r in range(ranks)]
    grad_output_weight = scatter_weight(
        [outer(back_attention, context[r]) for r in range(ranks)], device
    )

    back_land_heads = split_heads(back_mixed_land)
    back_inverse = jnp.einsum(
        "mhd,nhd->hmn", back_land_heads, split_heads(mixed), precision=highest
    )
    back_mixed = jnp.einsum("hmn,mhd->nhd", inverse, back_land_heads, precision=highest).reshape(
        marks, model
    )
    back_land_query_a, back_land_key_a = inverse_back(back_inverse)
    part_land_query, key_direct, back_values, value_bias_sums = call(
        key_back_kernel, (marked, full32, full, ((ranks, channels), f32)), "key_back",
        flops=10 * width * 768 * 192,
    )(*keys, values, land_query, state, mixed, back_mixed, conv_back)
    sum_land_query = segment_sum(part_land_query, flags)
    back_land_query = (sum_land_query + back_land_query_a.reshape(marks, model)) / own_count
    back_land_key = (sum_land_key + back_land_key_a.reshape(marks, model)) / own_count
    grad_row, query_bias_sums, *projection = call(
        input_back_kernel,
        (((width, model), bf16), ((ranks, channels), f32))
        + (((model, 3 * channels), bf16),) * ranks,
        "input_back",
        scratch=(pltpu.VMEM((model, width), bf16),),
        flops=2 * width * 768 * 768 * 6,
        limit=32 << 20,
    )(
        flat, query_direct, key_direct, back_values, back_land_query, back_land_key, member,
        back_input, *query_key, *value_blocks,
    )
    grad_projection = scatter_weight(projection, device)
    grad_rows = jnp.stack(spread_shards(grad_row))
    grad_tokens = by_rank(grad_rows).astype(f32)
    layer_rows = by_rank(jnp.stack(spread_shards(layer_out)))

    ranked = jnp.stack(
        [
            jnp.concatenate(
                (
                    grad_up_bias[r],
                    value_bias_sums[r],
                    query_bias_sums[r],
                    conv_part[r * own_heads : (r + 1) * own_heads].reshape(-1),
                )
            )
            for r in range(ranks)
        ]
    )
    ranked = by_rank(ranked)
    ranked_size = ranked.size
    shared = [norm_sums[k] for k in range(6)]
    bundle = jnp.concatenate([ranked.reshape(-1)] + shared)
    bundle = jnp.pad(bundle, (0, -bundle.shape[0] % (8 * LANES))).reshape(-1, LANES)
    bundle = sum_everywhere(bundle).reshape(-1)
    own_ranked = lax.dynamic_index_in_dim(
        bundle[:ranked_size].reshape(ranks, -1), rank, axis=0, keepdims=False
    )
    grad_up_bias = own_ranked[:hidden_units]
    at = hidden_units
    grad_value_bias = own_ranked[at : at + channels].reshape(own_heads, HEAD_DIM)
    at += channels
    share = HEAD_DIM // lax.axis_size("seq")
    grad_query_bias = lax.dynamic_slice_in_dim(
        own_ranked[at : at + channels].reshape(own_heads, HEAD_DIM), device * share, share, axis=1
    )
    at += channels
    grad_conv_weight = own_ranked[at : at + own_heads * TAPS].reshape(own_heads, TAPS)
    shared = [
        bundle[ranked_size + k * model : ranked_size + (k + 1) * model] for k in range(len(shared))
    ]
    return (
        layer_rows,
        grad_tokens,
        grad_projection[:, :channels],
        grad_query_bias,
        grad_projection[:, channels : 2 * channels],
        grad_projection[:, 2 * channels :],
        grad_value_bias,
        grad_conv_weight,
        grad_output_weight.T,
        shared[0],
        shared[1],
        shared[2],
        grad_up_weight,
        grad_up_bias,
        grad_down_weight.T,
        shared[3],
        shared[4],
        shared[5],
    )


def solution(mesh):
    placed = (
        P(None, "seq", None),
        P(None, "tp"),
        P("tp", None),
        P(None, "tp"),
        P(None, "tp"),
        P("tp", None),
        P("tp", None),
        P("tp", None),
        P(),
        P(),
        P(),
        P(None, "tp"),
        P("tp"),
        P("tp", None),
        P(),
        P(),
        P(),
        P(),
        P(None, "seq", None),
    )
    return jax.shard_map(
        per_device,
        mesh=mesh,
        in_specs=placed,
        out_specs=(
            P(None, "seq", None),
            P(None, "seq", None),
            P("seq", "tp"),
            P("tp", "seq"),
            P("seq", "tp"),
            P("seq", "tp"),
            P("tp", None),
            P("tp", None),
            P("tp", "seq"),
            P(),
            P(),
            P(),
            P("seq", "tp"),
            P("tp"),
            P("tp", "seq"),
            P(),
            P(),
            P(),
        ),
        check_vma=False,
    )
```

```python
import functools

import jax
import jax.numpy as jnp
from jax import lax
from jax.experimental import pallas as pl
from jax.experimental.pallas import tpu as pltpu
from jax.sharding import PartitionSpec as P

HEAD_DIM = 64
TAPS = 33
SWEEPS = 6
SPAN = 4096
LANES = 128
STRIPE = 128
TILE = 256
VMEM_LIMIT = 44 << 20


highest = lax.Precision.HIGHEST
epsilon = 1e-05
very_negative = -1e30
f32 = jnp.float32
bf16 = jnp.bfloat16


def swap(value, axis, step):
    return lax.ppermute(value, axis, [(i, i ^ step) for i in range(lax.axis_size(axis))])


def dot(a, b):
    return jnp.dot(a, b, preferred_element_type=f32)


def outer(a, b):
    return lax.dot_general(a, b, (((0,), (0,)), ((), ())), preferred_element_type=f32)


def dot_t(a, b):
    return lax.dot_general(a, b, (((1,), (1,)), ((), ())), preferred_element_type=f32)


def after(value, *others):
    return lax.optimization_barrier((value,) + others)[0]


def scatter_start(blocks):
    got = swap((blocks[1], blocks[3]), "tp", 1)
    return [
        (mine.astype(f32) + far.astype(f32)).astype(bf16)
        for mine, far in zip((blocks[0], blocks[2]), got)
    ]


def scatter_far(blocks):
    far = swap(blocks[1], "tp", 2)
    return [(blocks[0].astype(f32) + far.astype(f32)).astype(bf16)]


def scatter_level(blocks, seq_index, size, last=False):
    bit = (seq_index // size) % 2
    views = [b.reshape(b.shape[0] // 2, 2, b.shape[1], b.shape[2]) for b in blocks]
    keep = [lax.dynamic_index_in_dim(v, bit, axis=1, keepdims=False) for v in views]
    send = [lax.dynamic_index_in_dim(v, 1 - bit, axis=1, keepdims=False) for v in views]
    got = swap(tuple(send), "seq", size)
    total = [k.astype(f32) + g.astype(f32) for k, g in zip(keep, got)]
    return total if last else [t.astype(bf16) for t in total]


def by_targets(blocks, count):
    return [b.reshape(count, b.shape[0] // count, b.shape[1]) for b in blocks]


def sum_merge(a, b, use):
    return a + jnp.where(use, b, 0.0)


def flag(flags_ref, row):
    return flags_ref[row : row + 1, 0:1] > 0.5


def plain_parts():
    return sum_merge, lambda value: value.astype(bf16), lambda message: message.astype(f32)


def soft_parts(heads):
    return (
        functools.partial(merge_states, heads=heads),
        functools.partial(state_message, heads=heads),
        functools.partial(message_state, heads=heads),
    )


def edges_after(parts, flags_ref, level, facing, outer_edge, got, got_outer):
    merge = parts[0]
    near = merge(outer_edge, got, flag(flags_ref, 4 * level + 1))
    away = merge(got_outer, facing, flag(flags_ref, 4 * level + 2))
    turn = flag(flags_ref, 4 * level + 3)
    return jnp.where(turn, near, away), jnp.where(turn, away, near)


def merge_first_kernel(parts, flags_ref, own_ref, got_ref, new_ref, message_ref):
    merge, encode, decode = parts
    own, got = own_ref[...], decode(got_ref[...])
    new_ref[...] = merge(own, got, flag(flags_ref, 0))
    facing, outer_edge = edges_after(parts, flags_ref, 0, own, own, got, got)
    message_ref[...] = jnp.concatenate((encode(facing), encode(outer_edge)), axis=0)


def merge_next_kernel(parts, flags_ref, own_ref, sent_ref, got_ref, new_ref, message_ref):
    merge, encode, decode = parts
    marks = own_ref.shape[0]
    got, got_outer = decode(got_ref[:marks]), decode(got_ref[marks:])
    new_ref[...] = merge(own_ref[...], got, flag(flags_ref, 4))
    facing, _ = edges_after(
        parts, flags_ref, 1, decode(sent_ref[:marks]), decode(sent_ref[marks:]), got, got_outer
    )
    message_ref[...] = encode(facing)


def exchange(parts, name, flags, own, message):
    marks, width = own.shape
    first = call(
        functools.partial(merge_first_kernel, parts),
        (((marks, width), f32), ((2 * marks, width), bf16)),
        name + "_first",
    )
    following = call(
        functools.partial(merge_next_kernel, parts),
        (((marks, width), f32), ((marks, width), bf16)),
        name + "_next",
    )
    own, sent = first(flags, own, swap(message, "seq", 1))
    own, message = following(flags, own, sent, swap(sent, "seq", 2))
    return own, swap(message, "seq", 4)


def sum_everywhere(value):
    for axis in ("tp", "seq"):
        size = 1
        while size < lax.axis_size(axis):
            value = value + swap(value, axis, size)
            size *= 2
    return value


def newton_inverse(kernel):
    size = kernel.shape[-1]
    column_sums = jnp.sum(kernel, axis=-2)
    bound = jnp.sqrt(jnp.sum(column_sums * column_sums, axis=-1))[..., None, None]
    identity = jnp.eye(size, dtype=kernel.dtype)
    inverse = jnp.swapaxes(kernel, -1, -2) / bound
    for sweep in range(SWEEPS):
        product = jnp.matmul(kernel, inverse, precision=highest)
        inner = 7.0 * identity - product
        inner = 15.0 * identity - jnp.matmul(product, inner, precision=highest)
        inner = 13.0 * identity - jnp.matmul(product, inner, precision=highest)
        inverse = 0.25 * jnp.matmul(inverse, inner, precision=highest)
    return inverse


WHOLE = pl.BlockSpec(memory_space=pltpu.VMEM)


def call(kernel, outs, name, scratch=(), limit=24 << 20, flops=0, moved=0, scalars=0):
    outs = tuple(jax.ShapeDtypeStruct(shape, dtype) for shape, dtype in outs)

    def run(*operands):
        return pl.pallas_call(
            kernel,
            out_shape=outs,
            in_specs=[pl.BlockSpec(memory_space=pltpu.SMEM)] * scalars
            + [WHOLE] * (len(operands) - scalars),
            out_specs=(WHOLE,) * len(outs),
            scratch_shapes=list(scratch),
            compiler_params=pltpu.CompilerParams(vmem_limit_bytes=limit),
            cost_estimate=pl.CostEstimate(flops=flops, bytes_accessed=moved, transcendentals=0),
            name=name,
        )(*operands)

    return run


def lane_ids(shape):
    return lax.broadcasted_iota(jnp.int32, shape, len(shape) - 1)


def row_ids(shape):
    return lax.broadcasted_iota(jnp.int32, shape, len(shape) - 2)


def spread_heads(block):
    heads = block.shape[1] // HEAD_DIM
    tall = jnp.concatenate([block] * heads, axis=0)
    same = row_ids(tall.shape) // HEAD_DIM == lane_ids(tall.shape) // HEAD_DIM
    return jnp.where(same, tall, jnp.zeros_like(tall))


def gather_heads(square):
    heads = square.shape[1] // HEAD_DIM
    result = jnp.zeros((HEAD_DIM, square.shape[1]), square.dtype)
    lane = lane_ids(result.shape) // HEAD_DIM
    for j in range(heads):
        result = jnp.where(lane == j, square[j * HEAD_DIM : (j + 1) * HEAD_DIM], result)
    return result


def two_parts(value):
    high = value.astype(bf16)
    return high, (value - high.astype(f32)).astype(bf16)


def dot_fine(a, b):
    a_high, a_low = two_parts(a)
    b_high, b_low = two_parts(b)
    return dot(a_high, b_high) + (dot(a_high, b_low) + dot(a_low, b_high))


def dot_fine_t(a, b):
    a_high, a_low = two_parts(a)
    b_high, b_low = two_parts(b)
    return dot_t(a_high, b_high) + (dot_t(a_high, b_low) + dot_t(a_low, b_high))


def outer_fine(a, b):
    a_high, a_low = two_parts(a)
    b_high, b_low = two_parts(b)
    return outer(a_high, b_high) + (outer(a_high, b_low) + outer(a_low, b_high))


def group_of(array, r, channels):
    return array[:, r * channels : (r + 1) * channels]


def layout_kernel(place_ref, sizes_ref, member_ref, turned_ref, count_ref, flags_ref):
    row, local = place_ref[0], place_ref[1]
    sizes = sizes_ref[row].astype(f32)
    items, marks = sizes.shape
    width = turned_ref.shape[1]
    devices = SPAN // width

    def pick(condition, value, axis):
        return jnp.sum(jnp.where(condition, value, 0.0), axis=axis, keepdims=True)

    totals = jnp.sum(sizes, axis=1, keepdims=True)
    small = (items, items)
    totals_row = pick(row_ids(small) == lane_ids(small), jnp.broadcast_to(totals, small), 0)
    ends = pick(lane_ids(small) <= row_ids(small), jnp.broadcast_to(totals_row, small), 1)
    wide = (items, LANES)
    below = jnp.broadcast_to(ends, wide) <= (width * lane_ids(wide)).astype(f32)
    item_of = jnp.sum(jnp.where(below, 1.0, 0.0), axis=0, keepdims=True)

    def item_at(index):
        return pick(lane_ids(item_of.shape) == index, item_of, 1)

    own = item_at(local)
    item_rows = row_ids((items, 1)).astype(f32)
    own_sizes = pick(row_ids(sizes.shape).astype(f32) == own, sizes, 0)
    item_start = pick(item_rows < own, totals, 0)
    square = (marks, marks)
    spread = jnp.broadcast_to(own_sizes, square)
    size_column = pick(row_ids(square) == lane_ids(square), spread, 1)
    end_column = pick(lane_ids(square) <= row_ids(square), spread, 1)
    end_row = pick(row_ids(square) <= lane_ids(square), jnp.broadcast_to(size_column, square), 0)
    first = (local * width).astype(f32) - item_start
    along = lane_ids(turned_ref.shape).astype(f32) + first
    inside = (along >= end_column - size_column) & (along < end_column)
    turned_ref[...] = jnp.where(inside, 1.0, 0.0).astype(bf16)
    down = row_ids(member_ref.shape).astype(f32) + first
    inside = (down >= end_row - own_sizes) & (down < end_row)
    member_ref[...] = jnp.where(inside, 1.0, 0.0).astype(bf16)
    count_ref[...] = jnp.broadcast_to(jnp.maximum(size_column, 1.0), count_ref.shape)

    def put(at, value):
        flags_ref[at : at + 1, :] = jnp.broadcast_to(jnp.where(value, 1.0, 0.0), (1, LANES))

    level, size = 0, 1
    while size < devices:
        start = local - local % size
        is_left = (local // size) % 2 == 0
        other = jnp.where(is_left, start + size, start - size)
        far_facing = item_at(jnp.where(is_left, other, other + size - 1))
        far_outer = item_at(jnp.where(is_left, other + size - 1, other))
        facing = item_at(jnp.where(is_left, start + size - 1, start))
        outer_edge = item_at(jnp.where(is_left, start, start + size - 1))
        next_left = (local // (2 * size)) % 2 == 0
        put(4 * level, own == far_facing)
        put(4 * level + 1, outer_edge == far_facing)
        put(4 * level + 2, far_outer == facing)
        turn = jnp.where(is_left != next_left, 1.0, 0.0)
        flags_ref[4 * level + 3 : 4 * level + 4, :] = jnp.full((1, LANES), turn, f32)
        level, size = level + 1, 2 * size
    before = jnp.where(local > 0, 1.0, 0.0) * jnp.where(item_at(local - 1) == own, 1.0, 0.0)
    behind = jnp.where(local < devices - 1, 1.0, 0.0) * jnp.where(
        item_at(local + 1) == own, 1.0, 0.0
    )
    flags_ref[12:13, :] = jnp.broadcast_to(before, (1, LANES))
    flags_ref[13:14, :] = jnp.broadcast_to(behind, (1, LANES))
    flags_ref[14:16, :] = jnp.zeros((2, LANES), f32)


def query_key_kernel(flat_ref, w0, w1, bias_ref, member_ref, query_ref, keys_ref, part_ref, message_ref):
    channels = query_ref.shape[2]
    scale = HEAD_DIM ** (-0.25)
    parts = []
    for r, w in enumerate((w0, w1)):
        query = dot_t(flat_ref[...], w[:channels]) + bias_ref[r : r + 1, :]
        query = (scale * query).astype(bf16)
        keys = (scale * dot_t(flat_ref[...], w[channels:])).astype(bf16)
        query_ref[r] = query
        keys_ref[r] = keys
        parts += [dot(member_ref[...], query), dot(member_ref[...], keys)]
    part = jnp.concatenate(parts, axis=1)
    part_ref[...] = part
    message_ref[...] = part.astype(bf16)


def land_kernel(flags_ref, count_ref, own0, got0, own1, got1, query_ref, keys_ref, kernel_ref):
    channels = own0.shape[1] // 4
    heads = channels // HEAD_DIM
    count = count_ref[:, 0:1]
    queries, keys = [], []
    for own, got in ((own0, got0), (own1, got1)):
        land = sum_merge(own[...], got[...].astype(f32), flag(flags_ref, 8)) / count
        for r in range(2):
            queries.append(group_of(land, 2 * r, channels).astype(bf16))
            keys.append(group_of(land, 2 * r + 1, channels).astype(bf16))
    lane = lane_ids(queries[0].shape) // HEAD_DIM
    for r in range(len(queries)):
        for j in range(heads):
            alone = jnp.where(lane == j, queries[r], jnp.zeros_like(queries[r]))
            scores = dot_t(alone, keys[r])
            powers = jnp.exp(scores - jnp.max(scores, axis=1, keepdims=True))
            kernel_ref[r * heads + j] = powers / jnp.sum(powers, axis=1, keepdims=True)
    query_ref[...] = jnp.concatenate(queries, axis=1)
    keys_ref[...] = jnp.concatenate(keys, axis=1)


def value_kernel(flat_ref, w0, w1, w2, w3, bias_ref, values_ref, head_ref, tail_ref):
    reach = head_ref.shape[0]
    heads, tails = [], []
    for r, w in enumerate((w0, w1, w2, w3)):
        values = (dot_t(flat_ref[...], w[...]) + bias_ref[r : r + 1, :]).astype(bf16)
        values_ref[r] = values
        heads.append(values[:reach])
        tails.append(values[values.shape[0] - reach :])
    head_ref[...] = jnp.concatenate(heads, axis=1)
    tail_ref[...] = jnp.concatenate(tails, axis=1)


def key_kernel(k0, k1, values_ref, land_query_ref, state_ref, message_ref):
    channels = values_ref.shape[2]
    heads = channels // HEAD_DIM
    mixed = []
    marks = land_query_ref.shape[0]
    stats = jnp.zeros((marks, LANES), f32)
    lane = lane_ids(stats.shape)
    groups = values_ref.shape[0]
    for r in range(groups):
        keys = (k0, k1)[r // 2][r % 2]
        scores = dot_t(spread_heads(group_of(land_query_ref[...], r, channels)), keys)
        top = jnp.max(scores, axis=1, keepdims=True).astype(bf16).astype(f32)
        powers = jnp.exp(scores - top)
        total = jnp.sum(powers, axis=1, keepdims=True)
        mixed.append(gather_heads(dot(powers.astype(bf16), values_ref[r])))
        for j in range(heads):
            h = r * heads + j
            at = slice(j * marks, (j + 1) * marks)
            stats = jnp.where(lane == h, top[at], stats)
            stats = jnp.where(lane == groups * heads + h, total[at], stats)
    state = jnp.concatenate(mixed + [stats], axis=1)
    state_ref[...] = state
    message_ref[...] = state_message(state, groups * heads)


def state_message(state, heads):
    width = state.shape[1] - LANES
    stats = state[:, width:]
    lane = lane_ids(stats.shape)
    high = stats.astype(bf16).astype(f32)
    low = pltpu.roll(stats - high, heads, 1)
    last = jnp.where(lane < 2 * heads, high, jnp.where(lane < 3 * heads, low, 0.0))
    return jnp.concatenate((state[:, :width], last), axis=1).astype(bf16)


def message_state(message, heads):
    message = message.astype(f32)
    width = message.shape[1] - LANES
    stats = message[:, width:]
    lane = lane_ids(stats.shape)
    low = pltpu.roll(stats, LANES - heads, 1)
    stats = stats + jnp.where((lane >= heads) & (lane < 2 * heads), low, 0.0)
    stats = jnp.where(lane < 2 * heads, stats, 0.0)
    return jnp.concatenate((message[:, :width], stats), axis=1)


def widen(stats, first, width):
    pieces = []
    rows = stats.shape[0]
    for pair in range(width // LANES):
        lane = lane_ids((rows, LANES))
        at = first + 2 * pair
        pieces.append(
            jnp.where(lane < HEAD_DIM, stats[:, at : at + 1], stats[:, at + 1 : at + 2])
        )
    return jnp.concatenate(pieces, axis=1)


def merge_states(a, b, use, heads):
    width = a.shape[1] - LANES
    stats_a, stats_b = a[:, width:], b[:, width:]
    lane = lane_ids(stats_a.shape)
    top = jnp.where(use, jnp.maximum(stats_a, stats_b), stats_a)
    is_top = lane < heads
    scale_a = jnp.exp(jnp.where(is_top, stats_a - top, 0.0))
    scale_b = jnp.where(use, jnp.exp(jnp.where(is_top & use, stats_b - top, 0.0)), 0.0)
    values = a[:, :width] * widen(scale_a, 0, width) + b[:, :width] * widen(scale_b, 0, width)
    total = stats_a * pltpu.roll(scale_a, heads, 1) + stats_b * pltpu.roll(scale_b, heads, 1)
    stats = jnp.where(is_top, top, jnp.where(lane < 2 * heads, total, 0.0))
    return jnp.concatenate((values, stats), axis=1)


def token_kernel(q0, q1, land_key_ref, weights_ref):
    groups, rows, width = weights_ref.shape
    channels = q0.shape[2]
    heads = channels // HEAD_DIM
    for r in range(groups):
        query = (q0, q1)[r // 2][r % 2]
        scores = dot_t(spread_heads(group_of(land_key_ref[...], r, channels)), query)
        scores = scores.reshape(heads, rows // heads, width)
        powers = jnp.exp(scores - jnp.max(scores, axis=1, keepdims=True))
        weights = powers / jnp.sum(powers, axis=1, keepdims=True)
        weights_ref[r] = weights.reshape(rows, width)


def toeplitz(taps_row, rows, width):
    wide = jnp.broadcast_to(taps_row, (rows, taps_row.shape[1]))
    return pltpu.roll(wide, 0, 1, stride=1, stride_axis=0)[:, :width]


def with_rim(cells, before, after, flags_ref):
    return jnp.concatenate(
        (
            jnp.where(flag(flags_ref, 12), before, jnp.zeros_like(before)),
            cells,
            jnp.where(flag(flags_ref, 13), after, jnp.zeros_like(after)),
        ),
        axis=0,
    )


def convolve(rim, filters):
    tall = jnp.concatenate(filters, axis=0)
    span = tall.shape[1]
    pieces = []
    for start in range(0, rim.shape[0] - (span - STRIPE), STRIPE):
        product = dot(tall, rim[start : start + span])
        lane = lane_ids((STRIPE, rim.shape[1])) // HEAD_DIM
        piece = product[:STRIPE]
        for j in range(1, len(filters)):
            piece = jnp.where(lane == j, product[j * STRIPE : (j + 1) * STRIPE], piece)
        pieces.append(piece)
    return jnp.concatenate(pieces, axis=0)


def context_kernel(own_ref, got_ref, inverse_ref, weights_ref, values_ref, before_ref, after_ref,
                   flags_ref, taps_ref, context_ref, mixed_ref, low_ref, stats_ref):
    groups, width, channels = values_ref.shape
    heads = channels // HEAD_DIM
    reach = before_ref.shape[0]
    merge, _, decode = soft_parts(groups * heads)
    state = merge(own_ref[...], decode(got_ref[...]), flag(flags_ref, 8))
    model = groups * channels
    stats_ref[...] = state[:, model:]
    mixed = state[:, :model] / widen(state[:, model:], groups * heads, model)
    mixed_ref[...] = mixed
    lows = []
    for r in range(groups):
        mixed_group = group_of(mixed, r, channels)
        lane = lane_ids(mixed_group.shape) // HEAD_DIM
        land = jnp.zeros(mixed_group.shape, f32)
        for j in range(heads):
            land = jnp.where(lane == j, dot_fine(inverse_ref[r * heads + j], mixed_group), land)
        low = land.astype(bf16)
        lows.append(low)
        nystrom = outer(weights_ref[r].astype(bf16), spread_heads(low))
        rim = with_rim(
            values_ref[r],
            group_of(before_ref[...], r, channels),
            group_of(after_ref[...], r, channels),
            flags_ref,
        )
        filters = [
            toeplitz(taps_ref[r * heads + j : r * heads + j + 1, :], STRIPE, STRIPE + 2 * reach)
            .astype(bf16)
            for j in range(heads)
        ]
        context_ref[r] = (nystrom + convolve(rim, filters)).astype(bf16)
    low_ref[...] = jnp.concatenate(lows, axis=1)


def token_back_kernel(back_ref, weights_ref, low_ref, q0, q1, land_key_ref, part_ref,
                      message_ref, part_key_ref, message_key_ref, direct_ref, head_ref, tail_ref):
    groups, width, channels = back_ref.shape
    heads = channels // HEAD_DIM
    reach = head_ref.shape[0]
    parts, key_parts = [], []
    for r in range(groups):
        back = back_ref[r]
        query = (q0, q1)[r // 2][r % 2]
        weights = weights_ref[r]
        parts.append(gather_heads(dot(weights.astype(bf16), back)))
        slope = dot_t(spread_heads(group_of(low_ref[...], r, channels)), back)
        product = (weights * slope).reshape(heads, -1, width)
        rows = jnp.sum(product, axis=1, keepdims=True)
        rows = jnp.broadcast_to(rows, product.shape).reshape(weights.shape)
        scores = (weights * (slope - rows)).astype(bf16)
        key_parts.append(gather_heads(dot(scores, query)))
        direct_ref[r] = outer(scores, spread_heads(group_of(land_key_ref[...], r, channels)))
    for pieces, whole_ref, low in ((parts, part_ref, message_ref), (key_parts, part_key_ref, message_key_ref)):
        whole = jnp.concatenate(pieces, axis=1)
        whole_ref[...] = whole
        low[...] = whole.astype(bf16)
    head_ref[...] = jnp.concatenate([back_ref[r, :reach] for r in range(groups)], axis=1)
    tail_ref[...] = jnp.concatenate([back_ref[r, width - reach :] for r in range(groups)], axis=1)


def conv_back_kernel(back_ref, before_ref, after_ref, values_ref, vbefore_ref, vafter_ref, flags_ref,
                     flipped_ref, conv_ref, taps_ref):
    groups, width, channels = back_ref.shape
    heads = channels // HEAD_DIM
    reach = before_ref.shape[0]
    span = STRIPE + 2 * reach
    order = row_ids((STRIPE, STRIPE)) + lane_ids((STRIPE, STRIPE)) == STRIPE - 1
    order = jnp.where(order, 1.0, 0.0).astype(bf16)
    lane = lane_ids((STRIPE, channels)) // HEAD_DIM
    for r in range(groups):
        rim = with_rim(
            back_ref[r],
            group_of(before_ref[...], r, channels),
            group_of(after_ref[...], r, channels),
            flags_ref,
        )
        filters = [
            toeplitz(flipped_ref[r * heads + j : r * heads + j + 1, :], STRIPE, span).astype(bf16)
            for j in range(heads)
        ]
        conv_ref[r] = convolve(rim, filters)
        value_rim = with_rim(
            values_ref[r],
            group_of(vbefore_ref[...], r, channels),
            group_of(vafter_ref[...], r, channels),
            flags_ref,
        )
        total = jnp.zeros((heads * STRIPE, span), f32)
        for start in range(0, width, STRIPE):
            turned = dot(order, back_ref[r, start : start + STRIPE])
            tall = [jnp.where(lane == j, turned, 0.0).astype(bf16) for j in range(heads)]
            total = total + dot_t(jnp.concatenate(tall, axis=0), value_rim[start : start + span])
        total = jnp.concatenate(
            (total, jnp.zeros((heads * STRIPE, 2 * LANES - span), f32)), axis=1
        )
        for j in range(heads):
            skewed = pltpu.roll(
                total[j * STRIPE : (j + 1) * STRIPE], 0, 1, stride=1, stride_axis=0
            )
            h = r * heads + j
            taps_ref[h : h + 1, :] = jnp.sum(skewed, axis=0, keepdims=True)


def seed_kernel(flags_ref, own_ref, got_ref, inverse_ref, mixed_ref, back_inverse_ref, back_mixed_ref):
    back = sum_merge(own_ref[...], got_ref[...].astype(f32), flag(flags_ref, 8))
    heads = inverse_ref.shape[0]
    pairs = []
    for pair in range(heads // 2):
        near = back[:, pair * LANES : (pair + 1) * LANES]
        mixed = mixed_ref[:, pair * LANES : (pair + 1) * LANES]
        lane = lane_ids(near.shape) // HEAD_DIM
        sums = jnp.zeros(near.shape, f32)
        for j in range(2):
            h = 2 * pair + j
            alone = jnp.where(lane == j, near, 0.0)
            back_inverse_ref[h] = dot_fine_t(alone, mixed)
            sums = sums + outer_fine(inverse_ref[h], alone)
        pairs.append(sums)
    back_mixed_ref[...] = jnp.concatenate(pairs, axis=1).astype(bf16)


def key_back_kernel(k0, k1, values_ref, land_query_ref, state_ref, mixed_ref, back_mixed_ref,
                    conv_ref, part_ref, message_ref, direct_ref, back_values_ref, bias_ref):
    groups, width, channels = values_ref.shape
    heads = channels // HEAD_DIM
    stats = state_ref[...]
    parts = []
    for r in range(groups):
        keys = (k0, k1)[r // 2][r % 2]
        land = spread_heads(group_of(land_query_ref[...], r, channels))
        scores = dot_t(land, keys)
        first = r * heads
        tops = jnp.concatenate([stats[:, first + j : first + j + 1] for j in range(heads)], axis=0)
        first += groups * heads
        totals = jnp.concatenate(
            [stats[:, first + j : first + j + 1] for j in range(heads)], axis=0
        )
        weights = jnp.exp(scores - tops) * (1.0 / totals)
        back_mixed = group_of(back_mixed_ref[...], r, channels)
        spread = spread_heads(back_mixed)
        dots = jnp.sum(
            spread_heads(group_of(mixed_ref[...], r, channels)) * spread.astype(f32),
            axis=1,
            keepdims=True,
        )
        slope = dot_t(spread, values_ref[r])
        back_scores = (weights * (slope - dots)).astype(bf16)
        parts.append(gather_heads(dot(back_scores, keys)))
        direct_ref[r] = outer(back_scores, land)
        back_values = (outer(weights.astype(bf16), spread) + conv_ref[r]).astype(bf16)
        back_values_ref[r] = back_values
        bias_ref[r : r + 1, :] = jnp.sum(back_values.astype(f32), axis=0, keepdims=True)
    part = jnp.concatenate(parts, axis=1)
    part_ref[...] = part
    message_ref[...] = part.astype(bf16)


def input_back_kernel(flags_ref, count_ref, flat_ref, query_direct_ref, key_direct_ref, back_values_ref,
                      query_own_ref, query_got_ref, key_own_ref, key_got_ref, kernel_ref,
                      back_kernel_ref, land_query_ref, land_key_ref, member_ref, back_input_ref,
                      w0, w1, w2, w3, v0, v1, v2, v3, grad_ref, bias_ref, g0, g1, g2, g3,
                      turned_ref):
    groups, width, channels = back_values_ref.shape
    heads = channels // HEAD_DIM
    scale = HEAD_DIM ** (-0.25)
    member = member_ref[...]
    count = count_ref[:, 0:1]
    sides = [
        sum_merge(own[...], got[...].astype(f32), flag(flags_ref, 8))
        for own, got in ((query_own_ref, query_got_ref), (key_own_ref, key_got_ref))
    ]
    total = back_input_ref[...]
    turned_ref[...] = flat_ref[...].T
    for r in range(groups):
        w, v = (w0, w1, w2, w3)[r], (v0, v1, v2, v3)[r]
        land_query = group_of(land_query_ref[...], r, channels)
        land_key = group_of(land_key_ref[...], r, channels)
        lane = lane_ids(land_query.shape) // HEAD_DIM
        query_side = group_of(sides[0], r, channels)
        key_side = group_of(sides[1], r, channels)
        for j in range(heads):
            kernel, back = kernel_ref[r * heads + j], back_kernel_ref[r * heads + j]
            scores = kernel * (back - jnp.sum(kernel * back, axis=1, keepdims=True))
            high, low = two_parts(scores)
            more = dot(high, land_key) + dot(low, land_key)
            query_side = query_side + jnp.where(lane == j, more, 0.0)
            more = outer(high, land_query) + outer(low, land_query)
            key_side = key_side + jnp.where(lane == j, more, 0.0)
        both = []
        for side, direct_ref in ((query_side, query_direct_ref), (key_side, key_direct_ref)):
            high, low = two_parts(side / count)
            both.append((direct_ref[r] + (dot(member, high) + dot(member, low))).astype(bf16))
        bias_ref[r : r + 1, :] = scale * jnp.sum(both[0].astype(f32), axis=0, keepdims=True)
        both = jnp.concatenate(both, axis=1)
        total = total + scale * dot(both, w[...]) + dot(back_values_ref[r], v[...])
        (g0, g1, g2, g3)[r][...] = (scale * dot(turned_ref[...], both)).astype(bf16)
    grad_ref[...] = total.astype(bf16)


def value_output_kernel(flat_ref, back_values_ref, back_attention_ref, context_ref, g0, g1, g2, g3):
    flat, back = flat_ref[...].T, back_attention_ref[...].T
    for r, g in enumerate((g0, g1, g2, g3)):
        g[...] = jnp.concatenate(
            (
                dot(back, context_ref[r]).astype(bf16),
                dot(flat, back_values_ref[r]).astype(bf16),
            ),
            axis=1,
        )


def place_kernel(rank_ref, r0, r1, r2, r3, out_ref):
    step = pl.program_id(0)
    for k, ref in enumerate((r0, r1, r2, r3)):

        @pl.when(step == k)
        def _():
            out_ref[0] = ref[...].astype(out_ref.dtype)


def place_rows(rank, blocks, dtype):
    width, model = blocks[0].shape
    return pl.pallas_call(
        place_kernel,
        out_shape=jax.ShapeDtypeStruct((len(blocks), width, model), dtype),
        grid_spec=pltpu.PrefetchScalarGridSpec(
            num_scalar_prefetch=1,
            grid=(len(blocks),),
            in_specs=[pl.BlockSpec((width, model), lambda i, rank: (0, 0))] * len(blocks),
            out_specs=pl.BlockSpec((1, width, model), lambda i, rank: (i ^ rank[0], 0, 0)),
        ),
        compiler_params=pltpu.CompilerParams(vmem_limit_bytes=24 << 20),
        name="place_rows",
    )(rank.reshape(1).astype(jnp.int32), *blocks)


def feed_kernel(
    flat_ref, context_ref, out0, out1, out2, out3, up0, up1, up2, up3, down0, down1, down2, down3,
    up_bias_ref, params_ref, cotangent_ref,
    layer_ref, back_input_ref, back_attention_ref, back_context_ref, active_ref, back_hidden_ref,
    first_low_ref, back_feed_ref, sums_ref, up_sums_ref,
    slope_ref, first_ref, total_ref,
):
    outs, ups, downs = (out0, out1, out2, out3), (up0, up1, up2, up3), (down0, down1, down2, down3)
    units = up0.shape[1]
    tile = TILE
    steps = units // tile
    output_bias, first_gain, first_shift, down_bias, second_gain, second_shift = [
        params_ref[k : k + 1, :] for k in range(6)
    ]

    def mean(value):
        return jnp.mean(value, axis=1, keepdims=True)

    attention = dot(context_ref[0], out0[...])
    for r in range(1, len(outs)):
        attention = attention + dot(context_ref[r], outs[r][...])
    value = flat_ref[...].astype(f32) + attention + output_bias
    centred = value - mean(value)
    first_inverse = lax.rsqrt(mean(centred * centred) + epsilon)
    first_normed = centred * first_inverse
    first_ref[...] = first_normed
    first_out = first_normed * first_gain + first_shift
    first_low_ref[...] = first_out.astype(bf16)
    total_ref[...] = first_out + down_bias
    for r in range(len(ups)):

        def forward(step, carry):
            at = pl.multiple_of(step * tile, tile)
            whole = pl.multiple_of(r * units + at, tile)
            hidden = dot(first_low_ref[...], ups[r][:, pl.ds(at, tile)])
            hidden = hidden + up_bias_ref[:, pl.ds(whole, tile)]
            cdf = 0.5 * (1.0 + lax.erf(hidden * 0.7071067811865476))
            slope_ref[:, pl.ds(whole, tile)] = cdf + hidden * (
                0.3989422804014327 * jnp.exp(-0.5 * hidden * hidden)
            )
            active = (hidden * cdf).astype(bf16)
            active_ref[:, pl.ds(whole, tile)] = active
            total_ref[...] += dot(active, downs[r][pl.ds(at, tile), :])
            return carry

        lax.fori_loop(0, steps, forward, 0)

    value = total_ref[...]
    centred = value - mean(value)
    second_inverse = lax.rsqrt(mean(centred * centred) + epsilon)
    normed = centred * second_inverse
    layer_ref[...] = (normed * second_gain + second_shift).astype(bf16)
    upstream = cotangent_ref[...].astype(f32)
    sums_ref[4:5, :] = jnp.sum(upstream * normed, axis=0, keepdims=True)
    sums_ref[5:6, :] = jnp.sum(upstream, axis=0, keepdims=True)
    scaled = upstream * second_gain
    back_second = (scaled - mean(scaled) - normed * mean(scaled * normed)) * second_inverse
    back_feed = back_second.astype(bf16)
    back_feed_ref[...] = back_feed
    sums_ref[3:4, :] = jnp.sum(back_feed.astype(f32), axis=0, keepdims=True)
    total_ref[...] = back_second
    for r in range(len(ups)):

        def backward(step, carry):
            at = pl.multiple_of(step * tile, tile)
            whole = pl.multiple_of(r * units + at, tile)
            back_active = dot_t(back_feed_ref[...], downs[r][pl.ds(at, tile), :])
            back_hidden = (back_active * slope_ref[:, pl.ds(whole, tile)]).astype(bf16)
            back_hidden_ref[:, pl.ds(whole, tile)] = back_hidden
            up_sums_ref[:, pl.ds(whole, tile)] = jnp.sum(
                back_hidden.astype(f32), axis=0, keepdims=True
            )
            total_ref[...] += dot_t(back_hidden, ups[r][:, pl.ds(at, tile)])
            return carry

        lax.fori_loop(0, steps, backward, 0)

    back_first = total_ref[...]
    first_normed = first_ref[...]
    sums_ref[1:2, :] = jnp.sum(back_first * first_normed, axis=0, keepdims=True)
    sums_ref[2:3, :] = jnp.sum(back_first, axis=0, keepdims=True)
    scaled = back_first * first_gain
    back_input = (scaled - mean(scaled) - first_normed * mean(scaled * first_normed)) * first_inverse
    back_input_ref[...] = back_input
    back_attention = back_input.astype(bf16)
    back_attention_ref[...] = back_attention
    sums_ref[0:1, :] = jnp.sum(back_attention.astype(f32), axis=0, keepdims=True)
    for r in range(len(outs)):
        back_context_ref[r] = dot_t(back_attention, outs[r][...]).astype(bf16)


def feed_layer(flat, context, outputs, ups, downs, up_bias, params, cotangent):
    width, model = flat.shape
    ranks, units = len(ups), ups[0].shape[1]
    channels = outputs[0].shape[0]
    shape = jax.ShapeDtypeStruct
    whole = pl.BlockSpec(memory_space=pltpu.VMEM)
    return pl.pallas_call(
        feed_kernel,
        out_shape=(
            shape((width, model), bf16),
            shape((width, model), f32),
            shape((width, model), bf16),
            shape((ranks, width, channels), bf16),
            shape((width, ranks * units), bf16),
            shape((width, ranks * units), bf16),
            shape((width, model), bf16),
            shape((width, model), bf16),
            shape((6, model), f32),
            shape((1, ranks * units), f32),
        ),
        in_specs=[whole] * 17,
        out_specs=(whole,) * 10,
        scratch_shapes=[
            pltpu.VMEM((width, ranks * units), f32),
            pltpu.VMEM((width, model), f32),
            pltpu.VMEM((width, model), f32),
        ],
        compiler_params=pltpu.CompilerParams(vmem_limit_bytes=VMEM_LIMIT),
        cost_estimate=pl.CostEstimate(
            flops=2 * width * model * (4 * ranks * units + 2 * ranks * channels),
            bytes_accessed=30 << 20,
            transcendentals=2 * width * ranks * units,
        ),
        name="feed_layer",
    )(flat, context, *outputs, *ups, *downs, up_bias, params, cotangent)


def per_device(
    tokens,
    query_weight,
    query_bias,
    key_weight,
    value_weight,
    value_bias,
    conv_weight,
    output_weight,
    output_bias,
    first_gain,
    first_shift,
    up_weight,
    up_bias,
    down_weight,
    down_bias,
    second_gain,
    second_shift,
    segment_sizes,
    cotangent,
):
    rows, width, model = tokens.shape
    channels = query_weight.shape[1]
    ranks = lax.axis_size("tp")
    own_heads = channels // HEAD_DIM
    heads = ranks * own_heads
    hidden_units = up_weight.shape[1]
    items = segment_sizes.shape[1]
    marks = segment_sizes.shape[2]
    reach = TAPS // 2
    device = lax.axis_index("seq")
    rank = lax.axis_index("tp")
    group = SPAN // width
    groups = segment_sizes.shape[0] // rows
    place = jnp.stack((rank * groups + device // group, device % group)).astype(jnp.int32)

    def by_rank(stacked):
        return jnp.take(stacked, jnp.arange(ranks) ^ rank, axis=0)

    half = ((2, width, channels), bf16)
    full = ((ranks, width, channels), bf16)
    full32 = ((ranks, width, channels), f32)
    edge = ((reach, model), bf16)
    marked = ((marks, model), f32)
    message = ((marks, model), bf16)
    tall = ((marks, LANES), f32)
    squares = ((heads, marks, marks), f32)

    small = jnp.concatenate(
        (
            query_bias.reshape(-1),
            value_bias.reshape(-1),
            conv_weight.reshape(-1),
            up_bias.reshape(-1),
        )
    )
    small_rows = -(-small.shape[0] // model)
    small_rows += -small_rows % 16
    small = jnp.pad(small, (0, small_rows * model - small.shape[0])).reshape(small_rows, model)
    query_key = jnp.concatenate((query_weight.T, key_weight.T), axis=0)
    value_turned = value_weight.T
    first_far = swap(query_key, "tp", 2)
    small_far = swap(small, "tp", 2)
    first_core = swap(query_key, "tp", 1)
    small_core = swap(small, "tp", 1)
    smalls = [s.reshape(-1).astype(f32) for s in (small, small_core, small_far, swap(small_far, "tp", 1))]
    member, member_turned, count, flags = call(
        layout_kernel,
        (((width, marks), bf16), ((marks, width), bf16), tall, ((16, LANES), f32)),
        "layout",
        scalars=1,
    )(place, segment_sizes)
    query_bias_all = jnp.stack([s[:channels] for s in smalls])
    value_bias_all = jnp.stack([s[channels : 2 * channels] for s in smalls])
    taps_all = jnp.concatenate(
        [s[2 * channels : 2 * channels + own_heads * TAPS].reshape(own_heads, TAPS) for s in smalls]
    )
    up_start = 2 * channels + own_heads * TAPS
    up_bias_all = jnp.concatenate([s[up_start : up_start + hidden_units] for s in smalls])
    taps_wide = jnp.pad(taps_all, ((0, 0), (0, 2 * LANES - TAPS)))
    taps_flipped = jnp.pad(taps_all[:, ::-1], ((0, 0), (0, 2 * LANES - TAPS)))
    flat = lax.dynamic_index_in_dim(tokens, rank, axis=0, keepdims=False)
    upstream = lax.dynamic_index_in_dim(cotangent, rank, axis=0, keepdims=False)

    def shards(own, far):
        return (own, swap(own, "tp", 1), far, swap(far, "tp", 1))

    query_key = (query_key, first_core, first_far, swap(first_far, "tp", 1))
    value_far = swap(after(value_turned, first_far), "tp", 2)
    output_far = swap(after(output_weight, value_far), "tp", 2)
    up_far = swap(after(up_weight, output_far), "tp", 2)
    down_far = swap(after(down_weight, up_far), "tp", 2)
    value_blocks = shards(value_turned, value_far)
    output_blocks = shards(output_weight, output_far)
    up_blocks = shards(up_weight, up_far)
    down_blocks = shards(down_weight, down_far)

    query, keys, sums = [], [], []
    for pair in range(2):
        q, k, part, sent = call(
            query_key_kernel, (half, half, marked, message), "query_key",
            flops=2 * width * model * 768,
        )(
            flat,
            query_key[2 * pair],
            query_key[2 * pair + 1],
            query_bias_all[2 * pair : 2 * pair + 2],
            member_turned,
        )
        query.append(q)
        keys.append(k)
        sums += exchange(plain_parts(), "land", flags, part, sent)
    land_query, land_key, kernel = call(land_kernel, (message, message, squares), "land")(
        flags, count, *sums
    )
    values, value_head, value_tail = call(
        value_kernel, (full, edge, edge), "values", flops=2 * width * model * 768
    )(flat, *value_blocks, value_bias_all)

    def neighbours(head, tail):
        count = lax.axis_size("seq")
        before = lax.ppermute(tail, "seq", [(i, i + 1) for i in range(count - 1)])
        behind = lax.ppermute(head, "seq", [(i + 1, i) for i in range(count - 1)])
        return before, behind

    value_before, value_after = neighbours(value_head, value_tail)
    state, sent = call(
        key_kernel,
        (((marks, model + LANES), f32), ((marks, model + LANES), bf16)),
        "key_softmax",
        flops=4 * width * 768 * 192,
    )(*keys, values, land_query)
    state, state_got = exchange(soft_parts(heads), "soft", flags, state, sent)
    (token_weights,) = call(
        token_kernel, (((ranks, own_heads * marks, width), f32),), "token_softmax",
        flops=2 * width * 768 * 192,
    )(*query, land_key)
    inverse, inverse_back = jax.vjp(newton_inverse, kernel)
    context, mixed, mixed_low, stats = call(
        context_kernel, (full, marked, message, tall), "context", flops=6 * width * 768 * 192,
    )(
        state, state_got, inverse, token_weights, values, value_before, value_after, flags,
        taps_wide,
    )

    params = jnp.stack(
        (output_bias, first_gain, first_shift, down_bias, second_gain, second_shift)
    ).astype(f32)
    (
        layer_out,
        back_input,
        back_attention,
        back_context,
        active,
        back_hidden,
        first_low,
        back_feed,
        norm_sums,
        up_sums,
    ) = feed_layer(
        flat, context, output_blocks, up_blocks, down_blocks, up_bias_all[None, :], params, upstream
    )

    layer_far = swap(layer_out, "tp", 2)
    part_back, sent_back, part_key, sent_key, query_direct, back_head, back_tail = call(
        token_back_kernel, (marked, message, marked, message, full32, edge, edge), "token_back",
        flops=8 * width * 768 * 192,
    )(back_context, token_weights, mixed_low, *query, land_key)
    back_own, back_got = exchange(plain_parts(), "back", flags, part_back, sent_back)
    key_own, key_got = exchange(plain_parts(), "back_key", flags, part_key, sent_key)
    back_before, back_after = neighbours(back_head, back_tail)
    conv_back, tap_rows = call(
        conv_back_kernel, (full32, ((heads, 2 * LANES), f32)), "conv_back",
        flops=6 * width * 768 * 192,
    )(
        back_context, back_before, back_after, values, value_before, value_after, flags,
        taps_flipped,
    )
    conv_part = tap_rows[:, STRIPE - 1 : STRIPE - 1 + TAPS]
    units_of = functools.partial(group_of, channels=hidden_units)
    positions = lax.axis_size("seq")
    sizes = [1 << level for level in range(positions.bit_length() - 1)]
    down = scatter_start([outer(back_feed, units_of(active, r)).astype(bf16) for r in range(ranks)])
    up = scatter_start(
        [outer(first_low, units_of(back_hidden, r)).astype(bf16) for r in range(ranks)]
    )
    down = by_targets(scatter_far(down), positions)
    up = by_targets(up, positions)
    for size in sizes:
        up = scatter_level(up, device, size)
    for size in sizes:
        down = scatter_level(down, device, size, size == sizes[-1])
    grad_up_weight = scatter_far(up)[0][0].astype(f32)
    grad_down_weight = down[0][0]
    grad_up_bias = [units_of(up_sums, r)[0] for r in range(ranks)]

    back_inverse, back_mixed = call(seed_kernel, (squares, message), "seed")(
        flags, back_own, back_got, inverse, mixed
    )
    part_query, sent_query, key_direct, back_values, value_bias_sums = call(
        key_back_kernel, (marked, message, full32, full, ((ranks, channels), f32)), "key_back",
        flops=10 * width * 768 * 192,
    )(*keys, values, land_query, stats, mixed, back_mixed, conv_back)
    query_own, query_got = exchange(plain_parts(), "back_query", flags, part_query, sent_query)
    (back_kernel,) = inverse_back(back_inverse)
    pairs = (((model, 2 * channels), bf16),) * ranks
    value_output = call(value_output_kernel, pairs, "value_output", flops=4 * width * model * model)(
        flat, back_values, back_attention, context
    )
    value_output = by_targets(scatter_far(scatter_start(value_output)), positions)
    for size in sizes:
        value_output = scatter_level(value_output, device, size, size == sizes[-1])
    grad_output_weight = value_output[0][0][:, :channels].T
    grad_value_weight = value_output[0][0][:, channels:]
    grad_row, query_bias_sums, *projection = call(
        input_back_kernel,
        (((width, model), bf16), ((ranks, channels), f32)) + pairs,
        "input_back",
        scratch=(pltpu.VMEM((model, width), bf16),),
        flops=2 * width * 768 * 768 * 6,
        limit=32 << 20,
    )(
        flags, count, flat, query_direct, key_direct, back_values, query_own, query_got, key_own,
        key_got, kernel, back_kernel, land_query, land_key, member, back_input, *query_key,
        *value_blocks,
    )
    projection = by_targets(scatter_start(projection), positions)
    for size in sizes:
        projection = scatter_level(projection, device, size)
    projection = scatter_far(projection)[0][0].astype(f32)
    grad_far = swap(grad_row, "tp", 2)
    grad_tokens = place_rows(rank, shards(grad_row, grad_far), f32)
    layer_rows = place_rows(rank, shards(layer_out, layer_far), bf16)

    ranked = jnp.stack(
        [
            jnp.concatenate(
                (
                    grad_up_bias[r],
                    value_bias_sums[r],
                    query_bias_sums[r],
                    conv_part[r * own_heads : (r + 1) * own_heads].reshape(-1),
                )
            )
            for r in range(ranks)
        ]
    )
    ranked = by_rank(ranked)
    ranked_size = ranked.size
    shared = [norm_sums[k] for k in range(6)]
    bundle = jnp.concatenate([ranked.reshape(-1)] + shared)
    bundle = jnp.pad(bundle, (0, -bundle.shape[0] % (8 * LANES))).reshape(-1, LANES)
    bundle = sum_everywhere(bundle).reshape(-1)
    own_ranked = lax.dynamic_index_in_dim(
        bundle[:ranked_size].reshape(ranks, -1), rank, axis=0, keepdims=False
    )
    grad_up_bias = own_ranked[:hidden_units]
    at = hidden_units
    grad_value_bias = own_ranked[at : at + channels].reshape(own_heads, HEAD_DIM)
    at += channels
    share = HEAD_DIM // lax.axis_size("seq")
    grad_query_bias = lax.dynamic_slice_in_dim(
        own_ranked[at : at + channels].reshape(own_heads, HEAD_DIM), device * share, share, axis=1
    )
    at += channels
    grad_conv_weight = own_ranked[at : at + own_heads * TAPS].reshape(own_heads, TAPS)
    shared = [
        bundle[ranked_size + k * model : ranked_size + (k + 1) * model] for k in range(len(shared))
    ]
    return (
        layer_rows,
        grad_tokens,
        projection[:, :channels],
        grad_query_bias,
        projection[:, channels:],
        grad_value_weight,
        grad_value_bias,
        grad_conv_weight,
        grad_output_weight,
        shared[0],
        shared[1],
        shared[2],
        grad_up_weight,
        grad_up_bias,
        grad_down_weight.T,
        shared[3],
        shared[4],
        shared[5],
    )


def solution(mesh):
    placed = (
        P(None, "seq", None),
        P(None, "tp"),
        P("tp", None),
        P(None, "tp"),
        P(None, "tp"),
        P("tp", None),
        P("tp", None),
        P("tp", None),
        P(),
        P(),
        P(),
        P(None, "tp"),
        P("tp"),
        P("tp", None),
        P(),
        P(),
        P(),
        P(),
        P(None, "seq", None),
    )
    return jax.shard_map(
        per_device,
        mesh=mesh,
        in_specs=placed,
        out_specs=(
            P(None, "seq", None),
            P(None, "seq", None),
            P("seq", "tp"),
            P("tp", "seq"),
            P("seq", "tp"),
            P("seq", "tp"),
            P("tp", None),
            P("tp", None),
            P("tp", "seq"),
            P(),
            P(),
            P(),
            P("seq", "tp"),
            P("tp"),
            P("tp", "seq"),
            P(),
            P(),
            P(),
        ),
        check_vma=False,
    )
```

```python
import functools

import jax
import jax.numpy as jnp
from jax import lax
from jax.experimental import pallas as pl
from jax.experimental.pallas import tpu as pltpu
from jax.sharding import PartitionSpec as P

HEAD_DIM = 64
TAPS = 33
SWEEPS = 6
SPAN = 4096
LANES = 128
STRIPE = 128
TILE = 256
VMEM_LIMIT = 44 << 20


epsilon = 1e-05
very_negative = -1e30
f32 = jnp.float32
bf16 = jnp.bfloat16


def swap(value, axis, step):
    return lax.ppermute(value, axis, [(i, i ^ step) for i in range(lax.axis_size(axis))])


def dot(a, b):
    return jnp.dot(a, b, preferred_element_type=f32)


def outer(a, b):
    return lax.dot_general(a, b, (((0,), (0,)), ((), ())), preferred_element_type=f32)


def dot_t(a, b):
    return lax.dot_general(a, b, (((1,), (1,)), ((), ())), preferred_element_type=f32)


def after(value, *others):
    return lax.optimization_barrier((value,) + others)[0]


def scatter_start(blocks):
    got = swap((blocks[1], blocks[3]), "tp", 1)
    return [
        (mine.astype(f32) + far.astype(f32)).astype(bf16)
        for mine, far in zip((blocks[0], blocks[2]), got)
    ]


def scatter_far(blocks):
    far = swap(blocks[1], "tp", 2)
    return [(blocks[0].astype(f32) + far.astype(f32)).astype(bf16)]


def scatter_level(blocks, seq_index, size, last=False):
    bit = (seq_index // size) % 2
    views = [b.reshape(b.shape[0] // 2, 2, b.shape[1], b.shape[2]) for b in blocks]
    keep = [lax.dynamic_index_in_dim(v, bit, axis=1, keepdims=False) for v in views]
    send = [lax.dynamic_index_in_dim(v, 1 - bit, axis=1, keepdims=False) for v in views]
    got = swap(tuple(send), "seq", size)
    total = [k.astype(f32) + g.astype(f32) for k, g in zip(keep, got)]
    return total if last else [t.astype(bf16) for t in total]


def by_targets(blocks, count):
    return [b.reshape(count, b.shape[0] // count, b.shape[1]) for b in blocks]


def sum_merge(a, b, use):
    return a + jnp.where(use, b, 0.0)


def flag(flags_ref, row):
    return flags_ref[row : row + 1, 0:1] > 0.5


def plain_parts():
    return sum_merge, lambda value: value.astype(bf16), lambda message: message.astype(f32)


def soft_parts(heads):
    return (
        functools.partial(merge_states, heads=heads),
        functools.partial(state_message, heads=heads),
        functools.partial(message_state, heads=heads),
    )


def edges_after(parts, flags_ref, level, facing, outer_edge, got, got_outer):
    merge = parts[0]
    near = merge(outer_edge, got, flag(flags_ref, 4 * level + 1))
    away = merge(got_outer, facing, flag(flags_ref, 4 * level + 2))
    turn = flag(flags_ref, 4 * level + 3)
    return jnp.where(turn, near, away), jnp.where(turn, away, near)


def merge_first_kernel(parts, flags_ref, own_ref, got_ref, new_ref, message_ref):
    merge, encode, decode = parts
    own, got = own_ref[...], decode(got_ref[...])
    new_ref[...] = merge(own, got, flag(flags_ref, 0))
    facing, outer_edge = edges_after(parts, flags_ref, 0, own, own, got, got)
    message_ref[...] = jnp.concatenate((encode(facing), encode(outer_edge)), axis=0)


def merge_next_kernel(parts, flags_ref, own_ref, sent_ref, got_ref, new_ref, message_ref):
    merge, encode, decode = parts
    marks = own_ref.shape[0]
    got, got_outer = decode(got_ref[:marks]), decode(got_ref[marks:])
    new_ref[...] = merge(own_ref[...], got, flag(flags_ref, 4))
    facing, _ = edges_after(
        parts, flags_ref, 1, decode(sent_ref[:marks]), decode(sent_ref[marks:]), got, got_outer
    )
    message_ref[...] = encode(facing)


def exchange(parts, name, flags, own, message, waits=((), ())):
    marks, width = own.shape
    first = call(
        functools.partial(merge_first_kernel, parts),
        (((marks, width), f32), ((2 * marks, width), bf16)),
        name + "_first",
    )
    following = call(
        functools.partial(merge_next_kernel, parts),
        (((marks, width), f32), ((marks, width), bf16)),
        name + "_next",
    )
    own, sent = first(flags, after(own, *waits[0]), swap(message, "seq", 1))
    own, message = following(flags, after(own, *waits[1]), sent, swap(sent, "seq", 2))
    return own, swap(message, "seq", 4)


def sum_everywhere(value):
    for axis in ("tp", "seq"):
        size = 1
        while size < lax.axis_size(axis):
            value = value + swap(value, axis, size)
            size *= 2
    return value


WHOLE = pl.BlockSpec(memory_space=pltpu.VMEM)


def cost(us):
    return pl.CostEstimate(flops=0, bytes_accessed=int(us * 3.3e6), transcendentals=0)


def call(kernel, outs, name, scratch=(), limit=24 << 20, us=1.0, scalars=0):
    outs = tuple(jax.ShapeDtypeStruct(shape, dtype) for shape, dtype in outs)

    def run(*operands):
        return pl.pallas_call(
            kernel,
            out_shape=outs,
            in_specs=[pl.BlockSpec(memory_space=pltpu.SMEM)] * scalars
            + [WHOLE] * (len(operands) - scalars),
            out_specs=(WHOLE,) * len(outs),
            scratch_shapes=list(scratch),
            compiler_params=pltpu.CompilerParams(vmem_limit_bytes=limit),
            cost_estimate=cost(us),
            name=name,
        )(*operands)

    return run


def lane_ids(shape):
    return lax.broadcasted_iota(jnp.int32, shape, len(shape) - 1)


def row_ids(shape):
    return lax.broadcasted_iota(jnp.int32, shape, len(shape) - 2)


def spread_heads(block):
    heads = block.shape[1] // HEAD_DIM
    tall = jnp.concatenate([block] * heads, axis=0)
    same = row_ids(tall.shape) // HEAD_DIM == lane_ids(tall.shape) // HEAD_DIM
    return jnp.where(same, tall, jnp.zeros_like(tall))


def gather_heads(square):
    heads = square.shape[1] // HEAD_DIM
    result = jnp.zeros((HEAD_DIM, square.shape[1]), square.dtype)
    lane = lane_ids(result.shape) // HEAD_DIM
    for j in range(heads):
        result = jnp.where(lane == j, square[j * HEAD_DIM : (j + 1) * HEAD_DIM], result)
    return result


def two_parts(value):
    high = value.astype(bf16)
    return high, (value - high.astype(f32)).astype(bf16)


def first_half(shape):
    return lane_ids(shape) < HEAD_DIM


def pair_spread(pair):
    near = first_half(pair.shape)
    zero = jnp.zeros_like(pair)
    return jnp.concatenate((jnp.where(near, pair, zero), jnp.where(near, zero, pair)), axis=0)


def pair_gather(square):
    top, bottom = square[:HEAD_DIM], square[HEAD_DIM:]
    return jnp.where(first_half(top.shape), top, bottom)


def fine(product, a, b, turn=lambda value: value):
    a_high, a_low = two_parts(a)
    b_high, b_low = [turn(part) for part in two_parts(b)]
    return product(a_high, b_high) + (product(a_high, b_low) + product(a_low, b_high))


def pair_mul(a, b):
    return fine(dot, a, b, pair_spread)


def pair_mul_t(a, b):
    return fine(dot_t, a, b, pair_spread)


def pair_t_mul(a, b):
    return pair_gather(fine(outer, a, b))


def pair_sums(value, reduce=jnp.sum, neutral=0.0):
    near = first_half(value.shape)
    left = reduce(jnp.where(near, value, neutral), axis=1, keepdims=True)
    right = reduce(jnp.where(near, neutral, value), axis=1, keepdims=True)
    return jnp.where(near, left, right)


def pair_of(array, pair):
    return array[:, pair * LANES : (pair + 1) * LANES]


def pair_turned(value):
    tall = value.T
    return jnp.concatenate((tall[:HEAD_DIM], tall[HEAD_DIM:]), axis=1)


def start_bound(kernel):
    column_sums = jnp.sum(kernel, axis=0, keepdims=True)
    return column_sums, jnp.sqrt(pair_sums(column_sums * column_sums))


def pair_identity():
    shape = (HEAD_DIM, LANES)
    return jnp.where(row_ids(shape) == lane_ids(shape) % HEAD_DIM, 1.0, 0.0)


def newton_first_kernel(kernel_ref, inverse_ref, saved_ref):
    inverses = []
    for p in range(kernel_ref.shape[0]):
        kernel = kernel_ref[p]
        inverses.append(pair_turned(kernel) / start_bound(kernel)[1])
    newton_sweeps(kernel_ref, inverses, inverse_ref, saved_ref)


def newton_next_kernel(kernel_ref, last_ref, inverse_ref, saved_ref):
    inverses = [last_ref[p] for p in range(kernel_ref.shape[0])]
    newton_sweeps(kernel_ref, inverses, inverse_ref, saved_ref)


def newton_sweeps(kernel_ref, inverses, inverse_ref, saved_ref):
    pairs = range(kernel_ref.shape[0])
    identity = pair_identity()
    for sweep in range(saved_ref.shape[0]):
        products = [pair_mul(kernel_ref[p], inverses[p]) for p in pairs]
        inner = [15.0 * identity - pair_mul(products[p], 7.0 * identity - products[p]) for p in pairs]
        last = [13.0 * identity - pair_mul(products[p], inner[p]) for p in pairs]
        for p in pairs:
            saved_ref[sweep, 0, p] = inverses[p]
            saved_ref[sweep, 1, p] = products[p]
            saved_ref[sweep, 2, p] = inner[p]
            saved_ref[sweep, 3, p] = last[p]
        inverses = [0.25 * pair_mul(inverses[p], last[p]) for p in pairs]
    for p in pairs:
        inverse_ref[p] = inverses[p]


def newton_back_kernel(kernel_ref, saved_ref, inverse_in, kernel_in, inverse_out, kernel_out):
    pairs = range(kernel_ref.shape[0])
    identity = pair_identity()
    back = [inverse_in[p] for p in pairs]
    total = [kernel_in[p] for p in pairs]
    for sweep in reversed(range(saved_ref.shape[0])):
        inverse = [saved_ref[sweep, 0, p] for p in pairs]
        product = [saved_ref[sweep, 1, p] for p in pairs]
        third = [0.25 * pair_t_mul(inverse[p], back[p]) for p in pairs]
        second = [-pair_t_mul(product[p], third[p]) for p in pairs]
        first = [-pair_t_mul(product[p], second[p]) for p in pairs]
        slope = [
            -(
                pair_mul_t(third[p], saved_ref[sweep, 2, p])
                + pair_mul_t(second[p], 7.0 * identity - product[p])
                + first[p]
            )
            for p in pairs
        ]
        back = [
            0.25 * pair_mul_t(back[p], saved_ref[sweep, 3, p])
            + pair_t_mul(kernel_ref[p], slope[p])
            for p in pairs
        ]
        total = [total[p] + pair_mul_t(slope[p], inverse[p]) for p in pairs]
    for p in pairs:
        inverse_out[p] = back[p]
        kernel_out[p] = total[p]


def land_back_kernel(kernel_ref, back_start_ref, back_kernel_ref, land_query_ref, land_key_ref,
                     query_ref, key_ref):
    queries, keys = [], []
    for p in range(kernel_ref.shape[0]):
        kernel, start = kernel_ref[p], pair_turned(back_start_ref[p])
        column_sums, bound = start_bound(kernel)
        both = jnp.sum(start * kernel, axis=0, keepdims=True)
        back_bound = -pair_sums(both) / (bound * bound)
        back = back_kernel_ref[p] + start / bound + back_bound * column_sums / bound
        scores = kernel * (back - pair_sums(kernel * back))
        land_query, land_key = pair_of(land_query_ref[...], p), pair_of(land_key_ref[...], p)
        high, low = two_parts(scores)
        spread = pair_spread(land_key)
        queries.append(dot(high, spread) + dot(low, spread))
        keys.append(pair_gather(outer(high, land_query) + outer(low, land_query)))
    query_ref[...] = jnp.concatenate(queries, axis=1)
    key_ref[...] = jnp.concatenate(keys, axis=1)


def group_of(array, r, channels):
    return array[:, r * channels : (r + 1) * channels]


def layout_kernel(place_ref, sizes_ref, member_ref, turned_ref, count_ref, flags_ref):
    row, local = place_ref[0], place_ref[1]
    sizes = sizes_ref[row].astype(f32)
    items, marks = sizes.shape
    width = turned_ref.shape[1]
    devices = SPAN // width

    def pick(condition, value, axis):
        return jnp.sum(jnp.where(condition, value, 0.0), axis=axis, keepdims=True)

    totals = jnp.sum(sizes, axis=1, keepdims=True)
    small = (items, items)
    totals_row = pick(row_ids(small) == lane_ids(small), jnp.broadcast_to(totals, small), 0)
    ends = pick(lane_ids(small) <= row_ids(small), jnp.broadcast_to(totals_row, small), 1)
    wide = (items, LANES)
    below = jnp.broadcast_to(ends, wide) <= (width * lane_ids(wide)).astype(f32)
    item_of = jnp.sum(jnp.where(below, 1.0, 0.0), axis=0, keepdims=True)

    def item_at(index):
        return pick(lane_ids(item_of.shape) == index, item_of, 1)

    own = item_at(local)
    item_rows = row_ids((items, 1)).astype(f32)
    own_sizes = pick(row_ids(sizes.shape).astype(f32) == own, sizes, 0)
    item_start = pick(item_rows < own, totals, 0)
    square = (marks, marks)
    spread = jnp.broadcast_to(own_sizes, square)
    size_column = pick(row_ids(square) == lane_ids(square), spread, 1)
    end_column = pick(lane_ids(square) <= row_ids(square), spread, 1)
    end_row = pick(row_ids(square) <= lane_ids(square), jnp.broadcast_to(size_column, square), 0)
    first = (local * width).astype(f32) - item_start
    along = lane_ids(turned_ref.shape).astype(f32) + first
    inside = (along >= end_column - size_column) & (along < end_column)
    turned_ref[...] = jnp.where(inside, 1.0, 0.0).astype(bf16)
    down = row_ids(member_ref.shape).astype(f32) + first
    inside = (down >= end_row - own_sizes) & (down < end_row)
    member_ref[...] = jnp.where(inside, 1.0, 0.0).astype(bf16)
    count_ref[...] = jnp.broadcast_to(jnp.maximum(size_column, 1.0), count_ref.shape)

    def put(at, value):
        flags_ref[at : at + 1, :] = jnp.broadcast_to(jnp.where(value, 1.0, 0.0), (1, LANES))

    level, size = 0, 1
    while size < devices:
        start = local - local % size
        is_left = (local // size) % 2 == 0
        other = jnp.where(is_left, start + size, start - size)
        far_facing = item_at(jnp.where(is_left, other, other + size - 1))
        far_outer = item_at(jnp.where(is_left, other + size - 1, other))
        facing = item_at(jnp.where(is_left, start + size - 1, start))
        outer_edge = item_at(jnp.where(is_left, start, start + size - 1))
        next_left = (local // (2 * size)) % 2 == 0
        put(4 * level, own == far_facing)
        put(4 * level + 1, outer_edge == far_facing)
        put(4 * level + 2, far_outer == facing)
        turn = jnp.where(is_left != next_left, 1.0, 0.0)
        flags_ref[4 * level + 3 : 4 * level + 4, :] = jnp.full((1, LANES), turn, f32)
        level, size = level + 1, 2 * size
    before = jnp.where(local > 0, 1.0, 0.0) * jnp.where(item_at(local - 1) == own, 1.0, 0.0)
    behind = jnp.where(local < devices - 1, 1.0, 0.0) * jnp.where(
        item_at(local + 1) == own, 1.0, 0.0
    )
    flags_ref[12:13, :] = jnp.broadcast_to(before, (1, LANES))
    flags_ref[13:14, :] = jnp.broadcast_to(behind, (1, LANES))
    flags_ref[14:16, :] = jnp.zeros((2, LANES), f32)


def query_key_kernel(flat_ref, q0, k0, q1, k1, bias_ref, member_ref, query_ref, keys_ref, part_ref, message_ref):
    channels = query_ref.shape[2]
    scale = HEAD_DIM ** (-0.25)
    parts = []
    for r, (q, k) in enumerate(((q0, k0), (q1, k1))):
        query = dot_t(flat_ref[...], q[...]) + bias_ref[r : r + 1, :]
        query = (scale * query).astype(bf16)
        keys = (scale * dot_t(flat_ref[...], k[...])).astype(bf16)
        query_ref[r] = query
        keys_ref[r] = keys
        parts += [dot(member_ref[...], query), dot(member_ref[...], keys)]
    part = jnp.concatenate(parts, axis=1)
    part_ref[...] = part
    message_ref[...] = part.astype(bf16)


def land_kernel(flags_ref, count_ref, own0, got0, own1, got1, query_ref, keys_ref, kernel_ref):
    channels = own0.shape[1] // 4
    count = count_ref[:, 0:1]
    queries, keys = [], []
    for own, got in ((own0, got0), (own1, got1)):
        land = sum_merge(own[...], got[...].astype(f32), flag(flags_ref, 8)) / count
        for r in range(2):
            queries.append(group_of(land, 2 * r, channels).astype(bf16))
            keys.append(group_of(land, 2 * r + 1, channels).astype(bf16))
    land_query, land_key = jnp.concatenate(queries, axis=1), jnp.concatenate(keys, axis=1)
    query_ref[...] = land_query
    keys_ref[...] = land_key
    for p in range(kernel_ref.shape[0]):
        scores = dot_t(pair_of(land_query, p), pair_spread(pair_of(land_key, p)))
        powers = jnp.exp(scores - pair_sums(scores, jnp.max, very_negative))
        kernel_ref[p] = powers / pair_sums(powers)


def value_kernel(flat_ref, w0, w1, w2, w3, bias_ref, values_ref, head_ref, tail_ref):
    reach = head_ref.shape[0]
    heads, tails = [], []
    for r, w in enumerate((w0, w1, w2, w3)):
        values = (dot_t(flat_ref[...], w[...]) + bias_ref[r : r + 1, :]).astype(bf16)
        values_ref[r] = values
        heads.append(values[:reach])
        tails.append(values[values.shape[0] - reach :])
    head_ref[...] = jnp.concatenate(heads, axis=1)
    tail_ref[...] = jnp.concatenate(tails, axis=1)


def key_kernel(k0, k1, values_ref, land_query_ref, state_ref, message_ref):
    channels = values_ref.shape[2]
    heads = channels // HEAD_DIM
    mixed = []
    marks = land_query_ref.shape[0]
    stats = jnp.zeros((marks, LANES), f32)
    lane = lane_ids(stats.shape)
    groups = values_ref.shape[0]
    for r in range(groups):
        keys = (k0, k1)[r // 2][r % 2]
        scores = dot_t(spread_heads(group_of(land_query_ref[...], r, channels)), keys)
        top = jnp.max(scores, axis=1, keepdims=True).astype(bf16).astype(f32)
        powers = jnp.exp(scores - top)
        total = jnp.sum(powers, axis=1, keepdims=True)
        mixed.append(gather_heads(dot(powers.astype(bf16), values_ref[r])))
        for j in range(heads):
            h = r * heads + j
            at = slice(j * marks, (j + 1) * marks)
            stats = jnp.where(lane == h, top[at], stats)
            stats = jnp.where(lane == groups * heads + h, total[at], stats)
    state = jnp.concatenate(mixed + [stats], axis=1)
    state_ref[...] = state
    message_ref[...] = state_message(state, groups * heads)


def state_message(state, heads):
    width = state.shape[1] - LANES
    stats = state[:, width:]
    lane = lane_ids(stats.shape)
    high = stats.astype(bf16).astype(f32)
    low = pltpu.roll(stats - high, heads, 1)
    last = jnp.where(lane < 2 * heads, high, jnp.where(lane < 3 * heads, low, 0.0))
    return jnp.concatenate((state[:, :width], last), axis=1).astype(bf16)


def message_state(message, heads):
    message = message.astype(f32)
    width = message.shape[1] - LANES
    stats = message[:, width:]
    lane = lane_ids(stats.shape)
    low = pltpu.roll(stats, LANES - heads, 1)
    stats = stats + jnp.where((lane >= heads) & (lane < 2 * heads), low, 0.0)
    stats = jnp.where(lane < 2 * heads, stats, 0.0)
    return jnp.concatenate((message[:, :width], stats), axis=1)


def widen(stats, first, width):
    pieces = []
    rows = stats.shape[0]
    for pair in range(width // LANES):
        lane = lane_ids((rows, LANES))
        at = first + 2 * pair
        pieces.append(
            jnp.where(lane < HEAD_DIM, stats[:, at : at + 1], stats[:, at + 1 : at + 2])
        )
    return jnp.concatenate(pieces, axis=1)


def merge_states(a, b, use, heads):
    width = a.shape[1] - LANES
    stats_a, stats_b = a[:, width:], b[:, width:]
    lane = lane_ids(stats_a.shape)
    top = jnp.where(use, jnp.maximum(stats_a, stats_b), stats_a)
    is_top = lane < heads
    scale_a = jnp.exp(jnp.where(is_top, stats_a - top, 0.0))
    scale_b = jnp.where(use, jnp.exp(jnp.where(is_top & use, stats_b - top, 0.0)), 0.0)
    values = a[:, :width] * widen(scale_a, 0, width) + b[:, :width] * widen(scale_b, 0, width)
    total = stats_a * pltpu.roll(scale_a, heads, 1) + stats_b * pltpu.roll(scale_b, heads, 1)
    stats = jnp.where(is_top, top, jnp.where(lane < 2 * heads, total, 0.0))
    return jnp.concatenate((values, stats), axis=1)


def token_kernel(q0, q1, land_key_ref, weights_ref):
    groups, rows, width = weights_ref.shape
    channels = q0.shape[2]
    heads = channels // HEAD_DIM
    for r in range(groups):
        query = (q0, q1)[r // 2][r % 2]
        scores = dot_t(spread_heads(group_of(land_key_ref[...], r, channels)), query)
        scores = scores.reshape(heads, rows // heads, width)
        powers = jnp.exp(scores - jnp.max(scores, axis=1, keepdims=True))
        weights = powers / jnp.sum(powers, axis=1, keepdims=True)
        weights_ref[r] = weights.reshape(rows, width)


def toeplitz(taps_row, rows, width):
    wide = jnp.broadcast_to(taps_row, (rows, taps_row.shape[1]))
    return pltpu.roll(wide, 0, 1, stride=1, stride_axis=0)[:, :width]


def with_rim(cells, before, after, flags_ref):
    return jnp.concatenate(
        (
            jnp.where(flag(flags_ref, 12), before, jnp.zeros_like(before)),
            cells,
            jnp.where(flag(flags_ref, 13), after, jnp.zeros_like(after)),
        ),
        axis=0,
    )


def convolve(rim, filters):
    tall = jnp.concatenate(filters, axis=0)
    span = tall.shape[1]
    pieces = []
    for start in range(0, rim.shape[0] - (span - STRIPE), STRIPE):
        product = dot(tall, rim[start : start + span])
        lane = lane_ids((STRIPE, rim.shape[1])) // HEAD_DIM
        piece = product[:STRIPE]
        for j in range(1, len(filters)):
            piece = jnp.where(lane == j, product[j * STRIPE : (j + 1) * STRIPE], piece)
        pieces.append(piece)
    return jnp.concatenate(pieces, axis=0)


def context_kernel(own_ref, got_ref, inverse_ref, weights_ref, values_ref, before_ref, after_ref,
                   flags_ref, taps_ref, context_ref, mixed_ref, low_ref, stats_ref):
    groups, width, channels = values_ref.shape
    heads = channels // HEAD_DIM
    reach = before_ref.shape[0]
    merge, _, decode = soft_parts(groups * heads)
    state = merge(own_ref[...], decode(got_ref[...]), flag(flags_ref, 8))
    model = groups * channels
    stats_ref[...] = state[:, model:]
    mixed = state[:, :model] / widen(state[:, model:], groups * heads, model)
    mixed_ref[...] = mixed
    low = jnp.concatenate(
        [
            pair_mul(inverse_ref[p], pair_of(mixed, p)).astype(bf16)
            for p in range(inverse_ref.shape[0])
        ],
        axis=1,
    )
    low_ref[...] = low
    for r in range(groups):
        nystrom = outer(
            weights_ref[r].astype(bf16), spread_heads(group_of(low, r, channels))
        )
        rim = with_rim(
            values_ref[r],
            group_of(before_ref[...], r, channels),
            group_of(after_ref[...], r, channels),
            flags_ref,
        )
        filters = [
            toeplitz(taps_ref[r * heads + j : r * heads + j + 1, :], STRIPE, STRIPE + 2 * reach)
            .astype(bf16)
            for j in range(heads)
        ]
        context_ref[r] = (nystrom + convolve(rim, filters)).astype(bf16)


def token_back_kernel(back_ref, weights_ref, low_ref, q0, q1, land_key_ref, part_ref,
                      message_ref, part_key_ref, message_key_ref, direct_ref, head_ref, tail_ref):
    groups, width, channels = back_ref.shape
    heads = channels // HEAD_DIM
    reach = head_ref.shape[0]
    parts, key_parts = [], []
    for r in range(groups):
        back = back_ref[r]
        query = (q0, q1)[r // 2][r % 2]
        weights = weights_ref[r]
        parts.append(gather_heads(dot(weights.astype(bf16), back)))
        slope = dot_t(spread_heads(group_of(low_ref[...], r, channels)), back)
        product = (weights * slope).reshape(heads, -1, width)
        rows = jnp.sum(product, axis=1, keepdims=True)
        rows = jnp.broadcast_to(rows, product.shape).reshape(weights.shape)
        scores = (weights * (slope - rows)).astype(bf16)
        key_parts.append(gather_heads(dot(scores, query)))
        direct_ref[r] = outer(scores, spread_heads(group_of(land_key_ref[...], r, channels)))
    for pieces, whole_ref, low in ((parts, part_ref, message_ref), (key_parts, part_key_ref, message_key_ref)):
        whole = jnp.concatenate(pieces, axis=1)
        whole_ref[...] = whole
        low[...] = whole.astype(bf16)
    head_ref[...] = jnp.concatenate([back_ref[r, :reach] for r in range(groups)], axis=1)
    tail_ref[...] = jnp.concatenate([back_ref[r, width - reach :] for r in range(groups)], axis=1)


def conv_back_kernel(back_ref, before_ref, after_ref, values_ref, vbefore_ref, vafter_ref, flags_ref,
                     flipped_ref, conv_ref, taps_ref):
    groups, width, channels = back_ref.shape
    heads = channels // HEAD_DIM
    reach = before_ref.shape[0]
    span = STRIPE + 2 * reach
    order = row_ids((STRIPE, STRIPE)) + lane_ids((STRIPE, STRIPE)) == STRIPE - 1
    order = jnp.where(order, 1.0, 0.0).astype(bf16)
    lane = lane_ids((STRIPE, channels)) // HEAD_DIM
    for r in range(groups):
        rim = with_rim(
            back_ref[r],
            group_of(before_ref[...], r, channels),
            group_of(after_ref[...], r, channels),
            flags_ref,
        )
        filters = [
            toeplitz(flipped_ref[r * heads + j : r * heads + j + 1, :], STRIPE, span).astype(bf16)
            for j in range(heads)
        ]
        conv_ref[r] = convolve(rim, filters)
        value_rim = with_rim(
            values_ref[r],
            group_of(vbefore_ref[...], r, channels),
            group_of(vafter_ref[...], r, channels),
            flags_ref,
        )
        total = jnp.zeros((heads * STRIPE, span), f32)
        for start in range(0, width, STRIPE):
            turned = dot(order, back_ref[r, start : start + STRIPE])
            tall = [jnp.where(lane == j, turned, 0.0).astype(bf16) for j in range(heads)]
            total = total + dot_t(jnp.concatenate(tall, axis=0), value_rim[start : start + span])
        total = jnp.concatenate(
            (total, jnp.zeros((heads * STRIPE, 2 * LANES - span), f32)), axis=1
        )
        for j in range(heads):
            skewed = pltpu.roll(
                total[j * STRIPE : (j + 1) * STRIPE], 0, 1, stride=1, stride_axis=0
            )
            h = r * heads + j
            taps_ref[h : h + 1, :] = jnp.sum(skewed, axis=0, keepdims=True)


def seed_kernel(flags_ref, own_ref, got_ref, inverse_ref, mixed_ref, back_inverse_ref, back_mixed_ref):
    back = sum_merge(own_ref[...], got_ref[...].astype(f32), flag(flags_ref, 8))
    pairs = []
    for p in range(inverse_ref.shape[0]):
        near = pair_of(back, p)
        back_inverse_ref[p] = pair_mul_t(near, pair_of(mixed_ref[...], p))
        pairs.append(pair_t_mul(inverse_ref[p], near))
    back_mixed_ref[...] = jnp.concatenate(pairs, axis=1).astype(bf16)


def key_back_kernel(k0, k1, values_ref, land_query_ref, state_ref, mixed_ref, back_mixed_ref,
                    conv_ref, part_ref, message_ref, direct_ref, back_values_ref, bias_ref):
    groups, width, channels = values_ref.shape
    heads = channels // HEAD_DIM
    stats = state_ref[...]
    parts = []
    for r in range(groups):
        keys = (k0, k1)[r // 2][r % 2]
        land = spread_heads(group_of(land_query_ref[...], r, channels))
        scores = dot_t(land, keys)
        first = r * heads
        tops = jnp.concatenate([stats[:, first + j : first + j + 1] for j in range(heads)], axis=0)
        first += groups * heads
        totals = jnp.concatenate(
            [stats[:, first + j : first + j + 1] for j in range(heads)], axis=0
        )
        weights = jnp.exp(scores - tops) * (1.0 / totals)
        back_mixed = group_of(back_mixed_ref[...], r, channels)
        spread = spread_heads(back_mixed)
        dots = jnp.sum(
            spread_heads(group_of(mixed_ref[...], r, channels)) * spread.astype(f32),
            axis=1,
            keepdims=True,
        )
        slope = dot_t(spread, values_ref[r])
        back_scores = (weights * (slope - dots)).astype(bf16)
        parts.append(gather_heads(dot(back_scores, keys)))
        direct_ref[r] = outer(back_scores, land)
        back_values = (outer(weights.astype(bf16), spread) + conv_ref[r]).astype(bf16)
        back_values_ref[r] = back_values
        bias_ref[r : r + 1, :] = jnp.sum(back_values.astype(f32), axis=0, keepdims=True)
    part = jnp.concatenate(parts, axis=1)
    part_ref[...] = part
    message_ref[...] = part.astype(bf16)


def input_back_kernel(flags_ref, count_ref, flat_ref, query_direct_ref, key_direct_ref, back_values_ref,
                      query_own_ref, query_got_ref, query_more_ref, key_own_ref, key_got_ref,
                      key_more_ref, member_ref, back_input_ref, q0, q1, q2, q3, k0, k1, k2, k3, v0,
                      v1, v2, v3, grad_ref, bias_ref, g0, g1, g2, g3, turned_ref):
    groups, width, channels = back_values_ref.shape
    scale = HEAD_DIM ** (-0.25)
    member = member_ref[...]
    count = count_ref[:, 0:1]
    sides = [
        two_parts(
            (sum_merge(own[...], got[...].astype(f32), flag(flags_ref, 8)) + more[...]) / count
        )
        for own, got, more in (
            (query_own_ref, query_got_ref, query_more_ref),
            (key_own_ref, key_got_ref, key_more_ref),
        )
    ]
    total = back_input_ref[...]
    turned_ref[...] = flat_ref[...].T
    for r in range(groups):
        q, k, v = (q0, q1, q2, q3)[r], (k0, k1, k2, k3)[r], (v0, v1, v2, v3)[r]
        both = []
        for (high, low), direct_ref in zip(sides, (query_direct_ref, key_direct_ref)):
            far = dot(member, group_of(high, r, channels)) + dot(member, group_of(low, r, channels))
            both.append((direct_ref[r] + far).astype(bf16))
        bias_ref[r : r + 1, :] = scale * jnp.sum(both[0].astype(f32), axis=0, keepdims=True)
        total = total + scale * (dot(both[0], q[...]) + dot(both[1], k[...]))
        total = total + dot(back_values_ref[r], v[...])
        (g0, g1, g2, g3)[r][...] = jnp.concatenate(
            [(scale * dot(turned_ref[...], side)).astype(bf16) for side in both], axis=1
        )
    grad_ref[...] = total.astype(bf16)


def value_output_kernel(flat_ref, back_values_ref, back_attention_ref, context_ref, g0, g1, g2, g3):
    flat, back = flat_ref[...].T, back_attention_ref[...].T
    for r, g in enumerate((g0, g1, g2, g3)):
        g[...] = jnp.concatenate(
            (
                dot(back, context_ref[r]).astype(bf16),
                dot(flat, back_values_ref[r]).astype(bf16),
            ),
            axis=1,
        )


def place_kernel(rank_ref, r0, r1, r2, r3, out_ref):
    step = pl.program_id(0)
    for k, ref in enumerate((r0, r1, r2, r3)):

        @pl.when(step == k)
        def _():
            out_ref[0] = ref[...].astype(out_ref.dtype)


def place_rows(rank, blocks, dtype):
    width, model = blocks[0].shape
    return pl.pallas_call(
        place_kernel,
        out_shape=jax.ShapeDtypeStruct((len(blocks), width, model), dtype),
        grid_spec=pltpu.PrefetchScalarGridSpec(
            num_scalar_prefetch=1,
            grid=(len(blocks),),
            in_specs=[pl.BlockSpec((width, model), lambda i, rank: (0, 0))] * len(blocks),
            out_specs=pl.BlockSpec((1, width, model), lambda i, rank: (i ^ rank[0], 0, 0)),
        ),
        compiler_params=pltpu.CompilerParams(vmem_limit_bytes=24 << 20),
        cost_estimate=cost(2.5),
        name="place_rows",
    )(rank.reshape(1).astype(jnp.int32), *blocks)


def feed_kernel(
    flat_ref, context_ref, out0, out1, out2, out3, up0, up1, up2, up3, down0, down1, down2, down3,
    up_bias_ref, params_ref, cotangent_ref,
    layer_ref, back_input_ref, back_attention_ref, back_context_ref, active_ref, back_hidden_ref,
    first_low_ref, back_feed_ref, sums_ref, up_sums_ref,
    slope_ref, first_ref, total_ref,
):
    outs, ups, downs = (out0, out1, out2, out3), (up0, up1, up2, up3), (down0, down1, down2, down3)
    units = up0.shape[1]
    tile = TILE
    steps = units // tile
    output_bias, first_gain, first_shift, down_bias, second_gain, second_shift = [
        params_ref[k : k + 1, :] for k in range(6)
    ]

    def mean(value):
        return jnp.mean(value, axis=1, keepdims=True)

    attention = dot(context_ref[0], out0[...])
    for r in range(1, len(outs)):
        attention = attention + dot(context_ref[r], outs[r][...])
    value = flat_ref[...].astype(f32) + attention + output_bias
    centred = value - mean(value)
    first_inverse = lax.rsqrt(mean(centred * centred) + epsilon)
    first_normed = centred * first_inverse
    first_ref[...] = first_normed
    first_out = first_normed * first_gain + first_shift
    first_low_ref[...] = first_out.astype(bf16)
    total_ref[...] = first_out + down_bias
    for r in range(len(ups)):

        def forward(step, carry):
            at = pl.multiple_of(step * tile, tile)
            whole = pl.multiple_of(r * units + at, tile)
            hidden = dot(first_low_ref[...], ups[r][:, pl.ds(at, tile)])
            hidden = hidden + up_bias_ref[:, pl.ds(whole, tile)]
            cdf = 0.5 * (1.0 + lax.erf(hidden * 0.7071067811865476))
            slope_ref[:, pl.ds(whole, tile)] = cdf + hidden * (
                0.3989422804014327 * jnp.exp(-0.5 * hidden * hidden)
            )
            active = (hidden * cdf).astype(bf16)
            active_ref[:, pl.ds(whole, tile)] = active
            total_ref[...] += dot(active, downs[r][pl.ds(at, tile), :])
            return carry

        lax.fori_loop(0, steps, forward, 0)

    value = total_ref[...]
    centred = value - mean(value)
    second_inverse = lax.rsqrt(mean(centred * centred) + epsilon)
    normed = centred * second_inverse
    layer_ref[...] = (normed * second_gain + second_shift).astype(bf16)
    upstream = cotangent_ref[...].astype(f32)
    sums_ref[4:5, :] = jnp.sum(upstream * normed, axis=0, keepdims=True)
    sums_ref[5:6, :] = jnp.sum(upstream, axis=0, keepdims=True)
    scaled = upstream * second_gain
    back_second = (scaled - mean(scaled) - normed * mean(scaled * normed)) * second_inverse
    back_feed = back_second.astype(bf16)
    back_feed_ref[...] = back_feed
    sums_ref[3:4, :] = jnp.sum(back_feed.astype(f32), axis=0, keepdims=True)
    total_ref[...] = back_second
    for r in range(len(ups)):

        def backward(step, carry):
            at = pl.multiple_of(step * tile, tile)
            whole = pl.multiple_of(r * units + at, tile)
            back_active = dot_t(back_feed_ref[...], downs[r][pl.ds(at, tile), :])
            back_hidden = (back_active * slope_ref[:, pl.ds(whole, tile)]).astype(bf16)
            back_hidden_ref[:, pl.ds(whole, tile)] = back_hidden
            up_sums_ref[:, pl.ds(whole, tile)] = jnp.sum(
                back_hidden.astype(f32), axis=0, keepdims=True
            )
            total_ref[...] += dot_t(back_hidden, ups[r][:, pl.ds(at, tile)])
            return carry

        lax.fori_loop(0, steps, backward, 0)

    back_first = total_ref[...]
    first_normed = first_ref[...]
    sums_ref[1:2, :] = jnp.sum(back_first * first_normed, axis=0, keepdims=True)
    sums_ref[2:3, :] = jnp.sum(back_first, axis=0, keepdims=True)
    scaled = back_first * first_gain
    back_input = (scaled - mean(scaled) - first_normed * mean(scaled * first_normed)) * first_inverse
    back_input_ref[...] = back_input
    back_attention = back_input.astype(bf16)
    back_attention_ref[...] = back_attention
    sums_ref[0:1, :] = jnp.sum(back_attention.astype(f32), axis=0, keepdims=True)
    for r in range(len(outs)):
        back_context_ref[r] = dot_t(back_attention, outs[r][...]).astype(bf16)


def feed_layer(flat, context, outputs, ups, downs, up_bias, params, cotangent):
    width, model = flat.shape
    ranks, units = len(ups), ups[0].shape[1]
    channels = outputs[0].shape[0]
    shape = jax.ShapeDtypeStruct
    whole = pl.BlockSpec(memory_space=pltpu.VMEM)
    return pl.pallas_call(
        feed_kernel,
        out_shape=(
            shape((width, model), bf16),
            shape((width, model), f32),
            shape((width, model), bf16),
            shape((ranks, width, channels), bf16),
            shape((width, ranks * units), bf16),
            shape((width, ranks * units), bf16),
            shape((width, model), bf16),
            shape((width, model), bf16),
            shape((6, model), f32),
            shape((1, ranks * units), f32),
        ),
        in_specs=[whole] * 17,
        out_specs=(whole,) * 10,
        scratch_shapes=[
            pltpu.VMEM((width, ranks * units), f32),
            pltpu.VMEM((width, model), f32),
            pltpu.VMEM((width, model), f32),
        ],
        compiler_params=pltpu.CompilerParams(vmem_limit_bytes=VMEM_LIMIT),
        cost_estimate=cost(35.0),
        name="feed_layer",
    )(flat, context, *outputs, *ups, *downs, up_bias, params, cotangent)


def per_device(
    tokens,
    query_weight,
    query_bias,
    key_weight,
    value_weight,
    value_bias,
    conv_weight,
    output_weight,
    output_bias,
    first_gain,
    first_shift,
    up_weight,
    up_bias,
    down_weight,
    down_bias,
    second_gain,
    second_shift,
    segment_sizes,
    cotangent,
):
    rows, width, model = tokens.shape
    channels = query_weight.shape[1]
    ranks = lax.axis_size("tp")
    own_heads = channels // HEAD_DIM
    heads = ranks * own_heads
    hidden_units = up_weight.shape[1]
    items = segment_sizes.shape[1]
    marks = segment_sizes.shape[2]
    reach = TAPS // 2
    device = lax.axis_index("seq")
    rank = lax.axis_index("tp")
    group = SPAN // width
    groups = segment_sizes.shape[0] // rows
    place = jnp.stack((rank * groups + device // group, device % group)).astype(jnp.int32)

    def by_rank(stacked):
        return jnp.take(stacked, jnp.arange(ranks) ^ rank, axis=0)

    half = ((2, width, channels), bf16)
    full = ((ranks, width, channels), bf16)
    full32 = ((ranks, width, channels), f32)
    edge = ((reach, model), bf16)
    marked = ((marks, model), f32)
    message = ((marks, model), bf16)
    tall = ((marks, LANES), f32)
    squares = ((heads // 2, marks, LANES), f32)
    half_sweeps = SWEEPS // 2
    saved = ((half_sweeps, 4, heads // 2, marks, LANES), f32)

    small = jnp.concatenate(
        (
            query_bias.reshape(-1),
            value_bias.reshape(-1),
            conv_weight.reshape(-1),
            up_bias.reshape(-1),
        )
    )
    small_rows = -(-small.shape[0] // model)
    small_rows += -small_rows % 16
    small = jnp.pad(small, (0, small_rows * model - small.shape[0])).reshape(small_rows, model)
    turned = [w.T for w in (query_weight, key_weight, value_weight)]
    query_far, key_far = swap((turned[0], turned[1]), "tp", 2)
    query_core, key_core = swap((turned[0], turned[1]), "tp", 1)
    small_far = swap(small, "tp", 2)
    small_core = swap(small, "tp", 1)
    smalls = [s.reshape(-1).astype(f32) for s in (small, small_core, small_far, swap(small_far, "tp", 1))]
    member, member_turned, count, flags = call(
        layout_kernel,
        (((width, marks), bf16), ((marks, width), bf16), tall, ((16, LANES), f32)),
        "layout",
        scalars=1,
    )(place, segment_sizes)
    query_bias_all = jnp.stack([s[:channels] for s in smalls])
    value_bias_all = jnp.stack([s[channels : 2 * channels] for s in smalls])
    taps_all = jnp.concatenate(
        [s[2 * channels : 2 * channels + own_heads * TAPS].reshape(own_heads, TAPS) for s in smalls]
    )
    up_start = 2 * channels + own_heads * TAPS
    up_bias_all = jnp.concatenate([s[up_start : up_start + hidden_units] for s in smalls])
    taps_wide = jnp.pad(taps_all, ((0, 0), (0, 2 * LANES - TAPS)))
    taps_flipped = jnp.pad(taps_all[:, ::-1], ((0, 0), (0, 2 * LANES - TAPS)))
    flat = lax.dynamic_index_in_dim(tokens, rank, axis=0, keepdims=False)
    upstream = lax.dynamic_index_in_dim(cotangent, rank, axis=0, keepdims=False)

    def shards(own, far):
        return (own, swap(own, "tp", 1), far, swap(far, "tp", 1))

    query_blocks = (turned[0], query_core, query_far, swap(query_far, "tp", 1))
    key_blocks = (turned[1], key_core, key_far, swap(key_far, "tp", 1))
    value_far = swap(after(turned[2], key_far), "tp", 2)
    output_far = swap(after(output_weight, value_far), "tp", 2)
    up_far = swap(after(up_weight, output_far), "tp", 2)
    down_far = swap(after(down_weight, up_far), "tp", 2)
    value_blocks = shards(turned[2], value_far)
    output_blocks = shards(output_weight, output_far)
    up_blocks = shards(up_weight, up_far)
    down_blocks = shards(down_weight, down_far)

    query, keys, sums = [], [], []
    for pair in range(2):
        q, k, part, sent = call(
            query_key_kernel, (half, half, marked, message), "query_key", us=2.5,
        )(
            flat,
            query_blocks[2 * pair],
            key_blocks[2 * pair],
            query_blocks[2 * pair + 1],
            key_blocks[2 * pair + 1],
            query_bias_all[2 * pair : 2 * pair + 2],
            member_turned,
        )
        query.append(q)
        keys.append(k)
        sums += exchange(plain_parts(), "land", flags, part, sent)
    land_query, land_key, kernel = call(land_kernel, (message, message, squares), "land")(
        flags, count, *sums
    )
    values, value_head, value_tail = call(
        value_kernel, (full, edge, edge), "values", us=2.0
    )(flat, *value_blocks, value_bias_all)

    def neighbours(head, tail):
        count = lax.axis_size("seq")
        before = lax.ppermute(tail, "seq", [(i, i + 1) for i in range(count - 1)])
        behind = lax.ppermute(head, "seq", [(i + 1, i) for i in range(count - 1)])
        return before, behind

    value_before, value_after = neighbours(value_head, value_tail)
    state, sent = call(
        key_kernel,
        (((marks, model + LANES), f32), ((marks, model + LANES), bf16)),
        "key_softmax",
        us=1.4,
    )(*keys, values, after(land_query, up_far))
    state, state_got = exchange(soft_parts(heads), "soft", flags, state, sent)
    (token_weights,) = call(
        token_kernel, (((ranks, own_heads * marks, width), f32),), "token_softmax", us=0.8,
    )(*query, land_key)
    inverse, saved_first = call(newton_first_kernel, (squares, saved), "newton_first", us=6.0)(kernel)
    inverse, saved_last = call(newton_next_kernel, (squares, saved), "newton_next", us=6.0)(
        kernel, inverse
    )
    context, mixed, mixed_low, stats = call(
        context_kernel, (full, marked, message, tall), "context", us=2.0,
    )(
        after(state, down_far), state_got, inverse, token_weights, values, value_before, value_after, flags,
        taps_wide,
    )

    params = jnp.stack(
        (output_bias, first_gain, first_shift, down_bias, second_gain, second_shift)
    ).astype(f32)
    (
        layer_out,
        back_input,
        back_attention,
        back_context,
        active,
        back_hidden,
        first_low,
        back_feed,
        norm_sums,
        up_sums,
    ) = feed_layer(
        flat, context, output_blocks, up_blocks, down_blocks, up_bias_all[None, :], params, upstream
    )

    layer_far = swap(layer_out, "tp", 2)
    units_of = functools.partial(group_of, channels=hidden_units)
    positions = lax.axis_size("seq")
    sizes = [1 << level for level in range(positions.bit_length() - 1)]
    down = [outer(back_feed, units_of(active, r)).astype(bf16) for r in range(ranks)]
    part_back, sent_back, part_key, sent_key, query_direct, back_head, back_tail = call(
        token_back_kernel, (marked, message, marked, message, full32, edge, edge), "token_back",
        us=1.8,
    )(after(back_context, *down), token_weights, mixed_low, *query, land_key)
    down = scatter_start(down)
    up = [outer(first_low, units_of(back_hidden, r)).astype(bf16) for r in range(ranks)]
    back_own, back_got = exchange(
        plain_parts(), "back", flags, part_back, sent_back, (up[:2], up[2:] + down)
    )
    key_own, key_got = exchange(plain_parts(), "back_key", flags, part_key, sent_key)
    back_before, back_after = neighbours(back_head, back_tail)
    conv_back, tap_rows = call(
        conv_back_kernel, (full32, ((heads, 2 * LANES), f32)), "conv_back", us=2.8
    )(
        back_context, back_before, back_after, values, value_before, value_after, flags,
        taps_flipped,
    )
    conv_part = tap_rows[:, STRIPE - 1 : STRIPE - 1 + TAPS]
    up = scatter_start(up)
    back_inverse, back_mixed = call(seed_kernel, (squares, message), "seed")(
        flags, after(back_own, conv_back, layer_far, *up), back_got, inverse, mixed
    )
    down = by_targets(scatter_far([down[0], after(down[1], layer_far)]), positions)
    up = scatter_level(by_targets(up, positions), device, 1)
    part_query, sent_query, key_direct, back_values, value_bias_sums = call(
        key_back_kernel, (marked, message, full32, full, ((ranks, channels), f32)), "key_back",
        us=2.4,
    )(*keys, values, land_query, stats, mixed, back_mixed, conv_back)
    newton_back = call(newton_back_kernel, (squares, squares), "newton_back", us=10.0)
    back_middle = newton_back(kernel, saved_last, back_inverse, jnp.zeros(*squares))
    pairs = (((model, 2 * channels), bf16),) * ranks
    value_output = call(value_output_kernel, pairs, "value_output", us=2.0)(
        flat, back_values, back_attention, context
    )
    query_own, query_got = exchange(
        plain_parts(), "back_query", flags, part_query, sent_query,
        (list(back_middle), list(value_output)),
    )
    back_start, back_kernel = newton_back(kernel, saved_first, *back_middle)
    query_more, key_more = call(land_back_kernel, (marked, marked), "land_back")(
        kernel, back_start, back_kernel, land_query, land_key
    )
    value_output = scatter_start(value_output)
    grad_row, query_bias_sums, *projection = call(
        input_back_kernel,
        (((width, model), bf16), ((ranks, channels), f32)) + pairs,
        "input_back",
        scratch=(pltpu.VMEM((model, width), bf16),),
        us=7.0,
        limit=32 << 20,
    )(
        flags, count, flat, query_direct, key_direct, back_values,
        after(query_own, *down, *up, *value_output), query_got, query_more, key_own, key_got,
        key_more, member, back_input, *query_blocks, *key_blocks, *value_blocks,
    )
    for size in sizes[1:]:
        up = scatter_level(up, device, size)
    for size in sizes:
        down = scatter_level(down, device, size, size == sizes[-1])
    grad_up_weight = scatter_far(up)[0][0].astype(f32)
    grad_down_weight = down[0][0]
    grad_up_bias = [units_of(up_sums, r)[0] for r in range(ranks)]
    value_output = by_targets(scatter_far(value_output), positions)
    for size in sizes:
        value_output = scatter_level(value_output, device, size, size == sizes[-1])
    grad_output_weight = value_output[0][0][:, :channels].T
    grad_value_weight = value_output[0][0][:, channels:]
    projection = by_targets(scatter_start(projection), positions)
    for size in sizes:
        projection = scatter_level(projection, device, size)
    projection = scatter_far(projection)[0][0].astype(f32)
    grad_far = swap(grad_row, "tp", 2)
    grad_tokens = place_rows(rank, shards(grad_row, grad_far), f32)
    layer_rows = place_rows(rank, shards(layer_out, layer_far), bf16)

    ranked = jnp.stack(
        [
            jnp.concatenate(
                (
                    grad_up_bias[r],
                    value_bias_sums[r],
                    query_bias_sums[r],
                    conv_part[r * own_heads : (r + 1) * own_heads].reshape(-1),
                )
            )
            for r in range(ranks)
        ]
    )
    ranked = by_rank(ranked)
    ranked_size = ranked.size
    shared = [norm_sums[k] for k in range(6)]
    bundle = jnp.concatenate([ranked.reshape(-1)] + shared)
    bundle = jnp.pad(bundle, (0, -bundle.shape[0] % (8 * LANES))).reshape(-1, LANES)
    bundle = sum_everywhere(bundle).reshape(-1)
    own_ranked = lax.dynamic_index_in_dim(
        bundle[:ranked_size].reshape(ranks, -1), rank, axis=0, keepdims=False
    )
    grad_up_bias = own_ranked[:hidden_units]
    at = hidden_units
    grad_value_bias = own_ranked[at : at + channels].reshape(own_heads, HEAD_DIM)
    at += channels
    share = HEAD_DIM // lax.axis_size("seq")
    grad_query_bias = lax.dynamic_slice_in_dim(
        own_ranked[at : at + channels].reshape(own_heads, HEAD_DIM), device * share, share, axis=1
    )
    at += channels
    grad_conv_weight = own_ranked[at : at + own_heads * TAPS].reshape(own_heads, TAPS)
    shared = [
        bundle[ranked_size + k * model : ranked_size + (k + 1) * model] for k in range(len(shared))
    ]
    return (
        layer_rows,
        grad_tokens,
        projection[:, :channels],
        grad_query_bias,
        projection[:, channels:],
        grad_value_weight,
        grad_value_bias,
        grad_conv_weight,
        grad_output_weight,
        shared[0],
        shared[1],
        shared[2],
        grad_up_weight,
        grad_up_bias,
        grad_down_weight.T,
        shared[3],
        shared[4],
        shared[5],
    )


def solution(mesh):
    placed = (
        P(None, "seq", None),
        P(None, "tp"),
        P("tp", None),
        P(None, "tp"),
        P(None, "tp"),
        P("tp", None),
        P("tp", None),
        P("tp", None),
        P(),
        P(),
        P(),
        P(None, "tp"),
        P("tp"),
        P("tp", None),
        P(),
        P(),
        P(),
        P(),
        P(None, "seq", None),
    )
    return jax.shard_map(
        per_device,
        mesh=mesh,
        in_specs=placed,
        out_specs=(
            P(None, "seq", None),
            P(None, "seq", None),
            P("seq", "tp"),
            P("tp", "seq"),
            P("seq", "tp"),
            P("seq", "tp"),
            P("tp", None),
            P("tp", None),
            P("tp", "seq"),
            P(),
            P(),
            P(),
            P("seq", "tp"),
            P("tp"),
            P("tp", "seq"),
            P(),
            P(),
            P(),
        ),
        check_vma=False,
    )
```

```python
import functools

import jax
import jax.numpy as jnp
from jax import lax
from jax.experimental import pallas as pl
from jax.experimental.pallas import tpu as pltpu
from jax.sharding import PartitionSpec as P

HEAD_DIM = 64
TAPS = 33
SWEEPS = 6
SPAN = 4096
LANES = 128
STRIPE = 128
VMEM_LIMIT = 28 << 20


epsilon = 1e-05
very_negative = -1e30
f32 = jnp.float32
bf16 = jnp.bfloat16


def swap(value, axis, step):
    return lax.ppermute(value, axis, [(i, i ^ step) for i in range(lax.axis_size(axis))])


def dot(a, b):
    return jnp.dot(a, b, preferred_element_type=f32)


def outer(a, b):
    return lax.dot_general(a, b, (((0,), (0,)), ((), ())), preferred_element_type=f32)


def dot_t(a, b):
    return lax.dot_general(a, b, (((1,), (1,)), ((), ())), preferred_element_type=f32)


def after(value, *others):
    return lax.optimization_barrier((value,) + others)[0]


class Scatter:
    def __init__(self, name, mine, theirs, bits, hops):
        self.name, self.bits, self.hops = name, bits, list(hops)
        self.keep, self.send, self.way = mine, theirs, ("tp", 1)

    def hop(self, other=None):
        operands = [self.keep, swap(self.send, *self.way)]
        tiles, rows, columns = self.keep.shape
        if other is not None:
            operands += [other.keep, swap(other.send, *other.way)]
            columns += other.keep.shape[2]
        if not self.hops:
            kernel, outs = last_tile_kernel, (((tiles, rows, columns), f32),)
        else:
            following = self.hops.pop(0)
            far = following == "far"
            self.way = ("tp", 2) if far else ("seq", 1 << following)
            kernel = functools.partial(route_kernel, None if far else following)
            outs = (((tiles // 2, rows, columns), bf16),) * 2
        size = tiles * rows * columns * 2
        result = call(
            kernel, outs, self.name + "_route", scalars=1, us=0.5 + size / 1.2e6, limit=16 << 20
        )(self.bits, *operands)
        self.keep = result[0]
        self.send = result[-1]
        return result

    def wait_for(self, *others):
        self.send = after(self.send, *others)


def sum_merge(a, b, use):
    return a + jnp.where(use, b, 0.0)


def flag(flags_ref, row):
    return flags_ref[row : row + 1, 0:1] > 0.5


def plain_parts():
    return sum_merge, lambda value: value.astype(bf16), lambda message: message.astype(f32)


def soft_parts(heads):
    return (
        functools.partial(merge_states, heads=heads),
        functools.partial(state_message, heads=heads),
        functools.partial(message_state, heads=heads),
    )


def edges_after(parts, flags_ref, level, facing, outer_edge, got, got_outer):
    merge = parts[0]
    near = merge(outer_edge, got, flag(flags_ref, 4 * level + 1))
    away = merge(got_outer, facing, flag(flags_ref, 4 * level + 2))
    turn = flag(flags_ref, 4 * level + 3)
    return jnp.where(turn, near, away), jnp.where(turn, away, near)


def merge_first_kernel(parts, flags_ref, own_ref, got_ref, new_ref, message_ref):
    merge, encode, decode = parts
    own, got = own_ref[...], decode(got_ref[...])
    new_ref[...] = merge(own, got, flag(flags_ref, 0))
    facing, outer_edge = edges_after(parts, flags_ref, 0, own, own, got, got)
    message_ref[...] = jnp.concatenate((encode(facing), encode(outer_edge)), axis=0)


def merge_next_kernel(parts, flags_ref, own_ref, sent_ref, got_ref, new_ref, message_ref):
    merge, encode, decode = parts
    marks = own_ref.shape[0]
    got, got_outer = decode(got_ref[:marks]), decode(got_ref[marks:])
    new_ref[...] = merge(own_ref[...], got, flag(flags_ref, 4))
    facing, _ = edges_after(
        parts, flags_ref, 1, decode(sent_ref[:marks]), decode(sent_ref[marks:]), got, got_outer
    )
    message_ref[...] = encode(facing)


def exchange(parts, name, flags, own, message, waits=((), ()), marks_of=None):
    marks, width = own.shape
    first = call(
        functools.partial(merge_first_kernel, parts),
        (((marks, width), f32), ((2 * marks, width), bf16)),
        name + "_first",
    )
    following = call(
        functools.partial(merge_next_kernel, parts),
        (((marks, width), f32), ((marks, width), bf16)),
        name + "_next",
    )
    own, sent = first(flags, after(own, *waits[0]), swap(message, "seq", 1))
    first_own = own
    own, message = following(flags, after(own, *waits[1]), sent, swap(sent, "seq", 2))
    if marks_of is not None:
        marks_of += [first_own, own]
    return own, swap(message, "seq", 4)


def sum_everywhere(value):
    for axis in ("tp", "seq"):
        size = 1
        while size < lax.axis_size(axis):
            value = value + swap(value, axis, size)
            size *= 2
    return value


WHOLE = pl.BlockSpec(memory_space=pltpu.VMEM)


def cost(us):
    return pl.CostEstimate(flops=0, bytes_accessed=int(us * 3.3e6), transcendentals=0)


def call(kernel, outs, name, scratch=(), limit=12 << 20, us=1.0, scalars=0):
    outs = tuple(jax.ShapeDtypeStruct(shape, dtype) for shape, dtype in outs)

    def run(*operands):
        return pl.pallas_call(
            kernel,
            out_shape=outs,
            in_specs=[pl.BlockSpec(memory_space=pltpu.SMEM)] * scalars
            + [WHOLE] * (len(operands) - scalars),
            out_specs=(WHOLE,) * len(outs),
            scratch_shapes=list(scratch),
            compiler_params=pltpu.CompilerParams(vmem_limit_bytes=limit),
            cost_estimate=cost(us),
            name=name,
        )(*operands)

    return run


def lane_ids(shape):
    return lax.broadcasted_iota(jnp.int32, shape, len(shape) - 1)


def row_ids(shape):
    return lax.broadcasted_iota(jnp.int32, shape, len(shape) - 2)


def spread_heads(block):
    heads = block.shape[1] // HEAD_DIM
    tall = jnp.concatenate([block] * heads, axis=0)
    same = row_ids(tall.shape) // HEAD_DIM == lane_ids(tall.shape) // HEAD_DIM
    return jnp.where(same, tall, jnp.zeros_like(tall))


def gather_heads(square):
    heads = square.shape[1] // HEAD_DIM
    result = jnp.zeros((HEAD_DIM, square.shape[1]), square.dtype)
    lane = lane_ids(result.shape) // HEAD_DIM
    for j in range(heads):
        result = jnp.where(lane == j, square[j * HEAD_DIM : (j + 1) * HEAD_DIM], result)
    return result


def two_parts(value):
    high = value.astype(bf16)
    return high, (value - high.astype(f32)).astype(bf16)


def first_half(shape):
    return lane_ids(shape) < HEAD_DIM


def pair_spread(pair):
    near = first_half(pair.shape)
    zero = jnp.zeros_like(pair)
    return jnp.concatenate((jnp.where(near, pair, zero), jnp.where(near, zero, pair)), axis=0)


def pair_gather(square):
    top, bottom = square[:HEAD_DIM], square[HEAD_DIM:]
    return jnp.where(first_half(top.shape), top, bottom)


def fine(product, a, b, turn=lambda value: value):
    a_high, a_low = two_parts(a)
    b_high, b_low = [turn(part) for part in two_parts(b)]
    return product(a_high, b_high) + (product(a_high, b_low) + product(a_low, b_high))


def pair_mul(a, b):
    return fine(dot, a, b, pair_spread)


def pair_mul_t(a, b):
    return fine(dot_t, a, b, pair_spread)


def pair_t_mul(a, b):
    return pair_gather(fine(outer, a, b))


def pair_sums(value, reduce=jnp.sum, neutral=0.0):
    near = first_half(value.shape)
    left = reduce(jnp.where(near, value, neutral), axis=1, keepdims=True)
    right = reduce(jnp.where(near, neutral, value), axis=1, keepdims=True)
    return jnp.where(near, left, right)


def pair_of(array, pair):
    return array[:, pair * LANES : (pair + 1) * LANES]


def pair_turned(value):
    tall = value.T
    return jnp.concatenate((tall[:HEAD_DIM], tall[HEAD_DIM:]), axis=1)


def start_bound(kernel):
    column_sums = jnp.sum(kernel, axis=0, keepdims=True)
    return column_sums, jnp.sqrt(pair_sums(column_sums * column_sums))


def pair_identity():
    shape = (HEAD_DIM, LANES)
    return jnp.where(row_ids(shape) == lane_ids(shape) % HEAD_DIM, 1.0, 0.0)


def newton_first_kernel(kernel_ref, inverse_ref, saved_ref):
    inverses = []
    for p in range(kernel_ref.shape[0]):
        kernel = kernel_ref[p]
        inverses.append(pair_turned(kernel) / start_bound(kernel)[1])
    newton_sweeps(kernel_ref, inverses, inverse_ref, saved_ref)


def newton_next_kernel(kernel_ref, last_ref, inverse_ref, saved_ref):
    inverses = [last_ref[p] for p in range(kernel_ref.shape[0])]
    newton_sweeps(kernel_ref, inverses, inverse_ref, saved_ref)


def newton_sweeps(kernel_ref, inverses, inverse_ref, saved_ref):
    pairs = range(kernel_ref.shape[0])
    identity = pair_identity()
    for sweep in range(saved_ref.shape[0]):
        products = [pair_mul(kernel_ref[p], inverses[p]) for p in pairs]
        inner = [15.0 * identity - pair_mul(products[p], 7.0 * identity - products[p]) for p in pairs]
        last = [13.0 * identity - pair_mul(products[p], inner[p]) for p in pairs]
        for p in pairs:
            saved_ref[sweep, 0, p] = inverses[p]
            saved_ref[sweep, 1, p] = products[p]
            saved_ref[sweep, 2, p] = inner[p]
            saved_ref[sweep, 3, p] = last[p]
        inverses = [0.25 * pair_mul(inverses[p], last[p]) for p in pairs]
    for p in pairs:
        inverse_ref[p] = inverses[p]


def newton_back_kernel(kernel_ref, saved_ref, inverse_in, kernel_in, inverse_out, kernel_out):
    pairs = range(kernel_ref.shape[0])
    identity = pair_identity()
    back = [inverse_in[p] for p in pairs]
    total = [kernel_in[p] for p in pairs]
    for sweep in reversed(range(saved_ref.shape[0])):
        inverse = [saved_ref[sweep, 0, p] for p in pairs]
        product = [saved_ref[sweep, 1, p] for p in pairs]
        third = [0.25 * pair_t_mul(inverse[p], back[p]) for p in pairs]
        second = [-pair_t_mul(product[p], third[p]) for p in pairs]
        first = [-pair_t_mul(product[p], second[p]) for p in pairs]
        slope = [
            -(
                pair_mul_t(third[p], saved_ref[sweep, 2, p])
                + pair_mul_t(second[p], 7.0 * identity - product[p])
                + first[p]
            )
            for p in pairs
        ]
        back = [
            0.25 * pair_mul_t(back[p], saved_ref[sweep, 3, p])
            + pair_t_mul(kernel_ref[p], slope[p])
            for p in pairs
        ]
        total = [total[p] + pair_mul_t(slope[p], inverse[p]) for p in pairs]
    for p in pairs:
        inverse_out[p] = back[p]
        kernel_out[p] = total[p]


def land_back_kernel(kernel_ref, back_start_ref, back_kernel_ref, land_query_ref, land_key_ref,
                     query_ref, key_ref):
    queries, keys = [], []
    for p in range(kernel_ref.shape[0]):
        kernel, start = kernel_ref[p], pair_turned(back_start_ref[p])
        column_sums, bound = start_bound(kernel)
        both = jnp.sum(start * kernel, axis=0, keepdims=True)
        back_bound = -pair_sums(both) / (bound * bound)
        back = back_kernel_ref[p] + start / bound + back_bound * column_sums / bound
        scores = kernel * (back - pair_sums(kernel * back))
        land_query, land_key = pair_of(land_query_ref[...], p), pair_of(land_key_ref[...], p)
        high, low = two_parts(scores)
        spread = pair_spread(land_key)
        queries.append(dot(high, spread) + dot(low, spread))
        keys.append(pair_gather(outer(high, land_query) + outer(low, land_query)))
    query_ref[...] = jnp.concatenate(queries, axis=1)
    key_ref[...] = jnp.concatenate(keys, axis=1)


def group_of(array, r, channels):
    return array[:, r * channels : (r + 1) * channels]


def layout_kernel(place_ref, sizes_ref, member_ref, turned_ref, count_ref, flags_ref):
    row, local = place_ref[0], place_ref[1]
    sizes = sizes_ref[row].astype(f32)
    items, marks = sizes.shape
    width = turned_ref.shape[1]
    devices = SPAN // width

    def pick(condition, value, axis):
        return jnp.sum(jnp.where(condition, value, 0.0), axis=axis, keepdims=True)

    totals = jnp.sum(sizes, axis=1, keepdims=True)
    small = (items, items)
    totals_row = pick(row_ids(small) == lane_ids(small), jnp.broadcast_to(totals, small), 0)
    ends = pick(lane_ids(small) <= row_ids(small), jnp.broadcast_to(totals_row, small), 1)
    wide = (items, LANES)
    below = jnp.broadcast_to(ends, wide) <= (width * lane_ids(wide)).astype(f32)
    item_of = jnp.sum(jnp.where(below, 1.0, 0.0), axis=0, keepdims=True)

    def item_at(index):
        return pick(lane_ids(item_of.shape) == index, item_of, 1)

    own = item_at(local)
    item_rows = row_ids((items, 1)).astype(f32)
    own_sizes = pick(row_ids(sizes.shape).astype(f32) == own, sizes, 0)
    item_start = pick(item_rows < own, totals, 0)
    square = (marks, marks)
    spread = jnp.broadcast_to(own_sizes, square)
    size_column = pick(row_ids(square) == lane_ids(square), spread, 1)
    end_column = pick(lane_ids(square) <= row_ids(square), spread, 1)
    end_row = pick(row_ids(square) <= lane_ids(square), jnp.broadcast_to(size_column, square), 0)
    first = (local * width).astype(f32) - item_start
    along = lane_ids(turned_ref.shape).astype(f32) + first
    inside = (along >= end_column - size_column) & (along < end_column)
    turned_ref[...] = jnp.where(inside, 1.0, 0.0).astype(bf16)
    down = row_ids(member_ref.shape).astype(f32) + first
    inside = (down >= end_row - own_sizes) & (down < end_row)
    member_ref[...] = jnp.where(inside, 1.0, 0.0).astype(bf16)
    count_ref[...] = jnp.broadcast_to(jnp.maximum(size_column, 1.0), count_ref.shape)

    def put(at, value):
        flags_ref[at : at + 1, :] = jnp.broadcast_to(jnp.where(value, 1.0, 0.0), (1, LANES))

    level, size = 0, 1
    while size < devices:
        start = local - local % size
        is_left = (local // size) % 2 == 0
        other = jnp.where(is_left, start + size, start - size)
        far_facing = item_at(jnp.where(is_left, other, other + size - 1))
        far_outer = item_at(jnp.where(is_left, other + size - 1, other))
        facing = item_at(jnp.where(is_left, start + size - 1, start))
        outer_edge = item_at(jnp.where(is_left, start, start + size - 1))
        next_left = (local // (2 * size)) % 2 == 0
        put(4 * level, own == far_facing)
        put(4 * level + 1, outer_edge == far_facing)
        put(4 * level + 2, far_outer == facing)
        turn = jnp.where(is_left != next_left, 1.0, 0.0)
        flags_ref[4 * level + 3 : 4 * level + 4, :] = jnp.full((1, LANES), turn, f32)
        level, size = level + 1, 2 * size
    before = jnp.where(local > 0, 1.0, 0.0) * jnp.where(item_at(local - 1) == own, 1.0, 0.0)
    behind = jnp.where(local < devices - 1, 1.0, 0.0) * jnp.where(
        item_at(local + 1) == own, 1.0, 0.0
    )
    flags_ref[12:13, :] = jnp.broadcast_to(before, (1, LANES))
    flags_ref[13:14, :] = jnp.broadcast_to(behind, (1, LANES))
    flags_ref[14:16, :] = jnp.zeros((2, LANES), f32)


def query_key_kernel(flat_ref, q0, k0, q1, k1, s0, s1, member_ref, query_ref, keys_ref, part_ref, message_ref):
    channels = query_ref.shape[2]
    scale = HEAD_DIM ** (-0.25)
    parts = []
    for r, (q, k, small) in enumerate(((q0, k0, s0), (q1, k1, s1))):
        query = dot_t(flat_ref[...], q[...]) + small_row(small, 0, channels)
        query = (scale * query).astype(bf16)
        keys = (scale * dot_t(flat_ref[...], k[...])).astype(bf16)
        query_ref[r] = query
        keys_ref[r] = keys
        parts += [dot(member_ref[...], query), dot(member_ref[...], keys)]
    part = jnp.concatenate(parts, axis=1)
    part_ref[...] = part
    message_ref[...] = part.astype(bf16)


def route_kernel(level, bits_ref, *refs):
    keep_out, send_out = refs[-2:]
    half = keep_out.shape[0]

    def total(i):
        sums = [
            (refs[k][i].astype(f32) + refs[k + 1][i].astype(f32)).astype(bf16)
            for k in range(0, len(refs) - 2, 2)
        ]
        return jnp.concatenate(sums, axis=1) if len(sums) > 1 else sums[0]

    for i in range(half):
        if level is None:
            keep, send = i, half + i
        else:
            bit = bits_ref[level]
            keep, send = 2 * i + bit, 2 * i + 1 - bit
        keep_out[i] = total(keep)
        send_out[i] = total(send)


def last_tile_kernel(bits_ref, keep_ref, got_ref, out_ref):
    for i in range(out_ref.shape[0]):
        out_ref[i] = keep_ref[i].astype(f32) + got_ref[i].astype(f32)


def put_tiles(product, r, mine_ref, theirs_ref):
    ref = theirs_ref if r % 2 else mine_ref
    places = ref.shape[0] // 2
    rows = product.shape[0] // places
    first = places if r >= 2 else 0
    for place in range(places):
        ref[first + place, :rows] = product[place * rows : (place + 1) * rows].astype(bf16)


def weight_gradient_kernel(side_ref, units_ref, mine_ref, theirs_ref, turned_ref):
    turned_ref[...] = side_ref[...].T
    columns = mine_ref.shape[2]
    for r in range(units_ref.shape[1] // columns):
        product = dot(turned_ref[...], units_ref[:, r * columns : (r + 1) * columns])
        put_tiles(product, r, mine_ref, theirs_ref)


def small_kernel(query_ref, value_ref, taps_ref, flipped_ref, up_ref, out_ref):
    columns = out_ref.shape[1]

    def row(pieces):
        width = sum(piece.shape[1] for piece in pieces)
        return jnp.concatenate(pieces + [jnp.zeros((1, columns - width), f32)], axis=1)

    heads = range(query_ref.shape[0])
    rows = []
    for ref in (query_ref, value_ref):
        value = ref[...].astype(f32)
        rows.append(row([value[j : j + 1] for j in heads]))
    for ref in (taps_ref, flipped_ref):
        value = ref[...].astype(f32)
        rows += [row([value[j : j + 1]]) for j in heads]
    rows.append(up_ref[...].astype(f32).reshape(1, columns))
    rows.append(jnp.zeros((out_ref.shape[0] - len(rows), columns), f32))
    out_ref[...] = jnp.concatenate(rows, axis=0).astype(bf16)


def small_row(ref, at, width):
    return ref[:, :width].astype(f32)[at : at + 1]


def bundle_kernel(rank_ref, up_ref, value_ref, taps_ref, norm_ref, out_ref):
    ranks, channels = value_ref.shape
    columns = out_ref.shape[1]
    heads = taps_ref.shape[0] // ranks
    for r in range(ranks):
        at = 4 * (r ^ rank_ref[0])
        value = value_ref[r : r + 1, :]
        rows = (
            up_ref[:, r * columns : (r + 1) * columns],
            jnp.concatenate((value, jnp.zeros((1, columns - channels), f32)), axis=1),
            jnp.concatenate([taps_ref[r * heads + j : r * heads + j + 1] for j in range(heads)], axis=1),
        )
        for k, row in enumerate(rows):
            out_ref[pl.ds(at + k, 1), :] = row
        out_ref[pl.ds(at + 3, 1), :] = jnp.zeros((1, columns), f32)
    norms = norm_ref.shape[0]
    out_ref[4 * ranks : 4 * ranks + norms, :] = norm_ref[...]
    out_ref[4 * ranks + norms :, :] = jnp.zeros((out_ref.shape[0] - 4 * ranks - norms, columns), f32)


def land_kernel(flags_ref, count_ref, own0, got0, own1, got1, query_ref, keys_ref, kernel_ref):
    channels = own0.shape[1] // 4
    count = count_ref[:, 0:1]
    queries, keys = [], []
    for own, got in ((own0, got0), (own1, got1)):
        land = sum_merge(own[...], got[...].astype(f32), flag(flags_ref, 8)) / count
        for r in range(2):
            queries.append(group_of(land, 2 * r, channels).astype(bf16))
            keys.append(group_of(land, 2 * r + 1, channels).astype(bf16))
    land_query, land_key = jnp.concatenate(queries, axis=1), jnp.concatenate(keys, axis=1)
    query_ref[...] = land_query
    keys_ref[...] = land_key
    for p in range(kernel_ref.shape[0]):
        scores = dot_t(pair_of(land_query, p), pair_spread(pair_of(land_key, p)))
        powers = jnp.exp(scores - pair_sums(scores, jnp.max, very_negative))
        kernel_ref[p] = powers / pair_sums(powers)


def value_kernel(flat_ref, w0, w1, w2, w3, s0, s1, s2, s3, values_ref, head_ref, tail_ref):
    reach = head_ref.shape[0]
    heads, tails = [], []
    channels = values_ref.shape[2]
    for r, (w, small) in enumerate(((w0, s0), (w1, s1), (w2, s2), (w3, s3))):
        values = (dot_t(flat_ref[...], w[...]) + small_row(small, 1, channels)).astype(bf16)
        values_ref[r] = values
        heads.append(values[:reach])
        tails.append(values[values.shape[0] - reach :])
    head_ref[...] = jnp.concatenate(heads, axis=1)
    tail_ref[...] = jnp.concatenate(tails, axis=1)


def key_kernel(k0, k1, values_ref, land_query_ref, state_ref, message_ref):
    channels = values_ref.shape[2]
    heads = channels // HEAD_DIM
    mixed = []
    marks = land_query_ref.shape[0]
    stats = jnp.zeros((marks, LANES), f32)
    lane = lane_ids(stats.shape)
    groups = values_ref.shape[0]
    for r in range(groups):
        keys = (k0, k1)[r // 2][r % 2]
        scores = dot_t(spread_heads(group_of(land_query_ref[...], r, channels)), keys)
        top = jnp.max(scores, axis=1, keepdims=True).astype(bf16).astype(f32)
        powers = jnp.exp(scores - top)
        total = jnp.sum(powers, axis=1, keepdims=True)
        mixed.append(gather_heads(dot(powers.astype(bf16), values_ref[r])))
        for j in range(heads):
            h = r * heads + j
            at = slice(j * marks, (j + 1) * marks)
            stats = jnp.where(lane == h, top[at], stats)
            stats = jnp.where(lane == groups * heads + h, total[at], stats)
    state = jnp.concatenate(mixed + [stats], axis=1)
    state_ref[...] = state
    message_ref[...] = state_message(state, groups * heads)


def state_message(state, heads):
    width = state.shape[1] - LANES
    stats = state[:, width:]
    lane = lane_ids(stats.shape)
    high = stats.astype(bf16).astype(f32)
    low = pltpu.roll(stats - high, heads, 1)
    last = jnp.where(lane < 2 * heads, high, jnp.where(lane < 3 * heads, low, 0.0))
    return jnp.concatenate((state[:, :width], last), axis=1).astype(bf16)


def message_state(message, heads):
    message = message.astype(f32)
    width = message.shape[1] - LANES
    stats = message[:, width:]
    lane = lane_ids(stats.shape)
    low = pltpu.roll(stats, LANES - heads, 1)
    stats = stats + jnp.where((lane >= heads) & (lane < 2 * heads), low, 0.0)
    stats = jnp.where(lane < 2 * heads, stats, 0.0)
    return jnp.concatenate((message[:, :width], stats), axis=1)


def widen(stats, first, width):
    pieces = []
    rows = stats.shape[0]
    for pair in range(width // LANES):
        lane = lane_ids((rows, LANES))
        at = first + 2 * pair
        pieces.append(
            jnp.where(lane < HEAD_DIM, stats[:, at : at + 1], stats[:, at + 1 : at + 2])
        )
    return jnp.concatenate(pieces, axis=1)


def merge_states(a, b, use, heads):
    width = a.shape[1] - LANES
    stats_a, stats_b = a[:, width:], b[:, width:]
    lane = lane_ids(stats_a.shape)
    top = jnp.where(use, jnp.maximum(stats_a, stats_b), stats_a)
    is_top = lane < heads
    scale_a = jnp.exp(jnp.where(is_top, stats_a - top, 0.0))
    scale_b = jnp.where(use, jnp.exp(jnp.where(is_top & use, stats_b - top, 0.0)), 0.0)
    values = a[:, :width] * widen(scale_a, 0, width) + b[:, :width] * widen(scale_b, 0, width)
    total = stats_a * pltpu.roll(scale_a, heads, 1) + stats_b * pltpu.roll(scale_b, heads, 1)
    stats = jnp.where(is_top, top, jnp.where(lane < 2 * heads, total, 0.0))
    return jnp.concatenate((values, stats), axis=1)


def token_kernel(q0, q1, land_key_ref, weights_ref):
    groups, rows, width = weights_ref.shape
    channels = q0.shape[2]
    heads = channels // HEAD_DIM
    for r in range(groups):
        query = (q0, q1)[r // 2][r % 2]
        scores = dot_t(spread_heads(group_of(land_key_ref[...], r, channels)), query)
        scores = scores.reshape(heads, rows // heads, width)
        powers = jnp.exp(scores - jnp.max(scores, axis=1, keepdims=True))
        weights = powers / jnp.sum(powers, axis=1, keepdims=True)
        weights_ref[r] = weights.reshape(rows, width)


def toeplitz(taps_row, rows, width):
    wide = jnp.broadcast_to(taps_row, (rows, taps_row.shape[1]))
    return pltpu.roll(wide, 0, 1, stride=1, stride_axis=0)[:, :width]


def with_rim(cells, before, after, flags_ref):
    return jnp.concatenate(
        (
            jnp.where(flag(flags_ref, 12), before, jnp.zeros_like(before)),
            cells,
            jnp.where(flag(flags_ref, 13), after, jnp.zeros_like(after)),
        ),
        axis=0,
    )


def convolve(rim, filters):
    tall = jnp.concatenate(filters, axis=0)
    span = tall.shape[1]
    pieces = []
    for start in range(0, rim.shape[0] - (span - STRIPE), STRIPE):
        product = dot(tall, rim[start : start + span])
        lane = lane_ids((STRIPE, rim.shape[1])) // HEAD_DIM
        piece = product[:STRIPE]
        for j in range(1, len(filters)):
            piece = jnp.where(lane == j, product[j * STRIPE : (j + 1) * STRIPE], piece)
        pieces.append(piece)
    return jnp.concatenate(pieces, axis=0)


def context_kernel(own_ref, got_ref, inverse_ref, weights_ref, values_ref, before_ref, after_ref,
                   flags_ref, s0, s1, s2, s3, context_ref, mixed_ref, low_ref, stats_ref):
    groups, width, channels = values_ref.shape
    heads = channels // HEAD_DIM
    reach = before_ref.shape[0]
    merge, _, decode = soft_parts(groups * heads)
    state = merge(own_ref[...], decode(got_ref[...]), flag(flags_ref, 8))
    model = groups * channels
    stats_ref[...] = state[:, model:]
    mixed = state[:, :model] / widen(state[:, model:], groups * heads, model)
    mixed_ref[...] = mixed
    low = jnp.concatenate(
        [
            pair_mul(inverse_ref[p], pair_of(mixed, p)).astype(bf16)
            for p in range(inverse_ref.shape[0])
        ],
        axis=1,
    )
    low_ref[...] = low
    for r in range(groups):
        nystrom = outer(
            weights_ref[r].astype(bf16), spread_heads(group_of(low, r, channels))
        )
        rim = with_rim(
            values_ref[r],
            group_of(before_ref[...], r, channels),
            group_of(after_ref[...], r, channels),
            flags_ref,
        )
        filters = [
            toeplitz(
                small_row((s0, s1, s2, s3)[r], 2 + j, 2 * LANES), STRIPE, STRIPE + 2 * reach
            ).astype(bf16)
            for j in range(heads)
        ]
        context_ref[r] = (nystrom + convolve(rim, filters)).astype(bf16)


def token_back_kernel(back_ref, weights_ref, low_ref, q0, q1, land_key_ref, part_ref,
                      message_ref, part_key_ref, message_key_ref, direct_ref, head_ref, tail_ref):
    groups, width, channels = back_ref.shape
    heads = channels // HEAD_DIM
    reach = head_ref.shape[0]
    parts, key_parts = [], []
    for r in range(groups):
        back = back_ref[r]
        query = (q0, q1)[r // 2][r % 2]
        weights = weights_ref[r]
        parts.append(gather_heads(dot(weights.astype(bf16), back)))
        slope = dot_t(spread_heads(group_of(low_ref[...], r, channels)), back)
        product = (weights * slope).reshape(heads, -1, width)
        rows = jnp.sum(product, axis=1, keepdims=True)
        rows = jnp.broadcast_to(rows, product.shape).reshape(weights.shape)
        scores = (weights * (slope - rows)).astype(bf16)
        key_parts.append(gather_heads(dot(scores, query)))
        direct_ref[r] = outer(scores, spread_heads(group_of(land_key_ref[...], r, channels)))
    for pieces, whole_ref, low in ((parts, part_ref, message_ref), (key_parts, part_key_ref, message_key_ref)):
        whole = jnp.concatenate(pieces, axis=1)
        whole_ref[...] = whole
        low[...] = whole.astype(bf16)
    head_ref[...] = jnp.concatenate([back_ref[r, :reach] for r in range(groups)], axis=1)
    tail_ref[...] = jnp.concatenate([back_ref[r, width - reach :] for r in range(groups)], axis=1)


def conv_back_kernel(back_ref, before_ref, after_ref, values_ref, vbefore_ref, vafter_ref, flags_ref,
                     s0, s1, s2, s3, conv_ref, taps_ref):
    groups, width, channels = back_ref.shape
    heads = channels // HEAD_DIM
    reach = before_ref.shape[0]
    span = STRIPE + 2 * reach
    order = row_ids((STRIPE, STRIPE)) + lane_ids((STRIPE, STRIPE)) == STRIPE - 1
    order = jnp.where(order, 1.0, 0.0).astype(bf16)
    lane = lane_ids((STRIPE, channels)) // HEAD_DIM
    for r in range(groups):
        rim = with_rim(
            back_ref[r],
            group_of(before_ref[...], r, channels),
            group_of(after_ref[...], r, channels),
            flags_ref,
        )
        filters = [
            toeplitz(
                small_row((s0, s1, s2, s3)[r], 2 + heads + j, 2 * LANES), STRIPE, span
            ).astype(bf16)
            for j in range(heads)
        ]
        conv_ref[r] = convolve(rim, filters)
        value_rim = with_rim(
            values_ref[r],
            group_of(vbefore_ref[...], r, channels),
            group_of(vafter_ref[...], r, channels),
            flags_ref,
        )
        total = jnp.zeros((heads * STRIPE, span), f32)
        for start in range(0, width, STRIPE):
            turned = dot(order, back_ref[r, start : start + STRIPE])
            tall = [jnp.where(lane == j, turned, 0.0).astype(bf16) for j in range(heads)]
            total = total + dot_t(jnp.concatenate(tall, axis=0), value_rim[start : start + span])
        total = jnp.concatenate(
            (total, jnp.zeros((heads * STRIPE, 2 * LANES - span), f32)), axis=1
        )
        for j in range(heads):
            skewed = pltpu.roll(
                total[j * STRIPE : (j + 1) * STRIPE], 0, 1, stride=1, stride_axis=0
            )
            h = r * heads + j
            taps_ref[h : h + 1, :] = jnp.sum(skewed, axis=0, keepdims=True)


def seed_kernel(flags_ref, own_ref, got_ref, inverse_ref, mixed_ref, back_inverse_ref, back_mixed_ref):
    back = sum_merge(own_ref[...], got_ref[...].astype(f32), flag(flags_ref, 8))
    pairs = []
    for p in range(inverse_ref.shape[0]):
        near = pair_of(back, p)
        back_inverse_ref[p] = pair_mul_t(near, pair_of(mixed_ref[...], p))
        pairs.append(pair_t_mul(inverse_ref[p], near))
    back_mixed_ref[...] = jnp.concatenate(pairs, axis=1).astype(bf16)


def key_back_kernel(k0, k1, values_ref, land_query_ref, state_ref, mixed_ref, back_mixed_ref,
                    conv_ref, part_ref, message_ref, direct_ref, back_values_ref, bias_ref):
    groups, width, channels = values_ref.shape
    heads = channels // HEAD_DIM
    stats = state_ref[...]
    parts = []
    for r in range(groups):
        keys = (k0, k1)[r // 2][r % 2]
        land = spread_heads(group_of(land_query_ref[...], r, channels))
        scores = dot_t(land, keys)
        first = r * heads
        tops = jnp.concatenate([stats[:, first + j : first + j + 1] for j in range(heads)], axis=0)
        first += groups * heads
        totals = jnp.concatenate(
            [stats[:, first + j : first + j + 1] for j in range(heads)], axis=0
        )
        weights = jnp.exp(scores - tops) * (1.0 / totals)
        back_mixed = group_of(back_mixed_ref[...], r, channels)
        spread = spread_heads(back_mixed)
        dots = jnp.sum(
            spread_heads(group_of(mixed_ref[...], r, channels)) * spread.astype(f32),
            axis=1,
            keepdims=True,
        )
        slope = dot_t(spread, values_ref[r])
        back_scores = (weights * (slope - dots)).astype(bf16)
        parts.append(gather_heads(dot(back_scores, keys)))
        direct_ref[r] = outer(back_scores, land)
        back_values = (outer(weights.astype(bf16), spread) + conv_ref[r]).astype(bf16)
        back_values_ref[r] = back_values
        bias_ref[r : r + 1, :] = jnp.sum(back_values.astype(f32), axis=0, keepdims=True)
    part = jnp.concatenate(parts, axis=1)
    part_ref[...] = part
    message_ref[...] = part.astype(bf16)


def input_back_kernel(flags_ref, count_ref, flat_ref, query_direct_ref, key_direct_ref, back_values_ref,
                      query_own_ref, query_got_ref, query_more_ref, key_own_ref, key_got_ref,
                      key_more_ref, member_ref, back_input_ref, q0, q1, q2, q3, k0, k1, k2, k3, v0,
                      v1, v2, v3, grad_ref, mine_ref, theirs_ref, turned_ref, both_ref, weight_ref):
    groups, width, channels = back_values_ref.shape
    model = flat_ref.shape[1]
    scale = HEAD_DIM ** (-0.25)
    member = member_ref[...]
    count = count_ref[:, 0:1]
    sides = [
        two_parts(
            (sum_merge(own[...], got[...].astype(f32), flag(flags_ref, 8)) + more[...]) / count
        )
        for own, got, more in (
            (query_own_ref, query_got_ref, query_more_ref),
            (key_own_ref, key_got_ref, key_more_ref),
        )
    ]
    turned_ref[...] = flat_ref[...].T
    for r in range(groups):
        q, k = (q0, q1, q2, q3)[r], (k0, k1, k2, k3)[r]
        both = []
        for (high, low), direct_ref in zip(sides, (query_direct_ref, key_direct_ref)):
            far = dot(member, group_of(high, r, channels)) + dot(member, group_of(low, r, channels))
            both.append((direct_ref[r] + far).astype(bf16))
        bias = scale * jnp.sum(both[0].astype(f32), axis=0, keepdims=True)
        bias = jnp.concatenate((bias, jnp.zeros_like(bias)), axis=1)
        at = slice(2 * r * channels, 2 * (r + 1) * channels)
        both_ref[:, at] = jnp.concatenate(both, axis=1)
        weight_ref[at, :] = jnp.concatenate((q[...], k[...]), axis=0)
        put_tiles(scale * dot(turned_ref[...], both_ref[:, at]), r, mine_ref, theirs_ref)
        ref = theirs_ref if r % 2 else mine_ref
        places = ref.shape[0] // 2
        more = ref.shape[1] - model // places
        for place in range(places):
            ref[(places if r >= 2 else 0) + place, model // places :] = jnp.broadcast_to(
                bias, (more, bias.shape[1])
            ).astype(bf16)
    total = back_input_ref[...] + scale * dot(both_ref[...], weight_ref[...])
    values = jnp.concatenate([back_values_ref[r] for r in range(groups)], axis=1)
    weights = jnp.concatenate([v[...] for v in (v0, v1, v2, v3)], axis=0)
    grad_ref[...] = (total + dot(values, weights)).astype(bf16)


def value_output_kernel(flat_ref, back_values_ref, back_attention_ref, context_ref, mine_ref, theirs_ref):
    flat, back = flat_ref[...].T, back_attention_ref[...].T
    for r in range(context_ref.shape[0]):
        product = (dot(back, context_ref[r]), dot(flat, back_values_ref[r]))
        put_tiles(jnp.concatenate(product, axis=1), r, mine_ref, theirs_ref)


def place_kernel(rank_ref, r0, r1, r2, r3, out_ref):
    step = pl.program_id(0)
    for k, ref in enumerate((r0, r1, r2, r3)):

        @pl.when(step == k)
        def _():
            out_ref[0] = ref[...].astype(out_ref.dtype)


def place_rows(rank, blocks, dtype):
    width, model = blocks[0].shape
    return pl.pallas_call(
        place_kernel,
        out_shape=jax.ShapeDtypeStruct((len(blocks), width, model), dtype),
        grid_spec=pltpu.PrefetchScalarGridSpec(
            num_scalar_prefetch=1,
            grid=(len(blocks),),
            in_specs=[pl.BlockSpec((width, model), lambda i, rank: (0, 0))] * len(blocks),
            out_specs=pl.BlockSpec((1, width, model), lambda i, rank: (i ^ rank[0], 0, 0)),
        ),
        compiler_params=pltpu.CompilerParams(vmem_limit_bytes=24 << 20),
        cost_estimate=cost(2.5),
        name="place_rows",
    )(rank.reshape(1).astype(jnp.int32), *blocks)


def feed_kernel(
    flat_ref, context_ref, out0, out1, out2, out3, up0, up1, up2, up3, down0, down1, down2, down3,
    s0, s1, s2, s3, p0, p1, p2, p3, p4, p5, cotangent_ref,
    layer_ref, back_input_ref, back_attention_ref, back_context_ref, active_ref, back_hidden_ref,
    first_low_ref, back_feed_ref, sums_ref, up_sums_ref,
    slope_ref, first_ref, total_ref,
):
    outs, ups, downs = (out0, out1, out2, out3), (up0, up1, up2, up3), (down0, down1, down2, down3)
    units = up0.shape[1]
    output_bias, first_gain, first_shift, down_bias, second_gain, second_shift = [
        p[...].astype(f32).reshape(1, flat_ref.shape[1]) for p in (p0, p1, p2, p3, p4, p5)
    ]

    def mean(value):
        return jnp.mean(value, axis=1, keepdims=True)

    attention = dot(context_ref[0], out0[...])
    for r in range(1, len(outs)):
        attention = attention + dot(context_ref[r], outs[r][...])
    value = flat_ref[...].astype(f32) + attention + output_bias
    centred = value - mean(value)
    first_inverse = lax.rsqrt(mean(centred * centred) + epsilon)
    first_normed = centred * first_inverse
    first_ref[...] = first_normed
    first_out = first_normed * first_gain + first_shift
    first_low_ref[...] = first_out.astype(bf16)
    total_ref[...] = first_out + down_bias
    for r in range(len(ups)):
        at = slice(r * units, (r + 1) * units)
        hidden = dot(first_low_ref[...], ups[r][...]) + small_row((s0, s1, s2, s3)[r], 8, units)
        cdf = 0.5 * (1.0 + lax.erf(hidden * 0.7071067811865476))
        slope_ref[:, at] = cdf + hidden * (0.3989422804014327 * jnp.exp(-0.5 * hidden * hidden))
        active = (hidden * cdf).astype(bf16)
        active_ref[:, at] = active
        total_ref[...] += dot(active, downs[r][...])

    value = total_ref[...]
    centred = value - mean(value)
    second_inverse = lax.rsqrt(mean(centred * centred) + epsilon)
    normed = centred * second_inverse
    layer_ref[...] = (normed * second_gain + second_shift).astype(bf16)
    upstream = cotangent_ref[...].astype(f32)
    sums_ref[4:5, :] = jnp.sum(upstream * normed, axis=0, keepdims=True)
    sums_ref[5:6, :] = jnp.sum(upstream, axis=0, keepdims=True)
    scaled = upstream * second_gain
    back_second = (scaled - mean(scaled) - normed * mean(scaled * normed)) * second_inverse
    back_feed = back_second.astype(bf16)
    back_feed_ref[...] = back_feed
    sums_ref[3:4, :] = jnp.sum(back_feed.astype(f32), axis=0, keepdims=True)
    total_ref[...] = back_second
    for r in range(len(ups)):
        at = slice(r * units, (r + 1) * units)
        back_active = dot_t(back_feed_ref[...], downs[r][...])
        back_hidden = (back_active * slope_ref[:, at]).astype(bf16)
        back_hidden_ref[:, at] = back_hidden
        up_sums_ref[:, at] = jnp.sum(back_hidden.astype(f32), axis=0, keepdims=True)
        total_ref[...] += dot_t(back_hidden, ups[r][...])

    back_first = total_ref[...]
    first_normed = first_ref[...]
    sums_ref[1:2, :] = jnp.sum(back_first * first_normed, axis=0, keepdims=True)
    sums_ref[2:3, :] = jnp.sum(back_first, axis=0, keepdims=True)
    scaled = back_first * first_gain
    back_input = (scaled - mean(scaled) - first_normed * mean(scaled * first_normed)) * first_inverse
    back_input_ref[...] = back_input
    back_attention = back_input.astype(bf16)
    back_attention_ref[...] = back_attention
    sums_ref[0:1, :] = jnp.sum(back_attention.astype(f32), axis=0, keepdims=True)
    for r in range(len(outs)):
        back_context_ref[r] = dot_t(back_attention, outs[r][...]).astype(bf16)


def feed_layer(flat, context, outputs, ups, downs, smalls, params, cotangent):
    width, model = flat.shape
    ranks, units = len(ups), ups[0].shape[1]
    channels = outputs[0].shape[0]
    shape = jax.ShapeDtypeStruct
    whole = pl.BlockSpec(memory_space=pltpu.VMEM)
    return pl.pallas_call(
        feed_kernel,
        out_shape=(
            shape((width, model), bf16),
            shape((width, model), f32),
            shape((width, model), bf16),
            shape((ranks, width, channels), bf16),
            shape((width, ranks * units), bf16),
            shape((width, ranks * units), bf16),
            shape((width, model), bf16),
            shape((width, model), bf16),
            shape((6, model), f32),
            shape((1, ranks * units), f32),
        ),
        in_specs=[whole] * (15 + len(smalls) + len(params)),
        out_specs=(whole,) * 10,
        scratch_shapes=[
            pltpu.VMEM((width, ranks * units), f32),
            pltpu.VMEM((width, model), f32),
            pltpu.VMEM((width, model), f32),
        ],
        compiler_params=pltpu.CompilerParams(vmem_limit_bytes=VMEM_LIMIT),
        cost_estimate=cost(19.0),
        name="feed_layer",
    )(flat, context, *outputs, *ups, *downs, *smalls, *params, cotangent)


def per_device(
    tokens,
    query_weight,
    query_bias,
    key_weight,
    value_weight,
    value_bias,
    conv_weight,
    output_weight,
    output_bias,
    first_gain,
    first_shift,
    up_weight,
    up_bias,
    down_weight,
    down_bias,
    second_gain,
    second_shift,
    segment_sizes,
    cotangent,
):
    rows, width, model = tokens.shape
    channels = query_weight.shape[1]
    ranks = lax.axis_size("tp")
    own_heads = channels // HEAD_DIM
    heads = ranks * own_heads
    hidden_units = up_weight.shape[1]
    items = segment_sizes.shape[1]
    marks = segment_sizes.shape[2]
    reach = TAPS // 2
    device = lax.axis_index("seq")
    rank = lax.axis_index("tp")
    group = SPAN // width
    groups = segment_sizes.shape[0] // rows
    place = jnp.stack((rank * groups + device // group, device % group)).astype(jnp.int32)

    half = ((2, width, channels), bf16)
    full = ((ranks, width, channels), bf16)
    full32 = ((ranks, width, channels), f32)
    edge = ((reach, model), bf16)
    marked = ((marks, model), f32)
    message = ((marks, model), bf16)
    tall = ((marks, LANES), f32)
    squares = ((heads // 2, marks, LANES), f32)
    half_sweeps = SWEEPS // 2
    saved = ((half_sweeps, 4, heads // 2, marks, LANES), f32)

    turned = [w.T for w in (query_weight, key_weight, value_weight)]
    (small,) = call(small_kernel, (((16, model), bf16),), "small")(
        query_bias, value_bias, conv_weight, conv_weight[:, ::-1], up_bias
    )
    query_far, key_far = swap((turned[0], turned[1]), "tp", 2)
    query_core, key_core = swap((turned[0], turned[1]), "tp", 1)
    small_far = swap(small, "tp", 2)
    smalls = (small, swap(small, "tp", 1), small_far, swap(small_far, "tp", 1))
    member, member_turned, count, flags = call(
        layout_kernel,
        (((width, marks), bf16), ((marks, width), bf16), tall, ((16, LANES), f32)),
        "layout",
        scalars=1,
    )(place, segment_sizes)
    flat = lax.dynamic_index_in_dim(tokens, rank, axis=0, keepdims=False)
    upstream = lax.dynamic_index_in_dim(cotangent, rank, axis=0, keepdims=False)

    def shards(own, far):
        return (own, swap(own, "tp", 1), far, swap(far, "tp", 1))

    query_blocks = (turned[0], query_core, query_far, swap(query_far, "tp", 1))
    key_blocks = (turned[1], key_core, key_far, swap(key_far, "tp", 1))
    query, keys, sums = [], [], []
    for pair in range(2):
        q, k, part, sent = call(
            query_key_kernel, (half, half, marked, message), "query_key", us=2.5,
        )(
            flat,
            query_blocks[2 * pair],
            key_blocks[2 * pair],
            query_blocks[2 * pair + 1],
            key_blocks[2 * pair + 1],
            *smalls[2 * pair : 2 * pair + 2],
            member_turned,
        )
        query.append(q)
        keys.append(k)
        if pair == 0:
            value_far = swap(after(turned[2], query_far, key_far, small_far, sent), "tp", 2)
            output_far = swap(after(output_weight, query_far, key_far, small_far, sent), "tp", 2)
        steps = []
        sums += exchange(plain_parts(), "land", flags, part, sent, marks_of=steps)
    up_far = swap(after(up_weight, value_far, steps[0]), "tp", 2)
    value_blocks = shards(turned[2], value_far)
    output_blocks = shards(output_weight, output_far)
    up_blocks = shards(up_weight, up_far)
    land_query, land_key, kernel = call(land_kernel, (message, message, squares), "land")(
        flags, count, *sums
    )
    values, value_head, value_tail = call(
        value_kernel, (full, edge, edge), "values", us=2.0
    )(after(flat, output_far), *value_blocks, *smalls)

    def neighbours(head, tail):
        count = lax.axis_size("seq")
        before = lax.ppermute(tail, "seq", [(i, i + 1) for i in range(count - 1)])
        behind = lax.ppermute(head, "seq", [(i + 1, i) for i in range(count - 1)])
        return before, behind

    value_before, value_after = neighbours(value_head, value_tail)
    state, sent = call(
        key_kernel,
        (((marks, model + LANES), f32), ((marks, model + LANES), bf16)),
        "key_softmax",
        us=1.4,
    )(*keys, values, land_query)
    steps = []
    state, state_got = exchange(soft_parts(heads), "soft", flags, state, sent, marks_of=steps)
    down_far = swap(after(down_weight, up_far, steps[0]), "tp", 2)
    down_blocks = shards(down_weight, after(down_far, steps[1]))
    (token_weights,) = call(
        token_kernel, (((ranks, own_heads * marks, width), f32),), "token_softmax", us=0.8,
    )(*query, land_key)
    inverse, saved_first = call(newton_first_kernel, (squares, saved), "newton_first", us=6.0)(kernel)
    inverse, saved_last = call(newton_next_kernel, (squares, saved), "newton_next", us=6.0)(
        kernel, inverse
    )
    context, mixed, mixed_low, stats = call(
        context_kernel, (full, marked, message, tall), "context", us=2.0,
    )(
        after(state, down_far), state_got, inverse, token_weights, values, value_before, value_after, flags,
        *smalls,
    )

    params = (output_bias, first_gain, first_shift, down_bias, second_gain, second_shift)
    (
        layer_out,
        back_input,
        back_attention,
        back_context,
        active,
        back_hidden,
        first_low,
        back_feed,
        norm_sums,
        up_sums,
    ) = feed_layer(
        flat, context, output_blocks, up_blocks, down_blocks, smalls, params, upstream
    )

    layer_far = swap(layer_out, "tp", 2)
    positions = lax.axis_size("seq")
    levels = list(range(positions.bit_length() - 1))
    bits = jnp.stack([(device >> level) & 1 for level in levels]).astype(jnp.int32)
    wide_tiles = (((2 * positions, model // positions, hidden_units), bf16),) * 2
    weight_gradient = call(
        weight_gradient_kernel, wide_tiles, "weight_gradient",
        scratch=(pltpu.VMEM((model, width), bf16),), us=4.5,
    )
    up = Scatter("up", *weight_gradient(first_low, back_hidden), bits, levels + ["far"])
    part_back, sent_back, part_key, sent_key, query_direct, back_head, back_tail = call(
        token_back_kernel, (marked, message, marked, message, full32, edge, edge), "token_back",
        us=1.8,
    )(after(back_context, up.send), token_weights, mixed_low, *query, land_key)
    down = Scatter("down", *weight_gradient(back_feed, active), bits, ["far"] + levels)
    back_own, back_got = exchange(
        plain_parts(), "back", flags, part_back, sent_back, ([down.send], ())
    )
    steps = []
    key_own, key_got = exchange(plain_parts(), "back_key", flags, part_key, sent_key, marks_of=steps)
    back_before, back_after = neighbours(back_head, back_tail)
    conv_back, tap_rows = call(
        conv_back_kernel, (full32, ((heads, 2 * LANES), f32)), "conv_back", us=2.8
    )(
        back_context, back_before, back_after, values, value_before, value_after, flags, *smalls
    )
    back_inverse, back_mixed = call(seed_kernel, (squares, message), "seed")(
        flags, after(back_own, conv_back, *up.hop(), *down.hop()), back_got, inverse, mixed
    )
    up.wait_for(back_before, back_after, steps[0])
    down.wait_for(layer_far)
    part_query, sent_query, key_direct, back_values, value_bias_sums = call(
        key_back_kernel, (marked, message, full32, full, ((ranks, channels), f32)), "key_back",
        us=2.4,
    )(*keys, values, land_query, stats, mixed, back_mixed, conv_back)
    newton_back = call(newton_back_kernel, (squares, squares), "newton_back", us=6.6)
    back_middle = newton_back(kernel, saved_last, back_inverse, jnp.zeros(*squares))
    tiles = (((2 * positions, model // positions, 2 * channels), bf16),) * 2
    value_output = call(value_output_kernel, tiles, "value_output", us=2.0)(
        flat, back_values, back_attention, context
    )
    value_output = Scatter("value_output", *value_output, bits, ["far"] + levels)
    steps = []
    query_own, query_got = exchange(
        plain_parts(), "back_query", flags, part_query, sent_query,
        (list(back_middle), [value_output.send]), steps,
    )
    back_start, back_kernel = newton_back(kernel, saved_first, *back_middle)
    query_more, key_more = call(land_back_kernel, (marked, marked), "land_back")(
        kernel, back_start, back_kernel, land_query, land_key
    )
    bundle_rows = 4 * ranks + norm_sums.shape[0]
    (bundle,) = call(
        bundle_kernel, (((bundle_rows + -bundle_rows % 8, model), f32),), "bundle", scalars=1
    )(rank.reshape(1).astype(jnp.int32), up_sums, value_bias_sums, tap_rows, norm_sums)
    rows_here = model // positions
    bias_rows = rows_here + -rows_here % 16
    taller = (((2 * positions, bias_rows + 16, 2 * channels), bf16),) * 2
    grad_row, *projection = call(
        input_back_kernel,
        (((width, model), bf16),) + taller,
        "input_back",
        scratch=(
            pltpu.VMEM((model, width), bf16),
            pltpu.VMEM((width, 2 * model), bf16),
            pltpu.VMEM((2 * model, model), bf16),
        ),
        us=5.0,
        limit=24 << 20,
    )(
        flags, count, flat, query_direct, key_direct, back_values,
        after(query_own, *up.hop(), *value_output.hop()), query_got, query_more,
        key_own, key_got, key_more, member, back_input, *query_blocks, *key_blocks, *value_blocks,
    )
    projection = Scatter("projection", *projection, bits, levels + ["far"])
    grad_far = swap(grad_row, "tp", 2)
    up.wait_for(steps[1])
    layer_blocks = shards(layer_out, layer_far)
    down.hop(value_output)
    for scatter in (projection, down, up):
        while scatter.hops:
            scatter.hop()
        scatter.hop()
    grad_up_weight = up.keep[0]
    grad_down_weight = down.keep[0][:, :hidden_units]
    grad_output_weight = down.keep[0][:, hidden_units : hidden_units + channels].T
    grad_value_weight = down.keep[0][:, hidden_units + channels :]
    projection = projection.keep[0]
    grad_tokens = place_rows(rank, shards(grad_row, grad_far), f32)
    layer_rows = place_rows(rank, (after(layer_blocks[0], grad_row),) + layer_blocks[1:], bf16)
    share = HEAD_DIM // positions
    grad_query_bias = lax.dynamic_slice_in_dim(
        projection[rows_here, :channels].reshape(own_heads, HEAD_DIM), device * share, share, axis=1
    )
    bundle = sum_everywhere(bundle)
    own = lax.dynamic_slice_in_dim(bundle, 4 * rank, 4, axis=0)
    grad_up_bias = own[0]
    grad_value_bias = own[1, :channels].reshape(own_heads, HEAD_DIM)
    grad_conv_weight = own[2].reshape(own_heads, 2 * LANES)[:, STRIPE - 1 : STRIPE - 1 + TAPS]
    shared = [bundle[4 * ranks + k] for k in range(6)]
    return (
        layer_rows,
        grad_tokens,
        projection[:rows_here, :channels],
        grad_query_bias,
        projection[:rows_here, channels:],
        grad_value_weight,
        grad_value_bias,
        grad_conv_weight,
        grad_output_weight,
        shared[0],
        shared[1],
        shared[2],
        grad_up_weight,
        grad_up_bias,
        grad_down_weight.T,
        shared[3],
        shared[4],
        shared[5],
    )


def solution(mesh):
    placed = (
        P(None, "seq", None),
        P(None, "tp"),
        P("tp", None),
        P(None, "tp"),
        P(None, "tp"),
        P("tp", None),
        P("tp", None),
        P("tp", None),
        P(),
        P(),
        P(),
        P(None, "tp"),
        P("tp"),
        P("tp", None),
        P(),
        P(),
        P(),
        P(),
        P(None, "seq", None),
    )
    return jax.shard_map(
        per_device,
        mesh=mesh,
        in_specs=placed,
        out_specs=(
            P(None, "seq", None),
            P(None, "seq", None),
            P("seq", "tp"),
            P("tp", "seq"),
            P("seq", "tp"),
            P("seq", "tp"),
            P("tp", None),
            P("tp", None),
            P("tp", "seq"),
            P(),
            P(),
            P(),
            P("seq", "tp"),
            P("tp"),
            P("tp", "seq"),
            P(),
            P(),
            P(),
        ),
        check_vma=False,
    )
```

```python
import functools

import jax
import jax.numpy as jnp
from jax import lax
from jax.experimental import pallas as pl
from jax.experimental.pallas import tpu as pltpu
from jax.sharding import PartitionSpec as P

HEAD_DIM = 64
TAPS = 33
SWEEPS = 6
SPAN = 4096
LANES = 128
STRIPE = 128
SMALL_ROWS = 16
VMEM_LIMIT = 28 << 20


epsilon = 1e-05
very_negative = -1e30
f32 = jnp.float32
bf16 = jnp.bfloat16


def swap(value, axis, step):
    return lax.ppermute(value, axis, [(i, i ^ step) for i in range(lax.axis_size(axis))])


def dot(a, b):
    return jnp.dot(a, b, preferred_element_type=f32)


def outer(a, b):
    return lax.dot_general(a, b, (((0,), (0,)), ((), ())), preferred_element_type=f32)


def dot_t(a, b):
    return lax.dot_general(a, b, (((1,), (1,)), ((), ())), preferred_element_type=f32)


def after(value, *others):
    return lax.optimization_barrier((value,) + others)[0]


class Scatter:
    def __init__(self, name, mine, theirs, bits, hops):
        self.name, self.bits, self.hops = name, bits, list(hops)
        self.keep, self.send, self.way = mine, theirs, ("tp", 1)
        self.left = sorted(level for level in hops if level != "far")

    def hop(self, *waits, other=None):
        operands = [after(self.keep, *waits), swap(self.send, *self.way)]
        tiles, rows, columns = self.keep.shape
        if other is not None:
            operands += [other.keep, swap(other.send, *other.way)]
            columns += other.keep.shape[2]
        if not self.hops:
            kernel, outs = last_tile_kernel, (((tiles, rows, columns), f32),)
        else:
            following = self.hops.pop(0)
            far = following == "far"
            self.way = ("tp", 2) if far else ("seq", 1 << following)
            place = None if far else self.left.index(following)
            kernel = functools.partial(route_kernel, following, place)
            if not far:
                self.left.remove(following)
            outs = (((tiles // 2, rows, columns), bf16),) * 2
        size = tiles * rows * columns * 2
        result = call(
            kernel, outs, self.name + "_route", scalars=1, us=0.5 + size / 1.2e6, limit=16 << 20
        )(self.bits, *operands)
        self.keep = result[0]
        self.send = result[-1]
        return result

    def wait_for(self, *others):
        self.send = after(self.send, *others)


def sum_merge(a, b, use):
    return a + jnp.where(use, b, 0.0)


def flag(flags_ref, row):
    return flags_ref[row : row + 1, 0:1] > 0.5


def plain_parts():
    return sum_merge, lambda value: value.astype(bf16), lambda message: message.astype(f32)


def soft_parts(heads):
    return (
        functools.partial(merge_states, heads=heads),
        functools.partial(state_message, heads=heads),
        functools.partial(message_state, heads=heads),
    )


def edges_after(parts, flags_ref, level, facing, outer_edge, got, got_outer):
    merge = parts[0]
    near = merge(outer_edge, got, flag(flags_ref, 4 * level + 1))
    away = merge(got_outer, facing, flag(flags_ref, 4 * level + 2))
    turn = flag(flags_ref, 4 * level + 3)
    return jnp.where(turn, near, away), jnp.where(turn, away, near)


def merge_first_kernel(parts, flags_ref, own_ref, got_ref, new_ref, message_ref):
    merge, encode, decode = parts
    own, got = own_ref[...], decode(got_ref[...])
    new_ref[...] = merge(own, got, flag(flags_ref, 0))
    facing, outer_edge = edges_after(parts, flags_ref, 0, own, own, got, got)
    message_ref[...] = jnp.concatenate((encode(facing), encode(outer_edge)), axis=0)


def merge_next_kernel(parts, flags_ref, own_ref, sent_ref, got_ref, new_ref, message_ref):
    merge, encode, decode = parts
    marks = own_ref.shape[0]
    got, got_outer = decode(got_ref[:marks]), decode(got_ref[marks:])
    new_ref[...] = merge(own_ref[...], got, flag(flags_ref, 4))
    facing, _ = edges_after(
        parts, flags_ref, 1, decode(sent_ref[:marks]), decode(sent_ref[marks:]), got, got_outer
    )
    message_ref[...] = encode(facing)


class Exchange:
    def __init__(self, parts, name, flags, own, message):
        self.parts, self.name, self.flags = parts, name, flags
        self.own, self.message = own, message

    def run(self, kernel, name, rows, *operands):
        marks, width = self.own.shape
        self.own, self.message = call(
            functools.partial(kernel, self.parts),
            (((marks, width), f32), ((rows, width), bf16)),
            self.name + name,
        )(self.flags, *operands)

    def first(self, *waits):
        got = swap(self.message, "seq", 1)
        self.run(merge_first_kernel, "_first", 2 * got.shape[0], after(self.own, *waits), got)
        return self

    def next(self, *waits):
        sent = self.message
        got = swap(sent, "seq", 2)
        self.run(merge_next_kernel, "_next", got.shape[0] // 2, after(self.own, *waits), sent, got)
        return self

    def got(self):
        return swap(self.message, "seq", 4)


WHOLE = pl.BlockSpec(memory_space=pltpu.VMEM)


def cost(us):
    return pl.CostEstimate(flops=0, bytes_accessed=int(us * 3.3e6), transcendentals=0)


def call(kernel, outs, name, scratch=(), limit=12 << 20, us=1.0, scalars=0):
    outs = tuple(jax.ShapeDtypeStruct(shape, dtype) for shape, dtype in outs)

    def run(*operands):
        return pl.pallas_call(
            kernel,
            out_shape=outs,
            in_specs=[pl.BlockSpec(memory_space=pltpu.SMEM)] * scalars
            + [WHOLE] * (len(operands) - scalars),
            out_specs=(WHOLE,) * len(outs),
            scratch_shapes=list(scratch),
            compiler_params=pltpu.CompilerParams(vmem_limit_bytes=limit),
            cost_estimate=cost(us),
            name=name,
        )(*operands)

    return run


def lane_ids(shape):
    return lax.broadcasted_iota(jnp.int32, shape, len(shape) - 1)


def row_ids(shape):
    return lax.broadcasted_iota(jnp.int32, shape, len(shape) - 2)


def spread_heads(block):
    heads = block.shape[1] // HEAD_DIM
    tall = jnp.concatenate([block] * heads, axis=0)
    same = row_ids(tall.shape) // HEAD_DIM == lane_ids(tall.shape) // HEAD_DIM
    return jnp.where(same, tall, jnp.zeros_like(tall))


def gather_heads(square):
    heads = square.shape[1] // HEAD_DIM
    result = jnp.zeros((HEAD_DIM, square.shape[1]), square.dtype)
    lane = lane_ids(result.shape) // HEAD_DIM
    for j in range(heads):
        result = jnp.where(lane == j, square[j * HEAD_DIM : (j + 1) * HEAD_DIM], result)
    return result


def two_parts(value):
    high = value.astype(bf16)
    return high, (value - high.astype(f32)).astype(bf16)


def first_half(shape):
    return lane_ids(shape) < HEAD_DIM


def pair_spread(pair):
    near = first_half(pair.shape)
    zero = jnp.zeros_like(pair)
    return jnp.concatenate((jnp.where(near, pair, zero), jnp.where(near, zero, pair)), axis=0)


def pair_gather(square):
    top, bottom = square[:HEAD_DIM], square[HEAD_DIM:]
    return jnp.where(first_half(top.shape), top, bottom)


def fine(product, a, b, turn=lambda value: value):
    a_high, a_low = two_parts(a)
    b_high, b_low = [turn(part) for part in two_parts(b)]
    return product(a_high, b_high) + (product(a_high, b_low) + product(a_low, b_high))


def pair_mul(a, b):
    return fine(dot, a, b, pair_spread)


def pair_mul_t(a, b):
    return fine(dot_t, a, b, pair_spread)


def pair_t_mul(a, b):
    return pair_gather(fine(outer, a, b))


def pair_sums(value, reduce=jnp.sum, neutral=0.0):
    near = first_half(value.shape)
    left = reduce(jnp.where(near, value, neutral), axis=1, keepdims=True)
    right = reduce(jnp.where(near, neutral, value), axis=1, keepdims=True)
    return jnp.where(near, left, right)


def pair_of(array, pair):
    return array[:, pair * LANES : (pair + 1) * LANES]


def pair_turned(value):
    tall = value.T
    return jnp.concatenate((tall[:HEAD_DIM], tall[HEAD_DIM:]), axis=1)


def start_bound(kernel):
    column_sums = jnp.sum(kernel, axis=0, keepdims=True)
    return column_sums, jnp.sqrt(pair_sums(column_sums * column_sums))


def pair_identity():
    shape = (HEAD_DIM, LANES)
    return jnp.where(row_ids(shape) == lane_ids(shape) % HEAD_DIM, 1.0, 0.0)


def newton_first_kernel(kernel_ref, inverse_ref, saved_ref):
    inverses = []
    for p in range(kernel_ref.shape[0]):
        kernel = kernel_ref[p]
        inverses.append(pair_turned(kernel) / start_bound(kernel)[1])
    newton_sweeps(kernel_ref, inverses, inverse_ref, saved_ref)


def newton_next_kernel(kernel_ref, last_ref, inverse_ref, saved_ref):
    inverses = [last_ref[p] for p in range(kernel_ref.shape[0])]
    newton_sweeps(kernel_ref, inverses, inverse_ref, saved_ref)


def newton_sweeps(kernel_ref, inverses, inverse_ref, saved_ref):
    pairs = range(kernel_ref.shape[0])
    identity = pair_identity()
    for sweep in range(saved_ref.shape[0]):
        products = [pair_mul(kernel_ref[p], inverses[p]) for p in pairs]
        inner = [15.0 * identity - pair_mul(products[p], 7.0 * identity - products[p]) for p in pairs]
        last = [13.0 * identity - pair_mul(products[p], inner[p]) for p in pairs]
        for p in pairs:
            saved_ref[sweep, 0, p] = inverses[p]
            saved_ref[sweep, 1, p] = products[p]
            saved_ref[sweep, 2, p] = inner[p]
            saved_ref[sweep, 3, p] = last[p]
        inverses = [0.25 * pair_mul(inverses[p], last[p]) for p in pairs]
    for p in pairs:
        inverse_ref[p] = inverses[p]


def newton_back_kernel(kernel_ref, saved_ref, inverse_in, kernel_in, inverse_out, kernel_out):
    pairs = range(kernel_ref.shape[0])
    identity = pair_identity()
    back = [inverse_in[p] for p in pairs]
    total = [kernel_in[p] for p in pairs]
    for sweep in reversed(range(saved_ref.shape[0])):
        inverse = [saved_ref[sweep, 0, p] for p in pairs]
        product = [saved_ref[sweep, 1, p] for p in pairs]
        third = [0.25 * pair_t_mul(inverse[p], back[p]) for p in pairs]
        second = [-pair_t_mul(product[p], third[p]) for p in pairs]
        first = [-pair_t_mul(product[p], second[p]) for p in pairs]
        slope = [
            -(
                pair_mul_t(third[p], saved_ref[sweep, 2, p])
                + pair_mul_t(second[p], 7.0 * identity - product[p])
                + first[p]
            )
            for p in pairs
        ]
        back = [
            0.25 * pair_mul_t(back[p], saved_ref[sweep, 3, p])
            + pair_t_mul(kernel_ref[p], slope[p])
            for p in pairs
        ]
        total = [total[p] + pair_mul_t(slope[p], inverse[p]) for p in pairs]
    for p in pairs:
        inverse_out[p] = back[p]
        kernel_out[p] = total[p]


def land_back_kernel(kernel_ref, back_start_ref, back_kernel_ref, land_query_ref, land_key_ref,
                     query_ref, key_ref):
    queries, keys = [], []
    for p in range(kernel_ref.shape[0]):
        kernel, start = kernel_ref[p], pair_turned(back_start_ref[p])
        column_sums, bound = start_bound(kernel)
        both = jnp.sum(start * kernel, axis=0, keepdims=True)
        back_bound = -pair_sums(both) / (bound * bound)
        back = back_kernel_ref[p] + start / bound + back_bound * column_sums / bound
        scores = kernel * (back - pair_sums(kernel * back))
        land_query, land_key = pair_of(land_query_ref[...], p), pair_of(land_key_ref[...], p)
        high, low = two_parts(scores)
        spread = pair_spread(land_key)
        queries.append(dot(high, spread) + dot(low, spread))
        keys.append(pair_gather(outer(high, land_query) + outer(low, land_query)))
    query_ref[...] = jnp.concatenate(queries, axis=1)
    key_ref[...] = jnp.concatenate(keys, axis=1)


def group_of(array, r, channels):
    return array[:, r * channels : (r + 1) * channels]


def layout_kernel(place_ref, sizes_ref, member_ref, turned_ref, count_ref, flags_ref):
    row, local = place_ref[0], place_ref[1]
    sizes = sizes_ref[row].astype(f32)
    items, marks = sizes.shape
    width = turned_ref.shape[1]
    devices = SPAN // width

    def pick(condition, value, axis):
        return jnp.sum(jnp.where(condition, value, 0.0), axis=axis, keepdims=True)

    totals = jnp.sum(sizes, axis=1, keepdims=True)
    small = (items, items)
    totals_row = pick(row_ids(small) == lane_ids(small), jnp.broadcast_to(totals, small), 0)
    ends = pick(lane_ids(small) <= row_ids(small), jnp.broadcast_to(totals_row, small), 1)
    wide = (items, LANES)
    below = jnp.broadcast_to(ends, wide) <= (width * lane_ids(wide)).astype(f32)
    item_of = jnp.sum(jnp.where(below, 1.0, 0.0), axis=0, keepdims=True)

    def item_at(index):
        return pick(lane_ids(item_of.shape) == index, item_of, 1)

    own = item_at(local)
    item_rows = row_ids((items, 1)).astype(f32)
    own_sizes = pick(row_ids(sizes.shape).astype(f32) == own, sizes, 0)
    item_start = pick(item_rows < own, totals, 0)
    square = (marks, marks)
    spread = jnp.broadcast_to(own_sizes, square)
    size_column = pick(row_ids(square) == lane_ids(square), spread, 1)
    end_column = pick(lane_ids(square) <= row_ids(square), spread, 1)
    end_row = pick(row_ids(square) <= lane_ids(square), jnp.broadcast_to(size_column, square), 0)
    first = (local * width).astype(f32) - item_start
    along = lane_ids(turned_ref.shape).astype(f32) + first
    inside = (along >= end_column - size_column) & (along < end_column)
    turned_ref[...] = jnp.where(inside, 1.0, 0.0).astype(bf16)
    down = row_ids(member_ref.shape).astype(f32) + first
    inside = (down >= end_row - own_sizes) & (down < end_row)
    member_ref[...] = jnp.where(inside, 1.0, 0.0).astype(bf16)
    count_ref[...] = jnp.broadcast_to(jnp.maximum(size_column, 1.0), count_ref.shape)

    def put(at, value):
        flags_ref[at : at + 1, :] = jnp.broadcast_to(jnp.where(value, 1.0, 0.0), (1, LANES))

    level, size = 0, 1
    while size < devices:
        start = local - local % size
        is_left = (local // size) % 2 == 0
        other = jnp.where(is_left, start + size, start - size)
        far_facing = item_at(jnp.where(is_left, other, other + size - 1))
        far_outer = item_at(jnp.where(is_left, other + size - 1, other))
        facing = item_at(jnp.where(is_left, start + size - 1, start))
        outer_edge = item_at(jnp.where(is_left, start, start + size - 1))
        next_left = (local // (2 * size)) % 2 == 0
        put(4 * level, own == far_facing)
        put(4 * level + 1, outer_edge == far_facing)
        put(4 * level + 2, far_outer == facing)
        turn = jnp.where(is_left != next_left, 1.0, 0.0)
        flags_ref[4 * level + 3 : 4 * level + 4, :] = jnp.full((1, LANES), turn, f32)
        level, size = level + 1, 2 * size
    before = jnp.where(local > 0, 1.0, 0.0) * jnp.where(item_at(local - 1) == own, 1.0, 0.0)
    behind = jnp.where(local < devices - 1, 1.0, 0.0) * jnp.where(
        item_at(local + 1) == own, 1.0, 0.0
    )
    flags_ref[12:13, :] = jnp.broadcast_to(before, (1, LANES))
    flags_ref[13:14, :] = jnp.broadcast_to(behind, (1, LANES))
    flags_ref[14:16, :] = jnp.zeros((2, LANES), f32)


def query_key_kernel(flat_ref, q0, k0, q1, k1, member_ref, query_ref, keys_ref, part_ref, message_ref):
    channels = query_ref.shape[2]
    scale = HEAD_DIM ** (-0.25)
    parts = []
    for r, (q, k) in enumerate(((q0, k0), (q1, k1))):
        query = dot_t(flat_ref[...], q[:channels]) + small_row(q, 0, channels)
        query = (scale * query).astype(bf16)
        keys = (scale * dot_t(flat_ref[...], k[...])).astype(bf16)
        query_ref[r] = query
        keys_ref[r] = keys
        parts += [dot(member_ref[...], query), dot(member_ref[...], keys)]
    part = jnp.concatenate(parts, axis=1)
    part_ref[...] = part
    message_ref[...] = part.astype(bf16)


def route_kernel(level, place, bits_ref, *refs):
    keep_out, send_out = refs[-2:]
    half = keep_out.shape[0]

    def total(i):
        sums = [
            (refs[k][i].astype(f32) + refs[k + 1][i].astype(f32)).astype(bf16)
            for k in range(0, len(refs) - 2, 2)
        ]
        return jnp.concatenate(sums, axis=1) if len(sums) > 1 else sums[0]

    for i in range(half):
        if place is None:
            keep, send = i, half + i
        else:
            bit = bits_ref[level] << place
            base = ((i >> place) << (place + 1)) + (i & ((1 << place) - 1))
            keep, send = base + bit, base + (1 << place) - bit
        keep_out[i] = total(keep)
        send_out[i] = total(send)


def last_tile_kernel(bits_ref, keep_ref, got_ref, out_ref):
    for i in range(out_ref.shape[0]):
        out_ref[i] = keep_ref[i].astype(f32) + got_ref[i].astype(f32)


def put_tiles(product, r, mine_ref, theirs_ref):
    ref = theirs_ref if r % 2 else mine_ref
    places = ref.shape[0] // 2
    rows = product.shape[0] // places
    first = places if r >= 2 else 0
    for place in range(places):
        ref[first + place, :rows] = product[place * rows : (place + 1) * rows].astype(bf16)


def weight_gradient_kernel(side_ref, units_ref, mine_ref, theirs_ref, turned_ref):
    turned_ref[...] = side_ref[...].T
    columns = mine_ref.shape[2]
    for r in range(units_ref.shape[1] // columns):
        product = dot(turned_ref[...], units_ref[:, r * columns : (r + 1) * columns])
        put_tiles(product, r, mine_ref, theirs_ref)


def small_kernel(weight_ref, query_ref, value_ref, taps_ref, flipped_ref, up_ref, out_ref):
    columns = out_ref.shape[1]

    def row(pieces):
        width = sum(piece.shape[1] for piece in pieces)
        return jnp.concatenate(pieces + [jnp.zeros((1, columns - width), f32)], axis=1)

    heads = range(query_ref.shape[0])
    rows = []
    for ref in (query_ref, value_ref):
        value = ref[...].astype(f32)
        rows.append(row([value[j : j + 1] for j in heads]))
    for ref in (taps_ref, flipped_ref):
        value = ref[...].astype(f32)
        rows += [row([value[j : j + 1]]) for j in heads]
    rows.append(up_ref[...].astype(f32).reshape(1, columns))
    rows.append(jnp.zeros((SMALL_ROWS - len(rows), columns), f32))
    channels = weight_ref.shape[0]
    out_ref[:channels] = weight_ref[...]
    out_ref[channels:] = jnp.concatenate(rows, axis=0).astype(bf16)


def small_row(ref, at, width):
    return ref[ref.shape[0] - SMALL_ROWS :, :width].astype(f32)[at : at + 1]


def bundle_kernel(rank_ref, up_ref, value_ref, taps_ref, norm_ref, out_ref):
    ranks, channels = value_ref.shape
    columns = out_ref.shape[1]
    heads = taps_ref.shape[0] // ranks
    for r in range(ranks):
        at = 4 * (r ^ rank_ref[0])
        value = value_ref[r : r + 1, :]
        rows = (
            up_ref[:, r * columns : (r + 1) * columns],
            jnp.concatenate((value, jnp.zeros((1, columns - channels), f32)), axis=1),
            jnp.concatenate([taps_ref[r * heads + j : r * heads + j + 1] for j in range(heads)], axis=1),
        )
        for k, row in enumerate(rows):
            out_ref[pl.ds(at + k, 1), :] = row
        out_ref[pl.ds(at + 3, 1), :] = jnp.zeros((1, columns), f32)
    norms = norm_ref.shape[0]
    out_ref[4 * ranks : 4 * ranks + norms, :] = norm_ref[...]
    out_ref[4 * ranks + norms :, :] = jnp.zeros((out_ref.shape[0] - 4 * ranks - norms, columns), f32)


def land_kernel(flags_ref, count_ref, own0, got0, own1, got1, query_ref, keys_ref, kernel_ref):
    channels = own0.shape[1] // 4
    count = count_ref[:, 0:1]
    queries, keys = [], []
    for own, got in ((own0, got0), (own1, got1)):
        land = sum_merge(own[...], got[...].astype(f32), flag(flags_ref, 8)) / count
        for r in range(2):
            queries.append(group_of(land, 2 * r, channels).astype(bf16))
            keys.append(group_of(land, 2 * r + 1, channels).astype(bf16))
    land_query, land_key = jnp.concatenate(queries, axis=1), jnp.concatenate(keys, axis=1)
    query_ref[...] = land_query
    keys_ref[...] = land_key
    for p in range(kernel_ref.shape[0]):
        scores = dot_t(pair_of(land_query, p), pair_spread(pair_of(land_key, p)))
        powers = jnp.exp(scores - pair_sums(scores, jnp.max, very_negative))
        kernel_ref[p] = powers / pair_sums(powers)


def value_kernel(flat_ref, w0, w1, w2, w3, s0, s1, s2, s3, values_ref, head_ref, tail_ref):
    reach = head_ref.shape[0]
    heads, tails = [], []
    channels = values_ref.shape[2]
    for r, (w, small) in enumerate(((w0, s0), (w1, s1), (w2, s2), (w3, s3))):
        values = (dot_t(flat_ref[...], w[...]) + small_row(small, 1, channels)).astype(bf16)
        values_ref[r] = values
        heads.append(values[:reach])
        tails.append(values[values.shape[0] - reach :])
    head_ref[...] = jnp.concatenate(heads, axis=1)
    tail_ref[...] = jnp.concatenate(tails, axis=1)


def key_kernel(k0, k1, values_ref, land_query_ref, state_ref, message_ref):
    channels = values_ref.shape[2]
    heads = channels // HEAD_DIM
    mixed = []
    marks = land_query_ref.shape[0]
    stats = jnp.zeros((marks, LANES), f32)
    lane = lane_ids(stats.shape)
    groups = values_ref.shape[0]
    for r in range(groups):
        keys = (k0, k1)[r // 2][r % 2]
        scores = dot_t(spread_heads(group_of(land_query_ref[...], r, channels)), keys)
        top = jnp.max(scores, axis=1, keepdims=True).astype(bf16).astype(f32)
        powers = jnp.exp(scores - top)
        total = jnp.sum(powers, axis=1, keepdims=True)
        mixed.append(gather_heads(dot(powers.astype(bf16), values_ref[r])))
        for j in range(heads):
            h = r * heads + j
            at = slice(j * marks, (j + 1) * marks)
            stats = jnp.where(lane == h, top[at], stats)
            stats = jnp.where(lane == groups * heads + h, total[at], stats)
    state = jnp.concatenate(mixed + [stats], axis=1)
    state_ref[...] = state
    message_ref[...] = state_message(state, groups * heads)


def state_message(state, heads):
    width = state.shape[1] - LANES
    stats = state[:, width:]
    lane = lane_ids(stats.shape)
    high = stats.astype(bf16).astype(f32)
    low = pltpu.roll(stats - high, heads, 1)
    last = jnp.where(lane < 2 * heads, high, jnp.where(lane < 3 * heads, low, 0.0))
    return jnp.concatenate((state[:, :width], last), axis=1).astype(bf16)


def message_state(message, heads):
    message = message.astype(f32)
    width = message.shape[1] - LANES
    stats = message[:, width:]
    lane = lane_ids(stats.shape)
    low = pltpu.roll(stats, LANES - heads, 1)
    stats = stats + jnp.where((lane >= heads) & (lane < 2 * heads), low, 0.0)
    stats = jnp.where(lane < 2 * heads, stats, 0.0)
    return jnp.concatenate((message[:, :width], stats), axis=1)


def widen(stats, first, width):
    pieces = []
    rows = stats.shape[0]
    for pair in range(width // LANES):
        lane = lane_ids((rows, LANES))
        at = first + 2 * pair
        pieces.append(
            jnp.where(lane < HEAD_DIM, stats[:, at : at + 1], stats[:, at + 1 : at + 2])
        )
    return jnp.concatenate(pieces, axis=1)


def merge_states(a, b, use, heads):
    width = a.shape[1] - LANES
    stats_a, stats_b = a[:, width:], b[:, width:]
    lane = lane_ids(stats_a.shape)
    top = jnp.where(use, jnp.maximum(stats_a, stats_b), stats_a)
    is_top = lane < heads
    scale_a = jnp.exp(jnp.where(is_top, stats_a - top, 0.0))
    scale_b = jnp.where(use, jnp.exp(jnp.where(is_top & use, stats_b - top, 0.0)), 0.0)
    values = a[:, :width] * widen(scale_a, 0, width) + b[:, :width] * widen(scale_b, 0, width)
    total = stats_a * pltpu.roll(scale_a, heads, 1) + stats_b * pltpu.roll(scale_b, heads, 1)
    stats = jnp.where(is_top, top, jnp.where(lane < 2 * heads, total, 0.0))
    return jnp.concatenate((values, stats), axis=1)


def token_kernel(q0, q1, land_key_ref, weights_ref):
    groups, rows, width = weights_ref.shape
    channels = q0.shape[2]
    heads = channels // HEAD_DIM
    for r in range(groups):
        query = (q0, q1)[r // 2][r % 2]
        scores = dot_t(spread_heads(group_of(land_key_ref[...], r, channels)), query)
        scores = scores.reshape(heads, rows // heads, width)
        powers = jnp.exp(scores - jnp.max(scores, axis=1, keepdims=True))
        weights = powers / jnp.sum(powers, axis=1, keepdims=True)
        weights_ref[r] = weights.reshape(rows, width)


def toeplitz(taps_row, rows, width):
    wide = jnp.broadcast_to(taps_row, (rows, taps_row.shape[1]))
    return pltpu.roll(wide, 0, 1, stride=1, stride_axis=0)[:, :width]


def with_rim(cells, before, after, flags_ref):
    return jnp.concatenate(
        (
            jnp.where(flag(flags_ref, 12), before, jnp.zeros_like(before)),
            cells,
            jnp.where(flag(flags_ref, 13), after, jnp.zeros_like(after)),
        ),
        axis=0,
    )


def convolve(rim, filters):
    tall = jnp.concatenate(filters, axis=0)
    span = tall.shape[1]
    pieces = []
    for start in range(0, rim.shape[0] - (span - STRIPE), STRIPE):
        product = dot(tall, rim[start : start + span])
        lane = lane_ids((STRIPE, rim.shape[1])) // HEAD_DIM
        piece = product[:STRIPE]
        for j in range(1, len(filters)):
            piece = jnp.where(lane == j, product[j * STRIPE : (j + 1) * STRIPE], piece)
        pieces.append(piece)
    return jnp.concatenate(pieces, axis=0)


def context_kernel(own_ref, got_ref, inverse_ref, weights_ref, values_ref, before_ref, after_ref,
                   flags_ref, s0, s1, s2, s3, context_ref, mixed_ref, low_ref, stats_ref):
    groups, width, channels = values_ref.shape
    heads = channels // HEAD_DIM
    reach = before_ref.shape[0]
    merge, _, decode = soft_parts(groups * heads)
    state = merge(own_ref[...], decode(got_ref[...]), flag(flags_ref, 8))
    model = groups * channels
    stats_ref[...] = state[:, model:]
    mixed = state[:, :model] / widen(state[:, model:], groups * heads, model)
    mixed_ref[...] = mixed
    low = jnp.concatenate(
        [
            pair_mul(inverse_ref[p], pair_of(mixed, p)).astype(bf16)
            for p in range(inverse_ref.shape[0])
        ],
        axis=1,
    )
    low_ref[...] = low
    for r in range(groups):
        nystrom = outer(
            weights_ref[r].astype(bf16), spread_heads(group_of(low, r, channels))
        )
        rim = with_rim(
            values_ref[r],
            group_of(before_ref[...], r, channels),
            group_of(after_ref[...], r, channels),
            flags_ref,
        )
        filters = [
            toeplitz(
                small_row((s0, s1, s2, s3)[r], 2 + j, 2 * LANES), STRIPE, STRIPE + 2 * reach
            ).astype(bf16)
            for j in range(heads)
        ]
        context_ref[r] = (nystrom + convolve(rim, filters)).astype(bf16)


def token_back_kernel(back_ref, weights_ref, low_ref, q0, q1, land_key_ref, part_ref,
                      message_ref, part_key_ref, message_key_ref, direct_ref, head_ref, tail_ref):
    groups, width, channels = back_ref.shape
    heads = channels // HEAD_DIM
    reach = head_ref.shape[0]
    parts, key_parts = [], []
    for r in range(groups):
        back = back_ref[r]
        query = (q0, q1)[r // 2][r % 2]
        weights = weights_ref[r]
        parts.append(gather_heads(dot(weights.astype(bf16), back)))
        slope = dot_t(spread_heads(group_of(low_ref[...], r, channels)), back)
        product = (weights * slope).reshape(heads, -1, width)
        rows = jnp.sum(product, axis=1, keepdims=True)
        rows = jnp.broadcast_to(rows, product.shape).reshape(weights.shape)
        scores = (weights * (slope - rows)).astype(bf16)
        key_parts.append(gather_heads(dot(scores, query)))
        direct_ref[r] = outer(scores, spread_heads(group_of(land_key_ref[...], r, channels)))
    for pieces, whole_ref, low in ((parts, part_ref, message_ref), (key_parts, part_key_ref, message_key_ref)):
        whole = jnp.concatenate(pieces, axis=1)
        whole_ref[...] = whole
        low[...] = whole.astype(bf16)
    head_ref[...] = jnp.concatenate([back_ref[r, :reach] for r in range(groups)], axis=1)
    tail_ref[...] = jnp.concatenate([back_ref[r, width - reach :] for r in range(groups)], axis=1)


def conv_back_kernel(back_ref, before_ref, after_ref, values_ref, vbefore_ref, vafter_ref, flags_ref,
                     direct_ref, s0, s1, s2, s3, back_values_ref, bias_ref, taps_ref):
    groups, width, channels = back_ref.shape
    heads = channels // HEAD_DIM
    reach = before_ref.shape[0]
    span = STRIPE + 2 * reach
    order = row_ids((STRIPE, STRIPE)) + lane_ids((STRIPE, STRIPE)) == STRIPE - 1
    order = jnp.where(order, 1.0, 0.0).astype(bf16)
    lane = lane_ids((STRIPE, channels)) // HEAD_DIM
    for r in range(groups):
        rim = with_rim(
            back_ref[r],
            group_of(before_ref[...], r, channels),
            group_of(after_ref[...], r, channels),
            flags_ref,
        )
        filters = [
            toeplitz(
                small_row((s0, s1, s2, s3)[r], 2 + heads + j, 2 * LANES), STRIPE, span
            ).astype(bf16)
            for j in range(heads)
        ]
        back_values = (direct_ref[r] + convolve(rim, filters)).astype(bf16)
        back_values_ref[r] = back_values
        bias_ref[r : r + 1, :] = jnp.sum(back_values.astype(f32), axis=0, keepdims=True)
        value_rim = with_rim(
            values_ref[r],
            group_of(vbefore_ref[...], r, channels),
            group_of(vafter_ref[...], r, channels),
            flags_ref,
        )
        total = jnp.zeros((heads * STRIPE, span), f32)
        for start in range(0, width, STRIPE):
            turned = dot(order, back_ref[r, start : start + STRIPE])
            tall = [jnp.where(lane == j, turned, 0.0).astype(bf16) for j in range(heads)]
            total = total + dot_t(jnp.concatenate(tall, axis=0), value_rim[start : start + span])
        total = jnp.concatenate(
            (total, jnp.zeros((heads * STRIPE, 2 * LANES - span), f32)), axis=1
        )
        for j in range(heads):
            skewed = pltpu.roll(
                total[j * STRIPE : (j + 1) * STRIPE], 0, 1, stride=1, stride_axis=0
            )
            h = r * heads + j
            taps_ref[h : h + 1, :] = jnp.sum(skewed, axis=0, keepdims=True)


def seed_kernel(flags_ref, own_ref, got_ref, inverse_ref, mixed_ref, back_inverse_ref, back_mixed_ref):
    back = sum_merge(own_ref[...], got_ref[...].astype(f32), flag(flags_ref, 8))
    pairs = []
    for p in range(inverse_ref.shape[0]):
        near = pair_of(back, p)
        back_inverse_ref[p] = pair_mul_t(near, pair_of(mixed_ref[...], p))
        pairs.append(pair_t_mul(inverse_ref[p], near))
    back_mixed_ref[...] = jnp.concatenate(pairs, axis=1).astype(bf16)


def key_back_kernel(k0, k1, values_ref, land_query_ref, state_ref, mixed_ref, back_mixed_ref,
                    part_ref, message_ref, direct_ref, values_direct_ref):
    groups, width, channels = values_ref.shape
    heads = channels // HEAD_DIM
    stats = state_ref[...]
    parts = []
    for r in range(groups):
        keys = (k0, k1)[r // 2][r % 2]
        land = spread_heads(group_of(land_query_ref[...], r, channels))
        scores = dot_t(land, keys)
        first = r * heads
        tops = jnp.concatenate([stats[:, first + j : first + j + 1] for j in range(heads)], axis=0)
        first += groups * heads
        totals = jnp.concatenate(
            [stats[:, first + j : first + j + 1] for j in range(heads)], axis=0
        )
        weights = jnp.exp(scores - tops) * (1.0 / totals)
        back_mixed = group_of(back_mixed_ref[...], r, channels)
        spread = spread_heads(back_mixed)
        dots = jnp.sum(
            spread_heads(group_of(mixed_ref[...], r, channels)) * spread.astype(f32),
            axis=1,
            keepdims=True,
        )
        slope = dot_t(spread, values_ref[r])
        back_scores = (weights * (slope - dots)).astype(bf16)
        parts.append(gather_heads(dot(back_scores, keys)))
        direct_ref[r] = outer(back_scores, land)
        values_direct_ref[r] = outer(weights.astype(bf16), spread)
    part = jnp.concatenate(parts, axis=1)
    part_ref[...] = part
    message_ref[...] = part.astype(bf16)


def input_back_kernel(flags_ref, count_ref, flat_ref, query_direct_ref, key_direct_ref, back_values_ref,
                      query_own_ref, query_got_ref, query_more_ref, key_own_ref, key_got_ref,
                      key_more_ref, member_ref, back_input_ref, q0, q1, q2, q3, k0, k1, k2, k3, v0,
                      v1, v2, v3, grad_ref, mine_ref, theirs_ref, turned_ref, both_ref, weight_ref):
    groups, width, channels = back_values_ref.shape
    model = flat_ref.shape[1]
    scale = HEAD_DIM ** (-0.25)
    member = member_ref[...]
    count = count_ref[:, 0:1]
    twice = jnp.concatenate((member, member), axis=1)
    sides = []
    for own, got, more in (
        (query_own_ref, query_got_ref, query_more_ref),
        (key_own_ref, key_got_ref, key_more_ref),
    ):
        side = sum_merge(own[...], got[...].astype(f32), flag(flags_ref, 8)) + more[...]
        sides.append(dot(twice, jnp.concatenate(two_parts(side / count), axis=0)))
    turned_ref[...] = flat_ref[...].T
    for r in range(groups):
        q, k = (q0, q1, q2, q3)[r], (k0, k1, k2, k3)[r]
        both = []
        for far, direct_ref in zip(sides, (query_direct_ref, key_direct_ref)):
            both.append((direct_ref[r] + group_of(far, r, channels)).astype(bf16))
        bias = scale * jnp.sum(both[0].astype(f32), axis=0, keepdims=True)
        bias = jnp.concatenate((bias, jnp.zeros_like(bias)), axis=1)
        at = slice(2 * r * channels, 2 * (r + 1) * channels)
        both_ref[:, at] = jnp.concatenate(both, axis=1)
        weight_ref[at, :] = jnp.concatenate((q[:channels], k[...]), axis=0)
        put_tiles(scale * dot(turned_ref[...], both_ref[:, at]), r, mine_ref, theirs_ref)
        ref = theirs_ref if r % 2 else mine_ref
        places = ref.shape[0] // 2
        more = ref.shape[1] - model // places
        for place in range(places):
            ref[(places if r >= 2 else 0) + place, model // places :] = jnp.broadcast_to(
                bias, (more, bias.shape[1])
            ).astype(bf16)
    total = back_input_ref[...] + scale * dot(both_ref[...], weight_ref[...])
    values = jnp.concatenate([back_values_ref[r] for r in range(groups)], axis=1)
    weights = jnp.concatenate([v[...] for v in (v0, v1, v2, v3)], axis=0)
    grad_ref[...] = (total + dot(values, weights)).astype(bf16)


def value_output_kernel(flat_ref, back_values_ref, back_attention_ref, context_ref, mine_ref, theirs_ref):
    flat, back = flat_ref[...].T, back_attention_ref[...].T
    for r in range(context_ref.shape[0]):
        product = (dot(back, context_ref[r]), dot(flat, back_values_ref[r]))
        put_tiles(jnp.concatenate(product, axis=1), r, mine_ref, theirs_ref)


def place_kernel(rank_ref, r0, r1, r2, r3, out_ref):
    step = pl.program_id(0)
    for k, ref in enumerate((r0, r1, r2, r3)):

        @pl.when(step == k)
        def _():
            out_ref[0] = ref[...].astype(out_ref.dtype)


def place_rows(rank, blocks, dtype):
    width, model = blocks[0].shape
    return pl.pallas_call(
        place_kernel,
        out_shape=jax.ShapeDtypeStruct((len(blocks), width, model), dtype),
        grid_spec=pltpu.PrefetchScalarGridSpec(
            num_scalar_prefetch=1,
            grid=(len(blocks),),
            in_specs=[pl.BlockSpec((width, model), lambda i, rank: (0, 0))] * len(blocks),
            out_specs=pl.BlockSpec((1, width, model), lambda i, rank: (i ^ rank[0], 0, 0)),
        ),
        compiler_params=pltpu.CompilerParams(vmem_limit_bytes=24 << 20),
        cost_estimate=cost(2.5),
        name="place_rows",
    )(rank.reshape(1).astype(jnp.int32), *blocks)


def feed_kernel(
    flat_ref, context_ref, out0, out1, out2, out3, up0, up1, up2, up3, down0, down1, down2, down3,
    s0, s1, s2, s3, p0, p1, p2, p3, p4, p5, cotangent_ref,
    layer_ref, back_input_ref, back_attention_ref, back_context_ref, active_ref, back_hidden_ref,
    first_low_ref, back_feed_ref, sums_ref, up_sums_ref,
    slope_ref, first_ref, total_ref,
):
    outs, ups, downs = (out0, out1, out2, out3), (up0, up1, up2, up3), (down0, down1, down2, down3)
    units = up0.shape[1]
    output_bias, first_gain, first_shift, down_bias, second_gain, second_shift = [
        p[...].astype(f32).reshape(1, flat_ref.shape[1]) for p in (p0, p1, p2, p3, p4, p5)
    ]

    def mean(value):
        return jnp.mean(value, axis=1, keepdims=True)

    attention = dot(context_ref[0], out0[...])
    for r in range(1, len(outs)):
        attention = attention + dot(context_ref[r], outs[r][...])
    value = flat_ref[...].astype(f32) + attention + output_bias
    centred = value - mean(value)
    first_inverse = lax.rsqrt(mean(centred * centred) + epsilon)
    first_normed = centred * first_inverse
    first_ref[...] = first_normed
    first_out = first_normed * first_gain + first_shift
    first_low_ref[...] = first_out.astype(bf16)
    total_ref[...] = first_out + down_bias
    for r in range(len(ups)):
        at = slice(r * units, (r + 1) * units)
        hidden = dot(first_low_ref[...], ups[r][...]) + small_row((s0, s1, s2, s3)[r], 8, units)
        cdf = 0.5 * (1.0 + lax.erf(hidden * 0.7071067811865476))
        slope_ref[:, at] = cdf + hidden * (0.3989422804014327 * jnp.exp(-0.5 * hidden * hidden))
        active = (hidden * cdf).astype(bf16)
        active_ref[:, at] = active
        total_ref[...] += dot(active, downs[r][...])

    value = total_ref[...]
    centred = value - mean(value)
    second_inverse = lax.rsqrt(mean(centred * centred) + epsilon)
    normed = centred * second_inverse
    layer_ref[...] = (normed * second_gain + second_shift).astype(bf16)
    upstream = cotangent_ref[...].astype(f32)
    sums_ref[4:5, :] = jnp.sum(upstream * normed, axis=0, keepdims=True)
    sums_ref[5:6, :] = jnp.sum(upstream, axis=0, keepdims=True)
    scaled = upstream * second_gain
    back_second = (scaled - mean(scaled) - normed * mean(scaled * normed)) * second_inverse
    back_feed = back_second.astype(bf16)
    back_feed_ref[...] = back_feed
    sums_ref[3:4, :] = jnp.sum(back_feed.astype(f32), axis=0, keepdims=True)
    total_ref[...] = back_second
    for r in range(len(ups)):
        at = slice(r * units, (r + 1) * units)
        back_active = dot_t(back_feed_ref[...], downs[r][...])
        back_hidden = (back_active * slope_ref[:, at]).astype(bf16)
        back_hidden_ref[:, at] = back_hidden
        up_sums_ref[:, at] = jnp.sum(back_hidden.astype(f32), axis=0, keepdims=True)
        total_ref[...] += dot_t(back_hidden, ups[r][...])

    back_first = total_ref[...]
    first_normed = first_ref[...]
    sums_ref[1:2, :] = jnp.sum(back_first * first_normed, axis=0, keepdims=True)
    sums_ref[2:3, :] = jnp.sum(back_first, axis=0, keepdims=True)
    scaled = back_first * first_gain
    back_input = (scaled - mean(scaled) - first_normed * mean(scaled * first_normed)) * first_inverse
    back_input_ref[...] = back_input
    back_attention = back_input.astype(bf16)
    back_attention_ref[...] = back_attention
    sums_ref[0:1, :] = jnp.sum(back_attention.astype(f32), axis=0, keepdims=True)
    for r in range(len(outs)):
        back_context_ref[r] = dot_t(back_attention, outs[r][...]).astype(bf16)


def feed_layer(flat, context, outputs, ups, downs, smalls, params, cotangent):
    width, model = flat.shape
    ranks, units = len(ups), ups[0].shape[1]
    channels = outputs[0].shape[0]
    shape = jax.ShapeDtypeStruct
    whole = pl.BlockSpec(memory_space=pltpu.VMEM)
    return pl.pallas_call(
        feed_kernel,
        out_shape=(
            shape((width, model), bf16),
            shape((width, model), f32),
            shape((width, model), bf16),
            shape((ranks, width, channels), bf16),
            shape((width, ranks * units), bf16),
            shape((width, ranks * units), bf16),
            shape((width, model), bf16),
            shape((width, model), bf16),
            shape((6, model), f32),
            shape((1, ranks * units), f32),
        ),
        in_specs=[whole] * (15 + len(smalls) + len(params)),
        out_specs=(whole,) * 10,
        scratch_shapes=[
            pltpu.VMEM((width, ranks * units), f32),
            pltpu.VMEM((width, model), f32),
            pltpu.VMEM((width, model), f32),
        ],
        compiler_params=pltpu.CompilerParams(vmem_limit_bytes=VMEM_LIMIT),
        cost_estimate=cost(19.0),
        name="feed_layer",
    )(flat, context, *outputs, *ups, *downs, *smalls, *params, cotangent)


def per_device(
    tokens,
    query_weight,
    query_bias,
    key_weight,
    value_weight,
    value_bias,
    conv_weight,
    output_weight,
    output_bias,
    first_gain,
    first_shift,
    up_weight,
    up_bias,
    down_weight,
    down_bias,
    second_gain,
    second_shift,
    segment_sizes,
    cotangent,
):
    rows, width, model = tokens.shape
    channels = query_weight.shape[1]
    ranks = lax.axis_size("tp")
    own_heads = channels // HEAD_DIM
    heads = ranks * own_heads
    hidden_units = up_weight.shape[1]
    items = segment_sizes.shape[1]
    marks = segment_sizes.shape[2]
    reach = TAPS // 2
    device = lax.axis_index("seq")
    rank = lax.axis_index("tp")
    group = SPAN // width
    groups = segment_sizes.shape[0] // rows
    place = jnp.stack((rank * groups + device // group, device % group)).astype(jnp.int32)

    half = ((2, width, channels), bf16)
    full = ((ranks, width, channels), bf16)
    full32 = ((ranks, width, channels), f32)
    edge = ((reach, model), bf16)
    marked = ((marks, model), f32)
    message = ((marks, model), bf16)
    tall = ((marks, LANES), f32)
    squares = ((heads // 2, marks, LANES), f32)
    half_sweeps = SWEEPS // 2
    saved = ((half_sweeps, 4, heads // 2, marks, LANES), f32)

    turned = [w.T for w in (query_weight, key_weight, value_weight)]
    (query_own,) = call(small_kernel, (((channels + SMALL_ROWS, model), bf16),), "small")(
        turned[0], query_bias, value_bias, conv_weight, conv_weight[:, ::-1], up_bias
    )
    key_far, key_core = swap(turned[1], "tp", 2), swap(turned[1], "tp", 1)
    query_far, query_core = swap(query_own, "tp", 2), swap(query_own, "tp", 1)
    query_blocks, key_blocks = [query_own, query_core], [turned[1], key_core]
    member, member_turned, count, flags = call(
        layout_kernel,
        (((width, marks), bf16), ((marks, width), bf16), tall, ((16, LANES), f32)),
        "layout",
        scalars=1,
    )(place, segment_sizes)
    flat = lax.dynamic_index_in_dim(tokens, rank, axis=0, keepdims=False)
    upstream = lax.dynamic_index_in_dim(cotangent, rank, axis=0, keepdims=False)

    def shards(own, far):
        return (own, swap(own, "tp", 1), far, swap(far, "tp", 1))

    query, keys, sums, first_step = [], [], [], flags
    for pair in range(2):
        q, k, part, sent = call(
            query_key_kernel, (half, half, marked, message), "query_key", us=2.5,
        )(
            after(flat, first_step),
            query_blocks[2 * pair],
            key_blocks[2 * pair],
            query_blocks[2 * pair + 1],
            key_blocks[2 * pair + 1],
            member_turned,
        )
        query.append(q)
        keys.append(k)
        if pair == 0:
            land = Exchange(plain_parts(), "land", flags, part, sent).first()
            first_step = land.own
            query_far, key_far = after(query_far, first_step), after(key_far, first_step)
            query_blocks += [query_far, swap(query_far, "tp", 1)]
            key_blocks += [key_far, swap(key_far, "tp", 1)]
            value_far = swap(after(turned[2], query_far, key_far), "tp", 2)
            output_far = swap(after(output_weight, query_far, key_far), "tp", 2)
        else:
            land = Exchange(plain_parts(), "land", flags, part, sent).first()
            first_step = land.own
        sums += [land.next().own, land.got()]
    smalls = query_blocks
    up_far = swap(after(up_weight, value_far, output_far, land.own), "tp", 2)
    value_blocks = shards(turned[2], value_far)
    output_blocks = shards(output_weight, output_far)
    up_blocks = shards(up_weight, up_far)
    land_query, land_key, kernel = call(land_kernel, (message, message, squares), "land")(
        flags, count, *sums
    )
    values, value_head, value_tail = call(
        value_kernel, (full, edge, edge), "values", us=2.0
    )(after(flat, output_far), *value_blocks, *smalls)

    def neighbours(head, tail):
        count = lax.axis_size("seq")
        before = lax.ppermute(tail, "seq", [(i, i + 1) for i in range(count - 1)])
        behind = lax.ppermute(head, "seq", [(i + 1, i) for i in range(count - 1)])
        return before, behind

    value_before, value_after = neighbours(value_head, value_tail)
    state, sent = call(
        key_kernel,
        (((marks, model + LANES), f32), ((marks, model + LANES), bf16)),
        "key_softmax",
        us=1.4,
    )(*keys, values, land_query)
    inverse, saved_first = call(newton_first_kernel, (squares, saved), "newton_first", us=2.5)(
        after(kernel, sent)
    )
    soft = Exchange(soft_parts(heads), "soft", flags, state, sent).first(inverse)
    down_far = swap(after(down_weight, up_far, soft.own), "tp", 2)
    inverse, saved_last = call(newton_next_kernel, (squares, saved), "newton_next", us=2.3)(
        kernel, after(inverse, soft.own)
    )
    state, state_got = soft.next(value_before, value_after).own, soft.got()
    (token_weights,) = call(
        token_kernel, (((ranks, own_heads * marks, width), f32),), "token_softmax", us=0.8,
    )(*query, land_key)
    down_core = swap(after(down_weight, sent), "tp", 1)
    context, mixed, mixed_low, stats = call(
        context_kernel, (full, marked, message, tall), "context", us=2.0,
    )(
        after(state, *output_blocks, *up_blocks, down_core), state_got, inverse, token_weights, values, value_before, value_after, flags,
        *smalls,
    )

    down_blocks = (down_weight, down_core, down_far, swap(after(down_far, context), "tp", 1))
    params = (output_bias, first_gain, first_shift, down_bias, second_gain, second_shift)
    (
        layer_out,
        back_input,
        back_attention,
        back_context,
        active,
        back_hidden,
        first_low,
        back_feed,
        norm_sums,
        up_sums,
    ) = feed_layer(
        flat, context, output_blocks, up_blocks, down_blocks, smalls, params, upstream
    )

    layer_far = swap(layer_out, "tp", 2)
    positions = lax.axis_size("seq")
    levels = list(range(positions.bit_length() - 1))
    bits = jnp.stack([(device >> level) & 1 for level in levels]).astype(jnp.int32)
    wide_tiles = (((2 * positions, model // positions, hidden_units), bf16),) * 2
    weight_gradient = call(
        weight_gradient_kernel, wide_tiles, "weight_gradient",
        scratch=(pltpu.VMEM((model, width), bf16),), us=4.5,
    )
    part_back, sent_back, part_key, sent_key, query_direct, back_head, back_tail = call(
        token_back_kernel, (marked, message, marked, message, full32, edge, edge), "token_back",
        us=1.8,
    )(back_context, token_weights, mixed_low, *query, land_key)
    turn = levels[:1] + ["far"] + levels[1:]
    up = Scatter("up", *weight_gradient(after(first_low, sent_back), back_hidden), bits, turn)
    back = Exchange(plain_parts(), "back", flags, part_back, sent_back).first(up.send)
    down = Scatter(
        "down", *weight_gradient(after(back_feed, back.own), active), bits, ["far"] + levels
    )
    key_side = Exchange(plain_parts(), "back_key", flags, part_key, sent_key).first()
    back.next(down.send, key_side.own, *up.hop())
    back_inverse, back_mixed = call(seed_kernel, (squares, message), "seed")(
        flags, back.own, back.got(), inverse, mixed
    )
    up.wait_for(key_side.own)
    part_query, sent_query, key_direct, values_direct = call(
        key_back_kernel, (marked, message, full32, full32), "key_back", us=2.4
    )(*keys, values, land_query, stats, mixed, after(back_mixed, layer_far))
    newton_back = call(newton_back_kernel, (squares, squares), "newton_back", us=6.6)
    back_middle = newton_back(
        kernel, saved_last, after(back_inverse, sent_query, *down.hop()), jnp.zeros(*squares)
    )
    query_side = Exchange(plain_parts(), "back_query", flags, part_query, sent_query)
    down.wait_for(layer_far)
    first_step = query_side.first(*back_middle, *up.hop()).own
    back_before, back_after = neighbours(*[after(x, first_step) for x in (back_head, back_tail)])
    back_values, value_bias_sums, tap_rows = call(
        conv_back_kernel, (full, ((ranks, channels), f32), ((heads, 2 * LANES), f32)), "conv_back",
        us=3.0,
    )(
        back_context, back_before, back_after, values, value_before, value_after, flags,
        values_direct, *smalls,
    )
    tiles = (((2 * positions, model // positions, 2 * channels), bf16),) * 2
    value_output = call(value_output_kernel, tiles, "value_output", us=2.0)(
        flat, back_values, back_attention, context
    )
    value_output = Scatter("value_output", *value_output, bits, ["far"] + levels)
    query_side.next(back_values, value_output.send)
    back_start, back_kernel = newton_back(
        kernel, saved_first, after(back_middle[0], query_side.own), back_middle[1]
    )
    query_more, key_more = call(land_back_kernel, (marked, marked), "land_back")(
        kernel, back_start, back_kernel, land_query, land_key
    )
    key_side.next()
    ready = [*down.hop(query_more), *value_output.hop(query_more), *up.hop(query_more)]
    bundle_rows = 4 * ranks + norm_sums.shape[0]
    (bundle,) = call(
        bundle_kernel, (((bundle_rows + -bundle_rows % 8, model), f32),), "bundle", scalars=1
    )(rank.reshape(1).astype(jnp.int32), up_sums, value_bias_sums, tap_rows, norm_sums)
    rows_here = model // positions
    bias_rows = rows_here + -rows_here % 16
    taller = (((2 * positions, bias_rows + 16, 2 * channels), bf16),) * 2
    grad_row, *projection = call(
        input_back_kernel,
        (((width, model), bf16),) + taller,
        "input_back",
        scratch=(
            pltpu.VMEM((model, width), bf16),
            pltpu.VMEM((width, 2 * model), bf16),
            pltpu.VMEM((2 * model, model), bf16),
        ),
        us=5.0,
        limit=24 << 20,
    )(
        flags, count, flat, query_direct, key_direct, back_values,
        after(query_side.own, *ready), query_side.got(), query_more,
        key_side.own, key_side.got(), key_more, member, back_input, *query_blocks, *key_blocks,
        *value_blocks,
    )
    projection = Scatter("projection", *projection, bits, turn)
    grad_far = swap(grad_row, "tp", 2)
    layer_blocks = shards(layer_out, layer_far)
    step = projection.hop()
    bundle = bundle + swap(after(bundle, *step), "tp", 1)
    step = up.hop(*step)
    step = value_output.hop(*step)
    step = down.hop(*step)
    step = projection.hop(*step)
    bundle = bundle + swap(after(bundle, *step), "seq", 1)
    step = up.hop(*step)
    layer_rows = place_rows(rank, (after(layer_blocks[0], *step),) + layer_blocks[1:], bf16)
    step = projection.hop(*step, layer_rows, bundle)
    step = down.hop(*step)
    step = value_output.hop(*step)
    bundle = bundle + swap(after(bundle, *step), "tp", 2)
    step = projection.hop(*step)
    grad_blocks = shards(grad_row, grad_far)
    grad_tokens = place_rows(rank, (after(grad_blocks[0], *step),) + grad_blocks[1:], f32)
    size = 2
    while size < positions:
        bundle = bundle + swap(after(bundle, *step), "seq", size)
        size *= 2
    step = value_output.hop(*step, grad_tokens)
    step = down.hop(*step)
    step = projection.hop(*step, bundle)
    step = value_output.hop(*step)
    for scatter in (projection, up, down, value_output):
        while scatter.hops:
            scatter.hop()
        if scatter.keep.dtype == bf16:
            scatter.hop()
    grad_up_weight = up.keep[0]
    grad_down_weight = down.keep[0]
    grad_output_weight = value_output.keep[0][:, :channels].T
    grad_value_weight = value_output.keep[0][:, channels:]
    projection = projection.keep[0]
    share = HEAD_DIM // positions
    grad_query_bias = lax.dynamic_slice_in_dim(
        projection[rows_here, :channels].reshape(own_heads, HEAD_DIM), device * share, share, axis=1
    )
    own = lax.dynamic_slice_in_dim(bundle, 4 * rank, 4, axis=0)
    grad_up_bias = own[0]
    grad_value_bias = own[1, :channels].reshape(own_heads, HEAD_DIM)
    grad_conv_weight = own[2].reshape(own_heads, 2 * LANES)[:, STRIPE - 1 : STRIPE - 1 + TAPS]
    shared = [bundle[4 * ranks + k] for k in range(6)]
    return (
        layer_rows,
        grad_tokens,
        projection[:rows_here, :channels],
        grad_query_bias,
        projection[:rows_here, channels:],
        grad_value_weight,
        grad_value_bias,
        grad_conv_weight,
        grad_output_weight,
        shared[0],
        shared[1],
        shared[2],
        grad_up_weight,
        grad_up_bias,
        grad_down_weight.T,
        shared[3],
        shared[4],
        shared[5],
    )


def solution(mesh):
    placed = (
        P(None, "seq", None),
        P(None, "tp"),
        P("tp", None),
        P(None, "tp"),
        P(None, "tp"),
        P("tp", None),
        P("tp", None),
        P("tp", None),
        P(),
        P(),
        P(),
        P(None, "tp"),
        P("tp"),
        P("tp", None),
        P(),
        P(),
        P(),
        P(),
        P(None, "seq", None),
    )
    return jax.shard_map(
        per_device,
        mesh=mesh,
        in_specs=placed,
        out_specs=(
            P(None, "seq", None),
            P(None, "seq", None),
            P("seq", "tp"),
            P("tp", "seq"),
            P("seq", "tp"),
            P("seq", "tp"),
            P("tp", None),
            P("tp", None),
            P("tp", "seq"),
            P(),
            P(),
            P(),
            P("seq", "tp"),
            P("tp"),
            P("tp", "seq"),
            P(),
            P(),
            P(),
        ),
        check_vma=False,
    )
```

```python
import functools

import jax
import jax.numpy as jnp
from jax import lax
from jax.experimental import pallas as pl
from jax.experimental.pallas import tpu as pltpu
from jax.sharding import PartitionSpec as P

HEAD_DIM = 64
TAPS = 33
SWEEPS = 6
SPAN = 4096
LANES = 128
STRIPE = 128
SMALL_ROWS = 16
VMEM_LIMIT = 28 << 20


epsilon = 1e-05
very_negative = -1e30
f32 = jnp.float32
bf16 = jnp.bfloat16


def swap(value, axis, step):
    return lax.ppermute(value, axis, [(i, i ^ step) for i in range(lax.axis_size(axis))])


def dot(a, b):
    return jnp.dot(a, b, preferred_element_type=f32)


def outer(a, b):
    return lax.dot_general(a, b, (((0,), (0,)), ((), ())), preferred_element_type=f32)


def dot_t(a, b):
    return lax.dot_general(a, b, (((1,), (1,)), ((), ())), preferred_element_type=f32)


def after(value, *others):
    return lax.optimization_barrier((value,) + others)[0]


class Scatter:
    def __init__(self, name, mine, theirs, bits, hops):
        self.name, self.bits, self.hops = name, bits, list(hops)
        self.keep, self.send, self.way = mine, theirs, ("tp", 1)
        self.left = sorted(level for level in hops if level != "far")

    def hop(self, *waits, other=None):
        operands = [after(self.keep, *waits), swap(self.send, *self.way)]
        tiles, rows, columns = self.keep.shape
        if other is not None:
            operands += [other.keep, swap(other.send, *other.way)]
            columns += other.keep.shape[2]
        if not self.hops:
            kernel, outs = last_tile_kernel, (((tiles, rows, columns), f32),)
        else:
            following = self.hops.pop(0)
            far = following == "far"
            self.way = ("tp", 2) if far else ("seq", 1 << following)
            place = None if far else self.left.index(following)
            kernel = functools.partial(route_kernel, following, place)
            if not far:
                self.left.remove(following)
            outs = (((tiles // 2, rows, columns), bf16),) * 2
        size = tiles * rows * columns * 2
        result = call(
            kernel, outs, self.name + "_route", scalars=1, us=0.5 + size / 1.2e6, limit=16 << 20
        )(self.bits, *operands)
        self.keep = result[0]
        self.send = result[-1]
        return result

    def wait_for(self, *others):
        self.send = after(self.send, *others)


def sum_merge(a, b, use):
    return a + jnp.where(use, b, 0.0)


def flag(flags_ref, row):
    return flags_ref[row : row + 1, 0:1] > 0.5


def plain_parts():
    return sum_merge, lambda value: value.astype(bf16), lambda message: message.astype(f32)


def soft_parts(heads):
    return (
        functools.partial(merge_states, heads=heads),
        functools.partial(state_message, heads=heads),
        functools.partial(message_state, heads=heads),
    )


def edges_after(parts, flags_ref, level, facing, outer_edge, got, got_outer):
    merge = parts[0]
    near = merge(outer_edge, got, flag(flags_ref, 4 * level + 1))
    away = merge(got_outer, facing, flag(flags_ref, 4 * level + 2))
    turn = flag(flags_ref, 4 * level + 3)
    return jnp.where(turn, near, away), jnp.where(turn, away, near)


def merge_first_kernel(parts, flags_ref, own_ref, got_ref, new_ref, message_ref):
    merge, encode, decode = parts
    own, got = own_ref[...], decode(got_ref[...])
    new_ref[...] = merge(own, got, flag(flags_ref, 0))
    facing, outer_edge = edges_after(parts, flags_ref, 0, own, own, got, got)
    message_ref[...] = jnp.concatenate((encode(facing), encode(outer_edge)), axis=0)


def merge_next_kernel(parts, flags_ref, own_ref, sent_ref, got_ref, new_ref, message_ref):
    merge, encode, decode = parts
    marks = own_ref.shape[0]
    got, got_outer = decode(got_ref[:marks]), decode(got_ref[marks:])
    new_ref[...] = merge(own_ref[...], got, flag(flags_ref, 4))
    facing, _ = edges_after(
        parts, flags_ref, 1, decode(sent_ref[:marks]), decode(sent_ref[marks:]), got, got_outer
    )
    message_ref[...] = encode(facing)


class Exchange:
    def __init__(self, parts, name, flags, own, message):
        self.parts, self.name, self.flags = parts, name, flags
        self.own, self.message = own, message

    def run(self, kernel, name, rows, *operands):
        marks, width = self.own.shape
        self.own, self.message = call(
            functools.partial(kernel, self.parts),
            (((marks, width), f32), ((rows, width), bf16)),
            self.name + name,
        )(self.flags, *operands)

    def first(self, *waits):
        got = swap(self.message, "seq", 1)
        self.run(merge_first_kernel, "_first", 2 * got.shape[0], after(self.own, *waits), got)
        return self

    def next(self, *waits):
        sent = self.message
        got = swap(sent, "seq", 2)
        self.run(merge_next_kernel, "_next", got.shape[0] // 2, after(self.own, *waits), sent, got)
        return self

    def got(self):
        return swap(self.message, "seq", 4)


WHOLE = pl.BlockSpec(memory_space=pltpu.VMEM)


def cost(us):
    return pl.CostEstimate(flops=0, bytes_accessed=int(us * 3.3e6), transcendentals=0)


def call(kernel, outs, name, scratch=(), limit=12 << 20, us=1.0, scalars=0):
    outs = tuple(jax.ShapeDtypeStruct(shape, dtype) for shape, dtype in outs)

    def run(*operands):
        return pl.pallas_call(
            kernel,
            out_shape=outs,
            in_specs=[pl.BlockSpec(memory_space=pltpu.SMEM)] * scalars
            + [WHOLE] * (len(operands) - scalars),
            out_specs=(WHOLE,) * len(outs),
            scratch_shapes=list(scratch),
            compiler_params=pltpu.CompilerParams(vmem_limit_bytes=limit),
            cost_estimate=cost(us),
            name=name,
        )(*operands)

    return run


def lane_ids(shape):
    return lax.broadcasted_iota(jnp.int32, shape, len(shape) - 1)


def row_ids(shape):
    return lax.broadcasted_iota(jnp.int32, shape, len(shape) - 2)


def spread_heads(block):
    heads = block.shape[1] // HEAD_DIM
    tall = jnp.concatenate([block] * heads, axis=0)
    same = row_ids(tall.shape) // HEAD_DIM == lane_ids(tall.shape) // HEAD_DIM
    return jnp.where(same, tall, jnp.zeros_like(tall))


def gather_heads(square):
    heads = square.shape[1] // HEAD_DIM
    result = jnp.zeros((HEAD_DIM, square.shape[1]), square.dtype)
    lane = lane_ids(result.shape) // HEAD_DIM
    for j in range(heads):
        result = jnp.where(lane == j, square[j * HEAD_DIM : (j + 1) * HEAD_DIM], result)
    return result


def two_parts(value):
    high = value.astype(bf16)
    return high, (value - high.astype(f32)).astype(bf16)


def first_half(shape):
    return lane_ids(shape) < HEAD_DIM


def pair_spread(pair):
    near = first_half(pair.shape)
    zero = jnp.zeros_like(pair)
    return jnp.concatenate((jnp.where(near, pair, zero), jnp.where(near, zero, pair)), axis=0)


def pair_gather(square):
    top, bottom = square[:HEAD_DIM], square[HEAD_DIM:]
    return jnp.where(first_half(top.shape), top, bottom)


def fine(product, a, b, turn=lambda value: value):
    a_high, a_low = two_parts(a)
    b_high, b_low = [turn(part) for part in two_parts(b)]
    return product(a_high, b_high) + (product(a_high, b_low) + product(a_low, b_high))


def pair_mul(a, b):
    return fine(dot, a, b, pair_spread)


def pair_mul_t(a, b):
    return fine(dot_t, a, b, pair_spread)


def pair_t_mul(a, b):
    return pair_gather(fine(outer, a, b))


def pair_sums(value, reduce=jnp.sum, neutral=0.0):
    near = first_half(value.shape)
    left = reduce(jnp.where(near, value, neutral), axis=1, keepdims=True)
    right = reduce(jnp.where(near, neutral, value), axis=1, keepdims=True)
    return jnp.where(near, left, right)


def pair_of(array, pair):
    return array[:, pair * LANES : (pair + 1) * LANES]


def pair_turned(value):
    tall = value.T
    return jnp.concatenate((tall[:HEAD_DIM], tall[HEAD_DIM:]), axis=1)


def start_bound(kernel):
    column_sums = jnp.sum(kernel, axis=0, keepdims=True)
    return column_sums, jnp.sqrt(pair_sums(column_sums * column_sums))


def pair_identity():
    shape = (HEAD_DIM, LANES)
    return jnp.where(row_ids(shape) == lane_ids(shape) % HEAD_DIM, 1.0, 0.0)


def newton_first_kernel(kernel_ref, inverse_ref, saved_ref):
    inverses = []
    for p in range(kernel_ref.shape[0]):
        kernel = kernel_ref[p]
        inverses.append(pair_turned(kernel) / start_bound(kernel)[1])
    newton_sweeps(kernel_ref, inverses, inverse_ref, saved_ref)


def newton_next_kernel(kernel_ref, last_ref, inverse_ref, saved_ref):
    inverses = [last_ref[p] for p in range(kernel_ref.shape[0])]
    newton_sweeps(kernel_ref, inverses, inverse_ref, saved_ref)


def newton_sweeps(kernel_ref, inverses, inverse_ref, saved_ref):
    pairs = range(kernel_ref.shape[0])
    identity = pair_identity()
    for sweep in range(saved_ref.shape[0]):
        products = [pair_mul(kernel_ref[p], inverses[p]) for p in pairs]
        inner = [15.0 * identity - pair_mul(products[p], 7.0 * identity - products[p]) for p in pairs]
        last = [13.0 * identity - pair_mul(products[p], inner[p]) for p in pairs]
        for p in pairs:
            saved_ref[sweep, 0, p] = inverses[p]
            saved_ref[sweep, 1, p] = products[p]
            saved_ref[sweep, 2, p] = inner[p]
            saved_ref[sweep, 3, p] = last[p]
        inverses = [0.25 * pair_mul(inverses[p], last[p]) for p in pairs]
    for p in pairs:
        inverse_ref[p] = inverses[p]


def newton_back_kernel(kernel_ref, saved_ref, inverse_in, kernel_in, inverse_out, kernel_out):
    pairs = range(kernel_ref.shape[0])
    identity = pair_identity()
    back = [inverse_in[p] for p in pairs]
    total = [kernel_in[p] for p in pairs]
    for sweep in reversed(range(saved_ref.shape[0])):
        inverse = [saved_ref[sweep, 0, p] for p in pairs]
        product = [saved_ref[sweep, 1, p] for p in pairs]
        third = [0.25 * pair_t_mul(inverse[p], back[p]) for p in pairs]
        second = [-pair_t_mul(product[p], third[p]) for p in pairs]
        first = [-pair_t_mul(product[p], second[p]) for p in pairs]
        slope = [
            -(
                pair_mul_t(third[p], saved_ref[sweep, 2, p])
                + pair_mul_t(second[p], 7.0 * identity - product[p])
                + first[p]
            )
            for p in pairs
        ]
        back = [
            0.25 * pair_mul_t(back[p], saved_ref[sweep, 3, p])
            + pair_t_mul(kernel_ref[p], slope[p])
            for p in pairs
        ]
        total = [total[p] + pair_mul_t(slope[p], inverse[p]) for p in pairs]
    for p in pairs:
        inverse_out[p] = back[p]
        kernel_out[p] = total[p]


def land_back_kernel(kernel_ref, back_start_ref, back_kernel_ref, land_query_ref, land_key_ref,
                     query_ref, key_ref):
    queries, keys = [], []
    for p in range(kernel_ref.shape[0]):
        kernel, start = kernel_ref[p], pair_turned(back_start_ref[p])
        column_sums, bound = start_bound(kernel)
        both = jnp.sum(start * kernel, axis=0, keepdims=True)
        back_bound = -pair_sums(both) / (bound * bound)
        back = back_kernel_ref[p] + start / bound + back_bound * column_sums / bound
        scores = kernel * (back - pair_sums(kernel * back))
        land_query, land_key = pair_of(land_query_ref[...], p), pair_of(land_key_ref[...], p)
        high, low = two_parts(scores)
        spread = pair_spread(land_key)
        queries.append(dot(high, spread) + dot(low, spread))
        keys.append(pair_gather(outer(high, land_query) + outer(low, land_query)))
    query_ref[...] = jnp.concatenate(queries, axis=1)
    key_ref[...] = jnp.concatenate(keys, axis=1)


def group_of(array, r, channels):
    return array[:, r * channels : (r + 1) * channels]


def layout_kernel(place_ref, sizes_ref, member_ref, turned_ref, count_ref, flags_ref):
    row, local = place_ref[0], place_ref[1]
    sizes = sizes_ref[row].astype(f32)
    items, marks = sizes.shape
    width = turned_ref.shape[1]
    devices = SPAN // width

    def pick(condition, value, axis):
        return jnp.sum(jnp.where(condition, value, 0.0), axis=axis, keepdims=True)

    totals = jnp.sum(sizes, axis=1, keepdims=True)
    small = (items, items)
    totals_row = pick(row_ids(small) == lane_ids(small), jnp.broadcast_to(totals, small), 0)
    ends = pick(lane_ids(small) <= row_ids(small), jnp.broadcast_to(totals_row, small), 1)
    wide = (items, LANES)
    below = jnp.broadcast_to(ends, wide) <= (width * lane_ids(wide)).astype(f32)
    item_of = jnp.sum(jnp.where(below, 1.0, 0.0), axis=0, keepdims=True)

    def item_at(index):
        return pick(lane_ids(item_of.shape) == index, item_of, 1)

    own = item_at(local)
    item_rows = row_ids((items, 1)).astype(f32)
    own_sizes = pick(row_ids(sizes.shape).astype(f32) == own, sizes, 0)
    item_start = pick(item_rows < own, totals, 0)
    square = (marks, marks)
    spread = jnp.broadcast_to(own_sizes, square)
    size_column = pick(row_ids(square) == lane_ids(square), spread, 1)
    end_column = pick(lane_ids(square) <= row_ids(square), spread, 1)
    end_row = pick(row_ids(square) <= lane_ids(square), jnp.broadcast_to(size_column, square), 0)
    first = (local * width).astype(f32) - item_start
    along = lane_ids(turned_ref.shape).astype(f32) + first
    inside = (along >= end_column - size_column) & (along < end_column)
    turned_ref[...] = jnp.where(inside, 1.0, 0.0).astype(bf16)
    down = row_ids(member_ref.shape).astype(f32) + first
    inside = (down >= end_row - own_sizes) & (down < end_row)
    member_ref[...] = jnp.where(inside, 1.0, 0.0).astype(bf16)
    count_ref[...] = jnp.broadcast_to(jnp.maximum(size_column, 1.0), count_ref.shape)

    def put(at, value):
        flags_ref[at : at + 1, :] = jnp.broadcast_to(jnp.where(value, 1.0, 0.0), (1, LANES))

    level, size = 0, 1
    while size < devices:
        start = local - local % size
        is_left = (local // size) % 2 == 0
        other = jnp.where(is_left, start + size, start - size)
        far_facing = item_at(jnp.where(is_left, other, other + size - 1))
        far_outer = item_at(jnp.where(is_left, other + size - 1, other))
        facing = item_at(jnp.where(is_left, start + size - 1, start))
        outer_edge = item_at(jnp.where(is_left, start, start + size - 1))
        next_left = (local // (2 * size)) % 2 == 0
        put(4 * level, own == far_facing)
        put(4 * level + 1, outer_edge == far_facing)
        put(4 * level + 2, far_outer == facing)
        turn = jnp.where(is_left != next_left, 1.0, 0.0)
        flags_ref[4 * level + 3 : 4 * level + 4, :] = jnp.full((1, LANES), turn, f32)
        level, size = level + 1, 2 * size
    before = jnp.where(local > 0, 1.0, 0.0) * jnp.where(item_at(local - 1) == own, 1.0, 0.0)
    behind = jnp.where(local < devices - 1, 1.0, 0.0) * jnp.where(
        item_at(local + 1) == own, 1.0, 0.0
    )
    flags_ref[12:13, :] = jnp.broadcast_to(before, (1, LANES))
    flags_ref[13:14, :] = jnp.broadcast_to(behind, (1, LANES))
    flags_ref[14:16, :] = jnp.zeros((2, LANES), f32)


def query_key_kernel(flat_ref, q0, k0, q1, k1, member_ref, query_ref, keys_ref, part_ref, message_ref):
    channels = query_ref.shape[2]
    scale = HEAD_DIM ** (-0.25)
    parts = []
    for r, (q, k) in enumerate(((q0, k0), (q1, k1))):
        query = dot_t(flat_ref[...], q[:channels]) + small_row(q, 0, channels)
        query = (scale * query).astype(bf16)
        keys = (scale * dot_t(flat_ref[...], k[...])).astype(bf16)
        query_ref[r] = query
        keys_ref[r] = keys
        parts += [dot(member_ref[...], query), dot(member_ref[...], keys)]
    part = jnp.concatenate(parts, axis=1)
    part_ref[...] = part
    message_ref[...] = part.astype(bf16)


def route_kernel(level, place, bits_ref, *refs):
    keep_out, send_out = refs[-2:]
    half = keep_out.shape[0]

    def total(i):
        sums = [
            (refs[k][i].astype(f32) + refs[k + 1][i].astype(f32)).astype(bf16)
            for k in range(0, len(refs) - 2, 2)
        ]
        return jnp.concatenate(sums, axis=1) if len(sums) > 1 else sums[0]

    for i in range(half):
        if place is None:
            keep, send = i, half + i
        else:
            bit = bits_ref[level] << place
            base = ((i >> place) << (place + 1)) + (i & ((1 << place) - 1))
            keep, send = base + bit, base + (1 << place) - bit
        keep_out[i] = total(keep)
        send_out[i] = total(send)


def last_tile_kernel(bits_ref, keep_ref, got_ref, out_ref):
    for i in range(out_ref.shape[0]):
        out_ref[i] = keep_ref[i].astype(f32) + got_ref[i].astype(f32)


def put_tiles(product, r, mine_ref, theirs_ref):
    ref = theirs_ref if r % 2 else mine_ref
    places = ref.shape[0] // 2
    rows = product.shape[0] // places
    first = places if r >= 2 else 0
    for place in range(places):
        ref[first + place, :rows] = product[place * rows : (place + 1) * rows].astype(bf16)


def weight_gradient_kernel(side_ref, units_ref, mine_ref, theirs_ref, turned_ref):
    turned_ref[...] = side_ref[...].T
    columns = mine_ref.shape[2]
    for r in range(units_ref.shape[1] // columns):
        product = dot(turned_ref[...], units_ref[:, r * columns : (r + 1) * columns])
        put_tiles(product, r, mine_ref, theirs_ref)


def small_kernel(weight_ref, query_ref, value_ref, taps_ref, flipped_ref, up_ref, out_ref):
    columns = out_ref.shape[1]

    def row(pieces):
        width = sum(piece.shape[1] for piece in pieces)
        return jnp.concatenate(pieces + [jnp.zeros((1, columns - width), f32)], axis=1)

    heads = range(query_ref.shape[0])
    rows = []
    for ref in (query_ref, value_ref):
        value = ref[...].astype(f32)
        rows.append(row([value[j : j + 1] for j in heads]))
    for ref in (taps_ref, flipped_ref):
        value = ref[...].astype(f32)
        rows += [row([value[j : j + 1]]) for j in heads]
    rows.append(up_ref[...].astype(f32).reshape(1, columns))
    rows.append(jnp.zeros((SMALL_ROWS - len(rows), columns), f32))
    channels = weight_ref.shape[0]
    out_ref[:channels] = weight_ref[...]
    out_ref[channels:] = jnp.concatenate(rows, axis=0).astype(bf16)


def small_row(ref, at, width):
    return ref[ref.shape[0] - SMALL_ROWS :, :width].astype(f32)[at : at + 1]


def bundle_kernel(rank_ref, up_ref, value_ref, taps_ref, norm_ref, out_ref):
    ranks, channels = value_ref.shape
    columns = out_ref.shape[1]
    heads = taps_ref.shape[0] // ranks
    for r in range(ranks):
        at = 4 * (r ^ rank_ref[0])
        value = value_ref[r : r + 1, :]
        rows = (
            up_ref[:, r * columns : (r + 1) * columns],
            jnp.concatenate((value, jnp.zeros((1, columns - channels), f32)), axis=1),
            jnp.concatenate([taps_ref[r * heads + j : r * heads + j + 1] for j in range(heads)], axis=1),
        )
        for k, row in enumerate(rows):
            out_ref[pl.ds(at + k, 1), :] = row
        out_ref[pl.ds(at + 3, 1), :] = jnp.zeros((1, columns), f32)
    norms = norm_ref.shape[0]
    out_ref[4 * ranks : 4 * ranks + norms, :] = norm_ref[...]
    out_ref[4 * ranks + norms :, :] = jnp.zeros((out_ref.shape[0] - 4 * ranks - norms, columns), f32)


def land_kernel(flags_ref, count_ref, own0, got0, own1, got1, query_ref, keys_ref, kernel_ref):
    channels = own0.shape[1] // 4
    count = count_ref[:, 0:1]
    queries, keys = [], []
    for own, got in ((own0, got0), (own1, got1)):
        land = sum_merge(own[...], got[...].astype(f32), flag(flags_ref, 8)) / count
        for r in range(2):
            queries.append(group_of(land, 2 * r, channels).astype(bf16))
            keys.append(group_of(land, 2 * r + 1, channels).astype(bf16))
    land_query, land_key = jnp.concatenate(queries, axis=1), jnp.concatenate(keys, axis=1)
    query_ref[...] = land_query
    keys_ref[...] = land_key
    for p in range(kernel_ref.shape[0]):
        scores = dot_t(pair_of(land_query, p), pair_spread(pair_of(land_key, p)))
        powers = jnp.exp(scores - pair_sums(scores, jnp.max, very_negative))
        kernel_ref[p] = powers / pair_sums(powers)


def value_kernel(flat_ref, w0, w1, w2, w3, s0, s1, s2, s3, values_ref, head_ref, tail_ref):
    reach = head_ref.shape[0]
    heads, tails = [], []
    channels = values_ref.shape[2]
    for r, (w, small) in enumerate(((w0, s0), (w1, s1), (w2, s2), (w3, s3))):
        values = (dot_t(flat_ref[...], w[...]) + small_row(small, 1, channels)).astype(bf16)
        values_ref[r] = values
        heads.append(values[:reach])
        tails.append(values[values.shape[0] - reach :])
    head_ref[...] = jnp.concatenate(heads, axis=1)
    tail_ref[...] = jnp.concatenate(tails, axis=1)


def key_kernel(k0, k1, values_ref, land_query_ref, state_ref, message_ref):
    channels = values_ref.shape[2]
    heads = channels // HEAD_DIM
    mixed = []
    marks = land_query_ref.shape[0]
    stats = jnp.zeros((marks, LANES), f32)
    lane = lane_ids(stats.shape)
    groups = values_ref.shape[0]
    for r in range(groups):
        keys = (k0, k1)[r // 2][r % 2]
        scores = dot_t(spread_heads(group_of(land_query_ref[...], r, channels)), keys)
        top = jnp.max(scores, axis=1, keepdims=True).astype(bf16).astype(f32)
        powers = jnp.exp(scores - top)
        total = jnp.sum(powers, axis=1, keepdims=True)
        mixed.append(gather_heads(dot(powers.astype(bf16), values_ref[r])))
        for j in range(heads):
            h = r * heads + j
            at = slice(j * marks, (j + 1) * marks)
            stats = jnp.where(lane == h, top[at], stats)
            stats = jnp.where(lane == groups * heads + h, total[at], stats)
    state = jnp.concatenate(mixed + [stats], axis=1)
    state_ref[...] = state
    message_ref[...] = state_message(state, groups * heads)


def state_message(state, heads):
    width = state.shape[1] - LANES
    stats = state[:, width:]
    lane = lane_ids(stats.shape)
    high = stats.astype(bf16).astype(f32)
    low = pltpu.roll(stats - high, heads, 1)
    last = jnp.where(lane < 2 * heads, high, jnp.where(lane < 3 * heads, low, 0.0))
    return jnp.concatenate((state[:, :width], last), axis=1).astype(bf16)


def message_state(message, heads):
    message = message.astype(f32)
    width = message.shape[1] - LANES
    stats = message[:, width:]
    lane = lane_ids(stats.shape)
    low = pltpu.roll(stats, LANES - heads, 1)
    stats = stats + jnp.where((lane >= heads) & (lane < 2 * heads), low, 0.0)
    stats = jnp.where(lane < 2 * heads, stats, 0.0)
    return jnp.concatenate((message[:, :width], stats), axis=1)


def widen(stats, first, width):
    pieces = []
    rows = stats.shape[0]
    for pair in range(width // LANES):
        lane = lane_ids((rows, LANES))
        at = first + 2 * pair
        pieces.append(
            jnp.where(lane < HEAD_DIM, stats[:, at : at + 1], stats[:, at + 1 : at + 2])
        )
    return jnp.concatenate(pieces, axis=1)


def merge_states(a, b, use, heads):
    width = a.shape[1] - LANES
    stats_a, stats_b = a[:, width:], b[:, width:]
    lane = lane_ids(stats_a.shape)
    top = jnp.where(use, jnp.maximum(stats_a, stats_b), stats_a)
    is_top = lane < heads
    scale_a = jnp.exp(jnp.where(is_top, stats_a - top, 0.0))
    scale_b = jnp.where(use, jnp.exp(jnp.where(is_top & use, stats_b - top, 0.0)), 0.0)
    values = a[:, :width] * widen(scale_a, 0, width) + b[:, :width] * widen(scale_b, 0, width)
    total = stats_a * pltpu.roll(scale_a, heads, 1) + stats_b * pltpu.roll(scale_b, heads, 1)
    stats = jnp.where(is_top, top, jnp.where(lane < 2 * heads, total, 0.0))
    return jnp.concatenate((values, stats), axis=1)


def token_kernel(q0, q1, land_key_ref, weights_ref):
    groups, rows, width = weights_ref.shape
    channels = q0.shape[2]
    heads = channels // HEAD_DIM
    for r in range(groups):
        query = (q0, q1)[r // 2][r % 2]
        scores = dot_t(spread_heads(group_of(land_key_ref[...], r, channels)), query)
        scores = scores.reshape(heads, rows // heads, width)
        powers = jnp.exp(scores - jnp.max(scores, axis=1, keepdims=True))
        weights = powers / jnp.sum(powers, axis=1, keepdims=True)
        weights_ref[r] = weights.reshape(rows, width)


def toeplitz(taps_row, rows, width):
    wide = jnp.broadcast_to(taps_row, (rows, taps_row.shape[1]))
    return pltpu.roll(wide, 0, 1, stride=1, stride_axis=0)[:, :width]


def with_rim(cells, before, after, flags_ref):
    return jnp.concatenate(
        (
            jnp.where(flag(flags_ref, 12), before, jnp.zeros_like(before)),
            cells,
            jnp.where(flag(flags_ref, 13), after, jnp.zeros_like(after)),
        ),
        axis=0,
    )


def convolve(rim, filters):
    tall = jnp.concatenate(filters, axis=0)
    span = tall.shape[1]
    pieces = []
    for start in range(0, rim.shape[0] - (span - STRIPE), STRIPE):
        product = dot(tall, rim[start : start + span])
        lane = lane_ids((STRIPE, rim.shape[1])) // HEAD_DIM
        piece = product[:STRIPE]
        for j in range(1, len(filters)):
            piece = jnp.where(lane == j, product[j * STRIPE : (j + 1) * STRIPE], piece)
        pieces.append(piece)
    return jnp.concatenate(pieces, axis=0)


def context_kernel(own_ref, got_ref, inverse_ref, weights_ref, values_ref, before_ref, after_ref,
                   flags_ref, s0, s1, s2, s3, context_ref, mixed_ref, low_ref, stats_ref):
    groups, width, channels = values_ref.shape
    heads = channels // HEAD_DIM
    reach = before_ref.shape[0]
    merge, _, decode = soft_parts(groups * heads)
    state = merge(own_ref[...], decode(got_ref[...]), flag(flags_ref, 8))
    model = groups * channels
    stats_ref[...] = state[:, model:]
    mixed = state[:, :model] / widen(state[:, model:], groups * heads, model)
    mixed_ref[...] = mixed
    low = jnp.concatenate(
        [
            pair_mul(inverse_ref[p], pair_of(mixed, p)).astype(bf16)
            for p in range(inverse_ref.shape[0])
        ],
        axis=1,
    )
    low_ref[...] = low
    for r in range(groups):
        nystrom = outer(
            weights_ref[r].astype(bf16), spread_heads(group_of(low, r, channels))
        )
        rim = with_rim(
            values_ref[r],
            group_of(before_ref[...], r, channels),
            group_of(after_ref[...], r, channels),
            flags_ref,
        )
        filters = [
            toeplitz(
                small_row((s0, s1, s2, s3)[r], 2 + j, 2 * LANES), STRIPE, STRIPE + 2 * reach
            ).astype(bf16)
            for j in range(heads)
        ]
        context_ref[r] = (nystrom + convolve(rim, filters)).astype(bf16)


def token_back_kernel(back_ref, weights_ref, low_ref, q0, q1, land_key_ref, part_ref,
                      message_ref, part_key_ref, message_key_ref, direct_ref, head_ref, tail_ref):
    groups, width, channels = back_ref.shape
    heads = channels // HEAD_DIM
    reach = head_ref.shape[0]
    parts, key_parts = [], []
    for r in range(groups):
        back = back_ref[r]
        query = (q0, q1)[r // 2][r % 2]
        weights = weights_ref[r]
        parts.append(gather_heads(dot(weights.astype(bf16), back)))
        slope = dot_t(spread_heads(group_of(low_ref[...], r, channels)), back)
        product = (weights * slope).reshape(heads, -1, width)
        rows = jnp.sum(product, axis=1, keepdims=True)
        rows = jnp.broadcast_to(rows, product.shape).reshape(weights.shape)
        scores = (weights * (slope - rows)).astype(bf16)
        key_parts.append(gather_heads(dot(scores, query)))
        direct_ref[r] = outer(scores, spread_heads(group_of(land_key_ref[...], r, channels)))
    for pieces, whole_ref, low in ((parts, part_ref, message_ref), (key_parts, part_key_ref, message_key_ref)):
        whole = jnp.concatenate(pieces, axis=1)
        whole_ref[...] = whole
        low[...] = whole.astype(bf16)
    head_ref[...] = jnp.concatenate([back_ref[r, :reach] for r in range(groups)], axis=1)
    tail_ref[...] = jnp.concatenate([back_ref[r, width - reach :] for r in range(groups)], axis=1)


def conv_back_kernel(back_ref, before_ref, after_ref, values_ref, vbefore_ref, vafter_ref, flags_ref,
                     direct_ref, s0, s1, s2, s3, back_values_ref, bias_ref, taps_ref):
    groups, width, channels = back_ref.shape
    heads = channels // HEAD_DIM
    reach = before_ref.shape[0]
    span = STRIPE + 2 * reach
    order = row_ids((STRIPE, STRIPE)) + lane_ids((STRIPE, STRIPE)) == STRIPE - 1
    order = jnp.where(order, 1.0, 0.0).astype(bf16)
    lane = lane_ids((STRIPE, channels)) // HEAD_DIM
    for r in range(groups):
        rim = with_rim(
            back_ref[r],
            group_of(before_ref[...], r, channels),
            group_of(after_ref[...], r, channels),
            flags_ref,
        )
        filters = [
            toeplitz(
                small_row((s0, s1, s2, s3)[r], 2 + heads + j, 2 * LANES), STRIPE, span
            ).astype(bf16)
            for j in range(heads)
        ]
        back_values = (direct_ref[r] + convolve(rim, filters)).astype(bf16)
        back_values_ref[r] = back_values
        bias_ref[r : r + 1, :] = jnp.sum(back_values.astype(f32), axis=0, keepdims=True)
        value_rim = with_rim(
            values_ref[r],
            group_of(vbefore_ref[...], r, channels),
            group_of(vafter_ref[...], r, channels),
            flags_ref,
        )
        total = jnp.zeros((heads * STRIPE, span), f32)
        for start in range(0, width, STRIPE):
            turned = dot(order, back_ref[r, start : start + STRIPE])
            tall = [jnp.where(lane == j, turned, 0.0).astype(bf16) for j in range(heads)]
            total = total + dot_t(jnp.concatenate(tall, axis=0), value_rim[start : start + span])
        total = jnp.concatenate(
            (total, jnp.zeros((heads * STRIPE, 2 * LANES - span), f32)), axis=1
        )
        for j in range(heads):
            skewed = pltpu.roll(
                total[j * STRIPE : (j + 1) * STRIPE], 0, 1, stride=1, stride_axis=0
            )
            h = r * heads + j
            taps_ref[h : h + 1, :] = jnp.sum(skewed, axis=0, keepdims=True)


def seed_kernel(flags_ref, own_ref, got_ref, inverse_ref, mixed_ref, back_inverse_ref, back_mixed_ref):
    back = sum_merge(own_ref[...], got_ref[...].astype(f32), flag(flags_ref, 8))
    pairs = []
    for p in range(inverse_ref.shape[0]):
        near = pair_of(back, p)
        back_inverse_ref[p] = pair_mul_t(near, pair_of(mixed_ref[...], p))
        pairs.append(pair_t_mul(inverse_ref[p], near))
    back_mixed_ref[...] = jnp.concatenate(pairs, axis=1).astype(bf16)


def key_back_kernel(k0, k1, values_ref, land_query_ref, state_ref, mixed_ref, back_mixed_ref,
                    part_ref, message_ref, direct_ref, values_direct_ref):
    groups, width, channels = values_ref.shape
    heads = channels // HEAD_DIM
    stats = state_ref[...]
    parts = []
    for r in range(groups):
        keys = (k0, k1)[r // 2][r % 2]
        land = spread_heads(group_of(land_query_ref[...], r, channels))
        scores = dot_t(land, keys)
        first = r * heads
        tops = jnp.concatenate([stats[:, first + j : first + j + 1] for j in range(heads)], axis=0)
        first += groups * heads
        totals = jnp.concatenate(
            [stats[:, first + j : first + j + 1] for j in range(heads)], axis=0
        )
        weights = jnp.exp(scores - tops) * (1.0 / totals)
        back_mixed = group_of(back_mixed_ref[...], r, channels)
        spread = spread_heads(back_mixed)
        dots = jnp.sum(
            spread_heads(group_of(mixed_ref[...], r, channels)) * spread.astype(f32),
            axis=1,
            keepdims=True,
        )
        slope = dot_t(spread, values_ref[r])
        back_scores = (weights * (slope - dots)).astype(bf16)
        parts.append(gather_heads(dot(back_scores, keys)))
        direct_ref[r] = outer(back_scores, land)
        values_direct_ref[r] = outer(weights.astype(bf16), spread)
    part = jnp.concatenate(parts, axis=1)
    part_ref[...] = part
    message_ref[...] = part.astype(bf16)


def input_back_kernel(flags_ref, count_ref, flat_ref, query_direct_ref, key_direct_ref, back_values_ref,
                      query_own_ref, query_got_ref, query_more_ref, key_own_ref, key_got_ref,
                      key_more_ref, member_ref, back_input_ref, q0, q1, q2, q3, k0, k1, k2, k3, v0,
                      v1, v2, v3, grad_ref, mine_ref, theirs_ref, turned_ref, both_ref, weight_ref):
    groups, width, channels = back_values_ref.shape
    model = flat_ref.shape[1]
    scale = HEAD_DIM ** (-0.25)
    member = member_ref[...]
    count = count_ref[:, 0:1]
    twice = jnp.concatenate((member, member), axis=1)
    sides = []
    for own, got, more in (
        (query_own_ref, query_got_ref, query_more_ref),
        (key_own_ref, key_got_ref, key_more_ref),
    ):
        side = sum_merge(own[...], got[...].astype(f32), flag(flags_ref, 8)) + more[...]
        sides.append(dot(twice, jnp.concatenate(two_parts(side / count), axis=0)))
    turned_ref[...] = flat_ref[...].T
    for r in range(groups):
        q, k = (q0, q1, q2, q3)[r], (k0, k1, k2, k3)[r]
        both = []
        for far, direct_ref in zip(sides, (query_direct_ref, key_direct_ref)):
            both.append((direct_ref[r] + group_of(far, r, channels)).astype(bf16))
        bias = scale * jnp.sum(both[0].astype(f32), axis=0, keepdims=True)
        bias = jnp.concatenate((bias, jnp.zeros_like(bias)), axis=1)
        at = slice(2 * r * channels, 2 * (r + 1) * channels)
        both_ref[:, at] = jnp.concatenate(both, axis=1)
        weight_ref[at, :] = jnp.concatenate((q[:channels], k[...]), axis=0)
        put_tiles(scale * dot(turned_ref[...], both_ref[:, at]), r, mine_ref, theirs_ref)
        ref = theirs_ref if r % 2 else mine_ref
        places = ref.shape[0] // 2
        more = ref.shape[1] - model // places
        for place in range(places):
            ref[(places if r >= 2 else 0) + place, model // places :] = jnp.broadcast_to(
                bias, (more, bias.shape[1])
            ).astype(bf16)
    total = back_input_ref[...] + scale * dot(both_ref[...], weight_ref[...])
    values = jnp.concatenate([back_values_ref[r] for r in range(groups)], axis=1)
    weights = jnp.concatenate([v[...] for v in (v0, v1, v2, v3)], axis=0)
    grad_ref[...] = (total + dot(values, weights)).astype(bf16)


def value_output_kernel(flat_ref, back_values_ref, back_attention_ref, context_ref, mine_ref, theirs_ref):
    flat, back = flat_ref[...].T, back_attention_ref[...].T
    for r in range(context_ref.shape[0]):
        product = (dot(back, context_ref[r]), dot(flat, back_values_ref[r]))
        put_tiles(jnp.concatenate(product, axis=1), r, mine_ref, theirs_ref)


def place_kernel(rank_ref, r0, r1, r2, r3, out_ref):
    step = pl.program_id(0)
    for k, ref in enumerate((r0, r1, r2, r3)):

        @pl.when(step == k)
        def _():
            out_ref[0] = ref[...].astype(out_ref.dtype)


def place_rows(rank, blocks, dtype):
    width, model = blocks[0].shape
    return pl.pallas_call(
        place_kernel,
        out_shape=jax.ShapeDtypeStruct((len(blocks), width, model), dtype),
        grid_spec=pltpu.PrefetchScalarGridSpec(
            num_scalar_prefetch=1,
            grid=(len(blocks),),
            in_specs=[pl.BlockSpec((width, model), lambda i, rank: (0, 0))] * len(blocks),
            out_specs=pl.BlockSpec((1, width, model), lambda i, rank: (i ^ rank[0], 0, 0)),
        ),
        compiler_params=pltpu.CompilerParams(vmem_limit_bytes=24 << 20),
        cost_estimate=cost(2.5),
        name="place_rows",
    )(rank.reshape(1).astype(jnp.int32), *blocks)


def feed_kernel(
    flat_ref, context_ref, out0, out1, out2, out3, up0, up1, up2, up3, down0, down1, down2, down3,
    s0, s1, s2, s3, p0, p1, p2, p3, p4, p5, cotangent_ref,
    layer_ref, back_input_ref, back_attention_ref, back_context_ref, active_ref, back_hidden_ref,
    first_low_ref, back_feed_ref, sums_ref, up_sums_ref,
    slope_ref, first_ref, total_ref,
):
    outs, ups, downs = (out0, out1, out2, out3), (up0, up1, up2, up3), (down0, down1, down2, down3)
    units = up0.shape[1]
    output_bias, first_gain, first_shift, down_bias, second_gain, second_shift = [
        p[...].astype(f32).reshape(1, flat_ref.shape[1]) for p in (p0, p1, p2, p3, p4, p5)
    ]

    def mean(value):
        return jnp.mean(value, axis=1, keepdims=True)

    attention = dot(context_ref[0], out0[...])
    for r in range(1, len(outs)):
        attention = attention + dot(context_ref[r], outs[r][...])
    value = flat_ref[...].astype(f32) + attention + output_bias
    centred = value - mean(value)
    first_inverse = lax.rsqrt(mean(centred * centred) + epsilon)
    first_normed = centred * first_inverse
    first_ref[...] = first_normed
    first_out = first_normed * first_gain + first_shift
    first_low_ref[...] = first_out.astype(bf16)
    total_ref[...] = first_out + down_bias
    for r in range(len(ups)):
        at = slice(r * units, (r + 1) * units)
        hidden = dot(first_low_ref[...], ups[r][...]) + small_row((s0, s1, s2, s3)[r], 8, units)
        cdf = 0.5 * (1.0 + lax.erf(hidden * 0.7071067811865476))
        slope_ref[:, at] = cdf + hidden * (0.3989422804014327 * jnp.exp(-0.5 * hidden * hidden))
        active = (hidden * cdf).astype(bf16)
        active_ref[:, at] = active
        total_ref[...] += dot(active, downs[r][...])

    value = total_ref[...]
    centred = value - mean(value)
    second_inverse = lax.rsqrt(mean(centred * centred) + epsilon)
    normed = centred * second_inverse
    layer_ref[...] = (normed * second_gain + second_shift).astype(bf16)
    upstream = cotangent_ref[...].astype(f32)
    sums_ref[4:5, :] = jnp.sum(upstream * normed, axis=0, keepdims=True)
    sums_ref[5:6, :] = jnp.sum(upstream, axis=0, keepdims=True)
    scaled = upstream * second_gain
    back_second = (scaled - mean(scaled) - normed * mean(scaled * normed)) * second_inverse
    back_feed = back_second.astype(bf16)
    back_feed_ref[...] = back_feed
    sums_ref[3:4, :] = jnp.sum(back_feed.astype(f32), axis=0, keepdims=True)
    total_ref[...] = back_second
    for r in range(len(ups)):
        at = slice(r * units, (r + 1) * units)
        back_active = dot_t(back_feed_ref[...], downs[r][...])
        back_hidden = (back_active * slope_ref[:, at]).astype(bf16)
        back_hidden_ref[:, at] = back_hidden
        up_sums_ref[:, at] = jnp.sum(back_hidden.astype(f32), axis=0, keepdims=True)
        total_ref[...] += dot_t(back_hidden, ups[r][...])

    back_first = total_ref[...]
    first_normed = first_ref[...]
    sums_ref[1:2, :] = jnp.sum(back_first * first_normed, axis=0, keepdims=True)
    sums_ref[2:3, :] = jnp.sum(back_first, axis=0, keepdims=True)
    scaled = back_first * first_gain
    back_input = (scaled - mean(scaled) - first_normed * mean(scaled * first_normed)) * first_inverse
    back_input_ref[...] = back_input
    back_attention = back_input.astype(bf16)
    back_attention_ref[...] = back_attention
    sums_ref[0:1, :] = jnp.sum(back_attention.astype(f32), axis=0, keepdims=True)
    for r in range(len(outs)):
        back_context_ref[r] = dot_t(back_attention, outs[r][...]).astype(bf16)


def feed_layer(flat, context, outputs, ups, downs, smalls, params, cotangent):
    width, model = flat.shape
    ranks, units = len(ups), ups[0].shape[1]
    channels = outputs[0].shape[0]
    shape = jax.ShapeDtypeStruct
    whole = pl.BlockSpec(memory_space=pltpu.VMEM)
    return pl.pallas_call(
        feed_kernel,
        out_shape=(
            shape((width, model), bf16),
            shape((width, model), f32),
            shape((width, model), bf16),
            shape((ranks, width, channels), bf16),
            shape((width, ranks * units), bf16),
            shape((width, ranks * units), bf16),
            shape((width, model), bf16),
            shape((width, model), bf16),
            shape((6, model), f32),
            shape((1, ranks * units), f32),
        ),
        in_specs=[whole] * (15 + len(smalls) + len(params)),
        out_specs=(whole,) * 10,
        scratch_shapes=[
            pltpu.VMEM((width, ranks * units), f32),
            pltpu.VMEM((width, model), f32),
            pltpu.VMEM((width, model), f32),
        ],
        compiler_params=pltpu.CompilerParams(vmem_limit_bytes=VMEM_LIMIT),
        cost_estimate=cost(19.0),
        name="feed_layer",
    )(flat, context, *outputs, *ups, *downs, *smalls, *params, cotangent)


def per_device(
    tokens,
    query_weight,
    query_bias,
    key_weight,
    value_weight,
    value_bias,
    conv_weight,
    output_weight,
    output_bias,
    first_gain,
    first_shift,
    up_weight,
    up_bias,
    down_weight,
    down_bias,
    second_gain,
    second_shift,
    segment_sizes,
    cotangent,
):
    rows, width, model = tokens.shape
    channels = query_weight.shape[1]
    ranks = lax.axis_size("tp")
    own_heads = channels // HEAD_DIM
    heads = ranks * own_heads
    hidden_units = up_weight.shape[1]
    items = segment_sizes.shape[1]
    marks = segment_sizes.shape[2]
    reach = TAPS // 2
    device = lax.axis_index("seq")
    rank = lax.axis_index("tp")
    group = SPAN // width
    groups = segment_sizes.shape[0] // rows
    place = jnp.stack((rank * groups + device // group, device % group)).astype(jnp.int32)

    half = ((2, width, channels), bf16)
    full = ((ranks, width, channels), bf16)
    full32 = ((ranks, width, channels), f32)
    edge = ((reach, model), bf16)
    marked = ((marks, model), f32)
    message = ((marks, model), bf16)
    tall = ((marks, LANES), f32)
    squares = ((heads // 2, marks, LANES), f32)
    half_sweeps = SWEEPS // 2
    saved = ((half_sweeps, 4, heads // 2, marks, LANES), f32)

    turned = [w.T for w in (query_weight, key_weight, value_weight)]
    (query_own,) = call(small_kernel, (((channels + SMALL_ROWS, model), bf16),), "small")(
        turned[0], query_bias, value_bias, conv_weight, conv_weight[:, ::-1], up_bias
    )
    key_far, key_core = swap(turned[1], "tp", 2), swap(turned[1], "tp", 1)
    query_far, query_core = swap(query_own, "tp", 2), swap(query_own, "tp", 1)
    query_blocks, key_blocks = [query_own, query_core], [turned[1], key_core]
    member, member_turned, count, flags = call(
        layout_kernel,
        (((width, marks), bf16), ((marks, width), bf16), tall, ((16, LANES), f32)),
        "layout",
        scalars=1,
    )(place, segment_sizes)
    flat = lax.dynamic_index_in_dim(tokens, rank, axis=0, keepdims=False)
    upstream = lax.dynamic_index_in_dim(cotangent, rank, axis=0, keepdims=False)

    def shards(own, far):
        return (own, swap(own, "tp", 1), far, swap(far, "tp", 1))

    query, keys, sums, first_step = [], [], [], flags
    for pair in range(2):
        q, k, part, sent = call(
            query_key_kernel, (half, half, marked, message), "query_key", us=2.5,
        )(
            after(flat, first_step),
            query_blocks[2 * pair],
            key_blocks[2 * pair],
            query_blocks[2 * pair + 1],
            key_blocks[2 * pair + 1],
            member_turned,
        )
        query.append(q)
        keys.append(k)
        if pair == 0:
            land = Exchange(plain_parts(), "land", flags, part, sent).first()
            first_step = land.own
            query_far, key_far = after(query_far, first_step), after(key_far, first_step)
            query_blocks += [query_far, swap(query_far, "tp", 1)]
            key_blocks += [key_far, swap(key_far, "tp", 1)]
            value_far = swap(after(turned[2], query_far, key_far), "tp", 2)
            output_far = swap(after(output_weight, query_far, key_far), "tp", 2)
        else:
            land = Exchange(plain_parts(), "land", flags, part, sent).first()
            first_step = land.own
        sums += [land.next().own, land.got()]
    smalls = query_blocks
    up_far = swap(after(up_weight, value_far, output_far, land.own), "tp", 2)
    value_blocks = shards(turned[2], value_far)
    output_blocks = shards(output_weight, output_far)
    up_blocks = shards(up_weight, up_far)
    land_query, land_key, kernel = call(land_kernel, (message, message, squares), "land")(
        flags, count, *sums
    )
    values, value_head, value_tail = call(
        value_kernel, (full, edge, edge), "values", us=2.0
    )(after(flat, output_far), *value_blocks, *smalls)

    def neighbours(head, tail):
        count = lax.axis_size("seq")
        before = lax.ppermute(tail, "seq", [(i, i + 1) for i in range(count - 1)])
        behind = lax.ppermute(head, "seq", [(i + 1, i) for i in range(count - 1)])
        return before, behind

    value_before, value_after = neighbours(value_head, value_tail)
    state, sent = call(
        key_kernel,
        (((marks, model + LANES), f32), ((marks, model + LANES), bf16)),
        "key_softmax",
        us=1.4,
    )(*keys, values, land_query)
    inverse, saved_first = call(newton_first_kernel, (squares, saved), "newton_first", us=2.5)(
        after(kernel, sent)
    )
    soft = Exchange(soft_parts(heads), "soft", flags, state, sent).first(inverse)
    down_far = swap(after(down_weight, up_far, soft.own), "tp", 2)
    inverse, saved_last = call(newton_next_kernel, (squares, saved), "newton_next", us=2.3)(
        kernel, after(inverse, soft.own)
    )
    state, state_got = soft.next().own, soft.got()
    (token_weights,) = call(
        token_kernel, (((ranks, own_heads * marks, width), f32),), "token_softmax", us=0.8,
    )(*query, land_key)
    down_core = swap(after(down_weight, sent), "tp", 1)
    context, mixed, mixed_low, stats = call(
        context_kernel, (full, marked, message, tall), "context", us=2.0,
    )(
        after(state, *output_blocks, *up_blocks, down_core), state_got, inverse, token_weights, values, value_before, value_after, flags,
        *smalls,
    )

    down_blocks = (down_weight, down_core, down_far, swap(after(down_far, context), "tp", 1))
    params = (output_bias, first_gain, first_shift, down_bias, second_gain, second_shift)
    (
        layer_out,
        back_input,
        back_attention,
        back_context,
        active,
        back_hidden,
        first_low,
        back_feed,
        norm_sums,
        up_sums,
    ) = feed_layer(
        flat, context, output_blocks, up_blocks, down_blocks, smalls, params, upstream
    )

    layer_far = swap(layer_out, "tp", 2)
    positions = lax.axis_size("seq")
    levels = list(range(positions.bit_length() - 1))
    bits = jnp.stack([(device >> level) & 1 for level in levels]).astype(jnp.int32)
    wide_tiles = (((2 * positions, model // positions, hidden_units), bf16),) * 2
    weight_gradient = call(
        weight_gradient_kernel, wide_tiles, "weight_gradient",
        scratch=(pltpu.VMEM((model, width), bf16),), us=4.5,
    )
    part_back, sent_back, part_key, sent_key, query_direct, back_head, back_tail = call(
        token_back_kernel, (marked, message, marked, message, full32, edge, edge), "token_back",
        us=1.8,
    )(back_context, token_weights, mixed_low, *query, land_key)
    turn = levels[:1] + ["far"] + levels[1:]
    up = Scatter("up", *weight_gradient(after(first_low, sent_back), back_hidden), bits, turn)
    back = Exchange(plain_parts(), "back", flags, part_back, sent_back).first(up.send)
    down = Scatter(
        "down", *weight_gradient(after(back_feed, back.own), active), bits, ["far"] + levels
    )
    key_side = Exchange(plain_parts(), "back_key", flags, part_key, sent_key).first()
    back_before, back_after = neighbours(*[after(x, back.own) for x in (back_head, back_tail)])
    back.next(down.send, key_side.own, *up.hop(), back_before, back_after)
    up.wait_for(back_before, back_after)
    back_inverse, back_mixed = call(seed_kernel, (squares, message), "seed")(
        flags, after(back.own, *down.hop()), back.got(), inverse, mixed
    )
    up.wait_for(key_side.own)
    part_query, sent_query, key_direct, values_direct = call(
        key_back_kernel, (marked, message, full32, full32), "key_back", us=2.4
    )(*keys, values, land_query, stats, mixed, back_mixed)
    newton_back = call(newton_back_kernel, (squares, squares), "newton_back", us=6.6)
    back_middle = newton_back(
        kernel, saved_last, after(back_inverse, sent_query), jnp.zeros(*squares)
    )
    query_side = Exchange(plain_parts(), "back_query", flags, part_query, sent_query)
    down.wait_for(layer_far)
    first_step = query_side.first(*back_middle, *up.hop(), layer_far).own
    back_values, value_bias_sums, tap_rows = call(
        conv_back_kernel, (full, ((ranks, channels), f32), ((heads, 2 * LANES), f32)), "conv_back",
        us=3.0,
    )(
        back_context, back_before, back_after, values, value_before, value_after, flags,
        values_direct, *smalls,
    )
    query_side.next(back_values)
    tiles = (((2 * positions, model // positions, 2 * channels), bf16),) * 2
    value_output = call(value_output_kernel, tiles, "value_output", us=2.0)(
        flat, after(back_values, query_side.own), back_attention, context
    )
    value_output = Scatter("value_output", *value_output, bits, ["far"] + levels)
    back_start, back_kernel = newton_back(
        kernel, saved_first, after(back_middle[0], query_side.own), back_middle[1]
    )
    query_more, key_more = call(land_back_kernel, (marked, marked), "land_back")(
        kernel, back_start, back_kernel, land_query, land_key
    )
    key_side.message = after(key_side.message, query_side.own)
    key_side.next()
    ready = value_output.hop(query_side.own)
    up.wait_for(*ready)
    ready = [*ready, *down.hop(query_more)]
    bundle_rows = 4 * ranks + norm_sums.shape[0]
    (bundle,) = call(
        bundle_kernel, (((bundle_rows + -bundle_rows % 8, model), f32),), "bundle", scalars=1
    )(rank.reshape(1).astype(jnp.int32), up_sums, value_bias_sums, tap_rows, norm_sums)
    rows_here = model // positions
    bias_rows = rows_here + -rows_here % 16
    taller = (((2 * positions, bias_rows + 16, 2 * channels), bf16),) * 2
    grad_row, *projection = call(
        input_back_kernel,
        (((width, model), bf16),) + taller,
        "input_back",
        scratch=(
            pltpu.VMEM((model, width), bf16),
            pltpu.VMEM((width, 2 * model), bf16),
            pltpu.VMEM((2 * model, model), bf16),
        ),
        us=5.0,
        limit=24 << 20,
    )(
        flags, count, flat, query_direct, key_direct, back_values,
        after(query_side.own, *ready), query_side.got(), query_more,
        key_side.own, key_side.got(), key_more, member, back_input, *query_blocks, *key_blocks,
        *value_blocks,
    )
    projection = Scatter("projection", *projection, bits, turn)
    layer_blocks = shards(layer_out, layer_far)
    step = projection.hop()
    down.wait_for(*step)
    step = value_output.hop(*step)
    grad_far = swap(after(grad_row, *step), "tp", 2)
    step = projection.hop(*step)
    bundle = bundle + swap(after(bundle, *step), "tp", 1)
    step = up.hop(*step)
    step = down.hop(*step, other=value_output)
    bundle = bundle + swap(after(bundle, *step), "seq", 1)
    layer_rows = place_rows(rank, (after(layer_blocks[0], *step),) + layer_blocks[1:], bf16)
    step = projection.hop(*step, layer_rows, bundle)
    step = up.hop(*step)
    step = projection.hop(*step)
    bundle = bundle + swap(after(bundle, *step), "tp", 2)
    step = down.hop(*step)
    grad_blocks = shards(grad_row, grad_far)
    grad_tokens = place_rows(rank, (after(grad_blocks[0], *step),) + grad_blocks[1:], f32)
    size = 2
    while size < positions:
        bundle = bundle + swap(after(bundle, *step), "seq", size)
        size *= 2
    step = up.hop(*step)
    for scatter in (projection, up, down):
        while scatter.hops:
            scatter.hop()
        if scatter.keep.dtype == bf16:
            scatter.hop()
    grad_up_weight = up.keep[0]
    grad_down_weight = down.keep[0][:, :hidden_units]
    grad_output_weight = down.keep[0][:, hidden_units : hidden_units + channels].T
    grad_value_weight = down.keep[0][:, hidden_units + channels :]
    projection = projection.keep[0]
    share = HEAD_DIM // positions
    grad_query_bias = lax.dynamic_slice_in_dim(
        projection[rows_here, :channels].reshape(own_heads, HEAD_DIM), device * share, share, axis=1
    )
    own = lax.dynamic_slice_in_dim(bundle, 4 * rank, 4, axis=0)
    grad_up_bias = own[0]
    grad_value_bias = own[1, :channels].reshape(own_heads, HEAD_DIM)
    grad_conv_weight = own[2].reshape(own_heads, 2 * LANES)[:, STRIPE - 1 : STRIPE - 1 + TAPS]
    shared = [bundle[4 * ranks + k] for k in range(6)]
    return (
        layer_rows,
        grad_tokens,
        projection[:rows_here, :channels],
        grad_query_bias,
        projection[:rows_here, channels:],
        grad_value_weight,
        grad_value_bias,
        grad_conv_weight,
        grad_output_weight,
        shared[0],
        shared[1],
        shared[2],
        grad_up_weight,
        grad_up_bias,
        grad_down_weight.T,
        shared[3],
        shared[4],
        shared[5],
    )


def solution(mesh):
    placed = (
        P(None, "seq", None),
        P(None, "tp"),
        P("tp", None),
        P(None, "tp"),
        P(None, "tp"),
        P("tp", None),
        P("tp", None),
        P("tp", None),
        P(),
        P(),
        P(),
        P(None, "tp"),
        P("tp"),
        P("tp", None),
        P(),
        P(),
        P(),
        P(),
        P(None, "seq", None),
    )
    return jax.shard_map(
        per_device,
        mesh=mesh,
        in_specs=placed,
        out_specs=(
            P(None, "seq", None),
            P(None, "seq", None),
            P("seq", "tp"),
            P("tp", "seq"),
            P("seq", "tp"),
            P("seq", "tp"),
            P("tp", None),
            P("tp", None),
            P("tp", "seq"),
            P(),
            P(),
            P(),
            P("seq", "tp"),
            P("tp"),
            P("tp", "seq"),
            P(),
            P(),
            P(),
        ),
        check_vma=False,
    )
```

```python
import functools

import jax
import jax.numpy as jnp
from jax import lax
from jax.experimental import pallas as pl
from jax.experimental.pallas import tpu as pltpu
from jax.sharding import PartitionSpec as P

HEAD_DIM = 64
TAPS = 33
SWEEPS = 6
SPAN = 4096
LANES = 128
STRIPE = 128
SMALL_ROWS = 16
VMEM_LIMIT = 28 << 20


epsilon = 1e-05
very_negative = -1e30
f32 = jnp.float32
bf16 = jnp.bfloat16


def swap(value, axis, step):
    return lax.ppermute(value, axis, [(i, i ^ step) for i in range(lax.axis_size(axis))])


def dot(a, b):
    return jnp.dot(a, b, preferred_element_type=f32)


def outer(a, b):
    return lax.dot_general(a, b, (((0,), (0,)), ((), ())), preferred_element_type=f32)


def dot_t(a, b):
    return lax.dot_general(a, b, (((1,), (1,)), ((), ())), preferred_element_type=f32)


def after(value, *others):
    return lax.optimization_barrier((value,) + others)[0]


class Scatter:
    def __init__(self, name, mine, theirs, bits, hops):
        self.name, self.bits, self.hops = name, bits, list(hops)
        self.keep, self.send, self.way = mine, theirs, ("tp", 1)
        self.left = sorted(level for level in hops if level != "far")

    def hop(self, *waits, other=None):
        operands = [after(self.keep, *waits), swap(self.send, *self.way)]
        tiles, rows, columns = self.keep.shape
        if other is not None:
            operands += [other.keep, swap(other.send, *other.way)]
            columns += other.keep.shape[2]
        if not self.hops:
            kernel, outs = last_tile_kernel, (((tiles, rows, columns), f32),)
        else:
            following = self.hops.pop(0)
            far = following == "far"
            self.way = ("tp", 2) if far else ("seq", 1 << following)
            place = None if far else self.left.index(following)
            kernel = functools.partial(route_kernel, following, place)
            if not far:
                self.left.remove(following)
            outs = (((tiles // 2, rows, columns), bf16),) * 2
        size = tiles * rows * columns * 2
        result = call(
            kernel, outs, self.name + "_route", scalars=1, us=0.5 + size / 1.2e6, limit=16 << 20
        )(self.bits, *operands)
        self.keep = result[0]
        self.send = result[-1]
        return result

    def wait_for(self, *others):
        self.send = after(self.send, *others)


def sum_merge(a, b, use):
    return a + jnp.where(use, b, 0.0)


def flag(flags_ref, row):
    return flags_ref[row : row + 1, 0:1] > 0.5


def plain_parts():
    return sum_merge, lambda value: value.astype(bf16), lambda message: message.astype(f32)


def soft_parts(heads):
    return (
        functools.partial(merge_states, heads=heads),
        functools.partial(state_message, heads=heads),
        functools.partial(message_state, heads=heads),
    )


def edges_after(parts, flags_ref, level, facing, outer_edge, got, got_outer):
    merge = parts[0]
    near = merge(outer_edge, got, flag(flags_ref, 4 * level + 1))
    away = merge(got_outer, facing, flag(flags_ref, 4 * level + 2))
    turn = flag(flags_ref, 4 * level + 3)
    return jnp.where(turn, near, away), jnp.where(turn, away, near)


def merge_first_kernel(parts, flags_ref, own_ref, got_ref, new_ref, message_ref):
    merge, encode, decode = parts
    own, got = own_ref[...], decode(got_ref[...])
    new_ref[...] = merge(own, got, flag(flags_ref, 0))
    facing, outer_edge = edges_after(parts, flags_ref, 0, own, own, got, got)
    message_ref[...] = jnp.concatenate((encode(facing), encode(outer_edge)), axis=0)


def merge_next_kernel(parts, flags_ref, own_ref, sent_ref, got_ref, new_ref, message_ref):
    merge, encode, decode = parts
    marks = own_ref.shape[0]
    got, got_outer = decode(got_ref[:marks]), decode(got_ref[marks:])
    new_ref[...] = merge(own_ref[...], got, flag(flags_ref, 4))
    facing, _ = edges_after(
        parts, flags_ref, 1, decode(sent_ref[:marks]), decode(sent_ref[marks:]), got, got_outer
    )
    message_ref[...] = encode(facing)


class Exchange:
    def __init__(self, parts, name, flags, own, message):
        self.parts, self.name, self.flags = parts, name, flags
        self.own, self.message = own, message

    def run(self, kernel, name, rows, *operands):
        marks, width = self.own.shape
        self.own, self.message = call(
            functools.partial(kernel, self.parts),
            (((marks, width), f32), ((rows, width), bf16)),
            self.name + name,
        )(self.flags, *operands)

    def first(self, *waits):
        got = swap(self.message, "seq", 1)
        self.run(merge_first_kernel, "_first", 2 * got.shape[0], after(self.own, *waits), got)
        return self

    def next(self, *waits):
        sent = self.message
        got = swap(sent, "seq", 2)
        self.run(merge_next_kernel, "_next", got.shape[0] // 2, after(self.own, *waits), sent, got)
        return self

    def got(self):
        return swap(self.message, "seq", 4)


WHOLE = pl.BlockSpec(memory_space=pltpu.VMEM)


def cost(us):
    return pl.CostEstimate(flops=0, bytes_accessed=int(us * 3.3e6), transcendentals=0)


def call(kernel, outs, name, scratch=(), limit=12 << 20, us=1.0, scalars=0):
    outs = tuple(jax.ShapeDtypeStruct(shape, dtype) for shape, dtype in outs)

    def run(*operands):
        return pl.pallas_call(
            kernel,
            out_shape=outs,
            in_specs=[pl.BlockSpec(memory_space=pltpu.SMEM)] * scalars
            + [WHOLE] * (len(operands) - scalars),
            out_specs=(WHOLE,) * len(outs),
            scratch_shapes=list(scratch),
            compiler_params=pltpu.CompilerParams(vmem_limit_bytes=limit),
            cost_estimate=cost(us),
            name=name,
        )(*operands)

    return run


def lane_ids(shape):
    return lax.broadcasted_iota(jnp.int32, shape, len(shape) - 1)


def row_ids(shape):
    return lax.broadcasted_iota(jnp.int32, shape, len(shape) - 2)


def spread_heads(block):
    heads = block.shape[1] // HEAD_DIM
    tall = jnp.concatenate([block] * heads, axis=0)
    same = row_ids(tall.shape) // HEAD_DIM == lane_ids(tall.shape) // HEAD_DIM
    return jnp.where(same, tall, jnp.zeros_like(tall))


def gather_heads(square):
    heads = square.shape[1] // HEAD_DIM
    result = jnp.zeros((HEAD_DIM, square.shape[1]), square.dtype)
    lane = lane_ids(result.shape) // HEAD_DIM
    for j in range(heads):
        result = jnp.where(lane == j, square[j * HEAD_DIM : (j + 1) * HEAD_DIM], result)
    return result


def two_parts(value):
    high = value.astype(bf16)
    return high, (value - high.astype(f32)).astype(bf16)


def first_half(shape):
    return lane_ids(shape) < HEAD_DIM


def pair_spread(pair):
    near = first_half(pair.shape)
    zero = jnp.zeros_like(pair)
    return jnp.concatenate((jnp.where(near, pair, zero), jnp.where(near, zero, pair)), axis=0)


def pair_gather(square):
    top, bottom = square[:HEAD_DIM], square[HEAD_DIM:]
    return jnp.where(first_half(top.shape), top, bottom)


def fine(product, a, b, turn=lambda value: value):
    a_high, a_low = two_parts(a)
    b_high, b_low = [turn(part) for part in two_parts(b)]
    return product(a_high, b_high) + (product(a_high, b_low) + product(a_low, b_high))


def pair_mul(a, b):
    return fine(dot, a, b, pair_spread)


def pair_mul_t(a, b):
    return fine(dot_t, a, b, pair_spread)


def pair_t_mul(a, b):
    return pair_gather(fine(outer, a, b))


def pair_sums(value, reduce=jnp.sum, neutral=0.0):
    near = first_half(value.shape)
    left = reduce(jnp.where(near, value, neutral), axis=1, keepdims=True)
    right = reduce(jnp.where(near, neutral, value), axis=1, keepdims=True)
    return jnp.where(near, left, right)


def pair_of(array, pair):
    return array[:, pair * LANES : (pair + 1) * LANES]


def pair_turned(value):
    tall = value.T
    return jnp.concatenate((tall[:HEAD_DIM], tall[HEAD_DIM:]), axis=1)


def start_bound(kernel):
    column_sums = jnp.sum(kernel, axis=0, keepdims=True)
    return column_sums, jnp.sqrt(pair_sums(column_sums * column_sums))


def pair_identity():
    shape = (HEAD_DIM, LANES)
    return jnp.where(row_ids(shape) == lane_ids(shape) % HEAD_DIM, 1.0, 0.0)


def newton_first_kernel(kernel_ref, inverse_ref, saved_ref):
    inverses = []
    for p in range(kernel_ref.shape[0]):
        kernel = kernel_ref[p]
        inverses.append(pair_turned(kernel) / start_bound(kernel)[1])
    newton_sweeps(kernel_ref, inverses, inverse_ref, saved_ref)


def newton_next_kernel(kernel_ref, last_ref, inverse_ref, saved_ref):
    inverses = [last_ref[p] for p in range(kernel_ref.shape[0])]
    newton_sweeps(kernel_ref, inverses, inverse_ref, saved_ref)


def newton_sweeps(kernel_ref, inverses, inverse_ref, saved_ref):
    pairs = range(kernel_ref.shape[0])
    identity = pair_identity()
    for sweep in range(saved_ref.shape[0]):
        products = [pair_mul(kernel_ref[p], inverses[p]) for p in pairs]
        inner = [15.0 * identity - pair_mul(products[p], 7.0 * identity - products[p]) for p in pairs]
        last = [13.0 * identity - pair_mul(products[p], inner[p]) for p in pairs]
        for p in pairs:
            saved_ref[sweep, 0, p] = inverses[p]
            saved_ref[sweep, 1, p] = products[p]
            saved_ref[sweep, 2, p] = inner[p]
            saved_ref[sweep, 3, p] = last[p]
        inverses = [0.25 * pair_mul(inverses[p], last[p]) for p in pairs]
    for p in pairs:
        inverse_ref[p] = inverses[p]


def newton_back_kernel(kernel_ref, saved_ref, inverse_in, kernel_in, inverse_out, kernel_out):
    pairs = range(kernel_ref.shape[0])
    identity = pair_identity()
    back = [inverse_in[p] for p in pairs]
    total = [kernel_in[p] for p in pairs]
    for sweep in reversed(range(saved_ref.shape[0])):
        inverse = [saved_ref[sweep, 0, p] for p in pairs]
        product = [saved_ref[sweep, 1, p] for p in pairs]
        third = [0.25 * pair_t_mul(inverse[p], back[p]) for p in pairs]
        second = [-pair_t_mul(product[p], third[p]) for p in pairs]
        first = [-pair_t_mul(product[p], second[p]) for p in pairs]
        slope = [
            -(
                pair_mul_t(third[p], saved_ref[sweep, 2, p])
                + pair_mul_t(second[p], 7.0 * identity - product[p])
                + first[p]
            )
            for p in pairs
        ]
        back = [
            0.25 * pair_mul_t(back[p], saved_ref[sweep, 3, p])
            + pair_t_mul(kernel_ref[p], slope[p])
            for p in pairs
        ]
        total = [total[p] + pair_mul_t(slope[p], inverse[p]) for p in pairs]
    for p in pairs:
        inverse_out[p] = back[p]
        kernel_out[p] = total[p]


def land_back_kernel(kernel_ref, back_start_ref, back_kernel_ref, land_query_ref, land_key_ref,
                     query_ref, key_ref):
    queries, keys = [], []
    for p in range(kernel_ref.shape[0]):
        kernel, start = kernel_ref[p], pair_turned(back_start_ref[p])
        column_sums, bound = start_bound(kernel)
        both = jnp.sum(start * kernel, axis=0, keepdims=True)
        back_bound = -pair_sums(both) / (bound * bound)
        back = back_kernel_ref[p] + start / bound + back_bound * column_sums / bound
        scores = kernel * (back - pair_sums(kernel * back))
        land_query, land_key = pair_of(land_query_ref[...], p), pair_of(land_key_ref[...], p)
        high, low = two_parts(scores)
        spread = pair_spread(land_key)
        queries.append(dot(high, spread) + dot(low, spread))
        keys.append(pair_gather(outer(high, land_query) + outer(low, land_query)))
    query_ref[...] = jnp.concatenate(queries, axis=1)
    key_ref[...] = jnp.concatenate(keys, axis=1)


def group_of(array, r, channels):
    return array[:, r * channels : (r + 1) * channels]


def layout_kernel(place_ref, sizes_ref, member_ref, turned_ref, count_ref, flags_ref):
    row, local = place_ref[0], place_ref[1]
    sizes = sizes_ref[row].astype(f32)
    items, marks = sizes.shape
    width = turned_ref.shape[1]
    devices = SPAN // width

    def pick(condition, value, axis):
        return jnp.sum(jnp.where(condition, value, 0.0), axis=axis, keepdims=True)

    totals = jnp.sum(sizes, axis=1, keepdims=True)
    small = (items, items)
    totals_row = pick(row_ids(small) == lane_ids(small), jnp.broadcast_to(totals, small), 0)
    ends = pick(lane_ids(small) <= row_ids(small), jnp.broadcast_to(totals_row, small), 1)
    wide = (items, LANES)
    below = jnp.broadcast_to(ends, wide) <= (width * lane_ids(wide)).astype(f32)
    item_of = jnp.sum(jnp.where(below, 1.0, 0.0), axis=0, keepdims=True)

    def item_at(index):
        return pick(lane_ids(item_of.shape) == index, item_of, 1)

    own = item_at(local)
    item_rows = row_ids((items, 1)).astype(f32)
    own_sizes = pick(row_ids(sizes.shape).astype(f32) == own, sizes, 0)
    item_start = pick(item_rows < own, totals, 0)
    square = (marks, marks)
    spread = jnp.broadcast_to(own_sizes, square)
    size_column = pick(row_ids(square) == lane_ids(square), spread, 1)
    end_column = pick(lane_ids(square) <= row_ids(square), spread, 1)
    end_row = pick(row_ids(square) <= lane_ids(square), jnp.broadcast_to(size_column, square), 0)
    first = (local * width).astype(f32) - item_start
    along = lane_ids(turned_ref.shape).astype(f32) + first
    inside = (along >= end_column - size_column) & (along < end_column)
    turned_ref[...] = jnp.where(inside, 1.0, 0.0).astype(bf16)
    down = row_ids(member_ref.shape).astype(f32) + first
    inside = (down >= end_row - own_sizes) & (down < end_row)
    member_ref[...] = jnp.where(inside, 1.0, 0.0).astype(bf16)
    count_ref[...] = jnp.broadcast_to(jnp.maximum(size_column, 1.0), count_ref.shape)

    def put(at, value):
        flags_ref[at : at + 1, :] = jnp.broadcast_to(jnp.where(value, 1.0, 0.0), (1, LANES))

    level, size = 0, 1
    while size < devices:
        start = local - local % size
        is_left = (local // size) % 2 == 0
        other = jnp.where(is_left, start + size, start - size)
        far_facing = item_at(jnp.where(is_left, other, other + size - 1))
        far_outer = item_at(jnp.where(is_left, other + size - 1, other))
        facing = item_at(jnp.where(is_left, start + size - 1, start))
        outer_edge = item_at(jnp.where(is_left, start, start + size - 1))
        next_left = (local // (2 * size)) % 2 == 0
        put(4 * level, own == far_facing)
        put(4 * level + 1, outer_edge == far_facing)
        put(4 * level + 2, far_outer == facing)
        turn = jnp.where(is_left != next_left, 1.0, 0.0)
        flags_ref[4 * level + 3 : 4 * level + 4, :] = jnp.full((1, LANES), turn, f32)
        level, size = level + 1, 2 * size
    before = jnp.where(local > 0, 1.0, 0.0) * jnp.where(item_at(local - 1) == own, 1.0, 0.0)
    behind = jnp.where(local < devices - 1, 1.0, 0.0) * jnp.where(
        item_at(local + 1) == own, 1.0, 0.0
    )
    flags_ref[12:13, :] = jnp.broadcast_to(before, (1, LANES))
    flags_ref[13:14, :] = jnp.broadcast_to(behind, (1, LANES))
    flags_ref[14:16, :] = jnp.zeros((2, LANES), f32)


def query_key_kernel(flat_ref, q0, k0, q1, k1, member_ref, query_ref, keys_ref, part_ref, message_ref):
    channels = query_ref.shape[2]
    scale = HEAD_DIM ** (-0.25)
    parts = []
    for r, (q, k) in enumerate(((q0, k0), (q1, k1))):
        query = dot_t(flat_ref[...], q[:channels]) + small_row(q, 0, channels)
        query = (scale * query).astype(bf16)
        keys = (scale * dot_t(flat_ref[...], k[...])).astype(bf16)
        query_ref[r] = query
        keys_ref[r] = keys
        parts += [dot(member_ref[...], query), dot(member_ref[...], keys)]
    part = jnp.concatenate(parts, axis=1)
    part_ref[...] = part
    message_ref[...] = part.astype(bf16)


def route_kernel(level, place, bits_ref, *refs):
    keep_out, send_out = refs[-2:]
    half = keep_out.shape[0]

    def total(i):
        sums = [
            (refs[k][i].astype(f32) + refs[k + 1][i].astype(f32)).astype(bf16)
            for k in range(0, len(refs) - 2, 2)
        ]
        return jnp.concatenate(sums, axis=1) if len(sums) > 1 else sums[0]

    for i in range(half):
        if place is None:
            keep, send = i, half + i
        else:
            bit = bits_ref[level] << place
            base = ((i >> place) << (place + 1)) + (i & ((1 << place) - 1))
            keep, send = base + bit, base + (1 << place) - bit
        keep_out[i] = total(keep)
        send_out[i] = total(send)


def last_tile_kernel(bits_ref, keep_ref, got_ref, out_ref):
    for i in range(out_ref.shape[0]):
        out_ref[i] = keep_ref[i].astype(f32) + got_ref[i].astype(f32)


def put_tiles(product, r, mine_ref, theirs_ref):
    ref = theirs_ref if r % 2 else mine_ref
    places = ref.shape[0] // 2
    rows = product.shape[0] // places
    first = places if r >= 2 else 0
    for place in range(places):
        ref[first + place, :rows] = product[place * rows : (place + 1) * rows].astype(bf16)


def weight_gradient_kernel(side_ref, units_ref, mine_ref, theirs_ref, turned_ref):
    turned_ref[...] = side_ref[...].T
    columns = mine_ref.shape[2]
    for r in range(units_ref.shape[1] // columns):
        product = dot(turned_ref[...], units_ref[:, r * columns : (r + 1) * columns])
        put_tiles(product, r, mine_ref, theirs_ref)


def small_kernel(weight_ref, query_ref, value_ref, taps_ref, flipped_ref, up_ref, out_ref):
    columns = out_ref.shape[1]

    def row(pieces):
        width = sum(piece.shape[1] for piece in pieces)
        return jnp.concatenate(pieces + [jnp.zeros((1, columns - width), f32)], axis=1)

    heads = range(query_ref.shape[0])
    rows = []
    for ref in (query_ref, value_ref):
        value = ref[...].astype(f32)
        rows.append(row([value[j : j + 1] for j in heads]))
    for ref in (taps_ref, flipped_ref):
        value = ref[...].astype(f32)
        rows += [row([value[j : j + 1]]) for j in heads]
    rows.append(up_ref[...].astype(f32).reshape(1, columns))
    rows.append(jnp.zeros((SMALL_ROWS - len(rows), columns), f32))
    channels = weight_ref.shape[0]
    out_ref[:channels] = weight_ref[...]
    out_ref[channels:] = jnp.concatenate(rows, axis=0).astype(bf16)


def small_row(ref, at, width):
    return ref[ref.shape[0] - SMALL_ROWS :, :width].astype(f32)[at : at + 1]


def bundle_kernel(rank_ref, up_ref, value_ref, taps_ref, norm_ref, out_ref):
    ranks, channels = value_ref.shape
    columns = out_ref.shape[1]
    heads = taps_ref.shape[0] // ranks
    for r in range(ranks):
        at = 4 * (r ^ rank_ref[0])
        value = value_ref[r : r + 1, :]
        rows = (
            up_ref[:, r * columns : (r + 1) * columns],
            jnp.concatenate((value, jnp.zeros((1, columns - channels), f32)), axis=1),
            jnp.concatenate([taps_ref[r * heads + j : r * heads + j + 1] for j in range(heads)], axis=1),
        )
        for k, row in enumerate(rows):
            out_ref[pl.ds(at + k, 1), :] = row
        out_ref[pl.ds(at + 3, 1), :] = jnp.zeros((1, columns), f32)
    norms = norm_ref.shape[0]
    out_ref[4 * ranks : 4 * ranks + norms, :] = norm_ref[...]
    out_ref[4 * ranks + norms :, :] = jnp.zeros((out_ref.shape[0] - 4 * ranks - norms, columns), f32)


def land_kernel(flags_ref, count_ref, own0, got0, own1, got1, query_ref, keys_ref, kernel_ref):
    channels = own0.shape[1] // 4
    count = count_ref[:, 0:1]
    queries, keys = [], []
    for own, got in ((own0, got0), (own1, got1)):
        land = sum_merge(own[...], got[...].astype(f32), flag(flags_ref, 8)) / count
        for r in range(2):
            queries.append(group_of(land, 2 * r, channels).astype(bf16))
            keys.append(group_of(land, 2 * r + 1, channels).astype(bf16))
    land_query, land_key = jnp.concatenate(queries, axis=1), jnp.concatenate(keys, axis=1)
    query_ref[...] = land_query
    keys_ref[...] = land_key
    for p in range(kernel_ref.shape[0]):
        scores = dot_t(pair_of(land_query, p), pair_spread(pair_of(land_key, p)))
        powers = jnp.exp(scores - pair_sums(scores, jnp.max, very_negative))
        kernel_ref[p] = powers / pair_sums(powers)


def value_kernel(flat_ref, w0, w1, w2, w3, s0, s1, s2, s3, values_ref, head_ref, tail_ref):
    reach = head_ref.shape[0]
    heads, tails = [], []
    channels = values_ref.shape[2]
    for r, (w, small) in enumerate(((w0, s0), (w1, s1), (w2, s2), (w3, s3))):
        values = (dot_t(flat_ref[...], w[...]) + small_row(small, 1, channels)).astype(bf16)
        values_ref[r] = values
        heads.append(values[:reach])
        tails.append(values[values.shape[0] - reach :])
    head_ref[...] = jnp.concatenate(heads, axis=1)
    tail_ref[...] = jnp.concatenate(tails, axis=1)


def key_kernel(k0, k1, values_ref, land_query_ref, state_ref, message_ref):
    channels = values_ref.shape[2]
    heads = channels // HEAD_DIM
    mixed = []
    marks = land_query_ref.shape[0]
    stats = jnp.zeros((marks, LANES), f32)
    lane = lane_ids(stats.shape)
    groups = values_ref.shape[0]
    for r in range(groups):
        keys = (k0, k1)[r // 2][r % 2]
        scores = dot_t(spread_heads(group_of(land_query_ref[...], r, channels)), keys)
        top = jnp.max(scores, axis=1, keepdims=True).astype(bf16).astype(f32)
        powers = jnp.exp(scores - top)
        total = jnp.sum(powers, axis=1, keepdims=True)
        mixed.append(gather_heads(dot(powers.astype(bf16), values_ref[r])))
        for j in range(heads):
            h = r * heads + j
            at = slice(j * marks, (j + 1) * marks)
            stats = jnp.where(lane == h, top[at], stats)
            stats = jnp.where(lane == groups * heads + h, total[at], stats)
    state = jnp.concatenate(mixed + [stats], axis=1)
    state_ref[...] = state
    message_ref[...] = state_message(state, groups * heads)


def state_message(state, heads):
    width = state.shape[1] - LANES
    stats = state[:, width:]
    lane = lane_ids(stats.shape)
    high = stats.astype(bf16).astype(f32)
    low = pltpu.roll(stats - high, heads, 1)
    last = jnp.where(lane < 2 * heads, high, jnp.where(lane < 3 * heads, low, 0.0))
    return jnp.concatenate((state[:, :width], last), axis=1).astype(bf16)


def message_state(message, heads):
    message = message.astype(f32)
    width = message.shape[1] - LANES
    stats = message[:, width:]
    lane = lane_ids(stats.shape)
    low = pltpu.roll(stats, LANES - heads, 1)
    stats = stats + jnp.where((lane >= heads) & (lane < 2 * heads), low, 0.0)
    stats = jnp.where(lane < 2 * heads, stats, 0.0)
    return jnp.concatenate((message[:, :width], stats), axis=1)


def widen(stats, first, width):
    pieces = []
    rows = stats.shape[0]
    for pair in range(width // LANES):
        lane = lane_ids((rows, LANES))
        at = first + 2 * pair
        pieces.append(
            jnp.where(lane < HEAD_DIM, stats[:, at : at + 1], stats[:, at + 1 : at + 2])
        )
    return jnp.concatenate(pieces, axis=1)


def merge_states(a, b, use, heads):
    width = a.shape[1] - LANES
    stats_a, stats_b = a[:, width:], b[:, width:]
    lane = lane_ids(stats_a.shape)
    top = jnp.where(use, jnp.maximum(stats_a, stats_b), stats_a)
    is_top = lane < heads
    scale_a = jnp.exp(jnp.where(is_top, stats_a - top, 0.0))
    scale_b = jnp.where(use, jnp.exp(jnp.where(is_top & use, stats_b - top, 0.0)), 0.0)
    values = a[:, :width] * widen(scale_a, 0, width) + b[:, :width] * widen(scale_b, 0, width)
    total = stats_a * pltpu.roll(scale_a, heads, 1) + stats_b * pltpu.roll(scale_b, heads, 1)
    stats = jnp.where(is_top, top, jnp.where(lane < 2 * heads, total, 0.0))
    return jnp.concatenate((values, stats), axis=1)


def token_kernel(q0, q1, land_key_ref, weights_ref):
    groups, rows, width = weights_ref.shape
    channels = q0.shape[2]
    heads = channels // HEAD_DIM
    for r in range(groups):
        query = (q0, q1)[r // 2][r % 2]
        scores = dot_t(spread_heads(group_of(land_key_ref[...], r, channels)), query)
        scores = scores.reshape(heads, rows // heads, width)
        powers = jnp.exp(scores - jnp.max(scores, axis=1, keepdims=True))
        weights = powers / jnp.sum(powers, axis=1, keepdims=True)
        weights_ref[r] = weights.reshape(rows, width)


def toeplitz(taps_row, rows, width):
    wide = jnp.broadcast_to(taps_row, (rows, taps_row.shape[1]))
    return pltpu.roll(wide, 0, 1, stride=1, stride_axis=0)[:, :width]


def with_rim(cells, before, after, flags_ref):
    return jnp.concatenate(
        (
            jnp.where(flag(flags_ref, 12), before, jnp.zeros_like(before)),
            cells,
            jnp.where(flag(flags_ref, 13), after, jnp.zeros_like(after)),
        ),
        axis=0,
    )


def convolve(rim, filters):
    tall = jnp.concatenate(filters, axis=0)
    span = tall.shape[1]
    pieces = []
    for start in range(0, rim.shape[0] - (span - STRIPE), STRIPE):
        product = dot(tall, rim[start : start + span])
        lane = lane_ids((STRIPE, rim.shape[1])) // HEAD_DIM
        piece = product[:STRIPE]
        for j in range(1, len(filters)):
            piece = jnp.where(lane == j, product[j * STRIPE : (j + 1) * STRIPE], piece)
        pieces.append(piece)
    return jnp.concatenate(pieces, axis=0)


def context_kernel(own_ref, got_ref, inverse_ref, weights_ref, values_ref, before_ref, after_ref,
                   flags_ref, s0, s1, s2, s3, context_ref, mixed_ref, low_ref, stats_ref):
    groups, width, channels = values_ref.shape
    heads = channels // HEAD_DIM
    reach = before_ref.shape[0]
    merge, _, decode = soft_parts(groups * heads)
    state = merge(own_ref[...], decode(got_ref[...]), flag(flags_ref, 8))
    model = groups * channels
    stats_ref[...] = state[:, model:]
    mixed = state[:, :model] / widen(state[:, model:], groups * heads, model)
    mixed_ref[...] = mixed
    low = jnp.concatenate(
        [
            pair_mul(inverse_ref[p], pair_of(mixed, p)).astype(bf16)
            for p in range(inverse_ref.shape[0])
        ],
        axis=1,
    )
    low_ref[...] = low
    for r in range(groups):
        nystrom = outer(
            weights_ref[r].astype(bf16), spread_heads(group_of(low, r, channels))
        )
        rim = with_rim(
            values_ref[r],
            group_of(before_ref[...], r, channels),
            group_of(after_ref[...], r, channels),
            flags_ref,
        )
        filters = [
            toeplitz(
                small_row((s0, s1, s2, s3)[r], 2 + j, 2 * LANES), STRIPE, STRIPE + 2 * reach
            ).astype(bf16)
            for j in range(heads)
        ]
        context_ref[r] = (nystrom + convolve(rim, filters)).astype(bf16)


def token_back_kernel(back_ref, weights_ref, low_ref, q0, q1, land_key_ref, part_ref,
                      message_ref, part_key_ref, message_key_ref, direct_ref, head_ref, tail_ref):
    groups, width, channels = back_ref.shape
    heads = channels // HEAD_DIM
    reach = head_ref.shape[0]
    parts, key_parts = [], []
    for r in range(groups):
        back = back_ref[r]
        query = (q0, q1)[r // 2][r % 2]
        weights = weights_ref[r]
        parts.append(gather_heads(dot(weights.astype(bf16), back)))
        slope = dot_t(spread_heads(group_of(low_ref[...], r, channels)), back)
        product = (weights * slope).reshape(heads, -1, width)
        rows = jnp.sum(product, axis=1, keepdims=True)
        rows = jnp.broadcast_to(rows, product.shape).reshape(weights.shape)
        scores = (weights * (slope - rows)).astype(bf16)
        key_parts.append(gather_heads(dot(scores, query)))
        direct_ref[r] = outer(scores, spread_heads(group_of(land_key_ref[...], r, channels)))
    for pieces, whole_ref, low in ((parts, part_ref, message_ref), (key_parts, part_key_ref, message_key_ref)):
        whole = jnp.concatenate(pieces, axis=1)
        whole_ref[...] = whole
        low[...] = whole.astype(bf16)
    head_ref[...] = jnp.concatenate([back_ref[r, :reach] for r in range(groups)], axis=1)
    tail_ref[...] = jnp.concatenate([back_ref[r, width - reach :] for r in range(groups)], axis=1)


def conv_back_kernel(back_ref, before_ref, after_ref, values_ref, vbefore_ref, vafter_ref, flags_ref,
                     direct_ref, s0, s1, s2, s3, back_values_ref, bias_ref, taps_ref):
    groups, width, channels = back_ref.shape
    heads = channels // HEAD_DIM
    reach = before_ref.shape[0]
    span = STRIPE + 2 * reach
    order = row_ids((STRIPE, STRIPE)) + lane_ids((STRIPE, STRIPE)) == STRIPE - 1
    order = jnp.where(order, 1.0, 0.0).astype(bf16)
    lane = lane_ids((STRIPE, channels)) // HEAD_DIM
    for r in range(groups):
        rim = with_rim(
            back_ref[r],
            group_of(before_ref[...], r, channels),
            group_of(after_ref[...], r, channels),
            flags_ref,
        )
        filters = [
            toeplitz(
                small_row((s0, s1, s2, s3)[r], 2 + heads + j, 2 * LANES), STRIPE, span
            ).astype(bf16)
            for j in range(heads)
        ]
        back_values = (direct_ref[r] + convolve(rim, filters)).astype(bf16)
        back_values_ref[r] = back_values
        bias_ref[r : r + 1, :] = jnp.sum(back_values.astype(f32), axis=0, keepdims=True)
        value_rim = with_rim(
            values_ref[r],
            group_of(vbefore_ref[...], r, channels),
            group_of(vafter_ref[...], r, channels),
            flags_ref,
        )
        total = jnp.zeros((heads * STRIPE, span), f32)
        for start in range(0, width, STRIPE):
            turned = dot(order, back_ref[r, start : start + STRIPE])
            tall = [jnp.where(lane == j, turned, 0.0).astype(bf16) for j in range(heads)]
            total = total + dot_t(jnp.concatenate(tall, axis=0), value_rim[start : start + span])
        total = jnp.concatenate(
            (total, jnp.zeros((heads * STRIPE, 2 * LANES - span), f32)), axis=1
        )
        for j in range(heads):
            skewed = pltpu.roll(
                total[j * STRIPE : (j + 1) * STRIPE], 0, 1, stride=1, stride_axis=0
            )
            h = r * heads + j
            taps_ref[h : h + 1, :] = jnp.sum(skewed, axis=0, keepdims=True)


def seed_kernel(flags_ref, own_ref, got_ref, inverse_ref, mixed_ref, back_inverse_ref, back_mixed_ref):
    back = sum_merge(own_ref[...], got_ref[...].astype(f32), flag(flags_ref, 8))
    pairs = []
    for p in range(inverse_ref.shape[0]):
        near = pair_of(back, p)
        back_inverse_ref[p] = pair_mul_t(near, pair_of(mixed_ref[...], p))
        pairs.append(pair_t_mul(inverse_ref[p], near))
    back_mixed_ref[...] = jnp.concatenate(pairs, axis=1).astype(bf16)


def key_back_kernel(k0, k1, values_ref, land_query_ref, state_ref, mixed_ref, back_mixed_ref,
                    part_ref, message_ref, direct_ref, values_direct_ref):
    groups, width, channels = values_ref.shape
    heads = channels // HEAD_DIM
    stats = state_ref[...]
    parts = []
    for r in range(groups):
        keys = (k0, k1)[r // 2][r % 2]
        land = spread_heads(group_of(land_query_ref[...], r, channels))
        scores = dot_t(land, keys)
        first = r * heads
        tops = jnp.concatenate([stats[:, first + j : first + j + 1] for j in range(heads)], axis=0)
        first += groups * heads
        totals = jnp.concatenate(
            [stats[:, first + j : first + j + 1] for j in range(heads)], axis=0
        )
        weights = jnp.exp(scores - tops) * (1.0 / totals)
        back_mixed = group_of(back_mixed_ref[...], r, channels)
        spread = spread_heads(back_mixed)
        dots = jnp.sum(
            spread_heads(group_of(mixed_ref[...], r, channels)) * spread.astype(f32),
            axis=1,
            keepdims=True,
        )
        slope = dot_t(spread, values_ref[r])
        back_scores = (weights * (slope - dots)).astype(bf16)
        parts.append(gather_heads(dot(back_scores, keys)))
        direct_ref[r] = outer(back_scores, land)
        values_direct_ref[r] = outer(weights.astype(bf16), spread)
    part = jnp.concatenate(parts, axis=1)
    part_ref[...] = part
    message_ref[...] = part.astype(bf16)


def input_back_kernel(flags_ref, count_ref, flat_ref, query_direct_ref, key_direct_ref, back_values_ref,
                      query_own_ref, query_got_ref, query_more_ref, key_own_ref, key_got_ref,
                      key_more_ref, member_ref, back_input_ref, q0, q1, q2, q3, k0, k1, k2, k3, v0,
                      v1, v2, v3, grad_ref, mine_ref, theirs_ref, turned_ref, both_ref, weight_ref):
    groups, width, channels = back_values_ref.shape
    model = flat_ref.shape[1]
    scale = HEAD_DIM ** (-0.25)
    member = member_ref[...]
    count = count_ref[:, 0:1]
    twice = jnp.concatenate((member, member), axis=1)
    sides = []
    for own, got, more in (
        (query_own_ref, query_got_ref, query_more_ref),
        (key_own_ref, key_got_ref, key_more_ref),
    ):
        side = sum_merge(own[...], got[...].astype(f32), flag(flags_ref, 8)) + more[...]
        sides.append(dot(twice, jnp.concatenate(two_parts(side / count), axis=0)))
    turned_ref[...] = flat_ref[...].T
    for r in range(groups):
        q, k = (q0, q1, q2, q3)[r], (k0, k1, k2, k3)[r]
        both = []
        for far, direct_ref in zip(sides, (query_direct_ref, key_direct_ref)):
            both.append((direct_ref[r] + group_of(far, r, channels)).astype(bf16))
        bias = scale * jnp.sum(both[0].astype(f32), axis=0, keepdims=True)
        bias = jnp.concatenate((bias, jnp.zeros_like(bias)), axis=1)
        at = slice(2 * r * channels, 2 * (r + 1) * channels)
        both_ref[:, at] = jnp.concatenate(both, axis=1)
        weight_ref[at, :] = jnp.concatenate((q[:channels], k[...]), axis=0)
        put_tiles(scale * dot(turned_ref[...], both_ref[:, at]), r, mine_ref, theirs_ref)
        ref = theirs_ref if r % 2 else mine_ref
        places = ref.shape[0] // 2
        more = ref.shape[1] - model // places
        for place in range(places):
            ref[(places if r >= 2 else 0) + place, model // places :] = jnp.broadcast_to(
                bias, (more, bias.shape[1])
            ).astype(bf16)
    total = back_input_ref[...] + scale * dot(both_ref[...], weight_ref[...])
    values = jnp.concatenate([back_values_ref[r] for r in range(groups)], axis=1)
    weights = jnp.concatenate([v[...] for v in (v0, v1, v2, v3)], axis=0)
    grad_ref[...] = (total + dot(values, weights)).astype(bf16)


def value_output_kernel(flat_ref, back_values_ref, back_attention_ref, context_ref, mine_ref, theirs_ref):
    flat, back = flat_ref[...].T, back_attention_ref[...].T
    for r in range(context_ref.shape[0]):
        product = (dot(back, context_ref[r]), dot(flat, back_values_ref[r]))
        put_tiles(jnp.concatenate(product, axis=1), r, mine_ref, theirs_ref)


def place_kernel(rank_ref, r0, r1, r2, r3, out_ref):
    step = pl.program_id(0)
    for k, ref in enumerate((r0, r1, r2, r3)):

        @pl.when(step == k)
        def _():
            out_ref[0] = ref[...].astype(out_ref.dtype)


def place_rows(rank, blocks, dtype):
    width, model = blocks[0].shape
    return pl.pallas_call(
        place_kernel,
        out_shape=jax.ShapeDtypeStruct((len(blocks), width, model), dtype),
        grid_spec=pltpu.PrefetchScalarGridSpec(
            num_scalar_prefetch=1,
            grid=(len(blocks),),
            in_specs=[pl.BlockSpec((width, model), lambda i, rank: (0, 0))] * len(blocks),
            out_specs=pl.BlockSpec((1, width, model), lambda i, rank: (i ^ rank[0], 0, 0)),
        ),
        compiler_params=pltpu.CompilerParams(vmem_limit_bytes=24 << 20),
        cost_estimate=cost(2.5),
        name="place_rows",
    )(rank.reshape(1).astype(jnp.int32), *blocks)


def feed_kernel(
    flat_ref, context_ref, out0, out1, out2, out3, up0, up1, up2, up3, down0, down1, down2, down3,
    s0, s1, s2, s3, p0, p1, p2, p3, p4, p5, cotangent_ref,
    layer_ref, back_input_ref, back_attention_ref, back_context_ref, active_ref, back_hidden_ref,
    first_low_ref, back_feed_ref, sums_ref, up_sums_ref,
    slope_ref, first_ref, total_ref,
):
    outs, ups, downs = (out0, out1, out2, out3), (up0, up1, up2, up3), (down0, down1, down2, down3)
    units = up0.shape[1]
    output_bias, first_gain, first_shift, down_bias, second_gain, second_shift = [
        p[...].astype(f32).reshape(1, flat_ref.shape[1]) for p in (p0, p1, p2, p3, p4, p5)
    ]

    def mean(value):
        return jnp.mean(value, axis=1, keepdims=True)

    attention = dot(context_ref[0], out0[...])
    for r in range(1, len(outs)):
        attention = attention + dot(context_ref[r], outs[r][...])
    value = flat_ref[...].astype(f32) + attention + output_bias
    centred = value - mean(value)
    first_inverse = lax.rsqrt(mean(centred * centred) + epsilon)
    first_normed = centred * first_inverse
    first_ref[...] = first_normed
    first_out = first_normed * first_gain + first_shift
    first_low_ref[...] = first_out.astype(bf16)
    total_ref[...] = first_out + down_bias
    for r in range(len(ups)):
        at = slice(r * units, (r + 1) * units)
        hidden = dot(first_low_ref[...], ups[r][...]) + small_row((s0, s1, s2, s3)[r], 8, units)
        cdf = 0.5 * (1.0 + lax.erf(hidden * 0.7071067811865476))
        slope_ref[:, at] = cdf + hidden * (0.3989422804014327 * jnp.exp(-0.5 * hidden * hidden))
        active = (hidden * cdf).astype(bf16)
        active_ref[:, at] = active
        total_ref[...] += dot(active, downs[r][...])

    value = total_ref[...]
    centred = value - mean(value)
    second_inverse = lax.rsqrt(mean(centred * centred) + epsilon)
    normed = centred * second_inverse
    layer_ref[...] = (normed * second_gain + second_shift).astype(bf16)
    upstream = cotangent_ref[...].astype(f32)
    sums_ref[4:5, :] = jnp.sum(upstream * normed, axis=0, keepdims=True)
    sums_ref[5:6, :] = jnp.sum(upstream, axis=0, keepdims=True)
    scaled = upstream * second_gain
    back_second = (scaled - mean(scaled) - normed * mean(scaled * normed)) * second_inverse
    back_feed = back_second.astype(bf16)
    back_feed_ref[...] = back_feed
    sums_ref[3:4, :] = jnp.sum(back_feed.astype(f32), axis=0, keepdims=True)
    total_ref[...] = back_second
    for r in range(len(ups)):
        at = slice(r * units, (r + 1) * units)
        back_active = dot_t(back_feed_ref[...], downs[r][...])
        back_hidden = (back_active * slope_ref[:, at]).astype(bf16)
        back_hidden_ref[:, at] = back_hidden
        up_sums_ref[:, at] = jnp.sum(back_hidden.astype(f32), axis=0, keepdims=True)
        total_ref[...] += dot_t(back_hidden, ups[r][...])

    back_first = total_ref[...]
    first_normed = first_ref[...]
    sums_ref[1:2, :] = jnp.sum(back_first * first_normed, axis=0, keepdims=True)
    sums_ref[2:3, :] = jnp.sum(back_first, axis=0, keepdims=True)
    scaled = back_first * first_gain
    back_input = (scaled - mean(scaled) - first_normed * mean(scaled * first_normed)) * first_inverse
    back_input_ref[...] = back_input
    back_attention = back_input.astype(bf16)
    back_attention_ref[...] = back_attention
    sums_ref[0:1, :] = jnp.sum(back_attention.astype(f32), axis=0, keepdims=True)
    for r in range(len(outs)):
        back_context_ref[r] = dot_t(back_attention, outs[r][...]).astype(bf16)


def feed_layer(flat, context, outputs, ups, downs, smalls, params, cotangent):
    width, model = flat.shape
    ranks, units = len(ups), ups[0].shape[1]
    channels = outputs[0].shape[0]
    shape = jax.ShapeDtypeStruct
    whole = pl.BlockSpec(memory_space=pltpu.VMEM)
    return pl.pallas_call(
        feed_kernel,
        out_shape=(
            shape((width, model), bf16),
            shape((width, model), f32),
            shape((width, model), bf16),
            shape((ranks, width, channels), bf16),
            shape((width, ranks * units), bf16),
            shape((width, ranks * units), bf16),
            shape((width, model), bf16),
            shape((width, model), bf16),
            shape((6, model), f32),
            shape((1, ranks * units), f32),
        ),
        in_specs=[whole] * (15 + len(smalls) + len(params)),
        out_specs=(whole,) * 10,
        scratch_shapes=[
            pltpu.VMEM((width, ranks * units), f32),
            pltpu.VMEM((width, model), f32),
            pltpu.VMEM((width, model), f32),
        ],
        compiler_params=pltpu.CompilerParams(vmem_limit_bytes=VMEM_LIMIT),
        cost_estimate=cost(19.0),
        name="feed_layer",
    )(flat, context, *outputs, *ups, *downs, *smalls, *params, cotangent)


def per_device(
    tokens,
    query_weight,
    query_bias,
    key_weight,
    value_weight,
    value_bias,
    conv_weight,
    output_weight,
    output_bias,
    first_gain,
    first_shift,
    up_weight,
    up_bias,
    down_weight,
    down_bias,
    second_gain,
    second_shift,
    segment_sizes,
    cotangent,
):
    rows, width, model = tokens.shape
    channels = query_weight.shape[1]
    ranks = lax.axis_size("tp")
    own_heads = channels // HEAD_DIM
    heads = ranks * own_heads
    hidden_units = up_weight.shape[1]
    items = segment_sizes.shape[1]
    marks = segment_sizes.shape[2]
    reach = TAPS // 2
    device = lax.axis_index("seq")
    rank = lax.axis_index("tp")
    group = SPAN // width
    groups = segment_sizes.shape[0] // rows
    place = jnp.stack((rank * groups + device // group, device % group)).astype(jnp.int32)

    half = ((2, width, channels), bf16)
    full = ((ranks, width, channels), bf16)
    full32 = ((ranks, width, channels), f32)
    edge = ((reach, model), bf16)
    marked = ((marks, model), f32)
    message = ((marks, model), bf16)
    tall = ((marks, LANES), f32)
    squares = ((heads // 2, marks, LANES), f32)
    half_sweeps = SWEEPS // 2
    saved = ((half_sweeps, 4, heads // 2, marks, LANES), f32)

    turned = [w.T for w in (query_weight, key_weight, value_weight)]
    (query_own,) = call(small_kernel, (((channels + SMALL_ROWS, model), bf16),), "small")(
        turned[0], query_bias, value_bias, conv_weight, conv_weight[:, ::-1], up_bias
    )
    key_far, key_core = swap(turned[1], "tp", 2), swap(turned[1], "tp", 1)
    query_far, query_core = swap(query_own, "tp", 2), swap(query_own, "tp", 1)
    query_blocks, key_blocks = [query_own, query_core], [turned[1], key_core]
    member, member_turned, count, flags = call(
        layout_kernel,
        (((width, marks), bf16), ((marks, width), bf16), tall, ((16, LANES), f32)),
        "layout",
        scalars=1,
    )(place, segment_sizes)
    flat = lax.dynamic_index_in_dim(tokens, rank, axis=0, keepdims=False)
    upstream = lax.dynamic_index_in_dim(cotangent, rank, axis=0, keepdims=False)

    def shards(own, far):
        return (own, swap(own, "tp", 1), far, swap(far, "tp", 1))

    query, keys, sums, first_step = [], [], [], flags
    for pair in range(2):
        q, k, part, sent = call(
            query_key_kernel, (half, half, marked, message), "query_key", us=2.5,
        )(
            after(flat, first_step),
            query_blocks[2 * pair],
            key_blocks[2 * pair],
            query_blocks[2 * pair + 1],
            key_blocks[2 * pair + 1],
            member_turned,
        )
        query.append(q)
        keys.append(k)
        if pair == 0:
            land = Exchange(plain_parts(), "land", flags, part, sent).first()
            first_step = land.own
            query_far, key_far = after(query_far, first_step), after(key_far, first_step)
            query_blocks += [query_far, swap(query_far, "tp", 1)]
            key_blocks += [key_far, swap(key_far, "tp", 1)]
            value_far = swap(after(turned[2], query_far, key_far), "tp", 2)
            output_far = swap(after(output_weight, query_far, key_far), "tp", 2)
        else:
            land = Exchange(plain_parts(), "land", flags, part, sent).first()
            first_step = land.own
        sums += [land.next().own, land.got()]
    smalls = query_blocks
    up_far = swap(after(up_weight, value_far, output_far, land.own), "tp", 2)
    value_blocks = shards(turned[2], value_far)
    output_blocks = shards(output_weight, output_far)
    up_blocks = shards(up_weight, up_far)
    land_query, land_key, kernel = call(land_kernel, (message, message, squares), "land")(
        flags, count, *sums
    )
    values, value_head, value_tail = call(
        value_kernel, (full, edge, edge), "values", us=2.0
    )(after(flat, output_far), *value_blocks, *smalls)

    def neighbours(head, tail):
        count = lax.axis_size("seq")
        before = lax.ppermute(tail, "seq", [(i, i + 1) for i in range(count - 1)])
        behind = lax.ppermute(head, "seq", [(i + 1, i) for i in range(count - 1)])
        return before, behind

    value_before, value_after = neighbours(value_head, value_tail)
    state, sent = call(
        key_kernel,
        (((marks, model + LANES), f32), ((marks, model + LANES), bf16)),
        "key_softmax",
        us=1.4,
    )(*keys, values, land_query)
    inverse, saved_first = call(newton_first_kernel, (squares, saved), "newton_first", us=2.5)(
        after(kernel, sent)
    )
    soft = Exchange(soft_parts(heads), "soft", flags, state, sent).first(inverse)
    down_far = swap(after(down_weight, up_far, soft.own), "tp", 2)
    inverse, saved_last = call(newton_next_kernel, (squares, saved), "newton_next", us=2.3)(
        kernel, after(inverse, soft.own)
    )
    state, state_got = soft.next().own, soft.got()
    (token_weights,) = call(
        token_kernel, (((ranks, own_heads * marks, width), f32),), "token_softmax", us=0.8,
    )(*query, land_key)
    down_core = swap(after(down_weight, sent), "tp", 1)
    context, mixed, mixed_low, stats = call(
        context_kernel, (full, marked, message, tall), "context", us=2.0,
    )(
        after(state, *output_blocks, *up_blocks, down_core), state_got, inverse, token_weights, values, value_before, value_after, flags,
        *smalls,
    )

    down_blocks = (down_weight, down_core, down_far, swap(after(down_far, context), "tp", 1))
    params = (output_bias, first_gain, first_shift, down_bias, second_gain, second_shift)
    (
        layer_out,
        back_input,
        back_attention,
        back_context,
        active,
        back_hidden,
        first_low,
        back_feed,
        norm_sums,
        up_sums,
    ) = feed_layer(
        flat, context, output_blocks, up_blocks, down_blocks, smalls, params, upstream
    )

    layer_far = swap(layer_out, "tp", 2)
    positions = lax.axis_size("seq")
    levels = list(range(positions.bit_length() - 1))
    bits = jnp.stack([(device >> level) & 1 for level in levels]).astype(jnp.int32)
    wide_tiles = (((2 * positions, model // positions, hidden_units), bf16),) * 2
    weight_gradient = call(
        weight_gradient_kernel, wide_tiles, "weight_gradient",
        scratch=(pltpu.VMEM((model, width), bf16),), us=4.5,
    )
    part_back, sent_back, part_key, sent_key, query_direct, back_head, back_tail = call(
        token_back_kernel, (marked, message, marked, message, full32, edge, edge), "token_back",
        us=1.8,
    )(back_context, token_weights, mixed_low, *query, land_key)
    turn = levels[:1] + ["far"] + levels[1:]
    up = Scatter("up", *weight_gradient(after(first_low, sent_back), back_hidden), bits, turn)
    back = Exchange(plain_parts(), "back", flags, part_back, sent_back).first(up.send)
    down = Scatter(
        "down", *weight_gradient(after(back_feed, back.own), active), bits, ["far"] + levels
    )
    key_side = Exchange(plain_parts(), "back_key", flags, part_key, sent_key).first()
    back_before, back_after = neighbours(*[after(x, back.own) for x in (back_head, back_tail)])
    back.next(down.send, key_side.own, *up.hop(), back_before, back_after)
    up.wait_for(back_before, back_after)
    back_inverse, back_mixed = call(seed_kernel, (squares, message), "seed")(
        flags, after(back.own, *down.hop()), back.got(), inverse, mixed
    )
    up.wait_for(key_side.own)
    part_query, sent_query, key_direct, values_direct = call(
        key_back_kernel, (marked, message, full32, full32), "key_back", us=2.4
    )(*keys, values, land_query, stats, mixed, back_mixed)
    newton_back = call(newton_back_kernel, (squares, squares), "newton_back", us=6.6)
    back_middle = newton_back(
        kernel, saved_last, after(back_inverse, sent_query), jnp.zeros(*squares)
    )
    query_side = Exchange(plain_parts(), "back_query", flags, part_query, sent_query)
    down.wait_for(layer_far)
    first_step = query_side.first(*back_middle, *up.hop(), layer_far).own
    back_values, value_bias_sums, tap_rows = call(
        conv_back_kernel, (full, ((ranks, channels), f32), ((heads, 2 * LANES), f32)), "conv_back",
        us=3.0,
    )(
        back_context, back_before, back_after, values, value_before, value_after, flags,
        values_direct, *smalls,
    )
    query_side.next(back_values)
    tiles = (((2 * positions, model // positions, 2 * channels), bf16),) * 2
    value_output = call(value_output_kernel, tiles, "value_output", us=2.0)(
        flat, after(back_values, query_side.own), back_attention, context
    )
    value_output = Scatter("value_output", *value_output, bits, ["far"] + levels)
    back_start, back_kernel = newton_back(
        kernel, saved_first, after(back_middle[0], query_side.own), back_middle[1]
    )
    query_more, key_more = call(land_back_kernel, (marked, marked), "land_back")(
        kernel, back_start, back_kernel, land_query, land_key
    )
    key_side.message = after(key_side.message, query_side.own)
    key_side.next()
    ready = value_output.hop(query_side.own)
    up.wait_for(*ready)
    ready = [*ready, *down.hop(query_more)]
    bundle_rows = 4 * ranks + norm_sums.shape[0]
    (bundle,) = call(
        bundle_kernel, (((bundle_rows + -bundle_rows % 8, model), f32),), "bundle", scalars=1
    )(rank.reshape(1).astype(jnp.int32), up_sums, value_bias_sums, tap_rows, norm_sums)
    rows_here = model // positions
    bias_rows = rows_here + -rows_here % 16
    taller = (((2 * positions, bias_rows + 16, 2 * channels), bf16),) * 2
    grad_row, *projection = call(
        input_back_kernel,
        (((width, model), bf16),) + taller,
        "input_back",
        scratch=(
            pltpu.VMEM((model, width), bf16),
            pltpu.VMEM((width, 2 * model), bf16),
            pltpu.VMEM((2 * model, model), bf16),
        ),
        us=5.0,
        limit=24 << 20,
    )(
        flags, count, flat, query_direct, key_direct, back_values,
        after(query_side.own, *ready), query_side.got(), query_more,
        key_side.own, key_side.got(), key_more, member, back_input, *query_blocks, *key_blocks,
        *value_blocks,
    )
    projection = Scatter("projection", *projection, bits, turn)
    layer_blocks = shards(layer_out, layer_far)
    step = projection.hop()
    down.wait_for(*step)
    step = value_output.hop(*step)
    up.wait_for(*step)
    step = projection.hop(*step)
    grad_far = swap(after(grad_row, *step), "tp", 2)
    bundle = bundle + swap(after(bundle, *step), "tp", 1)
    step = up.hop(*step)
    step = down.hop(*step, other=value_output)
    bundle = bundle + swap(after(bundle, *step), "seq", 1)
    layer_rows = place_rows(rank, (after(layer_blocks[0], *step),) + layer_blocks[1:], bf16)
    step = projection.hop(*step, layer_rows, bundle)
    step = up.hop(*step)
    step = projection.hop(*step)
    bundle = bundle + swap(after(bundle, *step), "tp", 2)
    step = down.hop(*step)
    grad_blocks = shards(grad_row, grad_far)
    grad_tokens = place_rows(rank, (after(grad_blocks[0], *step),) + grad_blocks[1:], f32)
    size = 2
    while size < positions:
        bundle = bundle + swap(after(bundle, *step), "seq", size)
        size *= 2
    step = up.hop(*step)
    for scatter in (projection, up, down):
        while scatter.hops:
            scatter.hop()
        if scatter.keep.dtype == bf16:
            scatter.hop()
    grad_up_weight = up.keep[0]
    grad_down_weight = down.keep[0][:, :hidden_units]
    grad_output_weight = down.keep[0][:, hidden_units : hidden_units + channels].T
    grad_value_weight = down.keep[0][:, hidden_units + channels :]
    projection = projection.keep[0]
    share = HEAD_DIM // positions
    grad_query_bias = lax.dynamic_slice_in_dim(
        projection[rows_here, :channels].reshape(own_heads, HEAD_DIM), device * share, share, axis=1
    )
    own = lax.dynamic_slice_in_dim(bundle, 4 * rank, 4, axis=0)
    grad_up_bias = own[0]
    grad_value_bias = own[1, :channels].reshape(own_heads, HEAD_DIM)
    grad_conv_weight = own[2].reshape(own_heads, 2 * LANES)[:, STRIPE - 1 : STRIPE - 1 + TAPS]
    shared = [bundle[4 * ranks + k] for k in range(6)]
    return (
        layer_rows,
        grad_tokens,
        projection[:rows_here, :channels],
        grad_query_bias,
        projection[:rows_here, channels:],
        grad_value_weight,
        grad_value_bias,
        grad_conv_weight,
        grad_output_weight,
        shared[0],
        shared[1],
        shared[2],
        grad_up_weight,
        grad_up_bias,
        grad_down_weight.T,
        shared[3],
        shared[4],
        shared[5],
    )


def solution(mesh):
    placed = (
        P(None, "seq", None),
        P(None, "tp"),
        P("tp", None),
        P(None, "tp"),
        P(None, "tp"),
        P("tp", None),
        P("tp", None),
        P("tp", None),
        P(),
        P(),
        P(),
        P(None, "tp"),
        P("tp"),
        P("tp", None),
        P(),
        P(),
        P(),
        P(),
        P(None, "seq", None),
    )
    return jax.shard_map(
        per_device,
        mesh=mesh,
        in_specs=placed,
        out_specs=(
            P(None, "seq", None),
            P(None, "seq", None),
            P("seq", "tp"),
            P("tp", "seq"),
            P("seq", "tp"),
            P("seq", "tp"),
            P("tp", None),
            P("tp", None),
            P("tp", "seq"),
            P(),
            P(),
            P(),
            P("seq", "tp"),
            P("tp"),
            P("tp", "seq"),
            P(),
            P(),
            P(),
        ),
        check_vma=False,
    )
```
